128 devices in a mesh: ctx: 32 (over x, z, y_hi), fsdp: 4 (over y_lo, core).
Axes of the slice: x: 4, y: 4 (y_hi: 2, y_lo: 2; y = y_hi * 2 + y_lo), z: 4, core: 2. Of those that a mesh axis runs over, the one named last changes fastest.
Arguments:
- block_input: bfloat16 [4, 4096, 1024], P('fsdp', 'ctx'), may hold values from -6 to 6
- routes: int32 [4, 4096, 8], P('fsdp', 'ctx'), may hold values from 0 to 31, all different within a row; in each aligned block of 128 rows (0 to 127, 128 to 255, ..., all dimensions but the last counted through in order) at most 48 rows name the same one
- block_pairs: int32 [32], replicated, may hold values from 0 to 31, each once
- norm1_gain: bfloat16 [1024], P('fsdp'), may hold values from 0.5 to 1.5
- w_query: bfloat16 [1024, 1024], P('fsdp'), may hold values from -0.75 to 0.75
- w_key: bfloat16 [1024, 512], P('fsdp'), may hold values from -0.75 to 0.75
- w_value: bfloat16 [1024, 512], P('fsdp'), may hold values from -0.1875 to 0.1875
- w_out: bfloat16 [1024, 1024], P('fsdp'), may hold values from -4 to 4
- norm2_gain: bfloat16 [1024], P('fsdp'), may hold values from 0.5 to 1.5
- w_router: bfloat16 [1024, 32], P('fsdp'), may hold values from -0.09375 to 0.09375
- w_gate: bfloat16 [32, 1024, 512], P('ctx', 'fsdp'), may hold values from -0.1875 to 0.1875
- w_up: bfloat16 [32, 1024, 512], P('ctx', 'fsdp'), may hold values from -0.1875 to 0.1875
- w_down: bfloat16 [32, 512, 1024], P('ctx', 'fsdp'), may hold values from -4 to 4
- cotangent: bfloat16 [4, 4096, 1024], P('fsdp', 'ctx'), may hold values from -6 to 6
Outputs:
- block_output: bfloat16 [4, 4096, 1024], P('fsdp', 'ctx')
- input_grad: float32 [4, 4096, 1024], P('fsdp', 'ctx')
- norm1_gain_grad: float32 [1024], P('fsdp')
- w_query_grad: float32 [1024, 1024], P('fsdp')
- w_key_grad: float32 [1024, 512], P('fsdp')
- w_value_grad: float32 [1024, 512], P('fsdp')
- w_out_grad: float32 [1024, 1024], P('fsdp')
- norm2_gain_grad: float32 [1024], P('fsdp')
- w_router_grad: float32 [1024, 32], P('fsdp')
- w_gate_grad: float32 [32, 1024, 512], P('ctx', 'fsdp')
- w_up_grad: float32 [32, 1024, 512], P('ctx', 'fsdp')
- w_down_grad: float32 [32, 512, 1024], P('ctx', 'fsdp')
The draws below stay inside these ranges and needn't reach their ends.
Inputs may be any that keep to these rules, and one draw needn't show every extreme that they name: `routes`: each row names 8 different experts; among the 128 rows of one device no expert is named more than 48 times, a bound that some block reaches. `block_pairs`: each number appears once. Index c of ctx holds, in this order, the blocks of half of 128 tokens numbered block_pairs[c] and 63 - block_pairs[c].
All inputs are finite; a program needn't handle non-finite values.
Results may differ from the reference program's by a relative error of at most 0.035.
Values may be sent and summed in bfloat16 or wider, within the bound.
No kernel may reach another device: no remote copies, remote signals or barrier semaphores. Data moves between devices by JAX's collectives and lax.ppermute only.
A program may use at most 128 MiB of HBM per device.

```python
import math
import jax
import jax.numpy as jnp
import numpy as np
from jax import lax

D = 1024
HEADS = 16
KV_HEADS = 8
HEAD_DIM = 64
FF = 512
EXPERTS = 32
TOP = 8
TOK_DEV = 128
CAP = 48
SEQ = 4096
NSEQ = 4
N_CTX = 32


def levels(key, dims, split, low, high):
    level, own = 1.0, jax.random.fold_in(key, 6)
    for dim, shards_of in split:
        draws = jnp.exp(jax.random.uniform(jax.random.fold_in(own, dim), (shards_of,), jnp.float32, low / len(split), high / len(split)))
        level = level * jnp.repeat(draws, dims[dim] // shards_of).reshape([-1 if axis == dim else 1 for axis in range(len(dims))])
    return level


def shared_out(key, own, number, rows, count, top, most, slope):
    sequence = jax.random.permutation(key, count)
    heavy_load, ordinary = portions_of(count, rows * top, most, slope, True), portions_of(count, rows * top, most, slope, False)
    places = jnp.arange(count)

    def named(lengths, turn):
        used = int((lengths > 0).sum())
        fixed = max(1, used // 4)
        passed = fixed + (places - fixed + turn * (used - fixed)) % max(1, count - fixed)
        return jnp.zeros((count,), jnp.int32).at[sequence[jnp.where(places < fixed, places, passed)]].set(jnp.asarray(lengths, jnp.int32))

    lengths = jnp.where(number % 4 == 0, named(heavy_load, number // 4), named(ordinary, number - number // 4 - 1))
    mixed = jax.random.permutation(jax.random.fold_in(own, 3), count)
    source_of, taker = mixed[0:count // 2 * 2:2], mixed[1:count // 2 * 2:2]
    margin = jnp.minimum(lengths[source_of] - 1, most - lengths[taker]) // 2
    margin = jnp.where((source_of == sequence[0]) | (taker == sequence[0]) | (lengths[taker] == 0), 0, jnp.maximum(margin, 0))
    passed = jax.random.randint(jax.random.fold_in(own, 4), (count // 2,), 0, 1 << 20) % (margin + 1)
    lengths = lengths.at[source_of].add(-passed).at[taker].add(passed)
    items = jnp.searchsorted(jnp.cumsum(lengths), jnp.arange(rows * top), side="right").astype(jnp.int32)
    table = items.reshape(top, rows).T
    table = table[jax.random.permutation(jax.random.fold_in(own, 1), rows)]
    turn = jax.random.randint(jax.random.fold_in(own, 2), (rows, 1), 0, top)
    return jnp.take_along_axis(table, (jnp.arange(top)[None, :] + turn) % top, axis=1)


def portions_of(count, total, bound, lean, full):
    loads = [(1 << 20) // math.isqrt(grade ** lean) + 1 for grade in range(1, count + 1)]
    largest = bound if full else min(bound, max(-(-total // count), total * loads[0] // sum(loads)))
    least = 1 if total - largest >= count - 1 else 0
    holding, surplus = [largest] + [least] * (count - 1), total - largest - least * (count - 1)
    while surplus > 0:
        movable = [i for i in range(1, count) if holding[i] < largest] or [i for i in range(1, count) if holding[i] < bound]
        mass, remaining = sum([loads[i] for i in movable]), surplus
        for i in movable:
            more = min(bound - holding[i], max(1, remaining * loads[i] // mass), surplus)
            holding[i] = holding[i] + more
            surplus = surplus - more
    return np.array(holding)


def normal_values(rng, dims, scale, reach, shards=(), kind=jnp.bfloat16):
    values = scale * jax.random.normal(rng, dims, jnp.float32)
    if shards:
        values = values * levels(rng, dims, shards, -0.22, 0.18)
    return jnp.clip(values, -reach, reach).astype(kind)


def setup_inputs(seed: int = 0) -> dict:
    splits = jax.random.split(jax.random.key(seed), 15)
    block_input = normal_values(splits[0], (NSEQ, SEQ, D), 1.0, 6.0, ((0, 4), (1, 32)))
    routes_keys = jax.random.split(jax.random.fold_in(splits[1], 1), NSEQ * SEQ // TOK_DEV)
    routes_turns = jax.random.permutation(jax.random.fold_in(splits[1], 3), NSEQ * SEQ // TOK_DEV)
    routes = jax.vmap(lambda own, number: shared_out(jax.random.fold_in(splits[1], 2), own, number, TOK_DEV, EXPERTS, TOP, CAP, 2))(routes_keys, routes_turns).reshape((NSEQ, SEQ, TOP))
    block_pairs = jax.random.permutation(splits[2], N_CTX).astype(jnp.int32)
    norm1_gain = jnp.clip(1.0 + 0.1 * jax.random.normal(splits[3], (D,), jnp.float32), 0.5, 1.5).astype(jnp.bfloat16)
    w_query = normal_values(splits[4], (D, HEADS * HEAD_DIM), (D // 16) ** -0.5, 0.75, ((0, 4),))
    w_key = normal_values(splits[5], (D, KV_HEADS * HEAD_DIM), (D // 16) ** -0.5, 0.75, ((0, 4),))
    w_value = normal_values(splits[6], (D, KV_HEADS * HEAD_DIM), D ** -0.5, 0.1875, ((0, 4),))
    w_out = normal_values(splits[7], (HEADS * HEAD_DIM, D), 2 ** -0.5, 4.0, ((0, 4),))
    norm2_gain = jnp.clip(1.0 + 0.1 * jax.random.normal(splits[8], (D,), jnp.float32), 0.5, 1.5).astype(jnp.bfloat16)
    w_router = normal_values(splits[9], (D, EXPERTS), (4 * D) ** -0.5, 0.09375, ((0, 4),))
    w_gate = normal_values(splits[10], (EXPERTS, D, FF), D ** -0.5, 0.1875, ((0, 32), (1, 4)))
    w_up = normal_values(splits[11], (EXPERTS, D, FF), D ** -0.5, 0.1875, ((0, 32), (1, 4)))
    w_down = normal_values(splits[12], (EXPERTS, FF, D), 2 ** -0.5, 4.0, ((0, 32), (1, 4)))
    cotangent = normal_values(splits[13], (NSEQ, SEQ, D), 1.0, 6.0, ((0, 4), (1, 32)))
    return dict(block_input=block_input, routes=routes, block_pairs=block_pairs, norm1_gain=norm1_gain, w_query=w_query, w_key=w_key, w_value=w_value, w_out=w_out, norm2_gain=norm2_gain, w_router=w_router, w_gate=w_gate, w_up=w_up, w_down=w_down, cotangent=cotangent)


epsilon = 1e-06
attn_scale = 0.015625
residual_scale = 0.22
masked_value = -1e+30

@jax.custom_vjp
def low(v):
    return lax.optimization_barrier(v.astype(jnp.bfloat16)).astype(jnp.float32)

@jax.custom_vjp
def low_back(v):
    return v

def low_keep(v):
    return (low(v), None)

def low_pass(kept, grad):
    return (grad,)

def back_keep(v):
    return (v, None)

def back_low(kept, grad):
    return (low(grad),)
low.defvjp(low_keep, low_pass)
low_back.defvjp(back_keep, back_low)

def matmul(left, right):
    return jnp.einsum('...i,ij->...j', left, right, precision=lax.Precision.HIGHEST)

def positions_of(rows, block_pairs, tok_rows, ctx_count):
    device = rows // tok_rows
    local = rows % tok_rows
    half_rows = tok_rows // 2
    first = lax.optimization_barrier(jnp.sum(jnp.where(device[:, None] == jnp.arange(ctx_count, dtype=jnp.int32)[None, :], block_pairs[None, :], 0), axis=1)).astype(jnp.int32)
    number = jnp.where(local < half_rows, first, 2 * ctx_count - 1 - first)
    return (number * half_rows + local % half_rows).astype(jnp.int32)

def rope_tables(positions, head_width):
    freqs = jnp.power(10000.0, -jnp.arange(0, head_width, 2, dtype=jnp.float32) / head_width)
    angles = positions.astype(jnp.float32)[:, None] * freqs[None, :]
    angles = jnp.concatenate([angles, angles], axis=-1)
    return (jnp.cos(angles), jnp.sin(angles))

def rotate(values, cosine, sine):
    middle = values.shape[-1] // 2
    turned = jnp.concatenate([-values[..., middle:], values[..., :middle]], axis=-1)
    return values * cosine[:, None, :] + turned * sine[:, None, :]

def attend(query_rows, key_rows, value_rows, positions):
    group_share = HEADS // KV_HEADS
    length = query_rows.shape[0]
    span_rows = math.gcd(512, length)

    def one_span(pieces):
        queries, query_pos = pieces
        grouped = queries.reshape(span_rows, KV_HEADS, group_share, HEAD_DIM)
        scores = jnp.einsum('qjgd,kjd->jgqk', grouped, key_rows, precision=lax.Precision.HIGHEST) * attn_scale
        scores = jnp.where(positions[None, None, None, :] <= query_pos[None, None, :, None], scores, masked_value)
        scores = low_back(scores)
        attn_probs = low(jax.nn.softmax(scores, axis=-1))
        mixed = jnp.einsum('jgqk,kjd->qjgd', attn_probs, value_rows, precision=lax.Precision.HIGHEST)
        return mixed.reshape(span_rows, HEADS * HEAD_DIM)
    spans = (query_rows.reshape(length // span_rows, span_rows, HEADS, HEAD_DIM), positions.reshape(length // span_rows, span_rows))
    return lax.map(jax.checkpoint(one_span), spans).reshape(length, HEADS * HEAD_DIM)

def experts_one(pieces, w_gate, w_up, w_down):
    normed, chosen = pieces
    length = normed.shape[0]
    width = normed.shape[1]
    blocks = length // TOK_DEV
    flat_routes = chosen.reshape(blocks, TOK_DEV * TOP)
    onehot = (flat_routes[..., None] == jnp.arange(EXPERTS, dtype=jnp.int32)).astype(jnp.int32)
    slot_rank = lax.optimization_barrier(jnp.sum((jnp.cumsum(onehot, axis=1) - onehot) * onehot, axis=-1))
    slot_index = ((flat_routes * blocks + jnp.arange(blocks, dtype=jnp.int32)[:, None]) * CAP + slot_rank).reshape(-1).astype(jnp.int32)
    route_rows = jnp.repeat(normed, TOP, axis=0)
    buffer = jnp.zeros((EXPERTS * blocks * CAP, width), jnp.float32).at[slot_index].set(route_rows)
    buffer = low_back(buffer).reshape(EXPERTS, blocks * CAP, width)
    gate_pre = low_back(jnp.einsum('erd,edf->erf', buffer, w_gate, precision=lax.Precision.HIGHEST))
    up_pre = low_back(jnp.einsum('erd,edf->erf', buffer, w_up, precision=lax.Precision.HIGHEST))
    inner_act = low(jax.nn.silu(gate_pre) * up_pre)
    expert_out = low(low_back(jnp.einsum('erf,efd->erd', inner_act, w_down, precision=lax.Precision.HIGHEST)))
    return expert_out.reshape(-1, width)[slot_index].reshape(length, TOP, width)

def forward(inputs, gain_one, w_query, w_key, w_value, w_out, gain_two, w_router, w_gate, w_up, w_down, routes, positions):
    cosine, sine = rope_tables(positions, HEAD_DIM)
    nseqs, length, width = inputs.shape
    inv_rms1 = lax.rsqrt(lax.optimization_barrier(jnp.mean(inputs * inputs, axis=-1, keepdims=True)) + epsilon)
    normed1 = low(inputs * inv_rms1 * gain_one)
    queries = low_back(matmul(normed1, w_query)).reshape(nseqs, length, HEADS, HEAD_DIM)
    queries = low(rotate(queries, cosine, sine))
    keys = low_back(matmul(normed1, w_key)).reshape(nseqs, length, KV_HEADS, HEAD_DIM)
    keys = low(rotate(keys, cosine, sine))
    values = low(low_back(matmul(normed1, w_value))).reshape(nseqs, length, KV_HEADS, HEAD_DIM)
    mixed = lax.map(lambda parts: attend(parts[0], parts[1], parts[2], positions), (queries, keys, values))
    mixed = low(low_back(mixed))
    hidden = inputs + residual_scale * low_back(matmul(mixed, w_out))
    inv_rms2 = lax.rsqrt(lax.optimization_barrier(jnp.mean(hidden * hidden, axis=-1, keepdims=True)) + epsilon)
    normed2 = low(hidden * inv_rms2 * gain_two)
    logits = low_back(matmul(normed2, w_router))
    selected = jnp.take_along_axis(logits, routes, axis=-1)
    gate_probs = jax.nn.softmax(selected, axis=-1)
    expert_fn = jax.checkpoint(lambda parts: experts_one(parts, w_gate, w_up, w_down))
    expert_out = lax.map(expert_fn, (normed2, routes))
    mixture = lax.optimization_barrier(jnp.sum(gate_probs[..., None] * expert_out, axis=2))
    return hidden + residual_scale * mixture

def reference(block_input, routes, block_pairs, norm1_gain, w_query, w_key, w_value, w_out, norm2_gain, w_router, w_gate, w_up, w_down, cotangent):
    positions = positions_of(jnp.arange(TOK_DEV * N_CTX, dtype=jnp.int32), block_pairs, TOK_DEV, N_CTX)

    def run(inputs, gain_one, wq_f, wk_f, wv_f, wo_f, gain_two, wr_f, wg_f, wu_f, wd_f):
        return forward(inputs, gain_one, wq_f, wk_f, wv_f, wo_f, gain_two, wr_f, wg_f, wu_f, wd_f, routes, positions)
    output, pull = jax.vjp(run, block_input.astype(jnp.float32), norm1_gain.astype(jnp.float32), w_query.astype(jnp.float32), w_key.astype(jnp.float32), w_value.astype(jnp.float32), w_out.astype(jnp.float32), norm2_gain.astype(jnp.float32), w_router.astype(jnp.float32), w_gate.astype(jnp.float32), w_up.astype(jnp.float32), w_down.astype(jnp.float32))
    grads = pull(cotangent.astype(jnp.float32))
    return (output.astype(jnp.bfloat16), grads[0], grads[1], grads[2], grads[3], grads[4], grads[5], grads[6], grads[7], grads[8], grads[9], grads[10])
```

```python
import functools

import jax
import jax.numpy as jnp
from jax import lax
from jax.experimental import pallas as pl
from jax.experimental.pallas import tpu as pltpu
from jax.sharding import Mesh
from jax.sharding import PartitionSpec as P

HEADS = 16
KV_HEADS = 8
HEAD_DIM = 64
EXPERTS = 32
TOP = 8
CAP = 48
HALF = 64
TILE = 512

epsilon = 1e-06
attn_scale = 0.015625
residual_scale = 0.22
masked_value = -1e30

CTX = ("x", "z", "yh")
ZY = ("z", "yh")
EVERY = ("x", "z", "yh", "yl", "core")
bf16 = jnp.bfloat16
f32 = jnp.float32


def product(left, right):
    return jnp.dot(left, right, preferred_element_type=f32)


def product_nt(left, right):
    return lax.dot_general(left, right, (((1,), (1,)), ((), ())), preferred_element_type=f32)


def product_tn(left, right):
    return lax.dot_general(left, right, (((0,), (0,)), ((), ())), preferred_element_type=f32)


def swap(values, axis):
    return lax.ppermute(values, axis, [(0, 1), (1, 0)])


def turn(values, axis, step):
    return lax.ppermute(values, axis, [(i, (i + step) % 4) for i in range(4)])


def exchange(values, axes):
    return lax.all_to_all(values, axes, 0, 0, tiled=True)


def after(values, *others):
    return lax.optimization_barrier((values,) + others)[0]


def gather_fsdp(shard):
    row, core = lax.axis_index("yl"), lax.axis_index("core")
    pair = jnp.zeros((2, 2) + shard.shape, shard.dtype)
    zero = (0,) * shard.ndim
    other = swap(shard, "yl")
    mine = lax.dynamic_update_slice(jnp.zeros((2,) + shard.shape, shard.dtype), shard[None], (row,) + zero)
    mine = lax.dynamic_update_slice(mine, other[None], (1 - row,) + zero)
    theirs = swap(mine, "core")
    pair = lax.dynamic_update_slice(pair, mine[:, None], (0, core) + zero)
    pair = lax.dynamic_update_slice(pair, theirs[:, None], (0, 1 - core) + zero)
    return pair.reshape((4,) + shard.shape)


def scatter_fsdp(parts):
    row, core = lax.axis_index("yl"), lax.axis_index("core")
    parts = parts.astype(bf16).reshape((2, 2) + parts.shape[1:])
    away = lax.dynamic_index_in_dim(parts, 1 - core, 1, keepdims=False)
    keep = lax.dynamic_index_in_dim(parts, core, 1, keepdims=False)
    both = keep.astype(f32) + swap(away, "core").astype(f32)
    away = lax.dynamic_index_in_dim(both, 1 - row, 0, keepdims=False).astype(bf16)
    keep = lax.dynamic_index_in_dim(both, row, 0, keepdims=False)
    return keep + swap(away, "yl").astype(f32)


def rope_tables(positions):
    freqs = jnp.power(10000.0, -jnp.arange(0, HEAD_DIM, 2, dtype=f32) / HEAD_DIM)
    angles = positions.astype(f32)[:, None] * freqs[None, :]
    angles = jnp.concatenate([angles, angles], axis=-1)
    return (jnp.cos(angles), jnp.sin(angles))


def rotate(values, cosine, sine):
    middle = HEAD_DIM // 2
    turned = jnp.concatenate([-values[..., middle:], values[..., :middle]], axis=-1)
    return values * cosine + turned * sine


def rotate_back(grads, cosine, sine):
    middle = HEAD_DIM // 2
    scaled = grads * sine
    turned = jnp.concatenate([scaled[..., middle:], -scaled[..., :middle]], axis=-1)
    return grads * cosine + turned


def norm_back(values, inv_rms, gain, grad):
    weighted = grad * gain
    gain_grad = jnp.sum(grad * values * inv_rms, axis=0)
    inner_mean = jnp.mean(weighted * values, axis=-1, keepdims=True)
    return (weighted * inv_rms - values * inv_rms * inv_rms * inv_rms * inner_mean, gain_grad)


def half(index):
    return pl.ds(pl.multiple_of(index * HALF, HALF), HALF)


def key_tile(counter):
    return pl.ds(pl.multiple_of(counter * TILE, TILE), TILE)


def sort_keys(knum_ref, kv_refs, kvs, kvt):
    blocks = kv_refs[0].shape[0] // HALF
    for slot, kv_ref in enumerate(kv_refs):
        for block in range(blocks):
            kvs[half(knum_ref[slot * blocks + block]), :] = kv_ref[block * HALF : (block + 1) * HALF, :]
    for tile in range(kvs.shape[0] // TILE):
        part = kvs[tile * TILE : (tile + 1) * TILE, :].astype(f32)
        kvt[:, tile * TILE : (tile + 1) * TILE] = part.T.astype(bf16)


def pair_rows(ref, first, second):
    return jnp.concatenate(
        [ref[0, half(first), :], ref[1, half(first), :], ref[0, half(second), :], ref[1, half(second), :]],
        axis=0,
    )


def pair_positions(low_number, high_number):
    column = lax.broadcasted_iota(jnp.int32, (1, 4 * HALF), 1)
    return jnp.where(column < 2 * HALF, low_number, high_number) * HALF + column % HALF


def score_tile(keys, queries, counter, positions, masked):
    scores = product_nt(keys, queries)
    if masked:
        key_pos = counter * TILE + lax.broadcasted_iota(jnp.int32, scores.shape, 0)
        scores = jnp.where(key_pos <= positions, scores, masked_value)
    return scores


def store_rows(ref, turned, first, second):
    rows = turned.T
    ref[half(first), :] = jnp.concatenate([rows[:HALF], rows[HALF : 2 * HALF]], axis=1).astype(ref.dtype)
    ref[half(second), :] = jnp.concatenate([rows[2 * HALF : 3 * HALF], rows[3 * HALF :]], axis=1).astype(ref.dtype)


def attend_kernel(order_ref, qnum_ref, knum_ref, q_ref, kv0, kv1, kv2, kv3, out_ref, turned_ref, lse_ref, kvs, kvt):
    sort_keys(knum_ref, (kv0, kv1, kv2, kv3), kvs, kvt)
    width = 4 * HALF

    @pl.loop(0, q_ref.shape[1] // (2 * HALF))
    def _(pair):
        first, second = order_ref[2 * pair], order_ref[2 * pair + 1]
        low_number, high_number = qnum_ref[first], qnum_ref[second]
        queries = pair_rows(q_ref, first, second)
        positions = pair_positions(low_number, high_number)

        def step(masked, counter, running):
            top, total, mixed = running
            scores = score_tile(kvs[key_tile(counter), :], queries, counter, positions, masked)
            new_top = jnp.maximum(top, jnp.max(scores, axis=0, keepdims=True))
            probs = jnp.exp(scores - new_top)
            shrink = jnp.exp(top - new_top)
            total = total * shrink + jnp.sum(probs, axis=0, keepdims=True)
            mixed = mixed * shrink + product(kvt[HEAD_DIM:, key_tile(counter)], probs.astype(bf16))
            return (new_top, total, mixed)

        start = (
            jnp.full((1, width), masked_value, f32),
            jnp.zeros((1, width), f32),
            jnp.zeros((HEAD_DIM, width), f32),
        )
        full = (low_number * HALF) // TILE
        last = (high_number * HALF) // TILE + 1
        running = lax.fori_loop(0, full, functools.partial(step, False), start)
        top, total, mixed = lax.fori_loop(full, last, functools.partial(step, True), running)
        mixed = mixed / total
        turned_ref[pair] = mixed
        lse_ref[pair] = top + jnp.log(total)
        store_rows(out_ref, mixed, first, second)


def attend_grad_kernel(
    order_ref, qnum_ref, knum_ref, q_ref, kv0, kv1, kv2, kv3, grad_ref, turned_ref, lse_ref,
    dq_ref, dkv0, dkv1, dkv2, dkv3, kvs, kvt, total_ref,
):
    sort_keys(knum_ref, (kv0, kv1, kv2, kv3), kvs, kvt)
    total_ref[...] = jnp.zeros_like(total_ref)
    width = 4 * HALF

    @pl.loop(0, q_ref.shape[1] // (2 * HALF))
    def _(pair):
        first, second = order_ref[2 * pair], order_ref[2 * pair + 1]
        low_number, high_number = qnum_ref[first], qnum_ref[second]
        queries = pair_rows(q_ref, first, second)
        grads = pair_rows(grad_ref, first, second)
        both = jnp.concatenate([queries, grads], axis=0)
        positions = pair_positions(low_number, high_number)
        lse = lse_ref[pair]
        dots = jnp.sum(grads.astype(f32).T[HEAD_DIM:] * turned_ref[pair], axis=0, keepdims=True)

        def step(masked, counter, query_acc):
            keys = kvs[key_tile(counter), :]
            probs = jnp.exp(score_tile(keys, queries, counter, positions, masked) - lse)
            score_grad = (probs * (product_nt(keys, grads) - dots)).astype(bf16)
            sides = jnp.concatenate([score_grad, probs.astype(bf16)], axis=1)
            total_ref[key_tile(counter), :] += product(sides, both)
            return query_acc + product(kvt[:HEAD_DIM, key_tile(counter)], score_grad)

        full = (low_number * HALF) // TILE
        last = (high_number * HALF) // TILE + 1
        query_acc = lax.fori_loop(0, full, functools.partial(step, False), jnp.zeros((HEAD_DIM, width), f32))
        query_acc = lax.fori_loop(full, last, functools.partial(step, True), query_acc)
        store_rows(dq_ref, query_acc * attn_scale, first, second)

    blocks = dkv0.shape[0] // HALF
    for slot, dkv in enumerate((dkv0, dkv1, dkv2, dkv3)):
        for block in range(blocks):
            dkv[block * HALF : (block + 1) * HALF, :] = total_ref[
                half(knum_ref[slot * blocks + block]), :
            ].astype(bf16)


SMEM = pl.BlockSpec(memory_space=pltpu.SMEM)
VMEM = pl.BlockSpec(memory_space=pltpu.VMEM)


def attend(numbers, queries, kv_parts):
    rows = queries.shape[1]
    keys = rows * len(kv_parts)
    pairs = rows // (2 * HALF)
    return pl.pallas_call(
        attend_kernel,
        out_shape=(
            jax.ShapeDtypeStruct((rows, 2 * HEAD_DIM), bf16),
            jax.ShapeDtypeStruct((pairs, HEAD_DIM, 4 * HALF), f32),
            jax.ShapeDtypeStruct((pairs, 1, 4 * HALF), f32),
        ),
        in_specs=[SMEM] * 3 + [VMEM] * 5,
        out_specs=(VMEM,) * 3,
        scratch_shapes=[pltpu.VMEM((keys, 2 * HEAD_DIM), bf16), pltpu.VMEM((2 * HEAD_DIM, keys), bf16)],
        compiler_params=pltpu.CompilerParams(vmem_limit_bytes=40 * 1024 * 1024),
        cost_estimate=pl.CostEstimate(flops=12_000_000_000, bytes_accessed=4_000_000, transcendentals=5_000_000),
    )(*numbers, queries, *kv_parts)


def attend_grad(numbers, queries, kv_parts, grads, turned, lse):
    rows = queries.shape[1]
    keys = rows * len(kv_parts)
    return pl.pallas_call(
        attend_grad_kernel,
        out_shape=(jax.ShapeDtypeStruct((rows, 2 * HEAD_DIM), f32),)
        + (jax.ShapeDtypeStruct((rows, 2 * HEAD_DIM), bf16),) * 4,
        in_specs=[SMEM] * 3 + [VMEM] * 8,
        out_specs=(VMEM,) * 5,
        scratch_shapes=[
            pltpu.VMEM((keys, 2 * HEAD_DIM), bf16),
            pltpu.VMEM((2 * HEAD_DIM, keys), bf16),
            pltpu.VMEM((keys, 2 * HEAD_DIM), f32),
        ],
        compiler_params=pltpu.CompilerParams(vmem_limit_bytes=40 * 1024 * 1024),
        cost_estimate=pl.CostEstimate(flops=30_000_000_000, bytes_accessed=6_000_000, transcendentals=5_000_000),
    )(*numbers, queries, *kv_parts, grads, turned, lse)


def block_numbers(block_pairs):
    place = lax.axis_index("x")
    groups = block_pairs.reshape(4, 8)
    groups = groups[(place - jnp.arange(4)) % 4]
    numbers = jnp.stack([groups, 63 - groups], axis=-1).reshape(-1)
    own = numbers[:16]
    rank = jnp.sum((own[None, :] < own[:, None]).astype(jnp.int32), axis=1)
    spots = jnp.arange(16, dtype=jnp.int32)
    order = jnp.sum(jnp.where(rank[None, :] == spots[:, None], spots[None, :], 0), axis=1)
    return (order, own, numbers)


def on_device(
    block_input,
    routes,
    block_pairs,
    norm1_gain,
    w_query,
    w_key,
    w_value,
    w_out,
    norm2_gain,
    w_router,
    w_gate,
    w_up,
    w_down,
    cotangent,
):
    tokens, width = block_input.shape[1:]
    head = lax.axis_index(ZY)
    expert = lax.axis_index(CTX)
    shard_rows = w_query.shape[0]
    own_input = block_input[0]

    group_input = exchange(jnp.tile(own_input, (KV_HEADS, 1)), ZY)
    by_head = jnp.concatenate(
        [
            w_query.reshape(shard_rows, KV_HEADS, 2 * HEAD_DIM),
            w_key.reshape(shard_rows, KV_HEADS, HEAD_DIM),
            w_value.reshape(shard_rows, KV_HEADS, HEAD_DIM),
        ],
        axis=2,
    )
    head_shard = lax.dynamic_index_in_dim(by_head, head, 1, keepdims=False)
    gains = jnp.stack([norm1_gain, norm2_gain])
    head_w = gather_fsdp(head_shard).reshape(width, 4 * HEAD_DIM)
    gains = gather_fsdp(gains)
    gain_one = gains[:, 0].reshape(width).astype(f32)
    gain_two = gains[:, 1].reshape(width).astype(f32)

    numbers = block_numbers(block_pairs)
    group_pos = (numbers[1][:, None] * HALF + jnp.arange(HALF, dtype=jnp.int32)[None, :]).reshape(-1)
    cosine, sine = rope_tables(group_pos)

    chosen = routes[0]
    uses = jnp.sum(
        (chosen[:, :, None] == jnp.arange(EXPERTS, dtype=jnp.int32)[None, None, :]).astype(f32), axis=1
    )
    earlier = jnp.tril(jnp.ones((tokens, tokens), bf16), -1)
    rank = product(earlier, uses.astype(bf16)).astype(jnp.int32)
    rank = jnp.where(uses > 0, rank, -1)
    slot_of = (
        rank.T[:, None, :] == jnp.arange(CAP, dtype=jnp.int32)[None, :, None]
    )
    send = slot_of.astype(bf16).reshape(EXPERTS * CAP, tokens)

    group_f = group_input.astype(f32)
    group_inv = lax.rsqrt(jnp.mean(group_f * group_f, axis=-1, keepdims=True) + epsilon)
    group_normed = (group_f * group_inv * gain_one).astype(bf16)
    projected = product(group_normed, head_w)
    key_rot = rotate(projected[:, 2 * HEAD_DIM : 3 * HEAD_DIM], cosine, sine)
    kv_own = jnp.concatenate([key_rot, projected[:, 3 * HEAD_DIM :]], axis=1).astype(bf16)
    kv_parts = [kv_own] + [turn(kv_own, "x", step) for step in (1, 2, 3)]
    queries = jnp.stack(
        [
            rotate(projected[:, :HEAD_DIM], cosine, sine),
            rotate(projected[:, HEAD_DIM : 2 * HEAD_DIM], cosine, sine),
        ]
    ).astype(bf16) * bf16(attn_scale)
    queries = jnp.pad(queries, ((0, 0), (0, 0), (0, HEAD_DIM)))

    shard_out, shard_router, shard_gu, shard_down, cot_rows, by_head = lax.optimization_barrier(
        (w_out, w_router, jnp.concatenate([w_gate[0], w_up[0]], axis=1), w_down[0], cotangent[0], by_head, kv_own)
    )[:6]
    out_w = gather_fsdp(shard_out).reshape(HEADS * HEAD_DIM, width)
    router_w = gather_fsdp(shard_router).reshape(width, EXPERTS)
    gu_w = gather_fsdp(shard_gu).reshape(width, -1)
    down_w = gather_fsdp(shard_down).reshape(-1, width)
    marked = jnp.concatenate(
        [cot_rows, uses.astype(bf16), jnp.zeros((tokens, 128 - EXPERTS), bf16)], axis=1
    )
    marked_arrived = exchange(product(send, marked).astype(bf16), CTX)

    attn_group, attn_turned, lse = attend(numbers, queries, kv_parts)

    attn_rows = exchange(attn_group, ZY).reshape(KV_HEADS, tokens, 2 * HEAD_DIM)
    attn_rows = attn_rows.transpose(1, 0, 2).reshape(tokens, HEADS * HEAD_DIM)
    inputs = own_input.astype(f32)
    hidden = inputs + residual_scale * product(attn_rows, out_w)
    inv_rms2 = lax.rsqrt(jnp.mean(hidden * hidden, axis=-1, keepdims=True) + epsilon)
    normed2 = (hidden * inv_rms2 * gain_two).astype(bf16)

    def gate_of(rows, mask):
        logits = jnp.where(mask > 0, product(rows, router_w), masked_value)
        exps = jnp.where(mask > 0, jnp.exp(logits - jnp.max(logits, axis=-1, keepdims=True)), 0.0)
        return exps / jnp.maximum(jnp.sum(exps, axis=-1, keepdims=True), 1e-30)

    arrived = exchange(product(send, normed2).astype(bf16), CTX)
    gate_probs = gate_of(normed2, uses)

    cot_arrived = marked_arrived[:, :width]
    uses_arrived = marked_arrived[:, width : width + EXPERTS].astype(f32)
    hidden_units = down_w.shape[0]
    pre = product(arrived, gu_w)
    gate_pre, up_pre = pre[:, :hidden_units], pre[:, hidden_units:]
    sigmoid_a = jax.nn.sigmoid(gate_pre)
    swish_act = gate_pre * sigmoid_a
    inner_act = (swish_act * up_pre).astype(bf16)
    expert_out = product(inner_act, down_w).astype(bf16)
    slot_probs = jnp.sum(
        jnp.where(jnp.arange(EXPERTS)[None, :] == expert, gate_of(arrived, uses_arrived), 0.0),
        axis=1,
        keepdims=True,
    )
    mix_grad = residual_scale * cot_arrived.astype(f32)
    slot_gate_grad = jnp.sum(mix_grad * expert_out.astype(f32), axis=1)
    route_grad = (slot_probs * mix_grad).astype(bf16)
    inner_grad = product_nt(route_grad, down_w)
    pre_grad = jnp.concatenate(
        [
            (inner_grad * up_pre * sigmoid_a * (1.0 + gate_pre * (1.0 - sigmoid_a))).astype(bf16),
            (inner_grad * swish_act).astype(bf16),
        ],
        axis=1,
    )
    expert_in_grad = product_nt(pre_grad, gu_w).astype(bf16)
    gate_grad_back = exchange(slot_gate_grad.reshape(EXPERTS, CAP), CTX)
    back = exchange(expert_in_grad, CTX)

    gate_grad = jnp.sum(jnp.where(slot_of, gate_grad_back[:, :, None], 0.0), axis=1).T
    mean_grad = jnp.sum(gate_probs * gate_grad, axis=-1, keepdims=True)
    logit_grad = (gate_probs * (gate_grad - mean_grad)).astype(bf16)
    normed2_grad = product_tn(send, back) + product_nt(logit_grad, router_w)
    hidden_part, gain_two_grad = norm_back(hidden, inv_rms2, gain_two, normed2_grad)
    hidden_grad = cotangent[0].astype(f32) + hidden_part
    branch_grad = (residual_scale * hidden_grad).astype(bf16)
    attn_grad = product_nt(branch_grad, out_w).astype(bf16)

    attn_grad = attn_grad.reshape(tokens, KV_HEADS, 2 * HEAD_DIM).transpose(1, 0, 2)
    group_grad = exchange(attn_grad.reshape(KV_HEADS * tokens, 2 * HEAD_DIM), ZY)
    group_grad = group_grad.reshape(KV_HEADS * tokens, 2, HEAD_DIM).transpose(1, 0, 2)
    group_grad_pad = jnp.pad(group_grad, ((0, 0), (0, 0), (HEAD_DIM, 0)))

    expert_out, pre_grad, inner_act, attn_rows_l, branch_grad_l, normed2_l, logit_grad_l, gain_two_grad, by_head = (
        lax.optimization_barrier(
            (expert_out, pre_grad, inner_act, attn_rows, branch_grad, normed2, logit_grad, gain_two_grad, by_head, attn_grad)
        )[:9]
    )
    dq, *dkv_parts = attend_grad(numbers, queries, kv_parts, group_grad_pad, attn_turned, lse)
    returned = exchange(expert_out, CTX)
    grad_gu = product_tn(arrived, pre_grad).reshape(4, -1, 2 * hidden_units)
    grad_down = product_tn(inner_act, route_grad).reshape(4, -1, width)
    expert_sums = scatter_fsdp(jnp.concatenate([grad_gu, grad_down], axis=1))
    dense = jnp.concatenate(
        [
            product_tn(attn_rows_l, branch_grad_l),
            product_tn(normed2_l, logit_grad_l),
            gain_two_grad[:, None],
            jnp.zeros((width, 128 - EXPERTS - 1), f32),
        ],
        axis=1,
    )
    dense = scatter_fsdp(dense.reshape(4, width // 4, width + 128))
    dense = exchange(dense.astype(bf16), CTX).reshape(32, -1, width + 128)
    dense = jnp.sum(dense.astype(f32), axis=0).astype(bf16)
    dense = exchange(jnp.tile(dense, (32, 1)), CTX).astype(f32)
    full_w = gather_fsdp(by_head).reshape(width, -1)

    weights = jnp.where(slot_of, gate_probs.T[:, None, :], 0.0).reshape(EXPERTS * CAP, tokens)
    weights_hi = weights.astype(bf16)
    weights_lo = (weights - weights_hi.astype(f32)).astype(bf16)
    mixture = product_tn(weights_hi, returned) + product_tn(weights_lo, returned)
    output = hidden + residual_scale * mixture

    dkv = dkv_parts[0].astype(f32)
    for step in (1, 2, 3):
        dkv = dkv + turn(dkv_parts[step], "x", -step).astype(f32)
    grads = jnp.concatenate(
        [
            rotate_back(dq[:, :HEAD_DIM], cosine, sine),
            rotate_back(dq[:, HEAD_DIM:], cosine, sine),
            rotate_back(dkv[:, :HEAD_DIM], cosine, sine),
            dkv[:, HEAD_DIM:],
        ],
        axis=1,
    ).astype(bf16)
    token_grads = exchange(grads, ZY).reshape(KV_HEADS, tokens, 4 * HEAD_DIM)
    token_grads = token_grads.transpose(1, 0, 2).reshape(tokens, -1)
    head_grad = scatter_fsdp(product_tn(group_normed, grads).reshape(4, shard_rows, 4 * HEAD_DIM)).astype(bf16)
    head_sum = head_grad.astype(f32)
    for step in (1, 2, 3):
        head_sum = head_sum + turn(head_grad, "x", step).astype(f32)
    head_sum = exchange(jnp.tile(head_sum.astype(bf16), (KV_HEADS, 1)), ZY)
    head_sum = head_sum.reshape(KV_HEADS, shard_rows, 4 * HEAD_DIM).transpose(1, 0, 2).astype(f32)
    grad_query = head_sum[:, :, : 2 * HEAD_DIM].reshape(shard_rows, -1)
    grad_key = head_sum[:, :, 2 * HEAD_DIM : 3 * HEAD_DIM].reshape(shard_rows, -1)
    grad_value = head_sum[:, :, 3 * HEAD_DIM :].reshape(shard_rows, -1)

    normed1_grad = product_nt(token_grads, full_w)
    inv_rms1 = lax.rsqrt(jnp.mean(inputs * inputs, axis=-1, keepdims=True) + epsilon)
    input_part, gain_one_grad = norm_back(inputs, inv_rms1, gain_one, normed1_grad)
    input_grad = hidden_grad + input_part
    gain_one_grad = jnp.sum(exchange(jnp.tile(gain_one_grad.reshape(4, -1), (32, 1)), EVERY), axis=0)

    return (
        output.astype(bf16)[None],
        input_grad[None],
        gain_one_grad,
        grad_query,
        grad_key,
        grad_value,
        dense[:, :width],
        dense[:, width + EXPERTS],
        dense[:, width : width + EXPERTS],
        expert_sums[None, :shard_rows, :hidden_units],
        expert_sums[None, :shard_rows, hidden_units:],
        expert_sums[None, shard_rows:],
    )


def solution(mesh):
    fine = Mesh(mesh.devices.reshape(4, 4, 2, 2, 2), EVERY)
    rows, shards = P(("yl", "core"), CTX, None), P(("yl", "core"), None)
    gain, experts = P(("yl", "core")), P(CTX, ("yl", "core"), None)
    return jax.shard_map(
        on_device,
        mesh=fine,
        in_specs=(
            rows, rows, P(), gain, shards, shards, shards, shards, gain, shards, experts, experts, experts, rows,
        ),
        out_specs=(
            rows, rows, gain, shards, shards, shards, shards, gain, shards, experts, experts, experts,
        ),
        check_vma=False,
    )
```

```python
import functools

import jax
import jax.numpy as jnp
from jax import lax
from jax.experimental import pallas as pl
from jax.experimental.layout import Layout, with_layout_constraint
from jax.experimental.pallas import tpu as pltpu
from jax.sharding import Mesh
from jax.sharding import PartitionSpec as P

HEADS = 16
KV_HEADS = 8
HEAD_DIM = 64
EXPERTS = 32
TOP = 8
CAP = 48
HALF = 64
TILE = 512

epsilon = 1e-06
attn_scale = 0.015625
residual_scale = 0.22
masked_value = -1e30

CTX = ("x", "z", "yh")
ZY = ("z", "yh")
EVERY = ("x", "z", "yh", "yl", "core")
bf16 = jnp.bfloat16
f32 = jnp.float32


def product(left, right):
    return jnp.dot(left, right, preferred_element_type=f32)


def product_nt(left, right):
    return lax.dot_general(left, right, (((1,), (1,)), ((), ())), preferred_element_type=f32)


def product_tn(left, right):
    return lax.dot_general(left, right, (((0,), (0,)), ((), ())), preferred_element_type=f32)


def swap(values, axis):
    return lax.ppermute(values, axis, [(0, 1), (1, 0)])


def turn(values, axis, step):
    return lax.ppermute(values, axis, [(i, (i + step) % 4) for i in range(4)])


def rows_first(values):
    return with_layout_constraint(values, Layout(major_to_minor=tuple(range(values.ndim))))


def exchange(values, axes):
    return rows_first(lax.all_to_all(rows_first(values), axes, 0, 0, tiled=True))


def tie(values, *others):
    corner = tuple(slice(0, min(size, 8 if axis < values.ndim - 1 else 128)) for axis, size in enumerate(values.shape))
    nothing = sum(other[(0,) * other.ndim].astype(f32) * 0.0 for other in others)
    held = values[corner] + nothing.astype(values.dtype)
    return lax.dynamic_update_slice(values, held, (0,) * values.ndim)


def gather_fsdp(shard):
    row, core = lax.axis_index("yl"), lax.axis_index("core")
    pair = jnp.zeros((2, 2) + shard.shape, shard.dtype)
    zero = (0,) * shard.ndim
    other = swap(shard, "yl")
    mine = lax.dynamic_update_slice(jnp.zeros((2,) + shard.shape, shard.dtype), shard[None], (row,) + zero)
    mine = lax.dynamic_update_slice(mine, other[None], (1 - row,) + zero)
    theirs = swap(mine, "core")
    pair = lax.dynamic_update_slice(pair, mine[:, None], (0, core) + zero)
    pair = lax.dynamic_update_slice(pair, theirs[:, None], (0, 1 - core) + zero)
    return pair.reshape((4,) + shard.shape)


def scatter_core(parts):
    core = lax.axis_index("core")
    parts = parts.astype(bf16).reshape((2, 2) + parts.shape[1:])
    away = lax.dynamic_index_in_dim(parts, 1 - core, 1, keepdims=False)
    keep = lax.dynamic_index_in_dim(parts, core, 1, keepdims=False)
    return (keep.astype(f32) + swap(away, "core").astype(f32)).astype(bf16)


def scatter_row(both):
    row = lax.axis_index("yl")
    away = lax.dynamic_index_in_dim(both, 1 - row, 0, keepdims=False)
    keep = lax.dynamic_index_in_dim(both, row, 0, keepdims=False)
    return keep.astype(f32) + swap(away, "yl").astype(f32)


def scatter_fsdp(parts):
    return scatter_row(scatter_core(parts))


def scatter_to(parts, axes, count):
    me = lax.axis_index(axes)
    total = lax.dynamic_index_in_dim(parts, me, 0, keepdims=False).astype(f32)
    for step in range(1, count):
        away = lax.dynamic_index_in_dim(parts, (me + step) % count, 0, keepdims=False)
        total = total + lax.ppermute(away, axes, [(i, (i + step) % count) for i in range(count)]).astype(f32)
    return total


def sum_over(part, axes, count):
    total = part.astype(f32)
    for step in range(1, count):
        total = total + lax.ppermute(part, axes, [(i, (i + step) % count) for i in range(count)]).astype(f32)
    return total


def gather_x(shard):
    place = lax.axis_index("x")
    zero = (0,) * shard.ndim
    whole = lax.dynamic_update_slice(jnp.zeros((4,) + shard.shape, shard.dtype), shard[None], (place,) + zero)
    for step in (1, 2, 3):
        whole = lax.dynamic_update_slice(whole, turn(shard, "x", step)[None], ((place - step) % 4,) + zero)
    return whole


def rope_tables(positions):
    freqs = jnp.power(10000.0, -jnp.arange(0, HEAD_DIM, 2, dtype=f32) / HEAD_DIM)
    angles = positions.astype(f32)[:, None] * freqs[None, :]
    angles = jnp.concatenate([angles, angles], axis=-1)
    return (jnp.cos(angles), jnp.sin(angles))


def rotate(values, cosine, sine):
    middle = HEAD_DIM // 2
    turned = jnp.concatenate([-values[..., middle:], values[..., :middle]], axis=-1)
    return values * cosine + turned * sine


def rotate_back(grads, cosine, sine):
    middle = HEAD_DIM // 2
    scaled = grads * sine
    turned = jnp.concatenate([scaled[..., middle:], -scaled[..., :middle]], axis=-1)
    return grads * cosine + turned


def norm_back(values, inv_rms, gain, grad):
    weighted = grad * gain
    gain_grad = jnp.sum(grad * values * inv_rms, axis=0)
    inner_mean = jnp.mean(weighted * values, axis=-1, keepdims=True)
    return (weighted * inv_rms - values * inv_rms * inv_rms * inv_rms * inner_mean, gain_grad)


def half(index):
    return pl.ds(pl.multiple_of(index * HALF, HALF), HALF)


def key_tile(counter):
    return pl.ds(pl.multiple_of(counter * TILE, TILE), TILE)


def sort_keys(knum_ref, kv_refs, kvs, kvt):
    blocks = kv_refs[0].shape[0] // HALF
    for slot, kv_ref in enumerate(kv_refs):
        for block in range(blocks):
            kvs[half(knum_ref[slot * blocks + block]), :] = kv_ref[block * HALF : (block + 1) * HALF, :]
    for tile in range(kvs.shape[0] // TILE):
        part = kvs[tile * TILE : (tile + 1) * TILE, :].astype(f32)
        kvt[:, tile * TILE : (tile + 1) * TILE] = part.T.astype(bf16)


def pair_rows(ref, first, second):
    return jnp.concatenate(
        [ref[0, half(first), :], ref[1, half(first), :], ref[0, half(second), :], ref[1, half(second), :]],
        axis=0,
    )


def pair_positions(low_number, high_number):
    column = lax.broadcasted_iota(jnp.int32, (1, 4 * HALF), 1)
    return jnp.where(column < 2 * HALF, low_number, high_number) * HALF + column % HALF


def score_tile(keys, queries, counter, positions, masked):
    scores = product_nt(keys, queries)
    if masked:
        key_pos = counter * TILE + lax.broadcasted_iota(jnp.int32, scores.shape, 0)
        scores = jnp.where(key_pos <= positions, scores, masked_value)
    return scores


def store_rows(ref, turned, first, second):
    rows = turned.T
    ref[half(first), :] = jnp.concatenate([rows[:HALF], rows[HALF : 2 * HALF]], axis=1).astype(ref.dtype)
    ref[half(second), :] = jnp.concatenate([rows[2 * HALF : 3 * HALF], rows[3 * HALF :]], axis=1).astype(ref.dtype)


def attend_kernel(order_ref, qnum_ref, knum_ref, q_ref, kv0, kv1, kv2, kv3, out_ref, turned_ref, lse_ref, kvs, kvt):
    sort_keys(knum_ref, (kv0, kv1, kv2, kv3), kvs, kvt)
    width = 4 * HALF

    @pl.loop(0, q_ref.shape[1] // (2 * HALF))
    def _(pair):
        first, second = order_ref[2 * pair], order_ref[2 * pair + 1]
        low_number, high_number = qnum_ref[first], qnum_ref[second]
        queries = pair_rows(q_ref, first, second)
        positions = pair_positions(low_number, high_number)

        def step(masked, counter, running):
            top, total, mixed = running
            scores = score_tile(kvs[key_tile(counter), :], queries, counter, positions, masked)
            new_top = jnp.maximum(top, jnp.max(scores, axis=0, keepdims=True))
            probs = jnp.exp(scores - new_top)
            shrink = jnp.exp(top - new_top)
            total = total * shrink + jnp.sum(probs, axis=0, keepdims=True)
            mixed = mixed * shrink + product(kvt[HEAD_DIM:, key_tile(counter)], probs.astype(bf16))
            return (new_top, total, mixed)

        start = (
            jnp.full((1, width), masked_value, f32),
            jnp.zeros((1, width), f32),
            jnp.zeros((HEAD_DIM, width), f32),
        )
        full = (low_number * HALF) // TILE
        last = (high_number * HALF) // TILE + 1
        running = lax.fori_loop(0, full, functools.partial(step, False), start)
        top, total, mixed = lax.fori_loop(full, last, functools.partial(step, True), running)
        mixed = mixed / total
        turned_ref[pair] = mixed
        lse_ref[pair] = top + jnp.log(total)
        store_rows(out_ref, mixed, first, second)


def attend_grad_kernel(
    order_ref, qnum_ref, knum_ref, q_ref, kv0, kv1, kv2, kv3, grad_ref, turned_ref, lse_ref,
    dq_ref, dkv0, dkv1, dkv2, dkv3, kvs, kvt, total_ref,
):
    sort_keys(knum_ref, (kv0, kv1, kv2, kv3), kvs, kvt)
    total_ref[...] = jnp.zeros_like(total_ref)
    width = 4 * HALF

    @pl.loop(0, q_ref.shape[1] // (2 * HALF))
    def _(pair):
        first, second = order_ref[2 * pair], order_ref[2 * pair + 1]
        low_number, high_number = qnum_ref[first], qnum_ref[second]
        queries = pair_rows(q_ref, first, second)
        grads = pair_rows(grad_ref, first, second)
        both = jnp.concatenate([queries, grads], axis=0)
        positions = pair_positions(low_number, high_number)
        lse = lse_ref[pair]
        dots = jnp.sum(grads.astype(f32).T[HEAD_DIM:] * turned_ref[pair], axis=0, keepdims=True)

        def step(masked, counter, query_acc):
            keys = kvs[key_tile(counter), :]
            probs = jnp.exp(score_tile(keys, queries, counter, positions, masked) - lse)
            score_grad = (probs * (product_nt(keys, grads) - dots)).astype(bf16)
            sides = jnp.concatenate([score_grad, probs.astype(bf16)], axis=1)
            total_ref[key_tile(counter), :] += product(sides, both)
            return query_acc + product(kvt[:HEAD_DIM, key_tile(counter)], score_grad)

        full = (low_number * HALF) // TILE
        last = (high_number * HALF) // TILE + 1
        query_acc = lax.fori_loop(0, full, functools.partial(step, False), jnp.zeros((HEAD_DIM, width), f32))
        query_acc = lax.fori_loop(full, last, functools.partial(step, True), query_acc)
        store_rows(dq_ref, query_acc * attn_scale, first, second)

    blocks = dkv0.shape[0] // HALF
    for slot, dkv in enumerate((dkv0, dkv1, dkv2, dkv3)):
        for block in range(blocks):
            dkv[block * HALF : (block + 1) * HALF, :] = total_ref[
                half(knum_ref[slot * blocks + block]), :
            ].astype(bf16)


def expert_kernel(
    expert_ref, rows_ref, marked_ref, gu_ref, down_ref, router_ref,
    out_ref, in_grad_ref, pre_grad_ref, inner_ref, route_grad_ref,
):
    rows = rows_ref[...]
    width = rows.shape[1]
    units = down_ref.shape[0]
    pre = product(rows, gu_ref[...])
    gate_pre, up_pre = pre[:, :units], pre[:, units:]
    sigmoid_a = 1.0 / (1.0 + jnp.exp(-gate_pre))
    swish_act = gate_pre * sigmoid_a
    inner_act = (swish_act * up_pre).astype(bf16)
    inner_ref[...] = inner_act
    expert_out = product(inner_act, down_ref[...]).astype(bf16)
    out_ref[...] = expert_out
    uses = marked_ref[:, width : width + EXPERTS].astype(f32)
    probs = gate_of(rows, uses, router_ref[...])
    column = lax.broadcasted_iota(jnp.int32, probs.shape, 1)
    slot_probs = jnp.sum(jnp.where(column == expert_ref[0], probs, 0.0), axis=1, keepdims=True)
    mix_grad = residual_scale * marked_ref[:, :width].astype(f32)
    gate_grad = jnp.sum(mix_grad * expert_out.astype(f32), axis=1, keepdims=True)
    route_grad = (slot_probs * mix_grad).astype(bf16)
    route_grad_ref[...] = route_grad
    inner_grad = product_nt(route_grad, down_ref[...])
    pre_grad_ref[:, :units] = (
        inner_grad * up_pre * sigmoid_a * (1.0 + gate_pre * (1.0 - sigmoid_a))
    ).astype(bf16)
    pre_grad_ref[:, units:] = (inner_grad * swish_act).astype(bf16)
    in_grad_ref[:, :width] = product_nt(pre_grad_ref[...], gu_ref[...]).astype(bf16)
    column = lax.broadcasted_iota(jnp.int32, (rows.shape[0], 128), 1)
    high = gate_grad.astype(bf16).astype(f32)
    in_grad_ref[:, width:] = jnp.where(
        column == 0, high, jnp.where(column == 1, gate_grad - high, 0.0)
    ).astype(bf16)


def gate_of(rows, mask, router_w):
    logits = jnp.where(mask > 0, product(rows, router_w), masked_value)
    exps = jnp.where(mask > 0, jnp.exp(logits - jnp.max(logits, axis=-1, keepdims=True)), 0.0)
    return exps / jnp.maximum(jnp.sum(exps, axis=-1, keepdims=True), 1e-30)


def run_experts(expert, rows, marked, gu_w, down_w, router_w):
    count, width = rows.shape
    units = down_w.shape[0]
    tile = 256

    def tiled(columns):
        return pl.BlockSpec((tile, columns), lambda i: (i, 0))

    def whole(array):
        return pl.BlockSpec(array.shape, lambda i: (0, 0))

    columns = (width, width + 128, 2 * units, units, width)
    return pl.pallas_call(
        expert_kernel,
        grid=(count // tile,),
        out_shape=tuple(jax.ShapeDtypeStruct((count, c), bf16) for c in columns),
        in_specs=[SMEM, tiled(width), tiled(width + 128), whole(gu_w), whole(down_w), whole(router_w)],
        out_specs=tuple(tiled(c) for c in columns),
        compiler_params=pltpu.CompilerParams(vmem_limit_bytes=40 * 1024 * 1024),
        cost_estimate=pl.CostEstimate(flops=10_000_000_000, bytes_accessed=22_000_000, transcendentals=1_000_000),
    )(expert.astype(jnp.int32).reshape(1), rows, marked, gu_w, down_w, router_w)


SMEM = pl.BlockSpec(memory_space=pltpu.SMEM)
VMEM = pl.BlockSpec(memory_space=pltpu.VMEM)


def attend(numbers, queries, kv_parts):
    rows = queries.shape[1]
    keys = rows * len(kv_parts)
    pairs = rows // (2 * HALF)
    return pl.pallas_call(
        attend_kernel,
        out_shape=(
            jax.ShapeDtypeStruct((rows, 2 * HEAD_DIM), bf16),
            jax.ShapeDtypeStruct((pairs, HEAD_DIM, 4 * HALF), f32),
            jax.ShapeDtypeStruct((pairs, 1, 4 * HALF), f32),
        ),
        in_specs=[SMEM] * 3 + [VMEM] * 5,
        out_specs=(VMEM,) * 3,
        scratch_shapes=[pltpu.VMEM((keys, 2 * HEAD_DIM), bf16), pltpu.VMEM((2 * HEAD_DIM, keys), bf16)],
        compiler_params=pltpu.CompilerParams(vmem_limit_bytes=40 * 1024 * 1024),
        cost_estimate=pl.CostEstimate(flops=12_000_000_000, bytes_accessed=4_000_000, transcendentals=5_000_000),
    )(*numbers, queries, *kv_parts)


def attend_grad(numbers, queries, kv_parts, grads, turned, lse):
    rows = queries.shape[1]
    keys = rows * len(kv_parts)
    return pl.pallas_call(
        attend_grad_kernel,
        out_shape=(jax.ShapeDtypeStruct((rows, 2 * HEAD_DIM), f32),)
        + (jax.ShapeDtypeStruct((rows, 2 * HEAD_DIM), bf16),) * 4,
        in_specs=[SMEM] * 3 + [VMEM] * 8,
        out_specs=(VMEM,) * 5,
        scratch_shapes=[
            pltpu.VMEM((keys, 2 * HEAD_DIM), bf16),
            pltpu.VMEM((2 * HEAD_DIM, keys), bf16),
            pltpu.VMEM((keys, 2 * HEAD_DIM), f32),
        ],
        compiler_params=pltpu.CompilerParams(vmem_limit_bytes=40 * 1024 * 1024),
        cost_estimate=pl.CostEstimate(flops=30_000_000_000, bytes_accessed=6_000_000, transcendentals=5_000_000),
    )(*numbers, queries, *kv_parts, grads, turned, lse)


def block_numbers(block_pairs):
    place = lax.axis_index("x")
    groups = block_pairs.reshape(4, 8)
    groups = groups[(place - jnp.arange(4)) % 4]
    numbers = jnp.stack([groups, 63 - groups], axis=-1).reshape(-1)
    own = numbers[:16]
    rank = jnp.sum((own[None, :] < own[:, None]).astype(jnp.int32), axis=1)
    spots = jnp.arange(16, dtype=jnp.int32)
    order = jnp.sum(jnp.where(rank[None, :] == spots[:, None], spots[None, :], 0), axis=1)
    return (order, own, numbers)


def on_device(
    block_input,
    routes,
    block_pairs,
    norm1_gain,
    w_query,
    w_key,
    w_value,
    w_out,
    norm2_gain,
    w_router,
    w_gate,
    w_up,
    w_down,
    cotangent,
):
    tokens, width = block_input.shape[1:]
    head = lax.axis_index(ZY)
    expert = lax.axis_index(CTX)
    shard_rows = w_query.shape[0]
    own_input = block_input[0]

    group_input = exchange(jnp.tile(own_input, (KV_HEADS, 1)), ZY)
    by_head = jnp.concatenate(
        [
            w_query.reshape(shard_rows, KV_HEADS, 2 * HEAD_DIM),
            w_key.reshape(shard_rows, KV_HEADS, HEAD_DIM),
            w_value.reshape(shard_rows, KV_HEADS, HEAD_DIM),
        ],
        axis=2,
    )
    head_shard = lax.dynamic_index_in_dim(by_head, head, 1, keepdims=False)
    gains = jnp.stack([norm1_gain, norm2_gain])
    head_w = gather_fsdp(head_shard).reshape(width, 4 * HEAD_DIM)
    gains = gather_fsdp(gains)
    gain_one = gains[:, 0].reshape(width).astype(f32)
    gain_two = gains[:, 1].reshape(width).astype(f32)

    numbers = block_numbers(block_pairs)
    group_pos = (numbers[1][:, None] * HALF + jnp.arange(HALF, dtype=jnp.int32)[None, :]).reshape(-1)
    cosine, sine = rope_tables(group_pos)

    chosen = routes[0]
    uses = jnp.sum(
        (chosen[:, :, None] == jnp.arange(EXPERTS, dtype=jnp.int32)[None, None, :]).astype(f32), axis=1
    )
    earlier = jnp.tril(jnp.ones((tokens, tokens), bf16), -1)
    rank = product(earlier, uses.astype(bf16)).astype(jnp.int32)
    rank = jnp.where(uses > 0, rank, -1)
    slot_of = (
        rank.T[:, None, :] == jnp.arange(CAP, dtype=jnp.int32)[None, :, None]
    )
    send = slot_of.astype(bf16).reshape(EXPERTS * CAP, tokens)

    group_f = group_input.astype(f32)
    group_inv = lax.rsqrt(jnp.mean(group_f * group_f, axis=-1, keepdims=True) + epsilon)
    group_normed = (group_f * group_inv * gain_one).astype(bf16)
    projected = product(group_normed, head_w)
    key_rot = rotate(projected[:, 2 * HEAD_DIM : 3 * HEAD_DIM], cosine, sine)
    kv_own = jnp.concatenate([key_rot, projected[:, 3 * HEAD_DIM :]], axis=1).astype(bf16)
    kv_parts = [kv_own] + [turn(kv_own, "x", step) for step in (1, 2, 3)]
    queries = jnp.stack(
        [
            rotate(projected[:, :HEAD_DIM], cosine, sine),
            rotate(projected[:, HEAD_DIM : 2 * HEAD_DIM], cosine, sine),
        ]
    ).astype(bf16) * bf16(attn_scale)
    queries = jnp.pad(queries, ((0, 0), (0, 0), (0, HEAD_DIM)))

    marked = jnp.concatenate(
        [cotangent[0], uses.astype(bf16), jnp.zeros((tokens, 128 - EXPERTS), bf16)], axis=1
    )
    marked_arrived = exchange(product(send, tie(marked, group_input)).astype(bf16), CTX)
    out_w = gather_fsdp(tie(w_out, group_input)).reshape(HEADS * HEAD_DIM, width)
    router_w = gather_fsdp(tie(w_router, group_input)).reshape(width, EXPERTS)
    gu_w = gather_fsdp(tie(jnp.concatenate([w_gate[0], w_up[0]], axis=1), group_input)).reshape(width, -1)
    down_w = gather_fsdp(tie(w_down[0], group_input)).reshape(-1, width)

    attn_group, attn_turned, lse = attend(numbers, queries, kv_parts)

    attn_rows = exchange(tie(attn_group, marked_arrived, out_w), ZY).reshape(KV_HEADS, tokens, 2 * HEAD_DIM)
    attn_rows = attn_rows.transpose(1, 0, 2).reshape(tokens, HEADS * HEAD_DIM)
    inputs = own_input.astype(f32)
    hidden = inputs + residual_scale * product(attn_rows, out_w)
    inv_rms2 = lax.rsqrt(jnp.mean(hidden * hidden, axis=-1, keepdims=True) + epsilon)
    normed2 = (hidden * inv_rms2 * gain_two).astype(bf16)
    arrived = exchange(product(send, tie(normed2, gu_w, down_w, router_w)).astype(bf16), CTX)
    gate_probs = gate_of(normed2, uses, router_w)

    hidden_units = down_w.shape[0]
    expert_out, in_grad, pre_grad, inner_act, route_grad = run_experts(
        expert, arrived, marked_arrived, gu_w, down_w, router_w
    )
    back = exchange(in_grad, CTX)
    grad_gu = product_tn(arrived, pre_grad).astype(bf16).reshape(4, -1, 2 * hidden_units)
    grad_down = product_tn(inner_act, route_grad).astype(bf16).reshape(4, -1, width)
    expert_both = scatter_core(jnp.concatenate([grad_gu, grad_down], axis=1))
    full_w = gather_fsdp(tie(by_head, arrived)).reshape(width, -1)

    slot_gate_grad = back[:, width].astype(f32) + back[:, width + 1].astype(f32)
    gate_grad = jnp.sum(
        jnp.where(slot_of, slot_gate_grad.reshape(EXPERTS, CAP)[:, :, None], 0.0), axis=1
    ).T
    mean_grad = jnp.sum(gate_probs * gate_grad, axis=-1, keepdims=True)
    logit_grad = (gate_probs * (gate_grad - mean_grad)).astype(bf16)
    normed2_grad = product_tn(send, back[:, :width]) + product_nt(logit_grad, router_w)
    normed2_grad = tie(normed2_grad, expert_both, full_w)
    hidden_part, gain_two_grad = norm_back(hidden, inv_rms2, gain_two, normed2_grad)
    hidden_grad = cotangent[0].astype(f32) + hidden_part
    branch_grad = (residual_scale * hidden_grad).astype(bf16)
    attn_grad = product_nt(branch_grad, out_w).astype(bf16)

    attn_grad = attn_grad.reshape(tokens, KV_HEADS, 2 * HEAD_DIM).transpose(1, 0, 2)
    group_grad = exchange(attn_grad.reshape(KV_HEADS * tokens, 2 * HEAD_DIM), ZY)
    group_grad_heads = group_grad.reshape(KV_HEADS * tokens, 2, HEAD_DIM).transpose(1, 0, 2)
    group_grad_pad = jnp.pad(group_grad_heads, ((0, 0), (0, 0), (HEAD_DIM, 0)))
    dq, *dkv_parts = attend_grad(numbers, queries, kv_parts, group_grad_pad, attn_turned, lse)

    returned = exchange(tie(expert_out, group_grad), CTX)
    expert_sums = scatter_row(tie(expert_both, group_grad))
    dense = jnp.concatenate(
        [
            product_tn(attn_rows, branch_grad).astype(bf16),
            product_tn(normed2, logit_grad).astype(bf16),
            gain_two_grad[:, None].astype(bf16),
            jnp.zeros((width, 128 - EXPERTS - 1), bf16),
        ],
        axis=1,
    )
    dense = scatter_fsdp(dense.reshape(4, width // 4, width + 128))
    dense = scatter_to(dense.astype(bf16).reshape(4, -1, width + 128), "x", 4)
    dense = scatter_to(dense.astype(bf16).reshape(KV_HEADS, -1, width + 128), ZY, KV_HEADS)
    dense = gather_x(dense.astype(bf16))

    dkv = dkv_parts[0].astype(f32)
    for step in (1, 2, 3):
        dkv = dkv + turn(dkv_parts[step], "x", -step).astype(f32)
    grads = jnp.concatenate(
        [
            rotate_back(dq[:, :HEAD_DIM], cosine, sine),
            rotate_back(dq[:, HEAD_DIM:], cosine, sine),
            rotate_back(dkv[:, :HEAD_DIM], cosine, sine),
            dkv[:, HEAD_DIM:],
        ],
        axis=1,
    ).astype(bf16)
    grads = tie(grads, returned, expert_sums)
    token_grads = exchange(grads, ZY)
    head_grad = scatter_fsdp(product_tn(group_normed, grads).reshape(4, shard_rows, 4 * HEAD_DIM))
    head_sum = sum_over(head_grad.astype(bf16), "x", 4)

    dense_rows = dense.shape[0] * dense.shape[1]
    dense = exchange(jnp.tile(tie(dense, token_grads).reshape(dense_rows, -1), (KV_HEADS, 1)), ZY)
    dense = dense.reshape(KV_HEADS, 4, -1, width + 128).transpose(1, 0, 2, 3)
    dense = dense.reshape(shard_rows, width + 128).astype(f32)

    token_grads = token_grads.reshape(KV_HEADS, tokens, 4 * HEAD_DIM).transpose(1, 0, 2)
    normed1_grad = product_nt(token_grads.reshape(tokens, -1), full_w)
    inv_rms1 = lax.rsqrt(jnp.mean(inputs * inputs, axis=-1, keepdims=True) + epsilon)
    input_part, gain_one_grad = norm_back(inputs, inv_rms1, gain_one, normed1_grad)
    input_grad = hidden_grad + input_part
    gain_sum = scatter_to(gain_one_grad.reshape(4, -1), ("yl", "core"), 4)
    gain_sum = sum_over(gain_sum, "x", 4)
    gain_high = gain_sum.astype(bf16)
    gain_rows = jnp.stack([gain_high, (gain_sum - gain_high.astype(f32)).astype(bf16)])

    last = jnp.concatenate([head_sum.astype(bf16), jnp.pad(gain_rows, ((0, 14), (0, 0)))], axis=0)
    last = exchange(jnp.tile(tie(last, dense), (KV_HEADS, 1)), ZY).reshape(KV_HEADS, -1, 4 * HEAD_DIM)
    gain_one_grad = jnp.sum(last[:, shard_rows : shard_rows + 2].astype(f32), axis=(0, 1))
    head_sum = last[:, :shard_rows].transpose(1, 0, 2).astype(f32)
    grad_query = head_sum[:, :, : 2 * HEAD_DIM].reshape(shard_rows, -1)
    grad_key = head_sum[:, :, 2 * HEAD_DIM : 3 * HEAD_DIM].reshape(shard_rows, -1)
    grad_value = head_sum[:, :, 3 * HEAD_DIM :].reshape(shard_rows, -1)

    weights = jnp.where(slot_of, gate_probs.T[:, None, :], 0.0).reshape(EXPERTS * CAP, tokens)
    weights_hi = weights.astype(bf16)
    weights_lo = (weights - weights_hi.astype(f32)).astype(bf16)
    mixture = product_tn(weights_hi, returned) + product_tn(weights_lo, returned)
    output = hidden + residual_scale * mixture

    return (
        output.astype(bf16)[None],
        input_grad[None],
        gain_one_grad,
        grad_query,
        grad_key,
        grad_value,
        dense[:, :width],
        dense[:, width + EXPERTS],
        dense[:, width : width + EXPERTS],
        expert_sums[None, :shard_rows, :hidden_units],
        expert_sums[None, :shard_rows, hidden_units:],
        expert_sums[None, shard_rows:],
    )


def solution(mesh):
    fine = Mesh(mesh.devices.reshape(4, 4, 2, 2, 2), EVERY)
    rows, shards = P(("yl", "core"), CTX, None), P(("yl", "core"), None)
    gain, experts = P(("yl", "core")), P(CTX, ("yl", "core"), None)
    return jax.shard_map(
        on_device,
        mesh=fine,
        in_specs=(
            rows, rows, P(), gain, shards, shards, shards, shards, gain, shards, experts, experts, experts, rows,
        ),
        out_specs=(
            rows, rows, gain, shards, shards, shards, shards, gain, shards, experts, experts, experts,
        ),
        check_vma=False,
    )
```

```python
import functools

import jax
import jax.numpy as jnp
from jax import lax
from jax.experimental import pallas as pl
from jax.experimental.layout import Layout, with_layout_constraint
from jax.experimental.pallas import tpu as pltpu
from jax.sharding import Mesh
from jax.sharding import PartitionSpec as P

HEADS = 16
KV_HEADS = 8
HEAD_DIM = 64
EXPERTS = 32
TOP = 8
CAP = 48
HALF = 64
TILE = 512

epsilon = 1e-06
attn_scale = 0.015625
residual_scale = 0.22
masked_value = -1e30

CTX = ("x", "z", "yh")
ZY = ("z", "yh")
EVERY = ("x", "z", "yh", "yl", "core")
bf16 = jnp.bfloat16
f32 = jnp.float32


def product(left, right):
    return jnp.dot(left, right, preferred_element_type=f32)


def product_nt(left, right):
    return lax.dot_general(left, right, (((1,), (1,)), ((), ())), preferred_element_type=f32)


def product_tn(left, right):
    return lax.dot_general(left, right, (((0,), (0,)), ((), ())), preferred_element_type=f32)


def swap(values, axis):
    return lax.ppermute(values, axis, [(0, 1), (1, 0)])


def turn(values, axis, step):
    return lax.ppermute(values, axis, [(i, (i + step) % 4) for i in range(4)])


def rows_first(values):
    return with_layout_constraint(values, Layout(major_to_minor=tuple(range(values.ndim))))


def exchange(values, axes):
    return rows_first(lax.all_to_all(rows_first(values), axes, 0, 0, tiled=True))


def tie(values, *others):
    corner = tuple(slice(0, min(size, 8 if axis < values.ndim - 1 else 128)) for axis, size in enumerate(values.shape))
    nothing = sum(other[(0,) * other.ndim].astype(f32) * 0.0 for other in others)
    held = values[corner] + nothing.astype(values.dtype)
    return lax.dynamic_update_slice(values, held, (0,) * values.ndim)


def gather_direct(shard):
    me = lax.axis_index(("yl", "core"))
    whole = jnp.broadcast_to(shard[None], (4,) + shard.shape)
    for step in (1, 2, 3):
        other = lax.ppermute(shard, ("yl", "core"), [(i, i ^ step) for i in range(4)])
        whole = lax.dynamic_update_slice(whole, other[None], (me ^ step,) + (0,) * shard.ndim)
    return whole


def gather_core(shard, other):
    row, core = lax.axis_index("yl"), lax.axis_index("core")
    zero = (0,) * shard.ndim
    mine = jnp.broadcast_to(shard[None], (2,) + shard.shape)
    mine = lax.dynamic_update_slice(mine, other[None], (1 - row,) + zero)
    theirs = swap(mine, "core")
    pair = jnp.broadcast_to(mine[:, None], (2, 2) + shard.shape)
    pair = lax.dynamic_update_slice(pair, theirs[:, None], (0, 1 - core) + zero)
    return pair.reshape((4,) + shard.shape)


def gather_fsdp(shard):
    return gather_core(shard, swap(shard, "yl"))


def scatter_core(parts):
    core = lax.axis_index("core")
    parts = parts.astype(bf16).reshape((2, 2) + parts.shape[1:])
    away = lax.dynamic_index_in_dim(parts, 1 - core, 1, keepdims=False)
    keep = lax.dynamic_index_in_dim(parts, core, 1, keepdims=False)
    return (keep.astype(f32) + swap(away, "core").astype(f32)).astype(bf16)


def scatter_row(both):
    row = lax.axis_index("yl")
    away = lax.dynamic_index_in_dim(both, 1 - row, 0, keepdims=False)
    keep = lax.dynamic_index_in_dim(both, row, 0, keepdims=False)
    return keep.astype(f32) + swap(away, "yl").astype(f32)


def scatter_fsdp(parts):
    return scatter_row(scatter_core(parts))


def scatter_to(parts, axes, count):
    me = lax.axis_index(axes)
    total = lax.dynamic_index_in_dim(parts, me, 0, keepdims=False).astype(f32)
    for step in range(1, count):
        away = lax.dynamic_index_in_dim(parts, (me + step) % count, 0, keepdims=False)
        total = total + lax.ppermute(away, axes, [(i, (i + step) % count) for i in range(count)]).astype(f32)
    return total


def sum_over(part, axes, count):
    total = part.astype(f32)
    for step in range(1, count):
        total = total + lax.ppermute(part, axes, [(i, (i + step) % count) for i in range(count)]).astype(f32)
    return total


def gather_x(shard):
    place = lax.axis_index("x")
    zero = (0,) * shard.ndim
    whole = lax.dynamic_update_slice(jnp.zeros((4,) + shard.shape, shard.dtype), shard[None], (place,) + zero)
    for step in (1, 2, 3):
        whole = lax.dynamic_update_slice(whole, turn(shard, "x", step)[None], ((place - step) % 4,) + zero)
    return whole


def rope_tables(positions):
    freqs = jnp.power(10000.0, -jnp.arange(0, HEAD_DIM, 2, dtype=f32) / HEAD_DIM)
    angles = positions.astype(f32)[:, None] * freqs[None, :]
    angles = jnp.concatenate([angles, angles], axis=-1)
    return (jnp.cos(angles), jnp.sin(angles))


def rotate(values, cosine, sine):
    middle = HEAD_DIM // 2
    turned = jnp.concatenate([-values[..., middle:], values[..., :middle]], axis=-1)
    return values * cosine + turned * sine


def rotate_back(grads, cosine, sine):
    middle = HEAD_DIM // 2
    scaled = grads * sine
    turned = jnp.concatenate([scaled[..., middle:], -scaled[..., :middle]], axis=-1)
    return grads * cosine + turned


def norm_back(values, inv_rms, gain, grad):
    weighted = grad * gain
    gain_grad = jnp.sum(grad * values * inv_rms, axis=0)
    inner_mean = jnp.mean(weighted * values, axis=-1, keepdims=True)
    return (weighted * inv_rms - values * inv_rms * inv_rms * inv_rms * inner_mean, gain_grad)


def half(index):
    return pl.ds(pl.multiple_of(index * HALF, HALF), HALF)


def key_tile(counter):
    return pl.ds(pl.multiple_of(counter * TILE, TILE), TILE)


def sort_keys(knum_ref, kv_refs, kvs, kvt):
    blocks = kv_refs[0].shape[0] // HALF
    for slot, kv_ref in enumerate(kv_refs):
        for block in range(blocks):
            kvs[half(knum_ref[slot * blocks + block]), :] = kv_ref[block * HALF : (block + 1) * HALF, :]
    for tile in range(kvs.shape[0] // TILE):
        part = kvs[tile * TILE : (tile + 1) * TILE, :].astype(f32)
        kvt[:, tile * TILE : (tile + 1) * TILE] = part.T.astype(bf16)


def pair_rows(ref, first, second):
    return jnp.concatenate(
        [ref[0, half(first), :], ref[1, half(first), :], ref[0, half(second), :], ref[1, half(second), :]],
        axis=0,
    )


def pair_positions(low_number, high_number):
    column = lax.broadcasted_iota(jnp.int32, (1, 4 * HALF), 1)
    return jnp.where(column < 2 * HALF, low_number, high_number) * HALF + column % HALF


def score_tile(keys, queries, counter, positions, masked):
    scores = product_nt(keys, queries)
    if masked:
        key_pos = counter * TILE + lax.broadcasted_iota(jnp.int32, scores.shape, 0)
        scores = jnp.where(key_pos <= positions, scores, masked_value)
    return scores


def store_rows(ref, turned, first, second):
    rows = turned.T
    ref[half(first), :] = jnp.concatenate([rows[:HALF], rows[HALF : 2 * HALF]], axis=1).astype(ref.dtype)
    ref[half(second), :] = jnp.concatenate([rows[2 * HALF : 3 * HALF], rows[3 * HALF :]], axis=1).astype(ref.dtype)


def attend_kernel(
    order_ref, qnum_ref, knum_ref, q_ref, kv0, kv1, kv2, kv3, held_ref, out_ref, turned_ref, lse_ref, kvs, kvt
):
    del held_ref
    sort_keys(knum_ref, (kv0, kv1, kv2, kv3), kvs, kvt)
    width = 4 * HALF

    @pl.loop(0, q_ref.shape[1] // (2 * HALF))
    def _(pair):
        first, second = order_ref[2 * pair], order_ref[2 * pair + 1]
        low_number, high_number = qnum_ref[first], qnum_ref[second]
        queries = pair_rows(q_ref, first, second)
        positions = pair_positions(low_number, high_number)

        def step(masked, counter, running):
            top, total, mixed = running
            scores = score_tile(kvs[key_tile(counter), :], queries, counter, positions, masked)
            new_top = jnp.maximum(top, jnp.max(scores, axis=0, keepdims=True))
            probs = jnp.exp(scores - new_top)
            shrink = jnp.exp(top - new_top)
            total = total * shrink + jnp.sum(probs, axis=0, keepdims=True)
            mixed = mixed * shrink + product(kvt[HEAD_DIM:, key_tile(counter)], probs.astype(bf16))
            return (new_top, total, mixed)

        start = (
            jnp.full((1, width), masked_value, f32),
            jnp.zeros((1, width), f32),
            jnp.zeros((HEAD_DIM, width), f32),
        )
        full = (low_number * HALF) // TILE
        last = (high_number * HALF) // TILE + 1
        running = lax.fori_loop(0, full, functools.partial(step, False), start)
        top, total, mixed = lax.fori_loop(full, last, functools.partial(step, True), running)
        mixed = mixed / total
        turned_ref[pair] = mixed
        lse_ref[pair] = top + jnp.log(total)
        store_rows(out_ref, mixed, first, second)


def attend_grad_kernel(
    order_ref, qnum_ref, knum_ref, q_ref, kv0, kv1, kv2, kv3, grad_ref, turned_ref, lse_ref, held_ref,
    dq_ref, dkv0, dkv1, dkv2, dkv3, kvs, kvt, total_ref,
):
    del held_ref
    sort_keys(knum_ref, (kv0, kv1, kv2, kv3), kvs, kvt)
    total_ref[...] = jnp.zeros_like(total_ref)
    width = 4 * HALF

    @pl.loop(0, q_ref.shape[1] // (2 * HALF))
    def _(pair):
        first, second = order_ref[2 * pair], order_ref[2 * pair + 1]
        low_number, high_number = qnum_ref[first], qnum_ref[second]
        queries = pair_rows(q_ref, first, second)
        grads = pair_rows(grad_ref, first, second)
        both = jnp.concatenate([queries, grads], axis=0)
        positions = pair_positions(low_number, high_number)
        lse = lse_ref[pair]
        dots = jnp.sum(grads.astype(f32).T[HEAD_DIM:] * turned_ref[pair], axis=0, keepdims=True)

        def step(masked, counter, query_acc):
            keys = kvs[key_tile(counter), :]
            probs = jnp.exp(score_tile(keys, queries, counter, positions, masked) - lse)
            score_grad = (probs * (product_nt(keys, grads) - dots)).astype(bf16)
            sides = jnp.concatenate([score_grad, probs.astype(bf16)], axis=1)
            total_ref[key_tile(counter), :] += product(sides, both)
            return query_acc + product(kvt[:HEAD_DIM, key_tile(counter)], score_grad)

        full = (low_number * HALF) // TILE
        last = (high_number * HALF) // TILE + 1
        query_acc = lax.fori_loop(0, full, functools.partial(step, False), jnp.zeros((HEAD_DIM, width), f32))
        query_acc = lax.fori_loop(full, last, functools.partial(step, True), query_acc)
        store_rows(dq_ref, query_acc * attn_scale, first, second)

    blocks = dkv0.shape[0] // HALF
    for slot, dkv in enumerate((dkv0, dkv1, dkv2, dkv3)):
        for block in range(blocks):
            dkv[block * HALF : (block + 1) * HALF, :] = total_ref[
                half(knum_ref[slot * blocks + block]), :
            ].astype(bf16)


def expert_kernel(
    expert_ref, rows_ref, marked_ref, gu_ref, down_ref, router_ref,
    out_ref, in_grad_ref, pre_grad_ref, inner_ref, route_grad_ref,
):
    rows = rows_ref[...]
    width = rows.shape[1]
    units = down_ref.shape[0]
    pre = product(rows, gu_ref[...])
    gate_pre, up_pre = pre[:, :units], pre[:, units:]
    sigmoid_a = 1.0 / (1.0 + jnp.exp(-gate_pre))
    swish_act = gate_pre * sigmoid_a
    inner_act = (swish_act * up_pre).astype(bf16)
    inner_ref[...] = inner_act
    expert_out = product(inner_act, down_ref[...]).astype(bf16)
    out_ref[...] = expert_out
    uses = marked_ref[:, width : width + EXPERTS].astype(f32)
    probs = gate_of(rows, uses, router_ref[...])
    column = lax.broadcasted_iota(jnp.int32, probs.shape, 1)
    slot_probs = jnp.sum(jnp.where(column == expert_ref[0], probs, 0.0), axis=1, keepdims=True)
    mix_grad = residual_scale * marked_ref[:, :width].astype(f32)
    gate_grad = jnp.sum(mix_grad * expert_out.astype(f32), axis=1, keepdims=True)
    route_grad = (slot_probs * mix_grad).astype(bf16)
    route_grad_ref[...] = route_grad
    inner_grad = product_nt(route_grad, down_ref[...])
    pre_grad_ref[:, :units] = (
        inner_grad * up_pre * sigmoid_a * (1.0 + gate_pre * (1.0 - sigmoid_a))
    ).astype(bf16)
    pre_grad_ref[:, units:] = (inner_grad * swish_act).astype(bf16)
    in_grad_ref[:, :width] = product_nt(pre_grad_ref[...], gu_ref[...]).astype(bf16)
    column = lax.broadcasted_iota(jnp.int32, (rows.shape[0], 128), 1)
    high = gate_grad.astype(bf16).astype(f32)
    in_grad_ref[:, width:] = jnp.where(
        column == 0, high, jnp.where(column == 1, gate_grad - high, 0.0)
    ).astype(bf16)


def spread_kernel(last_ref, query_ref, key_ref, value_ref, gain_ref):
    rows = query_ref.shape[0]
    gain = jnp.zeros(gain_ref.shape, f32)
    for head in range(KV_HEADS):
        query_ref[:, head * 2 * HEAD_DIM : (head + 1) * 2 * HEAD_DIM] = last_ref[head, :rows, : 2 * HEAD_DIM].astype(f32)
        gain += jnp.sum(last_ref[head, rows : rows + 16, :].astype(f32), axis=0, keepdims=True)
    gain_ref[...] = gain
    for pair in range(KV_HEADS // 2):
        sides = [last_ref[2 * pair + side, :rows, 2 * HEAD_DIM :].astype(f32) for side in (0, 1)]
        columns = slice(pair * 2 * HEAD_DIM, (pair + 1) * 2 * HEAD_DIM)
        key_ref[:, columns] = jnp.concatenate([side[:, :HEAD_DIM] for side in sides], axis=1)
        value_ref[:, columns] = jnp.concatenate([side[:, HEAD_DIM:] for side in sides], axis=1)


def spread_heads(last, rows):
    heads, _, width = last.shape
    return pl.pallas_call(
        spread_kernel,
        out_shape=(
            jax.ShapeDtypeStruct((rows, heads * 2 * HEAD_DIM), f32),
            jax.ShapeDtypeStruct((rows, heads * HEAD_DIM), f32),
            jax.ShapeDtypeStruct((rows, heads * HEAD_DIM), f32),
            jax.ShapeDtypeStruct((1, width), f32),
        ),
        in_specs=[VMEM],
        out_specs=(VMEM,) * 4,
        compiler_params=pltpu.CompilerParams(vmem_limit_bytes=24 * 1024 * 1024),
        cost_estimate=pl.CostEstimate(flops=1_000_000, bytes_accessed=4_000_000, transcendentals=0),
    )(last)


def gate_of(rows, mask, router_w):
    logits = jnp.where(mask > 0, product(rows, router_w), masked_value)
    exps = jnp.where(mask > 0, jnp.exp(logits - jnp.max(logits, axis=-1, keepdims=True)), 0.0)
    return exps / jnp.maximum(jnp.sum(exps, axis=-1, keepdims=True), 1e-30)


def run_experts(expert, rows, marked, gu_w, down_w, router_w):
    count, width = rows.shape
    units = down_w.shape[0]
    tile = 256

    def tiled(columns):
        return pl.BlockSpec((tile, columns), lambda i: (i, 0))

    def whole(array):
        return pl.BlockSpec(array.shape, lambda i: (0, 0))

    columns = (width, width + 128, 2 * units, units, width)
    return pl.pallas_call(
        expert_kernel,
        grid=(count // tile,),
        out_shape=tuple(jax.ShapeDtypeStruct((count, c), bf16) for c in columns),
        in_specs=[SMEM, tiled(width), tiled(width + 128), whole(gu_w), whole(down_w), whole(router_w)],
        out_specs=tuple(tiled(c) for c in columns),
        compiler_params=pltpu.CompilerParams(vmem_limit_bytes=40 * 1024 * 1024),
        cost_estimate=pl.CostEstimate(flops=10_000_000_000, bytes_accessed=22_000_000, transcendentals=1_000_000),
    )(expert.astype(jnp.int32).reshape(1), rows, marked, gu_w, down_w, router_w)


SMEM = pl.BlockSpec(memory_space=pltpu.SMEM)
VMEM = pl.BlockSpec(memory_space=pltpu.VMEM)


def attend(numbers, queries, kv_parts, held):
    rows = queries.shape[1]
    keys = rows * len(kv_parts)
    pairs = rows // (2 * HALF)
    return pl.pallas_call(
        attend_kernel,
        out_shape=(
            jax.ShapeDtypeStruct((rows, 2 * HEAD_DIM), bf16),
            jax.ShapeDtypeStruct((pairs, HEAD_DIM, 4 * HALF), f32),
            jax.ShapeDtypeStruct((pairs, 1, 4 * HALF), f32),
        ),
        in_specs=[SMEM] * 3 + [VMEM] * 5 + [pl.BlockSpec(memory_space=pl.ANY)],
        out_specs=(VMEM,) * 3,
        scratch_shapes=[pltpu.VMEM((keys, 2 * HEAD_DIM), bf16), pltpu.VMEM((2 * HEAD_DIM, keys), bf16)],
        compiler_params=pltpu.CompilerParams(vmem_limit_bytes=40 * 1024 * 1024),
        cost_estimate=pl.CostEstimate(flops=12_000_000_000, bytes_accessed=4_000_000, transcendentals=5_000_000),
    )(*numbers, queries, *kv_parts, held)


def attend_grad(numbers, queries, kv_parts, grads, turned, lse, held):
    rows = queries.shape[1]
    keys = rows * len(kv_parts)
    return pl.pallas_call(
        attend_grad_kernel,
        out_shape=(jax.ShapeDtypeStruct((rows, 2 * HEAD_DIM), f32),)
        + (jax.ShapeDtypeStruct((rows, 2 * HEAD_DIM), bf16),) * 4,
        in_specs=[SMEM] * 3 + [VMEM] * 8 + [pl.BlockSpec(memory_space=pl.ANY)],
        out_specs=(VMEM,) * 5,
        scratch_shapes=[
            pltpu.VMEM((keys, 2 * HEAD_DIM), bf16),
            pltpu.VMEM((2 * HEAD_DIM, keys), bf16),
            pltpu.VMEM((keys, 2 * HEAD_DIM), f32),
        ],
        compiler_params=pltpu.CompilerParams(vmem_limit_bytes=40 * 1024 * 1024),
        cost_estimate=pl.CostEstimate(flops=30_000_000_000, bytes_accessed=6_000_000, transcendentals=5_000_000),
    )(*numbers, queries, *kv_parts, grads, turned, lse, held)


def block_numbers(block_pairs):
    place = lax.axis_index("x")
    groups = block_pairs.reshape(4, 8)
    groups = groups[(place - jnp.arange(4)) % 4]
    numbers = jnp.stack([groups, 63 - groups], axis=-1).reshape(-1)
    own = numbers[:16]
    rank = jnp.sum((own[None, :] < own[:, None]).astype(jnp.int32), axis=1)
    spots = jnp.arange(16, dtype=jnp.int32)
    order = jnp.sum(jnp.where(rank[None, :] == spots[:, None], spots[None, :], 0), axis=1)
    return (order, own, numbers)


def on_device(
    block_input,
    routes,
    block_pairs,
    norm1_gain,
    w_query,
    w_key,
    w_value,
    w_out,
    norm2_gain,
    w_router,
    w_gate,
    w_up,
    w_down,
    cotangent,
):
    tokens, width = block_input.shape[1:]
    head = lax.axis_index(ZY)
    expert = lax.axis_index(CTX)
    shard_rows = w_query.shape[0]
    own_input = block_input[0]

    by_head = jnp.concatenate(
        [
            w_query.reshape(shard_rows, KV_HEADS, 2 * HEAD_DIM),
            w_key.reshape(shard_rows, KV_HEADS, HEAD_DIM),
            w_value.reshape(shard_rows, KV_HEADS, HEAD_DIM),
        ],
        axis=2,
    ).reshape(shard_rows, -1)
    small_shard = jnp.concatenate(
        [
            lax.dynamic_slice_in_dim(by_head, head * 4 * HEAD_DIM, 4 * HEAD_DIM, 1),
            w_router,
            norm1_gain[:, None],
            norm2_gain[:, None],
            jnp.zeros((shard_rows, 128 - EXPERTS - 2), bf16),
        ],
        axis=1,
    )
    small_w = gather_direct(small_shard).reshape(width, -1)
    head_w, small_w = small_w[:, : 4 * HEAD_DIM], small_w[:, 4 * HEAD_DIM :]
    router_w = small_w[:, :EXPERTS]
    gain_one = small_w[:, EXPERTS].astype(f32)
    gain_two = small_w[:, EXPERTS + 1].astype(f32)
    group_input = exchange(jnp.tile(own_input, (KV_HEADS, 1)), ZY)

    numbers = block_numbers(block_pairs)
    group_pos = (numbers[1][:, None] * HALF + jnp.arange(HALF, dtype=jnp.int32)[None, :]).reshape(-1)
    cosine, sine = rope_tables(group_pos)

    chosen = routes[0]
    uses = jnp.sum(
        (chosen[:, :, None] == jnp.arange(EXPERTS, dtype=jnp.int32)[None, None, :]).astype(f32), axis=1
    )
    earlier = jnp.tril(jnp.ones((tokens, tokens), bf16), -1)
    rank = product(earlier, uses.astype(bf16)).astype(jnp.int32)
    rank = jnp.where(uses > 0, rank, -1)
    slot_of = (
        rank.T[:, None, :] == jnp.arange(CAP, dtype=jnp.int32)[None, :, None]
    )
    send = slot_of.astype(bf16).reshape(EXPERTS * CAP, tokens)

    group_f = group_input.astype(f32)
    group_inv = lax.rsqrt(jnp.mean(group_f * group_f, axis=-1, keepdims=True) + epsilon)
    group_normed = (group_f * group_inv * gain_one).astype(bf16)
    projected = product(group_normed, head_w)
    key_rot = rotate(projected[:, 2 * HEAD_DIM : 3 * HEAD_DIM], cosine, sine)
    kv_own = jnp.concatenate([key_rot, projected[:, 3 * HEAD_DIM :]], axis=1).astype(bf16)
    kv_parts = [kv_own] + [turn(kv_own, "x", step) for step in (1, 2, 3)]
    queries = jnp.stack(
        [
            rotate(projected[:, :HEAD_DIM], cosine, sine),
            rotate(projected[:, HEAD_DIM : 2 * HEAD_DIM], cosine, sine),
        ]
    ).astype(bf16) * bf16(attn_scale)
    queries = jnp.pad(queries, ((0, 0), (0, 0), (0, HEAD_DIM)))

    out_shard = tie(w_out, group_input)
    out_other = swap(out_shard, "yl")

    marked = jnp.concatenate(
        [cotangent[0], uses.astype(bf16), jnp.zeros((tokens, 128 - EXPERTS), bf16)], axis=1
    )
    marked_arrived = exchange(product(send, tie(marked, *kv_parts[1:], out_other)).astype(bf16), CTX)
    attn_group, attn_turned, lse = attend(numbers, queries, kv_parts, out_other)

    out_w = gather_core(out_shard, out_other).reshape(HEADS * HEAD_DIM, width)
    gu_shard = tie(jnp.concatenate([w_gate[0], w_up[0]], axis=1), attn_group)
    down_shard = tie(w_down[0], attn_group)
    gu_other, down_other = swap(gu_shard, "yl"), swap(down_shard, "yl")

    attn_rows = exchange(tie(attn_group, marked_arrived, out_w), ZY).reshape(KV_HEADS, tokens, 2 * HEAD_DIM)
    attn_rows = attn_rows.transpose(1, 0, 2).reshape(tokens, HEADS * HEAD_DIM)
    gu_w = gather_core(gu_shard, tie(gu_other, attn_rows)).reshape(width, -1)
    down_w = gather_core(down_shard, tie(down_other, attn_rows)).reshape(-1, width)
    inputs = own_input.astype(f32)
    hidden = inputs + residual_scale * product(attn_rows, out_w)
    inv_rms2 = lax.rsqrt(jnp.mean(hidden * hidden, axis=-1, keepdims=True) + epsilon)
    normed2 = (hidden * inv_rms2 * gain_two).astype(bf16)
    arrived = exchange(product(send, tie(normed2, gu_w, down_w)).astype(bf16), CTX)
    gate_probs = gate_of(normed2, uses, router_w)

    hidden_units = down_w.shape[0]
    expert_out, in_grad, pre_grad, inner_act, route_grad = run_experts(
        expert, arrived, marked_arrived, gu_w, down_w, router_w
    )
    back = exchange(in_grad, CTX)
    grad_gu = product_tn(arrived, pre_grad).astype(bf16).reshape(4, -1, 2 * hidden_units)
    grad_down = product_tn(inner_act, route_grad).astype(bf16).reshape(4, -1, width)
    expert_both = scatter_core(jnp.concatenate([grad_gu, grad_down], axis=1))
    full_w = gather_fsdp(tie(by_head, arrived)).reshape(width, -1)

    slot_gate_grad = back[:, width].astype(f32) + back[:, width + 1].astype(f32)
    gate_grad = jnp.sum(
        jnp.where(slot_of, slot_gate_grad.reshape(EXPERTS, CAP)[:, :, None], 0.0), axis=1
    ).T
    mean_grad = jnp.sum(gate_probs * gate_grad, axis=-1, keepdims=True)
    logit_grad = (gate_probs * (gate_grad - mean_grad)).astype(bf16)
    normed2_grad = product_tn(send, back[:, :width]) + product_nt(logit_grad, router_w)
    normed2_grad = tie(normed2_grad, expert_both, full_w)
    hidden_part, gain_two_grad = norm_back(hidden, inv_rms2, gain_two, normed2_grad)
    hidden_grad = cotangent[0].astype(f32) + hidden_part
    branch_grad = (residual_scale * hidden_grad).astype(bf16)
    attn_grad = product_nt(branch_grad, out_w).astype(bf16)

    attn_grad = attn_grad.reshape(tokens, KV_HEADS, 2 * HEAD_DIM).transpose(1, 0, 2)
    group_grad = exchange(attn_grad.reshape(KV_HEADS * tokens, 2 * HEAD_DIM), ZY)
    group_grad_heads = group_grad.reshape(KV_HEADS * tokens, 2, HEAD_DIM).transpose(1, 0, 2)
    group_grad_pad = jnp.pad(group_grad_heads, ((0, 0), (0, 0), (HEAD_DIM, 0)))

    dense = jnp.concatenate(
        [
            product_tn(attn_rows, branch_grad).astype(bf16),
            product_tn(normed2, logit_grad).astype(bf16),
            gain_two_grad[:, None].astype(bf16),
            jnp.zeros((width, 128 - EXPERTS - 1), bf16),
        ],
        axis=1,
    )
    dense_both = scatter_core(dense.reshape(4, width // 4, width + 128))
    dq, *dkv_parts = attend_grad(numbers, queries, kv_parts, group_grad_pad, attn_turned, lse, dense_both)
    returned = exchange(tie(expert_out, group_grad), CTX)
    dense = scatter_row(dense_both)
    expert_sums = scatter_row(tie(expert_both, dq))

    dkv = dkv_parts[0].astype(f32)
    for step in (1, 2, 3):
        dkv = dkv + turn(dkv_parts[step], "x", -step).astype(f32)
    grads = jnp.concatenate(
        [
            rotate_back(dq[:, :HEAD_DIM], cosine, sine),
            rotate_back(dq[:, HEAD_DIM:], cosine, sine),
            rotate_back(dkv[:, :HEAD_DIM], cosine, sine),
            dkv[:, HEAD_DIM:],
        ],
        axis=1,
    ).astype(bf16)
    grads = tie(grads, returned)
    token_grads = exchange(grads, ZY)
    head_grad = scatter_fsdp(product_tn(group_normed, grads).reshape(4, shard_rows, 4 * HEAD_DIM))
    head_sum = sum_over(head_grad.astype(bf16), "x", 4)

    dense = exchange(tie(dense.astype(bf16), token_grads, expert_sums), CTX).reshape(EXPERTS, -1, width + 128)
    dense = gather_x(jnp.sum(dense.astype(f32), axis=0).astype(bf16))
    dense_rows = dense.shape[0] * dense.shape[1]

    token_grads = token_grads.reshape(KV_HEADS, tokens, 4 * HEAD_DIM).transpose(1, 0, 2)
    normed1_grad = product_nt(token_grads.reshape(tokens, -1), full_w)
    inv_rms1 = lax.rsqrt(jnp.mean(inputs * inputs, axis=-1, keepdims=True) + epsilon)
    input_part, gain_one_grad = norm_back(inputs, inv_rms1, gain_one, normed1_grad)
    input_grad = hidden_grad + input_part
    gain_sum = scatter_to(gain_one_grad.reshape(4, -1), ("yl", "core"), 4)
    gain_sum = sum_over(gain_sum, "x", 4)
    gain_high = gain_sum.astype(bf16)
    gain_rows = jnp.stack([gain_high, (gain_sum - gain_high.astype(f32)).astype(bf16)])

    last = jnp.concatenate(
        [
            head_sum.astype(bf16),
            jnp.pad(gain_rows, ((0, 14), (0, 0))),
            dense.reshape(-1, 4 * HEAD_DIM),
        ],
        axis=0,
    )
    last = exchange(jnp.tile(last, (KV_HEADS, 1)), ZY).reshape(KV_HEADS, -1, 4 * HEAD_DIM)
    grad_query, grad_key, grad_value, gain_one_grad = spread_heads(last, shard_rows)
    dense = last[:, shard_rows + 16 :].reshape(KV_HEADS, 4, -1, width + 128).transpose(1, 0, 2, 3)
    dense = dense.reshape(shard_rows, width + 128).astype(f32)

    weights = jnp.where(slot_of, gate_probs.T[:, None, :], 0.0).reshape(EXPERTS * CAP, tokens)
    weights_hi = weights.astype(bf16)
    weights_lo = (weights - weights_hi.astype(f32)).astype(bf16)
    mixture = product_tn(weights_hi, returned) + product_tn(weights_lo, returned)
    output = hidden + residual_scale * mixture

    return (
        output.astype(bf16)[None],
        input_grad[None],
        gain_one_grad.reshape(-1),
        grad_query,
        grad_key,
        grad_value,
        dense[:, :width],
        dense[:, width + EXPERTS],
        dense[:, width : width + EXPERTS],
        expert_sums[None, :shard_rows, :hidden_units],
        expert_sums[None, :shard_rows, hidden_units:],
        expert_sums[None, shard_rows:],
    )


def solution(mesh):
    fine = Mesh(mesh.devices.reshape(4, 4, 2, 2, 2), EVERY)
    rows, shards = P(("yl", "core"), CTX, None), P(("yl", "core"), None)
    gain, experts = P(("yl", "core")), P(CTX, ("yl", "core"), None)
    return jax.shard_map(
        on_device,
        mesh=fine,
        in_specs=(
            rows, rows, P(), gain, shards, shards, shards, shards, gain, shards, experts, experts, experts, rows,
        ),
        out_specs=(
            rows, rows, gain, shards, shards, shards, shards, gain, shards, experts, experts, experts,
        ),
        check_vma=False,
    )
```

```python
import functools

import jax
import jax.numpy as jnp
from jax import lax
from jax.experimental import pallas as pl
from jax.experimental.layout import Layout, with_layout_constraint
from jax.experimental.pallas import tpu as pltpu
from jax.sharding import Mesh
from jax.sharding import PartitionSpec as P

HEADS = 16
KV_HEADS = 8
HEAD_DIM = 64
EXPERTS = 32
TOP = 8
CAP = 48
HALF = 64
TILE = 512

epsilon = 1e-06
attn_scale = 0.015625
residual_scale = 0.22
masked_value = -1e30

CTX = ("x", "z", "yh")
ZY = ("z", "yh")
EVERY = ("x", "z", "yh", "yl", "core")
bf16 = jnp.bfloat16
f32 = jnp.float32


def product(left, right):
    return jnp.dot(left, right, preferred_element_type=f32)


def product_nt(left, right):
    return lax.dot_general(left, right, (((1,), (1,)), ((), ())), preferred_element_type=f32)


def product_tn(left, right):
    return lax.dot_general(left, right, (((0,), (0,)), ((), ())), preferred_element_type=f32)


def swap(values, axis):
    return lax.ppermute(values, axis, [(0, 1), (1, 0)])


def turn(values, axis, step):
    return lax.ppermute(values, axis, [(i, (i + step) % 4) for i in range(4)])


def rows_first(values):
    return with_layout_constraint(values, Layout(major_to_minor=tuple(range(values.ndim))))


def exchange(values, axes):
    return rows_first(lax.all_to_all(rows_first(values), axes, 0, 0, tiled=True))


def tie(values, *others):
    corner = tuple(slice(0, min(size, 8 if axis < values.ndim - 1 else 128)) for axis, size in enumerate(values.shape))
    nothing = sum(other[(0,) * other.ndim].astype(f32) * 0.0 for other in others)
    held = values[corner] + nothing.astype(values.dtype)
    return lax.dynamic_update_slice(values, held, (0,) * values.ndim)


def gather_direct(shard):
    me = lax.axis_index(("yl", "core"))
    whole = jnp.broadcast_to(shard[None], (4,) + shard.shape)
    for step in (1, 2, 3):
        other = lax.ppermute(shard, ("yl", "core"), [(i, i ^ step) for i in range(4)])
        whole = lax.dynamic_update_slice(whole, other[None], (me ^ step,) + (0,) * shard.ndim)
    return whole


def gather_core(shard, other):
    row, core = lax.axis_index("yl"), lax.axis_index("core")
    zero = (0,) * shard.ndim
    mine = jnp.broadcast_to(shard[None], (2,) + shard.shape)
    mine = lax.dynamic_update_slice(mine, other[None], (1 - row,) + zero)
    theirs = swap(mine, "core")
    pair = jnp.broadcast_to(mine[:, None], (2, 2) + shard.shape)
    pair = lax.dynamic_update_slice(pair, theirs[:, None], (0, 1 - core) + zero)
    return pair.reshape((4,) + shard.shape)


def gather_fsdp(shard):
    return gather_core(shard, swap(shard, "yl"))


def scatter_core(parts):
    core = lax.axis_index("core")
    parts = parts.astype(bf16).reshape((2, 2) + parts.shape[1:])
    away = lax.dynamic_index_in_dim(parts, 1 - core, 1, keepdims=False)
    keep = lax.dynamic_index_in_dim(parts, core, 1, keepdims=False)
    return (keep.astype(f32) + swap(away, "core").astype(f32)).astype(bf16)


def join_core(keep, away):
    return (keep.astype(f32) + swap(away, "core").astype(f32)).astype(bf16)


def scatter_row(both):
    row = lax.axis_index("yl")
    away = lax.dynamic_index_in_dim(both, 1 - row, 0, keepdims=False)
    keep = lax.dynamic_index_in_dim(both, row, 0, keepdims=False)
    return keep.astype(f32) + swap(away, "yl").astype(f32)


def scatter_fsdp(parts):
    return scatter_row(scatter_core(parts))


def scatter_to(parts, axes, count):
    me = lax.axis_index(axes)
    total = lax.dynamic_index_in_dim(parts, me, 0, keepdims=False).astype(f32)
    for step in range(1, count):
        away = lax.dynamic_index_in_dim(parts, (me + step) & (count - 1), 0, keepdims=False)
        total = total + lax.ppermute(away, axes, [(i, (i + step) % count) for i in range(count)]).astype(f32)
    return total


def sum_over(part, axes, count):
    total = part.astype(f32)
    for step in range(1, count):
        total = total + lax.ppermute(part, axes, [(i, (i + step) % count) for i in range(count)]).astype(f32)
    return total


def gather_x(shard):
    place = lax.axis_index("x")
    zero = (0,) * shard.ndim
    whole = lax.dynamic_update_slice(jnp.zeros((4,) + shard.shape, shard.dtype), shard[None], (place,) + zero)
    for step in (1, 2, 3):
        whole = lax.dynamic_update_slice(whole, turn(shard, "x", step)[None], ((place - step) & 3,) + zero)
    return whole


def rope_tables(positions):
    freqs = jnp.power(10000.0, -jnp.arange(0, HEAD_DIM, 2, dtype=f32) / HEAD_DIM)
    angles = positions.astype(f32)[:, None] * freqs[None, :]
    cosine, sine = jnp.cos(angles), jnp.sin(angles)
    ones, zeros = jnp.ones_like(cosine), jnp.zeros_like(cosine)
    return (
        jnp.concatenate([cosine] * 6 + [ones] * 2, axis=1),
        jnp.concatenate([-sine, sine] * 3 + [zeros] * 2, axis=1),
    )


def turned(values):
    width = values.shape[1]
    column = lax.broadcasted_iota(jnp.int32, values.shape, 1)
    return jnp.where(
        column % HEAD_DIM < HEAD_DIM // 2,
        pltpu.roll(values, width - HEAD_DIM // 2, 1),
        pltpu.roll(values, HEAD_DIM // 2, 1),
    )


def norm_back(values, inv_rms, gain, grad):
    weighted = grad * gain
    gain_grad = jnp.sum(grad * values * inv_rms, axis=0, keepdims=True)
    inner_mean = jnp.mean(weighted * values, axis=-1, keepdims=True)
    return (weighted * inv_rms - values * inv_rms * inv_rms * inv_rms * inner_mean, gain_grad)


def inv_rms_of(values):
    return lax.rsqrt(jnp.mean(values * values, axis=-1, keepdims=True) + epsilon)


def half(index):
    return pl.ds(pl.multiple_of(index * HALF, HALF), HALF)


def key_tile(counter):
    return pl.ds(pl.multiple_of(counter * TILE, TILE), TILE)


def sort_keys(knum_ref, kv_refs, kvs, kvt):
    blocks = kv_refs[0].shape[0] // HALF
    for slot, kv_ref in enumerate(kv_refs):
        for block in range(blocks):
            kvs[half(knum_ref[slot * blocks + block]), :] = kv_ref[block * HALF : (block + 1) * HALF, :]
    for tile in range(kvs.shape[0] // TILE):
        part = kvs[tile * TILE : (tile + 1) * TILE, :].astype(f32)
        kvt[:, tile * TILE : (tile + 1) * TILE] = part.T.astype(bf16)


def pair_rows(ref, first, second, upper):
    rows = []
    for block in (first, second):
        values = ref[half(block), :].astype(f32)
        column = lax.broadcasted_iota(jnp.int32, values.shape, 1)
        inside = (column >= HEAD_DIM) if upper else (column < HEAD_DIM)
        moved = pltpu.roll(values, HEAD_DIM, 1)
        heads = (moved, values) if upper else (values, moved)
        rows += [jnp.where(inside, head, 0.0) for head in heads]
    return jnp.concatenate(rows, axis=0)


def pair_positions(low_number, high_number):
    column = lax.broadcasted_iota(jnp.int32, (1, 4 * HALF), 1)
    return jnp.where(column < 2 * HALF, low_number, high_number) * HALF + column % HALF


def score_tile(keys, queries, counter, positions, masked):
    scores = product_nt(keys, queries)
    if masked:
        key_pos = counter * TILE + lax.broadcasted_iota(jnp.int32, scores.shape, 0)
        scores = jnp.where(key_pos <= positions, scores, masked_value)
    return scores


def store_rows(ref, turned, first, second):
    rows = turned.T
    ref[half(first), :] = jnp.concatenate([rows[:HALF], rows[HALF : 2 * HALF]], axis=1).astype(ref.dtype)
    ref[half(second), :] = jnp.concatenate([rows[2 * HALF : 3 * HALF], rows[3 * HALF :]], axis=1).astype(ref.dtype)


def attend_kernel(
    order_ref, qnum_ref, knum_ref, q_ref, kv0, kv1, kv2, kv3, held_ref, out_ref, turned_ref, lse_ref, kvs, kvt
):
    del held_ref
    sort_keys(knum_ref, (kv0, kv1, kv2, kv3), kvs, kvt)
    width = 4 * HALF

    @pl.loop(0, q_ref.shape[0] // (2 * HALF))
    def _(pair):
        first, second = order_ref[2 * pair], order_ref[2 * pair + 1]
        low_number, high_number = qnum_ref[first], qnum_ref[second]
        queries = pair_rows(q_ref, first, second, False).astype(bf16)
        positions = pair_positions(low_number, high_number)

        def step(masked, counter, running):
            top, total, mixed = running
            scores = score_tile(kvs[key_tile(counter), :], queries, counter, positions, masked)
            new_top = jnp.maximum(top, jnp.max(scores, axis=0, keepdims=True))
            probs = jnp.exp(scores - new_top)
            shrink = jnp.exp(top - new_top)
            total = total * shrink + jnp.sum(probs, axis=0, keepdims=True)
            mixed = mixed * shrink + product(kvt[HEAD_DIM:, key_tile(counter)], probs.astype(bf16))
            return (new_top, total, mixed)

        start = (
            jnp.full((1, width), masked_value, f32),
            jnp.zeros((1, width), f32),
            jnp.zeros((HEAD_DIM, width), f32),
        )
        full = (low_number * HALF) // TILE
        last = (high_number * HALF) // TILE + 1
        running = lax.fori_loop(0, full, functools.partial(step, False), start)
        top, total, mixed = lax.fori_loop(full, last, functools.partial(step, True), running)
        mixed = mixed / total
        turned_ref[pair] = mixed
        lse_ref[pair] = top + jnp.log(total)
        store_rows(out_ref, mixed, first, second)


def attend_grad_kernel(
    order_ref, qnum_ref, knum_ref, q_ref, kv0, kv1, kv2, kv3, grad_ref, turned_ref, lse_ref, held_ref,
    dq_ref, dkv0, dkv1, dkv2, dkv3, kvs, kvt, total_ref,
):
    del held_ref
    sort_keys(knum_ref, (kv0, kv1, kv2, kv3), kvs, kvt)
    total_ref[...] = jnp.zeros_like(total_ref)
    width = 4 * HALF

    @pl.loop(0, q_ref.shape[0] // (2 * HALF))
    def _(pair):
        first, second = order_ref[2 * pair], order_ref[2 * pair + 1]
        low_number, high_number = qnum_ref[first], qnum_ref[second]
        queries = pair_rows(q_ref, first, second, False).astype(bf16)
        grads_f = pair_rows(grad_ref, first, second, True)
        grads = grads_f.astype(bf16)
        both = jnp.concatenate([queries, grads], axis=0)
        positions = pair_positions(low_number, high_number)
        lse = lse_ref[pair]
        dots = jnp.sum(grads_f.T[HEAD_DIM:] * turned_ref[pair], axis=0, keepdims=True)

        def step(masked, counter, query_acc):
            keys = kvs[key_tile(counter), :]
            probs = jnp.exp(score_tile(keys, queries, counter, positions, masked) - lse)
            score_grad = (probs * (product_nt(keys, grads) - dots)).astype(bf16)
            sides = jnp.concatenate([score_grad, probs.astype(bf16)], axis=1)
            total_ref[key_tile(counter), :] += product(sides, both)
            return query_acc + product(kvt[:HEAD_DIM, key_tile(counter)], score_grad)

        full = (low_number * HALF) // TILE
        last = (high_number * HALF) // TILE + 1
        query_acc = lax.fori_loop(0, full, functools.partial(step, False), jnp.zeros((HEAD_DIM, width), f32))
        query_acc = lax.fori_loop(full, last, functools.partial(step, True), query_acc)
        store_rows(dq_ref, query_acc * attn_scale, first, second)

    blocks = dkv0.shape[0] // HALF
    for slot, dkv in enumerate((dkv0, dkv1, dkv2, dkv3)):
        for block in range(blocks):
            dkv[block * HALF : (block + 1) * HALF, :] = total_ref[
                half(knum_ref[slot * blocks + block]), :
            ].astype(bf16)


def expert_kernel(
    expert_ref, rows_ref, marked_ref, gu_ref, down_ref, router_ref,
    out_ref, in_grad_ref, pre_grad_ref, inner_ref, route_grad_ref,
):
    rows = rows_ref[...]
    width = rows.shape[1]
    units = down_ref.shape[0]
    pre = product(rows, gu_ref[...])
    gate_pre, up_pre = pre[:, :units], pre[:, units:]
    sigmoid_a = 1.0 / (1.0 + jnp.exp(-gate_pre))
    swish_act = gate_pre * sigmoid_a
    inner_act = (swish_act * up_pre).astype(bf16)
    inner_ref[...] = inner_act
    expert_out = product(inner_act, down_ref[...]).astype(bf16)
    out_ref[...] = expert_out
    uses = marked_ref[:, width : width + EXPERTS].astype(f32)
    probs = gate_of(rows, uses, router_ref[...])
    column = lax.broadcasted_iota(jnp.int32, probs.shape, 1)
    slot_probs = jnp.sum(jnp.where(column == expert_ref[0], probs, 0.0), axis=1, keepdims=True)
    mix_grad = residual_scale * marked_ref[:, :width].astype(f32)
    gate_grad = jnp.sum(mix_grad * expert_out.astype(f32), axis=1, keepdims=True)
    route_grad = (slot_probs * mix_grad).astype(bf16)
    route_grad_ref[...] = route_grad
    inner_grad = product_nt(route_grad, down_ref[...])
    pre_grad_ref[:, :units] = (
        inner_grad * up_pre * sigmoid_a * (1.0 + gate_pre * (1.0 - sigmoid_a))
    ).astype(bf16)
    pre_grad_ref[:, units:] = (inner_grad * swish_act).astype(bf16)
    in_grad_ref[:, :width] = product_nt(pre_grad_ref[...], gu_ref[...]).astype(bf16)
    column = lax.broadcasted_iota(jnp.int32, (rows.shape[0], 128), 1)
    high = gate_grad.astype(bf16).astype(f32)
    in_grad_ref[:, width:] = jnp.where(
        column == expert_ref[0], high, jnp.where(column == EXPERTS + expert_ref[0], gate_grad - high, 0.0)
    ).astype(bf16)


def project_kernel(x_ref, w_ref, gain_ref, cos_ref, sin_ref, normed_ref, q_ref, kv_ref):
    values = x_ref[...].astype(f32)
    normed = (values * inv_rms_of(values) * gain_ref[...]).astype(bf16)
    normed_ref[...] = normed
    projected = product(normed, w_ref[...])
    rotated = projected * cos_ref[...] + turned(projected) * sin_ref[...]
    q_ref[...] = rotated[:, : 2 * HEAD_DIM].astype(bf16) * bf16(attn_scale)
    kv_ref[...] = rotated[:, 2 * HEAD_DIM :].astype(bf16)


def project(rows, head_w, gain, cosine, sine):
    count, width = rows.shape
    tile = 256

    def tiled(columns):
        return pl.BlockSpec((tile, columns), lambda i: (i, 0))

    def whole(array):
        return pl.BlockSpec(array.shape, lambda i: (0, 0))

    columns = (width, 2 * HEAD_DIM, 2 * HEAD_DIM)
    return pl.pallas_call(
        project_kernel,
        grid=(count // tile,),
        out_shape=tuple(jax.ShapeDtypeStruct((count, c), bf16) for c in columns),
        in_specs=[tiled(width), whole(head_w), whole(gain), tiled(4 * HEAD_DIM), tiled(4 * HEAD_DIM)],
        out_specs=tuple(tiled(c) for c in columns),
        compiler_params=pltpu.CompilerParams(vmem_limit_bytes=32 * 1024 * 1024),
        cost_estimate=pl.CostEstimate(flops=600_000_000, bytes_accessed=8_000_000, transcendentals=0),
    )(rows, head_w, gain, cosine, sine)


def call(kernel, outs, operands, flops, held=(), scalars=0):
    count = len(operands)

    def body(*refs):
        kernel(*refs[:count], *refs[count + len(held) :])

    return pl.pallas_call(
        body,
        out_shape=tuple(jax.ShapeDtypeStruct(shape, dtype) for shape, dtype in outs),
        in_specs=[SMEM] * scalars + [VMEM] * (count - scalars) + [pl.BlockSpec(memory_space=pl.ANY)] * len(held),
        out_specs=(VMEM,) * len(outs),
        compiler_params=pltpu.CompilerParams(vmem_limit_bytes=48 * 1024 * 1024),
        cost_estimate=pl.CostEstimate(flops=flops, bytes_accessed=8_000_000, transcendentals=0),
    )(*operands, *held)


def send_kernel(send_ref, rows_ref, out_ref):
    out_ref[...] = product(send_ref[...], rows_ref[...]).astype(bf16)


def middle_kernel(
    attn_ref, out_w_ref, x_ref, gain_ref, router_ref, uses_ref, send_ref,
    rows_ref, hidden_ref, normed_ref, probs_ref, out_ref,
):
    for head in range(KV_HEADS):
        rows_ref[:, head * 2 * HEAD_DIM : (head + 1) * 2 * HEAD_DIM] = attn_ref[head]
    hidden = x_ref[...].astype(f32) + residual_scale * product(rows_ref[...], out_w_ref[...])
    hidden_ref[...] = hidden
    normed = (hidden * inv_rms_of(hidden) * gain_ref[...]).astype(bf16)
    normed_ref[...] = normed
    out_ref[...] = product(send_ref[...], normed).astype(bf16)
    probs_ref[...] = gate_of(normed, uses_ref[...], router_ref[...])


def token_grad_kernel(
    fetch_ref, back_ref, probs_ref, router_ref, hidden_ref, gain_ref, cot_ref, out_w_ref,
    hidden_grad_ref, branch_ref, logit_ref, gain_grad_ref, attn_grad_ref,
):
    width = hidden_ref.shape[1]
    fetched = product(fetch_ref[...], back_ref[...])
    gate_grad = fetched[:, width : width + EXPERTS] + fetched[:, width + EXPERTS : width + 2 * EXPERTS]
    probs = probs_ref[...]
    mean_grad = jnp.sum(probs * gate_grad, axis=-1, keepdims=True)
    logit_grad = (probs * (gate_grad - mean_grad)).astype(bf16)
    logit_ref[...] = logit_grad
    normed_grad = fetched[:, :width] + product_nt(logit_grad, router_ref[...])
    hidden = hidden_ref[...]
    hidden_part, gain_grad = norm_back(hidden, inv_rms_of(hidden), gain_ref[...], normed_grad)
    gain_grad_ref[...] = gain_grad
    hidden_grad = cot_ref[...].astype(f32) + hidden_part
    hidden_grad_ref[...] = hidden_grad
    branch = (residual_scale * hidden_grad).astype(bf16)
    branch_ref[...] = branch
    attn_grad = product_nt(branch, out_w_ref[...]).astype(bf16)
    for head in range(KV_HEADS):
        attn_grad_ref[head] = attn_grad[:, head * 2 * HEAD_DIM : (head + 1) * 2 * HEAD_DIM]


def dense_grad_kernel(core_ref, rows_ref, branch_ref, normed_ref, logit_ref, gain_ref, keep_ref, away_ref):
    part, width = keep_ref.shape[1], branch_ref.shape[1]
    logit_grad = logit_ref[...].astype(f32)
    logit_grad = jnp.concatenate(
        [logit_grad, jnp.zeros((logit_grad.shape[0], 128 - EXPERTS), f32)], axis=1
    ).astype(bf16)
    column = lax.broadcasted_iota(jnp.int32, (part, 128), 1)
    for row in range(2):
        for ref, core in ((keep_ref, core_ref[0]), (away_ref, 1 - core_ref[0])):
            columns = pl.ds(pl.multiple_of((2 * row + core) * part, part), part)
            ref[row, :, :width] = product_tn(rows_ref[:, columns], branch_ref[...]).astype(bf16)
            router_grad = product_tn(normed_ref[:, columns], logit_grad)
            gain_grad = jnp.broadcast_to(gain_ref[:, columns], (128, part)).T
            ref[row, :, width:] = jnp.where(column == EXPERTS, gain_grad, router_grad).astype(bf16)


def head_grad_kernel(dq_ref, dkv0, dkv1, dkv2, dkv3, cos_ref, sin_ref, out_ref):
    dkv = dkv0[...].astype(f32) + dkv1[...].astype(f32) + dkv2[...].astype(f32) + dkv3[...].astype(f32)
    for side, grad in enumerate((dq_ref[...], dkv)):
        columns = slice(side * 2 * HEAD_DIM, (side + 1) * 2 * HEAD_DIM)
        out_ref[:, columns] = (grad * cos_ref[:, columns] - turned(grad) * sin_ref[:, columns]).astype(bf16)


def head_weight_kernel(core_ref, normed_ref, grads_ref, keep_ref, away_ref):
    part = keep_ref.shape[1]
    for row in range(2):
        for ref, core in ((keep_ref, core_ref[0]), (away_ref, 1 - core_ref[0])):
            columns = pl.ds(pl.multiple_of((2 * row + core) * part, part), part)
            ref[row] = product_tn(normed_ref[:, columns], grads_ref[...]).astype(bf16)


def input_grad_kernel(grads_ref, w_ref, x_ref, gain_ref, hidden_grad_ref, out_ref, gain_grad_ref):
    normed_grad = jnp.zeros(out_ref.shape, f32)
    width = 4 * HEAD_DIM
    for head in range(KV_HEADS):
        normed_grad += product_nt(grads_ref[head], w_ref[:, head * width : (head + 1) * width])
    values = x_ref[...].astype(f32)
    part, gain_grad = norm_back(values, inv_rms_of(values), gain_ref[...], normed_grad)
    out_ref[...] = hidden_grad_ref[...] + part
    gain_grad_ref[...] = gain_grad


def spread_kernel(last_ref, query_ref, key_ref, value_ref, gain_ref):
    rows = query_ref.shape[0]
    gain = jnp.zeros(gain_ref.shape, f32)
    for head in range(KV_HEADS):
        query_ref[:, head * 2 * HEAD_DIM : (head + 1) * 2 * HEAD_DIM] = last_ref[head, :rows, : 2 * HEAD_DIM].astype(f32)
        gain += jnp.sum(last_ref[head, rows : rows + 16, :].astype(f32), axis=0, keepdims=True)
    gain_ref[...] = gain
    for pair in range(KV_HEADS // 2):
        sides = [last_ref[2 * pair + side, :rows, 2 * HEAD_DIM :].astype(f32) for side in (0, 1)]
        columns = slice(pair * 2 * HEAD_DIM, (pair + 1) * 2 * HEAD_DIM)
        key_ref[:, columns] = jnp.concatenate([side[:, :HEAD_DIM] for side in sides], axis=1)
        value_ref[:, columns] = jnp.concatenate([side[:, HEAD_DIM:] for side in sides], axis=1)


def spread_heads(last, rows):
    heads, _, width = last.shape
    return pl.pallas_call(
        spread_kernel,
        out_shape=(
            jax.ShapeDtypeStruct((rows, heads * 2 * HEAD_DIM), f32),
            jax.ShapeDtypeStruct((rows, heads * HEAD_DIM), f32),
            jax.ShapeDtypeStruct((rows, heads * HEAD_DIM), f32),
            jax.ShapeDtypeStruct((1, width), f32),
        ),
        in_specs=[VMEM],
        out_specs=(VMEM,) * 4,
        compiler_params=pltpu.CompilerParams(vmem_limit_bytes=24 * 1024 * 1024),
        cost_estimate=pl.CostEstimate(flops=1_000_000, bytes_accessed=4_000_000, transcendentals=0),
    )(last)


def gate_of(rows, mask, router_w):
    logits = jnp.where(mask > 0, product(rows, router_w), masked_value)
    exps = jnp.where(mask > 0, jnp.exp(logits - jnp.max(logits, axis=-1, keepdims=True)), 0.0)
    return exps / jnp.maximum(jnp.sum(exps, axis=-1, keepdims=True), 1e-30)


def run_experts(expert, rows, marked, gu_w, down_w, router_w):
    count, width = rows.shape
    units = down_w.shape[0]
    tile = 256

    def tiled(columns):
        return pl.BlockSpec((tile, columns), lambda i: (i, 0))

    def whole(array):
        return pl.BlockSpec(array.shape, lambda i: (0, 0))

    columns = (width, width + 128, 2 * units, units, width)
    return pl.pallas_call(
        expert_kernel,
        grid=(count // tile,),
        out_shape=tuple(jax.ShapeDtypeStruct((count, c), bf16) for c in columns),
        in_specs=[SMEM, tiled(width), tiled(width + 128), whole(gu_w), whole(down_w), whole(router_w)],
        out_specs=tuple(tiled(c) for c in columns),
        compiler_params=pltpu.CompilerParams(vmem_limit_bytes=56 * 1024 * 1024),
        cost_estimate=pl.CostEstimate(flops=10_000_000_000, bytes_accessed=22_000_000, transcendentals=1_000_000),
    )(expert.astype(jnp.int32).reshape(1), rows, marked, gu_w, down_w, router_w)


SMEM = pl.BlockSpec(memory_space=pltpu.SMEM)
VMEM = pl.BlockSpec(memory_space=pltpu.VMEM)


def attend(numbers, queries, kv_parts, held):
    rows = queries.shape[0]
    keys = rows * len(kv_parts)
    pairs = rows // (2 * HALF)
    return pl.pallas_call(
        attend_kernel,
        out_shape=(
            jax.ShapeDtypeStruct((rows, 2 * HEAD_DIM), bf16),
            jax.ShapeDtypeStruct((pairs, HEAD_DIM, 4 * HALF), f32),
            jax.ShapeDtypeStruct((pairs, 1, 4 * HALF), f32),
        ),
        in_specs=[SMEM] * 3 + [VMEM] * 5 + [pl.BlockSpec(memory_space=pl.ANY)],
        out_specs=(VMEM,) * 3,
        scratch_shapes=[pltpu.VMEM((keys, 2 * HEAD_DIM), bf16), pltpu.VMEM((2 * HEAD_DIM, keys), bf16)],
        compiler_params=pltpu.CompilerParams(vmem_limit_bytes=40 * 1024 * 1024),
        cost_estimate=pl.CostEstimate(flops=12_000_000_000, bytes_accessed=4_000_000, transcendentals=5_000_000),
    )(*numbers, queries, *kv_parts, held)


def attend_grad(numbers, queries, kv_parts, grads, turned, lse, held):
    rows = queries.shape[0]
    keys = rows * len(kv_parts)
    return pl.pallas_call(
        attend_grad_kernel,
        out_shape=(jax.ShapeDtypeStruct((rows, 2 * HEAD_DIM), f32),)
        + (jax.ShapeDtypeStruct((rows, 2 * HEAD_DIM), bf16),) * 4,
        in_specs=[SMEM] * 3 + [VMEM] * 8 + [pl.BlockSpec(memory_space=pl.ANY)],
        out_specs=(VMEM,) * 5,
        scratch_shapes=[
            pltpu.VMEM((keys, 2 * HEAD_DIM), bf16),
            pltpu.VMEM((2 * HEAD_DIM, keys), bf16),
            pltpu.VMEM((keys, 2 * HEAD_DIM), f32),
        ],
        compiler_params=pltpu.CompilerParams(vmem_limit_bytes=40 * 1024 * 1024),
        cost_estimate=pl.CostEstimate(flops=30_000_000_000, bytes_accessed=6_000_000, transcendentals=5_000_000),
    )(*numbers, queries, *kv_parts, grads, turned, lse, held)


def block_numbers(block_pairs):
    place = lax.axis_index("x")
    groups = block_pairs.reshape(4, 8)
    groups = groups[(place - jnp.arange(4)) & 3]
    numbers = jnp.stack([groups, 63 - groups], axis=-1).reshape(-1)
    own = numbers[:16]
    rank = jnp.sum((own[None, :] < own[:, None]).astype(jnp.int32), axis=1)
    spots = jnp.arange(16, dtype=jnp.int32)
    order = jnp.sum(jnp.where(rank[None, :] == spots[:, None], spots[None, :], 0), axis=1)
    return (order, own, numbers)


def on_device(
    block_input,
    routes,
    block_pairs,
    norm1_gain,
    w_query,
    w_key,
    w_value,
    w_out,
    norm2_gain,
    w_router,
    w_gate,
    w_up,
    w_down,
    cotangent,
):
    tokens, width = block_input.shape[1:]
    head = lax.axis_index(ZY)
    expert = lax.axis_index(CTX)
    shard_rows = w_query.shape[0]
    own_input = block_input[0]

    core = lax.axis_index("core").astype(jnp.int32).reshape(1)
    small_shard = jnp.concatenate(
        [
            lax.dynamic_slice_in_dim(w_query, head * 2 * HEAD_DIM, 2 * HEAD_DIM, 1),
            lax.dynamic_slice_in_dim(w_key, head * HEAD_DIM, HEAD_DIM, 1),
            lax.dynamic_slice_in_dim(w_value, head * HEAD_DIM, HEAD_DIM, 1),
            w_router,
            norm1_gain[:, None],
            norm2_gain[:, None],
            jnp.zeros((shard_rows, 128 - EXPERTS - 2), bf16),
        ],
        axis=1,
    )
    small_w = gather_direct(small_shard).reshape(width, -1)
    head_w, small_w = small_w[:, : 4 * HEAD_DIM], small_w[:, 4 * HEAD_DIM :]
    router_w = small_w[:, :EXPERTS]
    gain_one = small_w[:, EXPERTS].astype(f32).reshape(1, width)
    gain_two = small_w[:, EXPERTS + 1].astype(f32).reshape(1, width)
    group_input = exchange(jnp.tile(own_input, (KV_HEADS, 1)), ZY)

    numbers = block_numbers(block_pairs)
    group_pos = (numbers[1][:, None] * HALF + jnp.arange(HALF, dtype=jnp.int32)[None, :]).reshape(-1)
    cosine, sine = rope_tables(group_pos)

    chosen = routes[0]
    uses = jnp.sum(
        (chosen[:, :, None] == jnp.arange(EXPERTS, dtype=jnp.int32)[None, None, :]).astype(f32), axis=1
    )
    earlier = jnp.tril(jnp.ones((tokens, tokens), bf16), -1)
    rank = product(earlier, uses.astype(bf16)).astype(jnp.int32)
    rank = jnp.where(uses > 0, rank, -1)
    slot = jnp.arange(CAP, dtype=jnp.int32)
    send = (rank.T[:, None, :] == slot[None, :, None]).astype(bf16).reshape(EXPERTS * CAP, tokens)
    fetch = (rank[:, :, None] == slot[None, None, :]).astype(bf16).reshape(tokens, EXPERTS * CAP)

    group_normed, queries, kv_own = project(group_input, head_w, gain_one, cosine, sine)
    kv_parts = [kv_own] + [turn(kv_own, "x", step) for step in (1, 2, 3)]

    out_shard = tie(w_out, group_input)
    out_other = swap(out_shard, "yl")
    marked = jnp.concatenate(
        [cotangent[0], uses.astype(bf16), jnp.zeros((tokens, 128 - EXPERTS), bf16)], axis=1
    )
    (marked_sent,) = call(
        send_kernel,
        [((EXPERTS * CAP, width + 128), bf16)],
        (send, marked),
        500_000_000,
        held=(*kv_parts[1:], out_other),
    )
    marked_arrived = exchange(marked_sent, CTX)

    attn_group, attn_turned, lse = attend(numbers, queries, kv_parts, out_other)

    out_w = gather_core(out_shard, out_other).reshape(HEADS * HEAD_DIM, width)
    gu_shard = tie(jnp.concatenate([w_gate[0], w_up[0]], axis=1), attn_group)
    down_shard = tie(w_down[0], attn_group)
    gu_other, down_other = swap(gu_shard, "yl"), swap(down_shard, "yl")

    attn_back = exchange(tie(attn_group, marked_arrived), ZY)
    gu_w = gather_core(gu_shard, tie(gu_other, attn_back)).reshape(width, -1)
    down_w = gather_core(down_shard, tie(down_other, attn_back)).reshape(-1, width)
    attn_rows, hidden, normed2, gate_probs, outgoing = call(
        middle_kernel,
        [
            ((tokens, HEADS * HEAD_DIM), bf16),
            ((tokens, width), f32),
            ((tokens, width), bf16),
            ((tokens, EXPERTS), f32),
            ((EXPERTS * CAP, width), bf16),
        ],
        (
            attn_back.reshape(KV_HEADS, tokens, 2 * HEAD_DIM), out_w, own_input, gain_two, router_w, uses, send,
        ),
        800_000_000,
        held=(gu_w, down_w),
    )
    arrived = exchange(outgoing, CTX)

    hidden_units = down_w.shape[0]
    expert_out, in_grad, pre_grad, inner_act, route_grad = run_experts(
        expert, arrived, marked_arrived, gu_w, down_w, router_w
    )
    back = exchange(in_grad, CTX)
    grad_gu = product_tn(arrived, pre_grad).astype(bf16).reshape(4, -1, 2 * hidden_units)
    grad_down = product_tn(inner_act, route_grad).astype(bf16).reshape(4, -1, width)
    expert_both = scatter_core(jnp.concatenate([grad_gu, grad_down], axis=1))
    by_head = jnp.concatenate(
        [
            w_query.reshape(shard_rows, KV_HEADS, 2 * HEAD_DIM),
            w_key.reshape(shard_rows, KV_HEADS, HEAD_DIM),
            w_value.reshape(shard_rows, KV_HEADS, HEAD_DIM),
        ],
        axis=2,
    ).reshape(shard_rows, -1)
    full_w = gather_fsdp(tie(by_head, arrived)).reshape(width, -1)

    hidden_grad, branch_grad, logit_grad, gain_two_grad, attn_grad = call(
        token_grad_kernel,
        [
            ((tokens, width), f32),
            ((tokens, width), bf16),
            ((tokens, EXPERTS), bf16),
            ((1, width), f32),
            ((KV_HEADS, tokens, 2 * HEAD_DIM), bf16),
        ],
        (fetch, back, gate_probs, router_w, hidden, gain_two, cotangent[0], out_w),
        800_000_000,
        held=(expert_both, full_w),
    )

    group_grad = exchange(attn_grad.reshape(KV_HEADS * tokens, 2 * HEAD_DIM), ZY)
    dense_shape = ((2, shard_rows, width + 128), bf16)
    dense_both = join_core(
        *call(
            dense_grad_kernel,
            [dense_shape, dense_shape],
            (core, attn_rows, branch_grad, normed2, logit_grad, gain_two_grad),
            400_000_000,
            scalars=1,
        )
    )
    dq, *dkv_parts = attend_grad(numbers, queries, kv_parts, group_grad, attn_turned, lse, dense_both)
    returned = exchange(tie(expert_out, group_grad), CTX)
    dense = scatter_row(dense_both)
    expert_sums = scatter_row(tie(expert_both, dq))

    (grads,) = call(
        head_grad_kernel,
        [((KV_HEADS * tokens, 4 * HEAD_DIM), bf16)],
        (dq, dkv_parts[0], *(turn(dkv_parts[step], "x", -step) for step in (1, 2, 3)), cosine, sine),
        100_000_000,
        held=(returned,),
    )
    token_grads = exchange(grads, ZY)
    head_shape = ((2, shard_rows, 4 * HEAD_DIM), bf16)
    head_both = join_core(
        *call(head_weight_kernel, [head_shape, head_shape], (core, group_normed, grads), 600_000_000, scalars=1)
    )
    head_sum = sum_over(scatter_row(head_both).astype(bf16), "x", 4)

    dense = exchange(tie(dense.astype(bf16), token_grads, expert_sums), CTX).reshape(EXPERTS, -1, width + 128)
    dense = gather_x(jnp.sum(dense.astype(f32), axis=0).astype(bf16))

    input_grad, gain_one_grad = call(
        input_grad_kernel,
        [((tokens, width), f32), ((1, width), f32)],
        (
            token_grads.reshape(KV_HEADS, tokens, 4 * HEAD_DIM), full_w, own_input, gain_one, hidden_grad,
        ),
        600_000_000,
    )
    gain_sum = scatter_to(gain_one_grad.reshape(4, -1), ("yl", "core"), 4)
    gain_sum = sum_over(tie(gain_sum, dense), "x", 4)
    gain_high = gain_sum.astype(bf16)
    gain_rows = jnp.stack([gain_high, (gain_sum - gain_high.astype(f32)).astype(bf16)])

    last = jnp.concatenate(
        [
            head_sum.astype(bf16),
            jnp.pad(gain_rows, ((0, 14), (0, 0))),
            dense.reshape(-1, 4 * HEAD_DIM),
        ],
        axis=0,
    )
    last = exchange(jnp.tile(last, (KV_HEADS, 1)), ZY).reshape(KV_HEADS, -1, 4 * HEAD_DIM)
    grad_query, grad_key, grad_value, gain_one_grad = spread_heads(last, shard_rows)
    dense = last[:, shard_rows + 16 :].reshape(KV_HEADS, 4, -1, width + 128).transpose(1, 0, 2, 3)
    dense = dense.reshape(shard_rows, width + 128).astype(f32)

    spread = gate_probs[:, :, None] * fetch.astype(f32).reshape(tokens, EXPERTS, CAP)
    weights = spread.reshape(tokens, EXPERTS * CAP)
    weights_hi = weights.astype(bf16)
    weights_lo = (weights - weights_hi.astype(f32)).astype(bf16)
    mixture = product(weights_hi, returned) + product(weights_lo, returned)
    output = hidden + residual_scale * mixture

    return (
        output.astype(bf16)[None],
        input_grad[None],
        gain_one_grad.reshape(-1),
        grad_query,
        grad_key,
        grad_value,
        dense[:, :width],
        dense[:, width + EXPERTS],
        dense[:, width : width + EXPERTS],
        expert_sums[None, :shard_rows, :hidden_units],
        expert_sums[None, :shard_rows, hidden_units:],
        expert_sums[None, shard_rows:],
    )


def solution(mesh):
    fine = Mesh(mesh.devices.reshape(4, 4, 2, 2, 2), EVERY)
    rows, shards = P(("yl", "core"), CTX, None), P(("yl", "core"), None)
    gain, experts = P(("yl", "core")), P(CTX, ("yl", "core"), None)
    return jax.shard_map(
        on_device,
        mesh=fine,
        in_specs=(
            rows, rows, P(), gain, shards, shards, shards, shards, gain, shards, experts, experts, experts, rows,
        ),
        out_specs=(
            rows, rows, gain, shards, shards, shards, shards, gain, shards, experts, experts, experts,
        ),
        check_vma=False,
    )
```

```python
import functools

import jax
import jax.numpy as jnp
from jax import lax
from jax.experimental import pallas as pl
from jax.experimental.layout import Layout, with_layout_constraint
from jax.experimental.pallas import tpu as pltpu
from jax.sharding import Mesh
from jax.sharding import PartitionSpec as P

HEADS = 16
KV_HEADS = 8
HEAD_DIM = 64
EXPERTS = 32
TOP = 8
CAP = 48
HALF = 64
TILE = 512

epsilon = 1e-06
attn_scale = 0.015625
residual_scale = 0.22
masked_value = -1e30

CTX = ("x", "z", "yh")
ZY = ("z", "yh")
EVERY = ("x", "z", "yh", "yl", "core")
bf16 = jnp.bfloat16
f32 = jnp.float32


def product(left, right):
    return jnp.dot(left, right, preferred_element_type=f32)


def product_nt(left, right):
    return lax.dot_general(left, right, (((1,), (1,)), ((), ())), preferred_element_type=f32)


def product_tn(left, right):
    return lax.dot_general(left, right, (((0,), (0,)), ((), ())), preferred_element_type=f32)


def swap(values, axis):
    return lax.ppermute(values, axis, [(0, 1), (1, 0)])


def turn(values, axis, step):
    return lax.ppermute(values, axis, [(i, (i + step) % 4) for i in range(4)])


def rows_first(values):
    return with_layout_constraint(values, Layout(major_to_minor=tuple(range(values.ndim))))


def exchange(values, axes):
    return rows_first(lax.all_to_all(rows_first(values), axes, 0, 0, tiled=True))


def tie(values, *others):
    if values.size <= 1024:
        return values + sum(other[(0,) * other.ndim].astype(f32) * 0.0 for other in others).astype(values.dtype)
    corner = tuple(slice(0, min(size, 8 if axis < values.ndim - 1 else 128)) for axis, size in enumerate(values.shape))
    nothing = sum(other[(0,) * other.ndim].astype(f32) * 0.0 for other in others)
    held = values[corner] + nothing.astype(values.dtype)
    return lax.dynamic_update_slice(values, held, (0,) * values.ndim)


def pieces_direct(shard):
    steps = [lax.ppermute(shard, ("yl", "core"), [(i, i ^ k) for i in range(4)]) for k in (1, 2, 3)]
    return (shard, *steps)


def pieces_by_row(shard, other):
    return (shard, swap(shard, "core"), other, swap(other, "core"))


def scatter_core(parts):
    core = lax.axis_index("core")
    parts = parts.astype(bf16).reshape((2, 2) + parts.shape[1:])
    away = lax.dynamic_index_in_dim(parts, 1 - core, 1, keepdims=False)
    keep = lax.dynamic_index_in_dim(parts, core, 1, keepdims=False)
    return (keep.astype(f32) + swap(away, "core").astype(f32)).astype(bf16)


def join_core(keep, away):
    return (keep.astype(f32) + swap(away, "core").astype(f32)).astype(bf16)


def scatter_row(both):
    row = lax.axis_index("yl")
    away = lax.dynamic_index_in_dim(both, 1 - row, 0, keepdims=False)
    keep = lax.dynamic_index_in_dim(both, row, 0, keepdims=False)
    return keep.astype(f32) + swap(away, "yl").astype(f32)


def scatter_fsdp(parts):
    return scatter_row(scatter_core(parts))


def all_x(part):
    return [part] + [turn(part, "x", step) for step in (1, 2, 3)]


def rope_tables(positions):
    freqs = jnp.power(10000.0, -jnp.arange(0, HEAD_DIM, 2, dtype=f32) / HEAD_DIM)
    angles = positions.astype(f32)[:, None] * freqs[None, :]
    cosine, sine = jnp.cos(angles), jnp.sin(angles)
    ones, zeros = jnp.ones_like(cosine), jnp.zeros_like(cosine)
    return (
        jnp.concatenate([cosine] * 6 + [ones] * 2, axis=1),
        jnp.concatenate([-sine, sine] * 3 + [zeros] * 2, axis=1),
    )


def turned(values):
    width = values.shape[1]
    column = lax.broadcasted_iota(jnp.int32, values.shape, 1)
    return jnp.where(
        column % HEAD_DIM < HEAD_DIM // 2,
        pltpu.roll(values, width - HEAD_DIM // 2, 1),
        pltpu.roll(values, HEAD_DIM // 2, 1),
    )


def norm_back(values, inv_rms, gain, grad):
    weighted = grad * gain
    gain_grad = jnp.sum(grad * values * inv_rms, axis=0, keepdims=True)
    inner_mean = jnp.mean(weighted * values, axis=-1, keepdims=True)
    return (weighted * inv_rms - values * inv_rms * inv_rms * inv_rms * inner_mean, gain_grad)


def inv_rms_of(values):
    return lax.rsqrt(jnp.mean(values * values, axis=-1, keepdims=True) + epsilon)


def half(index):
    return pl.ds(pl.multiple_of(index * HALF, HALF), HALF)


def key_tile(counter):
    return pl.ds(pl.multiple_of(counter * TILE, TILE), TILE)


def sort_keys(knum_ref, kv_refs, kvs, kvt):
    blocks = kv_refs[0].shape[0] // HALF
    for slot, kv_ref in enumerate(kv_refs):
        for block in range(blocks):
            kvs[half(knum_ref[slot * blocks + block]), :] = kv_ref[block * HALF : (block + 1) * HALF, :]
    for tile in range(kvs.shape[0] // TILE):
        part = kvs[tile * TILE : (tile + 1) * TILE, :].astype(f32)
        kvt[:, tile * TILE : (tile + 1) * TILE] = part.T.astype(bf16)


def pair_rows(ref, first, second, upper):
    rows = []
    for block in (first, second):
        values = ref[half(block), :].astype(f32)
        column = lax.broadcasted_iota(jnp.int32, values.shape, 1)
        inside = (column >= HEAD_DIM) if upper else (column < HEAD_DIM)
        moved = pltpu.roll(values, HEAD_DIM, 1)
        heads = (moved, values) if upper else (values, moved)
        rows += [jnp.where(inside, head, 0.0) for head in heads]
    return jnp.concatenate(rows, axis=0)


def pair_positions(low_number, high_number):
    column = lax.broadcasted_iota(jnp.int32, (1, 4 * HALF), 1)
    return jnp.where(column < 2 * HALF, low_number, high_number) * HALF + column % HALF


def score_tile(keys, queries, counter, positions, masked):
    scores = product_nt(keys, queries)
    if masked:
        key_pos = counter * TILE + lax.broadcasted_iota(jnp.int32, scores.shape, 0)
        scores = jnp.where(key_pos <= positions, scores, masked_value)
    return scores


def store_rows(ref, turned, first, second):
    rows = turned.T
    ref[half(first), :] = jnp.concatenate([rows[:HALF], rows[HALF : 2 * HALF]], axis=1).astype(ref.dtype)
    ref[half(second), :] = jnp.concatenate([rows[2 * HALF : 3 * HALF], rows[3 * HALF :]], axis=1).astype(ref.dtype)


def attend_kernel(
    order_ref, qnum_ref, knum_ref, q_ref, kv0, kv1, kv2, kv3, held_ref, out_ref, turned_ref, lse_ref, kvs, kvt
):
    del held_ref
    sort_keys(knum_ref, (kv0, kv1, kv2, kv3), kvs, kvt)
    width = 4 * HALF

    @pl.loop(0, q_ref.shape[0] // (2 * HALF))
    def _(pair):
        first, second = order_ref[2 * pair], order_ref[2 * pair + 1]
        low_number, high_number = qnum_ref[first], qnum_ref[second]
        queries = pair_rows(q_ref, first, second, False).astype(bf16)
        positions = pair_positions(low_number, high_number)

        def step(masked, counter, running):
            top, total, mixed = running
            scores = score_tile(kvs[key_tile(counter), :], queries, counter, positions, masked)
            new_top = jnp.maximum(top, jnp.max(scores, axis=0, keepdims=True))
            probs = jnp.exp(scores - new_top)
            shrink = jnp.exp(top - new_top)
            total = total * shrink + jnp.sum(probs, axis=0, keepdims=True)
            mixed = mixed * shrink + product(kvt[HEAD_DIM:, key_tile(counter)], probs.astype(bf16))
            return (new_top, total, mixed)

        start = (
            jnp.full((1, width), masked_value, f32),
            jnp.zeros((1, width), f32),
            jnp.zeros((HEAD_DIM, width), f32),
        )
        full = (low_number * HALF) // TILE
        last = (high_number * HALF) // TILE + 1
        running = lax.fori_loop(0, full, functools.partial(step, False), start)
        top, total, mixed = lax.fori_loop(full, last, functools.partial(step, True), running)
        mixed = mixed / total
        turned_ref[pair] = mixed
        lse_ref[pair] = top + jnp.log(total)
        store_rows(out_ref, mixed, first, second)


def attend_grad_kernel(
    order_ref, qnum_ref, knum_ref, q_ref, kv0, kv1, kv2, kv3, grad_ref, turned_ref, lse_ref,
    dq_ref, dkv0, dkv1, dkv2, dkv3, kvs, kvt, total_ref,
):
    sort_keys(knum_ref, (kv0, kv1, kv2, kv3), kvs, kvt)
    total_ref[...] = jnp.zeros_like(total_ref)
    width = 4 * HALF

    @pl.loop(0, q_ref.shape[0] // (2 * HALF))
    def _(pair):
        first, second = order_ref[2 * pair], order_ref[2 * pair + 1]
        low_number, high_number = qnum_ref[first], qnum_ref[second]
        queries = pair_rows(q_ref, first, second, False).astype(bf16)
        grads_f = pair_rows(grad_ref, first, second, True)
        grads = grads_f.astype(bf16)
        both = jnp.concatenate([queries, grads], axis=0)
        positions = pair_positions(low_number, high_number)
        lse = lse_ref[pair]
        dots = jnp.sum(grads_f.T[HEAD_DIM:] * turned_ref[pair], axis=0, keepdims=True)

        def step(masked, counter, query_acc):
            keys = kvs[key_tile(counter), :]
            probs = jnp.exp(score_tile(keys, queries, counter, positions, masked) - lse)
            score_grad = (probs * (product_nt(keys, grads) - dots)).astype(bf16)
            sides = jnp.concatenate([score_grad, probs.astype(bf16)], axis=1)
            total_ref[key_tile(counter), :] += product(sides, both)
            return query_acc + product(kvt[:HEAD_DIM, key_tile(counter)], score_grad)

        full = (low_number * HALF) // TILE
        last = (high_number * HALF) // TILE + 1
        query_acc = lax.fori_loop(0, full, functools.partial(step, False), jnp.zeros((HEAD_DIM, width), f32))
        query_acc = lax.fori_loop(full, last, functools.partial(step, True), query_acc)
        store_rows(dq_ref, query_acc * attn_scale, first, second)

    blocks = dkv0.shape[0] // HALF
    for slot, dkv in enumerate((dkv0, dkv1, dkv2, dkv3)):
        for block in range(blocks):
            dkv[block * HALF : (block + 1) * HALF, :] = total_ref[
                half(knum_ref[slot * blocks + block]), :
            ].astype(bf16)


def expert_kernel(
    expert_ref, me_ref, rows_ref, marked_ref, piece0, piece1, piece2, piece3, router_ref,
    out_ref, in_grad_ref, pre_grad_ref, inner_ref, route_grad_ref, gu_ref, down_ref,
):
    @pl.when(pl.program_id(0) == 0)
    def _():
        part = gu_ref.shape[0] // 4
        for step, piece in enumerate((piece0, piece1, piece2, piece3)):
            place = me_ref[0] ^ step
            gu_ref[pl.ds(pl.multiple_of(place * part, part), part), :] = piece[:part, :]
            down_ref[pl.ds(pl.multiple_of(place * (part // 2), part // 2), part // 2), :] = piece[part:, :]

    rows = rows_ref[...]
    width = rows.shape[1]
    units = down_ref.shape[0]
    pre = product(rows, gu_ref[...])
    gate_pre, up_pre = pre[:, :units], pre[:, units:]
    sigmoid_a = 1.0 / (1.0 + jnp.exp(-gate_pre))
    swish_act = gate_pre * sigmoid_a
    inner_act = (swish_act * up_pre).astype(bf16)
    inner_ref[...] = inner_act
    expert_out = product(inner_act, down_ref[...]).astype(bf16)
    out_ref[...] = expert_out
    uses = marked_ref[:, width : width + EXPERTS].astype(f32)
    probs = gate_of(rows, uses, router_ref[...])
    column = lax.broadcasted_iota(jnp.int32, probs.shape, 1)
    slot_probs = jnp.sum(jnp.where(column == expert_ref[0], probs, 0.0), axis=1, keepdims=True)
    mix_grad = residual_scale * marked_ref[:, :width].astype(f32)
    gate_grad = jnp.sum(mix_grad * expert_out.astype(f32), axis=1, keepdims=True)
    route_grad = (slot_probs * mix_grad).astype(bf16)
    route_grad_ref[...] = route_grad
    inner_grad = product_nt(route_grad, down_ref[...])
    pre_grad_ref[:, :units] = (
        inner_grad * up_pre * sigmoid_a * (1.0 + gate_pre * (1.0 - sigmoid_a))
    ).astype(bf16)
    pre_grad_ref[:, units:] = (inner_grad * swish_act).astype(bf16)
    in_grad_ref[:, :width] = product_nt(pre_grad_ref[...], gu_ref[...]).astype(bf16)
    column = lax.broadcasted_iota(jnp.int32, (rows.shape[0], 128), 1)
    high = gate_grad.astype(bf16).astype(f32)
    in_grad_ref[:, width:] = jnp.where(
        column == expert_ref[0], high, jnp.where(column == EXPERTS + expert_ref[0], gate_grad - high, 0.0)
    ).astype(bf16)


def project_kernel(x_ref, w_ref, gain_ref, cos_ref, sin_ref, normed_ref, q_ref, kv_ref):
    values = x_ref[...].astype(f32)
    normed = (values * inv_rms_of(values) * gain_ref[...]).astype(bf16)
    normed_ref[...] = normed
    projected = product(normed, w_ref[...])
    rotated = projected * cos_ref[...] + turned(projected) * sin_ref[...]
    q_ref[...] = rotated[:, : 2 * HEAD_DIM].astype(bf16) * bf16(attn_scale)
    kv_ref[...] = rotated[:, 2 * HEAD_DIM :].astype(bf16)


def project(rows, head_w, gain, cosine, sine):
    count, width = rows.shape
    tile = 256

    def tiled(columns):
        return pl.BlockSpec((tile, columns), lambda i: (i, 0))

    def whole(array):
        return pl.BlockSpec(array.shape, lambda i: (0, 0))

    columns = (width, 2 * HEAD_DIM, 2 * HEAD_DIM)
    return pl.pallas_call(
        project_kernel,
        grid=(count // tile,),
        out_shape=tuple(jax.ShapeDtypeStruct((count, c), bf16) for c in columns),
        in_specs=[tiled(width), whole(head_w), whole(gain), tiled(4 * HEAD_DIM), tiled(4 * HEAD_DIM)],
        out_specs=tuple(tiled(c) for c in columns),
        compiler_params=pltpu.CompilerParams(vmem_limit_bytes=32 * 1024 * 1024),
        cost_estimate=pl.CostEstimate(flops=600_000_000, bytes_accessed=8_000_000, transcendentals=0),
    )(rows, head_w, gain, cosine, sine)


def call(kernel, outs, operands, flops, held=(), scalars=0, scratch=()):
    count = len(operands)

    def body(*refs):
        kernel(*refs[:count], *refs[count + len(held) :])

    return pl.pallas_call(
        body,
        out_shape=tuple(jax.ShapeDtypeStruct(shape, dtype) for shape, dtype in outs),
        in_specs=[SMEM] * scalars + [VMEM] * (count - scalars) + [pl.BlockSpec(memory_space=pl.ANY)] * len(held),
        out_specs=(VMEM,) * len(outs),
        scratch_shapes=[pltpu.VMEM(shape, f32) for shape in scratch],
        compiler_params=pltpu.CompilerParams(vmem_limit_bytes=48 * 1024 * 1024),
        cost_estimate=pl.CostEstimate(flops=flops, bytes_accessed=8_000_000, transcendentals=0),
    )(*operands, *held)


def part_of(me_ref, step, part):
    return pl.ds(pl.multiple_of((me_ref[0] ^ step) * part, part), part)


def copies_kernel(x_ref, copies_ref):
    for copy in range(KV_HEADS):
        copies_ref[copy] = x_ref[...]


def shard_kernel(head_ref, query_ref, key_ref, value_ref, router_ref, gain1_ref, gain2_ref, out_ref):
    rows = query_ref.shape[0]
    head = head_ref[0]
    out_ref[...] = jnp.zeros_like(out_ref)
    out_ref[:rows, : 2 * HEAD_DIM] = query_ref[:, pl.ds(pl.multiple_of(head * 128, 128), 128)]
    pair = pl.ds(pl.multiple_of((head // 2) * 128, 128), 128)
    odd = jnp.full((rows, 128), head % 2, jnp.int32) == 1
    column = lax.broadcasted_iota(jnp.int32, (rows, 128), 1)
    keys, values = key_ref[:, pair].astype(f32), value_ref[:, pair].astype(f32)
    keys = jnp.where(odd, pltpu.roll(keys, HEAD_DIM, 1), keys)
    values = jnp.where(odd, values, pltpu.roll(values, HEAD_DIM, 1))
    out_ref[:rows, 2 * HEAD_DIM : 4 * HEAD_DIM] = jnp.where(column < HEAD_DIM, keys, values).astype(bf16)
    out_ref[:rows, 4 * HEAD_DIM : 4 * HEAD_DIM + EXPERTS] = router_ref[...]
    row = lax.broadcasted_iota(jnp.int32, (16, rows), 0)
    gains = jnp.where(row == 0, gain1_ref[...].astype(f32), jnp.where(row == 1, gain2_ref[...].astype(f32), 0.0))
    out_ref[rows:, :rows] = gains.astype(bf16)


def small_kernel(me_ref, piece0, piece1, piece2, piece3, head_w_ref, router_ref, gain1_ref, gain2_ref):
    rows = head_w_ref.shape[0] // 4
    for step, piece in enumerate((piece0, piece1, piece2, piece3)):
        place = part_of(me_ref, step, rows)
        head_w_ref[place, :] = piece[:rows, : 4 * HEAD_DIM]
        router_ref[place, :] = piece[:rows, 4 * HEAD_DIM : 4 * HEAD_DIM + EXPERTS]
        gains = piece[rows:, :rows].astype(f32)
        gain1_ref[:, place] = gains[0:1]
        gain2_ref[:, place] = gains[1:2]


def send_kernel(send_ref, rows_ref, out_ref):
    out_ref[...] = product(send_ref[...], rows_ref[...]).astype(bf16)


def middle_kernel(
    me_ref, attn_ref, out0, out1, out2, out3, x_ref, gain_ref, router_ref, uses_ref, send_ref,
    rows_ref, hidden_ref, normed_ref, probs_ref, out_ref,
):
    for head in range(KV_HEADS):
        rows_ref[:, head * 2 * HEAD_DIM : (head + 1) * 2 * HEAD_DIM] = attn_ref[head]
    branch = jnp.zeros(hidden_ref.shape, f32)
    for step, piece in enumerate((out0, out1, out2, out3)):
        branch += product(rows_ref[:, part_of(me_ref, step, piece.shape[0])], piece[...])
    hidden = x_ref[...].astype(f32) + residual_scale * branch
    hidden_ref[...] = hidden
    normed = (hidden * inv_rms_of(hidden) * gain_ref[...]).astype(bf16)
    normed_ref[...] = normed
    out_ref[...] = product(send_ref[...], normed).astype(bf16)
    probs_ref[...] = gate_of(normed, uses_ref[...], router_ref[...])


def token_grad_kernel(
    me_ref, fetch_ref, back_ref, probs_ref, router_ref, hidden_ref, gain_ref, cot_ref, out0, out1, out2, out3,
    hidden_grad_ref, branch_ref, logit_ref, gain_grad_ref, attn_grad_ref,
):
    width = hidden_ref.shape[1]
    fetched = product(fetch_ref[...], back_ref[...])
    gate_grad = fetched[:, width : width + EXPERTS] + fetched[:, width + EXPERTS : width + 2 * EXPERTS]
    probs = probs_ref[...]
    mean_grad = jnp.sum(probs * gate_grad, axis=-1, keepdims=True)
    logit_grad = (probs * (gate_grad - mean_grad)).astype(bf16)
    logit_ref[...] = logit_grad
    normed_grad = fetched[:, :width] + product_nt(logit_grad, router_ref[...])
    hidden = hidden_ref[...]
    hidden_part, gain_grad = norm_back(hidden, inv_rms_of(hidden), gain_ref[...], normed_grad)
    gain_grad_ref[...] = gain_grad
    hidden_grad = cot_ref[...].astype(f32) + hidden_part
    hidden_grad_ref[...] = hidden_grad
    branch = (residual_scale * hidden_grad).astype(bf16)
    branch_ref[...] = branch
    for step, piece in enumerate((out0, out1, out2, out3)):
        attn_grad = product_nt(branch, piece[...]).astype(bf16)
        heads = KV_HEADS // 4
        for head in range(heads):
            columns = slice(head * 2 * HEAD_DIM, (head + 1) * 2 * HEAD_DIM)
            attn_grad_ref[(me_ref[0] ^ step) * heads + head] = attn_grad[:, columns]


def dense_grad_kernel(core_ref, rows_ref, branch_ref, normed_ref, logit_ref, gain_ref, keep_ref, away_ref):
    part, width = keep_ref.shape[1], branch_ref.shape[1]
    logit_grad = logit_ref[...].astype(f32)
    logit_grad = jnp.concatenate(
        [logit_grad, jnp.zeros((logit_grad.shape[0], 128 - EXPERTS), f32)], axis=1
    ).astype(bf16)
    column = lax.broadcasted_iota(jnp.int32, (part, 128), 1)
    for row in range(2):
        for ref, core in ((keep_ref, core_ref[0]), (away_ref, 1 - core_ref[0])):
            columns = pl.ds(pl.multiple_of((2 * row + core) * part, part), part)
            ref[row, :, :width] = product_tn(rows_ref[:, columns], branch_ref[...]).astype(bf16)
            router_grad = product_tn(normed_ref[:, columns], logit_grad)
            gain_grad = jnp.broadcast_to(gain_ref[:, columns], (128, part)).T
            ref[row, :, width:] = jnp.where(column == EXPERTS, gain_grad, router_grad).astype(bf16)


def head_grad_kernel(dq_ref, dkv0, dkv1, dkv2, dkv3, cos_ref, sin_ref, out_ref):
    dkv = dkv0[...].astype(f32) + dkv1[...].astype(f32) + dkv2[...].astype(f32) + dkv3[...].astype(f32)
    for side, grad in enumerate((dq_ref[...], dkv)):
        columns = slice(side * 2 * HEAD_DIM, (side + 1) * 2 * HEAD_DIM)
        out_ref[:, columns] = (grad * cos_ref[:, columns] - turned(grad) * sin_ref[:, columns]).astype(bf16)


def head_weight_kernel(core_ref, normed_ref, grads_ref, keep_ref, away_ref):
    part = keep_ref.shape[1]
    for row in range(2):
        for ref, core in ((keep_ref, core_ref[0]), (away_ref, 1 - core_ref[0])):
            columns = pl.ds(pl.multiple_of((2 * row + core) * part, part), part)
            ref[row] = product_tn(normed_ref[:, columns], grads_ref[...]).astype(bf16)


def input_grad_kernel(
    me_ref, grads_ref, w0, w1, w2, w3, x_ref, gain_ref, hidden_grad_ref, out_ref, gain0, gain1, gain2, gain3, all_ref
):
    width = 4 * HEAD_DIM
    for step, piece in enumerate((w0, w1, w2, w3)):
        part = jnp.zeros((out_ref.shape[0], piece.shape[0]), f32)
        for head in range(KV_HEADS):
            part += product_nt(grads_ref[head], piece[:, head * width : (head + 1) * width])
        out_ref[:, part_of(me_ref, step, piece.shape[0])] = part
    values = x_ref[...].astype(f32)
    part, gain_grad = norm_back(values, inv_rms_of(values), gain_ref[...], out_ref[...])
    out_ref[...] = hidden_grad_ref[...] + part
    all_ref[...] = gain_grad
    for step, ref in enumerate((gain0, gain1, gain2, gain3)):
        ref[...] = all_ref[:, part_of(me_ref, step, ref.shape[1])]


def pack_kernel(
    place_ref, w0, w1, w2, w3, gain0, gain1, gain2, gain3, dense0, dense1, dense2, dense3, out_ref, rows_ref
):
    total = w0[...].astype(f32) + w1[...].astype(f32) + w2[...].astype(f32) + w3[...].astype(f32)
    total = total.astype(bf16)
    gain = gain0[...] + gain1[...] + gain2[...] + gain3[...]
    high = gain.astype(bf16).astype(f32)
    rows, columns = total.shape[0] // 4, total.shape[1]
    row = lax.broadcasted_iota(jnp.int32, (rows, 128), 0)
    block = jnp.zeros((rows, 128), f32)
    for line, part in enumerate((high[:, :128], high[:, 128:], (gain - high)[:, :128], (gain - high)[:, 128:])):
        block = jnp.where(row == line, part, block)
    for step, part in enumerate((dense0, dense1, dense2, dense3)):
        rows_ref[pl.ds(pl.multiple_of(((place_ref[0] + 4 - step) & 3) * 8, 8), 8), :] = part[...].astype(f32)
    dense = rows_ref[...].astype(bf16)
    for head in range(KV_HEADS):
        for side in range(4):
            out_ref[head, :rows, side * columns : (side + 1) * columns] = total[side * rows : (side + 1) * rows]
        out_ref[head, :rows, 4 * columns :] = block.astype(bf16)
        out_ref[head, rows:, :] = dense


def spread_kernel(
    last_ref, query_ref, key_ref, value_ref, gain_ref, out_grad_ref, router_ref, gain2_ref, column_ref
):
    columns = 4 * HEAD_DIM
    rows = last_ref.shape[1] - 32
    gain_lines = jnp.zeros((rows, 128), f32)
    for head in range(0, KV_HEADS, 2):
        for side in range(4):
            place = slice(side * rows, (side + 1) * rows)
            parts = []
            for step in (0, 1):
                part = last_ref[head + step, :rows, side * columns : (side + 1) * columns].astype(f32)
                query_ref[place, (head + step) * 2 * HEAD_DIM : (head + step + 1) * 2 * HEAD_DIM] = part[:, : 2 * HEAD_DIM]
                parts.append(part)
            pair = slice(head * HEAD_DIM, (head + 2) * HEAD_DIM)
            key_ref[place, pair] = jnp.concatenate([p[:, 2 * HEAD_DIM : 3 * HEAD_DIM] for p in parts], axis=1)
            value_ref[place, pair] = jnp.concatenate([p[:, 3 * HEAD_DIM :] for p in parts], axis=1)
    for head in range(KV_HEADS):
        gain_lines += last_ref[head, :rows, 4 * columns :].astype(f32)
        dense = last_ref[head, rows:, :].astype(f32)
        for place in range(4):
            part = dense[place * 8 : (place + 1) * 8]
            target = slice((place * KV_HEADS + head) * 8, (place * KV_HEADS + head + 1) * 8)
            out_grad_ref[target, :] = part[:, : 4 * columns]
            router_ref[target, :] = part[:, 4 * columns : 4 * columns + EXPERTS]
            column_ref[target, :] = part[:, 4 * columns :]
    gain_ref[:, :128] = gain_lines[0:1] + gain_lines[2:3]
    gain_ref[:, 128:] = gain_lines[1:2] + gain_lines[3:4]
    gain2_ref[...] = column_ref[...].T[EXPERTS : EXPERTS + 1, :]


def gate_of(rows, mask, router_w):
    logits = jnp.where(mask > 0, product(rows, router_w), masked_value)
    exps = jnp.where(mask > 0, jnp.exp(logits - jnp.max(logits, axis=-1, keepdims=True)), 0.0)
    return exps / jnp.maximum(jnp.sum(exps, axis=-1, keepdims=True), 1e-30)


def run_experts(expert, me, rows, marked, pieces, router_w):
    count, width = rows.shape
    part = pieces[0].shape[0] // 3
    units = 4 * part
    tile = 256

    def tiled(columns):
        return pl.BlockSpec((tile, columns), lambda i: (i, 0))

    def whole(array):
        return pl.BlockSpec(array.shape, lambda i: (0, 0))

    columns = (width, width + 128, 2 * units, units, width)
    return pl.pallas_call(
        expert_kernel,
        grid=(count // tile,),
        out_shape=tuple(jax.ShapeDtypeStruct((count, c), bf16) for c in columns),
        in_specs=[SMEM, SMEM, tiled(width), tiled(width + 128)] + [whole(p) for p in pieces] + [whole(router_w)],
        out_specs=tuple(tiled(c) for c in columns),
        scratch_shapes=[pltpu.VMEM((8 * part, 2 * units), bf16), pltpu.VMEM((units, width), bf16)],
        compiler_params=pltpu.CompilerParams(vmem_limit_bytes=56 * 1024 * 1024),
        cost_estimate=pl.CostEstimate(flops=10_000_000_000, bytes_accessed=22_000_000, transcendentals=1_000_000),
    )(expert.astype(jnp.int32).reshape(1), me, rows, marked, *pieces, router_w)


SMEM = pl.BlockSpec(memory_space=pltpu.SMEM)
VMEM = pl.BlockSpec(memory_space=pltpu.VMEM)


def attend(numbers, queries, kv_parts, held):
    rows = queries.shape[0]
    keys = rows * len(kv_parts)
    pairs = rows // (2 * HALF)
    return pl.pallas_call(
        attend_kernel,
        out_shape=(
            jax.ShapeDtypeStruct((rows, 2 * HEAD_DIM), bf16),
            jax.ShapeDtypeStruct((pairs, HEAD_DIM, 4 * HALF), f32),
            jax.ShapeDtypeStruct((pairs, 1, 4 * HALF), f32),
        ),
        in_specs=[SMEM] * 3 + [VMEM] * 5 + [pl.BlockSpec(memory_space=pl.ANY)],
        out_specs=(VMEM,) * 3,
        scratch_shapes=[pltpu.VMEM((keys, 2 * HEAD_DIM), bf16), pltpu.VMEM((2 * HEAD_DIM, keys), bf16)],
        compiler_params=pltpu.CompilerParams(vmem_limit_bytes=40 * 1024 * 1024),
        cost_estimate=pl.CostEstimate(flops=12_000_000_000, bytes_accessed=4_000_000, transcendentals=5_000_000),
    )(*numbers, queries, *kv_parts, held)


def attend_grad(numbers, queries, kv_parts, grads, turned, lse):
    rows = queries.shape[0]
    keys = rows * len(kv_parts)
    return pl.pallas_call(
        attend_grad_kernel,
        out_shape=(jax.ShapeDtypeStruct((rows, 2 * HEAD_DIM), f32),)
        + (jax.ShapeDtypeStruct((rows, 2 * HEAD_DIM), bf16),) * 4,
        in_specs=[SMEM] * 3 + [VMEM] * 8,
        out_specs=(VMEM,) * 5,
        scratch_shapes=[
            pltpu.VMEM((keys, 2 * HEAD_DIM), bf16),
            pltpu.VMEM((2 * HEAD_DIM, keys), bf16),
            pltpu.VMEM((keys, 2 * HEAD_DIM), f32),
        ],
        compiler_params=pltpu.CompilerParams(vmem_limit_bytes=40 * 1024 * 1024),
        cost_estimate=pl.CostEstimate(flops=30_000_000_000, bytes_accessed=6_000_000, transcendentals=5_000_000),
    )(*numbers, queries, *kv_parts, grads, turned, lse)


def block_numbers(block_pairs):
    place = lax.axis_index("x")
    groups = block_pairs.reshape(4, 8)
    groups = groups[(place - jnp.arange(4)) & 3]
    numbers = jnp.stack([groups, 63 - groups], axis=-1).reshape(-1)
    own = numbers[:16]
    rank = jnp.sum((own[None, :] < own[:, None]).astype(jnp.int32), axis=1)
    spots = jnp.arange(16, dtype=jnp.int32)
    order = jnp.sum(jnp.where(rank[None, :] == spots[:, None], spots[None, :], 0), axis=1)
    return (order, own, numbers)


def on_device(
    block_input,
    routes,
    block_pairs,
    norm1_gain,
    w_query,
    w_key,
    w_value,
    w_out,
    norm2_gain,
    w_router,
    w_gate,
    w_up,
    w_down,
    cotangent,
):
    tokens, width = block_input.shape[1:]
    head = lax.axis_index(ZY)
    expert = lax.axis_index(CTX)
    shard_rows = w_query.shape[0]
    own_input = block_input[0]

    core = lax.axis_index("core").astype(jnp.int32).reshape(1)
    place = lax.axis_index("x").astype(jnp.int32).reshape(1)
    me = lax.axis_index(("yl", "core")).astype(jnp.int32).reshape(1)
    (small_shard,) = call(
        shard_kernel,
        [((shard_rows + 16, 4 * HEAD_DIM + 128), bf16)],
        (
            head.astype(jnp.int32).reshape(1), w_query, w_key, w_value, w_router,
            norm1_gain.reshape(1, -1), norm2_gain.reshape(1, -1),
        ),
        1_000_000,
        scalars=1,
    )
    small_pieces = pieces_direct(small_shard)
    (copies,) = call(
        copies_kernel, [((KV_HEADS, tokens, width), bf16)], (own_input,), 1_000_000, held=(small_shard,)
    )
    group_input = exchange(copies.reshape(-1, width), ZY)
    head_w, router_w, gain_one, gain_two = call(
        small_kernel,
        [((width, 4 * HEAD_DIM), bf16), ((width, EXPERTS), bf16), ((1, width), f32), ((1, width), f32)],
        (me, *small_pieces),
        1_000_000,
        scalars=1,
    )

    numbers = block_numbers(block_pairs)
    group_pos = (numbers[1][:, None] * HALF + jnp.arange(HALF, dtype=jnp.int32)[None, :]).reshape(-1)
    cosine, sine = rope_tables(group_pos)

    chosen = routes[0]
    uses = jnp.sum(
        (chosen[:, :, None] == jnp.arange(EXPERTS, dtype=jnp.int32)[None, None, :]).astype(f32), axis=1
    )
    earlier = jnp.tril(jnp.ones((tokens, tokens), bf16), -1)
    rank = product(earlier, uses.astype(bf16)).astype(jnp.int32)
    rank = jnp.where(uses > 0, rank, -1)
    slot = jnp.arange(CAP, dtype=jnp.int32)
    send = (rank.T[:, None, :] == slot[None, :, None]).astype(bf16).reshape(EXPERTS * CAP, tokens)
    fetch = (rank[:, :, None] == slot[None, None, :]).astype(bf16).reshape(tokens, EXPERTS * CAP)

    group_normed, queries, kv_own = project(group_input, head_w, gain_one, cosine, sine)
    kv_parts = [kv_own] + [turn(kv_own, "x", step) for step in (1, 2, 3)]

    out_other = swap(w_out, "yl")
    expert_shard = jnp.concatenate([jnp.concatenate([w_gate[0], w_up[0]], axis=1), w_down[0]], axis=0)
    expert_other = swap(expert_shard, "yl")
    marked = jnp.concatenate(
        [cotangent[0], uses.astype(bf16), jnp.zeros((tokens, 128 - EXPERTS), bf16)], axis=1
    )
    (marked_sent,) = call(
        send_kernel,
        [((EXPERTS * CAP, width + 128), bf16)],
        (send, marked),
        500_000_000,
        held=(*kv_parts[1:], out_other, expert_other),
    )
    marked_arrived = exchange(marked_sent, CTX)

    attn_group, attn_turned, lse = attend(numbers, queries, kv_parts, expert_other)

    out_pieces = pieces_by_row(w_out, out_other)

    attn_back = exchange(tie(attn_group, marked_arrived), ZY)
    expert_pieces = pieces_by_row(expert_shard, expert_other)
    attn_rows, hidden, normed2, gate_probs, outgoing = call(
        middle_kernel,
        [
            ((tokens, HEADS * HEAD_DIM), bf16),
            ((tokens, width), f32),
            ((tokens, width), bf16),
            ((tokens, EXPERTS), f32),
            ((EXPERTS * CAP, width), bf16),
        ],
        (
            me, attn_back.reshape(KV_HEADS, tokens, 2 * HEAD_DIM), *out_pieces, own_input, gain_two, router_w,
            uses, send,
        ),
        800_000_000,
        held=expert_pieces,
        scalars=1,
    )
    arrived = exchange(outgoing, CTX)

    hidden_units = w_gate.shape[2]
    expert_out, in_grad, pre_grad, inner_act, route_grad = run_experts(
        expert, me, arrived, marked_arrived, expert_pieces, router_w
    )
    back = exchange(in_grad, CTX)
    grad_gu = product_tn(arrived, pre_grad).astype(bf16).reshape(4, -1, 2 * hidden_units)
    grad_down = product_tn(inner_act, route_grad).astype(bf16).reshape(4, -1, width)
    expert_both = scatter_core(jnp.concatenate([grad_gu, grad_down], axis=1))
    by_head = jnp.concatenate(
        [
            w_query.reshape(shard_rows, KV_HEADS, 2 * HEAD_DIM),
            w_key.reshape(shard_rows, KV_HEADS, HEAD_DIM),
            w_value.reshape(shard_rows, KV_HEADS, HEAD_DIM),
        ],
        axis=2,
    ).reshape(shard_rows, -1)
    by_head = tie(by_head, arrived)
    head_pieces = pieces_by_row(by_head, swap(by_head, "yl"))
    expert_sums = scatter_row(expert_both)

    hidden_grad, branch_grad, logit_grad, gain_two_grad, attn_grad = call(
        token_grad_kernel,
        [
            ((tokens, width), f32),
            ((tokens, width), bf16),
            ((tokens, EXPERTS), bf16),
            ((1, width), f32),
            ((KV_HEADS, tokens, 2 * HEAD_DIM), bf16),
        ],
        (me, fetch, back, gate_probs, router_w, hidden, gain_two, cotangent[0], *out_pieces),
        800_000_000,
        held=(expert_sums, *head_pieces),
        scalars=1,
    )

    group_grad = exchange(attn_grad.reshape(KV_HEADS * tokens, 2 * HEAD_DIM), ZY)
    dq, *dkv_parts = attend_grad(numbers, queries, kv_parts, group_grad, attn_turned, lse)
    returned = exchange(tie(expert_out, group_grad), CTX)
    dkv_turned = [turn(dkv_parts[step], "x", -step) for step in (1, 2, 3)]
    dense_shape = ((2, shard_rows, width + 128), bf16)
    dense_both = join_core(
        *call(
            dense_grad_kernel,
            [dense_shape, dense_shape],
            (core, attn_rows, branch_grad, normed2, logit_grad, gain_two_grad),
            400_000_000,
            held=tuple(dkv_turned),
            scalars=1,
        )
    )
    dense = scatter_row(dense_both)

    (grads,) = call(
        head_grad_kernel,
        [((KV_HEADS * tokens, 4 * HEAD_DIM), bf16)],
        (dq, dkv_parts[0], *dkv_turned, cosine, sine),
        100_000_000,
        held=(returned,),
    )
    token_grads = exchange(grads, ZY)
    head_shape = ((2, shard_rows, 4 * HEAD_DIM), bf16)
    head_both = join_core(
        *call(head_weight_kernel, [head_shape, head_shape], (core, group_normed, grads), 600_000_000, scalars=1)
    )
    head_part = scatter_row(head_both).astype(bf16)

    dense = exchange(tie(dense.astype(bf16), token_grads, head_part), CTX).reshape(EXPERTS, -1, width + 128)
    dense = jnp.sum(dense.astype(f32), axis=0).astype(bf16)

    gain_shape = ((1, shard_rows), f32)
    input_grad, *gain_parts = call(
        input_grad_kernel,
        [((tokens, width), f32)] + [gain_shape] * 4,
        (
            me, token_grads.reshape(KV_HEADS, tokens, 4 * HEAD_DIM), *head_pieces, own_input, gain_one, hidden_grad,
        ),
        600_000_000,
        scalars=1,
        scratch=[(1, width)],
    )
    gain_sum = gain_parts[0]
    for step in (1, 2, 3):
        gain_sum = gain_sum + lax.ppermute(gain_parts[step], ("yl", "core"), [(i, i ^ step) for i in range(4)])

    (last,) = call(
        pack_kernel,
        [((KV_HEADS, shard_rows // 4 + 32, width + 128), bf16)],
        (place, *all_x(tie(head_part, gain_parts[0])), *all_x(tie(gain_sum, dense)), *all_x(dense)),
        1_000_000,
        scalars=1,
        scratch=[(32, width + 128)],
    )
    last = exchange(last.reshape(-1, width + 128), ZY).reshape(last.shape)
    grad_query, grad_key, grad_value, gain_one_grad, grad_out, grad_router, gain_two_grad = call(
        spread_kernel,
        [
            ((shard_rows, HEADS * HEAD_DIM), f32),
            ((shard_rows, KV_HEADS * HEAD_DIM), f32),
            ((shard_rows, KV_HEADS * HEAD_DIM), f32),
            gain_shape,
            ((shard_rows, width), f32),
            ((shard_rows, EXPERTS), f32),
            gain_shape,
        ],
        (last,),
        1_000_000,
        scratch=[(shard_rows, 128)],
    )

    spread = gate_probs[:, :, None] * fetch.astype(f32).reshape(tokens, EXPERTS, CAP)
    weights = spread.reshape(tokens, EXPERTS * CAP)
    weights_hi = weights.astype(bf16)
    weights_lo = (weights - weights_hi.astype(f32)).astype(bf16)
    mixture = product(weights_hi, returned) + product(weights_lo, returned)
    output = hidden + residual_scale * mixture

    return (
        output.astype(bf16)[None],
        input_grad[None],
        gain_one_grad.reshape(-1),
        grad_query,
        grad_key,
        grad_value,
        grad_out,
        gain_two_grad.reshape(-1),
        grad_router,
        expert_sums[None, :shard_rows, :hidden_units],
        expert_sums[None, :shard_rows, hidden_units:],
        expert_sums[None, shard_rows:],
    )


def solution(mesh):
    fine = Mesh(mesh.devices.reshape(4, 4, 2, 2, 2), EVERY)
    rows, shards = P(("yl", "core"), CTX, None), P(("yl", "core"), None)
    gain, experts = P(("yl", "core")), P(CTX, ("yl", "core"), None)
    return jax.shard_map(
        on_device,
        mesh=fine,
        in_specs=(
            rows, rows, P(), gain, shards, shards, shards, shards, gain, shards, experts, experts, experts, rows,
        ),
        out_specs=(
            rows, rows, gain, shards, shards, shards, shards, gain, shards, experts, experts, experts,
        ),
        check_vma=False,
    )
```

```python
import functools

import jax
import jax.numpy as jnp
from jax import lax
from jax.experimental import pallas as pl
from jax.experimental.layout import Layout, with_layout_constraint
from jax.experimental.pallas import tpu as pltpu
from jax.sharding import Mesh
from jax.sharding import PartitionSpec as P

HEADS = 16
KV_HEADS = 8
HEAD_DIM = 64
EXPERTS = 32
TOP = 8
CAP = 48
HALF = 64
TILE = 512

epsilon = 1e-06
attn_scale = 0.015625
residual_scale = 0.22
masked_value = -1e30

CTX = ("x", "z", "yh")
ZY = ("z", "yh")
EVERY = ("x", "z", "yh", "yl", "core")
bf16 = jnp.bfloat16
f32 = jnp.float32


def product(left, right):
    return jnp.dot(left, right, preferred_element_type=f32)


def product_nt(left, right):
    return lax.dot_general(left, right, (((1,), (1,)), ((), ())), preferred_element_type=f32)


def product_tn(left, right):
    return lax.dot_general(left, right, (((0,), (0,)), ((), ())), preferred_element_type=f32)


def swap(values, axis):
    return lax.ppermute(values, axis, [(0, 1), (1, 0)])


def turn(values, axis, step):
    return lax.ppermute(values, axis, [(i, (i + step) % 4) for i in range(4)])


def rows_first(values):
    return with_layout_constraint(values, Layout(major_to_minor=tuple(range(values.ndim))))


def exchange(values, axes):
    return rows_first(lax.all_to_all(rows_first(values), axes, 0, 0, tiled=True))


def tie(values, *others):
    if values.size <= 1024:
        return values + sum(other[(0,) * other.ndim].astype(f32) * 0.0 for other in others).astype(values.dtype)
    corner = tuple(slice(0, min(size, 8 if axis < values.ndim - 1 else 128)) for axis, size in enumerate(values.shape))
    nothing = sum(other[(0,) * other.ndim].astype(f32) * 0.0 for other in others)
    held = values[corner] + nothing.astype(values.dtype)
    return lax.dynamic_update_slice(values, held, (0,) * values.ndim)


def pieces_direct(shard):
    steps = [lax.ppermute(shard, ("yl", "core"), [(i, i ^ k) for i in range(4)]) for k in (1, 2, 3)]
    return (shard, *steps)


def pieces_by_row(shard, other):
    return (shard, swap(shard, "core"), other, swap(other, "core"))


def scatter_core(parts):
    core = lax.axis_index("core")
    parts = parts.astype(bf16).reshape((2, 2) + parts.shape[1:])
    away = lax.dynamic_index_in_dim(parts, 1 - core, 1, keepdims=False)
    keep = lax.dynamic_index_in_dim(parts, core, 1, keepdims=False)
    return (keep.astype(f32) + swap(away, "core").astype(f32)).astype(bf16)


def join_core(keep, away):
    return (keep.astype(f32) + swap(away, "core").astype(f32)).astype(bf16)


def scatter_row(both):
    row = lax.axis_index("yl")
    away = lax.dynamic_index_in_dim(both, 1 - row, 0, keepdims=False)
    keep = lax.dynamic_index_in_dim(both, row, 0, keepdims=False)
    return keep.astype(f32) + swap(away, "yl").astype(f32)


def scatter_fsdp(parts):
    return scatter_row(scatter_core(parts))


def all_x(part):
    return [part] + [turn(part, "x", step) for step in (1, 2, 3)]


def rope_tables(positions):
    freqs = jnp.power(10000.0, -jnp.arange(0, HEAD_DIM, 2, dtype=f32) / HEAD_DIM)
    angles = positions.astype(f32)[:, None] * freqs[None, :]
    cosine, sine = jnp.cos(angles), jnp.sin(angles)
    ones, zeros = jnp.ones_like(cosine), jnp.zeros_like(cosine)
    return (
        jnp.concatenate([cosine] * 6 + [ones] * 2, axis=1),
        jnp.concatenate([-sine, sine] * 3 + [zeros] * 2, axis=1),
    )


def turned(values):
    width = values.shape[1]
    column = lax.broadcasted_iota(jnp.int32, values.shape, 1)
    return jnp.where(
        column % HEAD_DIM < HEAD_DIM // 2,
        pltpu.roll(values, width - HEAD_DIM // 2, 1),
        pltpu.roll(values, HEAD_DIM // 2, 1),
    )


def norm_back(values, inv_rms, gain, grad):
    weighted = grad * gain
    gain_grad = jnp.sum(grad * values * inv_rms, axis=0, keepdims=True)
    inner_mean = jnp.mean(weighted * values, axis=-1, keepdims=True)
    return (weighted * inv_rms - values * inv_rms * inv_rms * inv_rms * inner_mean, gain_grad)


def inv_rms_of(values):
    return lax.rsqrt(jnp.mean(values * values, axis=-1, keepdims=True) + epsilon)


def half(index):
    return pl.ds(pl.multiple_of(index * HALF, HALF), HALF)


def key_tile(counter):
    return pl.ds(pl.multiple_of(counter * TILE, TILE), TILE)


def sort_keys(knum_ref, kv_refs, kvs, kvt):
    blocks = kv_refs[0].shape[0] // HALF
    for slot, kv_ref in enumerate(kv_refs):
        for block in range(blocks):
            kvs[half(knum_ref[slot * blocks + block]), :] = kv_ref[block * HALF : (block + 1) * HALF, :]
    for tile in range(kvs.shape[0] // TILE):
        part = kvs[tile * TILE : (tile + 1) * TILE, :].astype(f32)
        kvt[:, tile * TILE : (tile + 1) * TILE] = part.T.astype(bf16)


def pair_rows(ref, first, second, upper):
    rows = []
    for block in (first, second):
        values = ref[half(block), :].astype(f32)
        column = lax.broadcasted_iota(jnp.int32, values.shape, 1)
        inside = (column >= HEAD_DIM) if upper else (column < HEAD_DIM)
        moved = pltpu.roll(values, HEAD_DIM, 1)
        heads = (moved, values) if upper else (values, moved)
        rows += [jnp.where(inside, head, 0.0) for head in heads]
    return jnp.concatenate(rows, axis=0)


def pair_positions(low_number, high_number):
    column = lax.broadcasted_iota(jnp.int32, (1, 4 * HALF), 1)
    return jnp.where(column < 2 * HALF, low_number, high_number) * HALF + column % HALF


def score_tile(keys, queries, counter, positions, masked):
    scores = product_nt(keys, queries)
    if masked:
        key_pos = counter * TILE + lax.broadcasted_iota(jnp.int32, scores.shape, 0)
        scores = jnp.where(key_pos <= positions, scores, masked_value)
    return scores


def store_rows(ref, turned, first, second):
    rows = turned.T
    ref[half(first), :] = jnp.concatenate([rows[:HALF], rows[HALF : 2 * HALF]], axis=1).astype(ref.dtype)
    ref[half(second), :] = jnp.concatenate([rows[2 * HALF : 3 * HALF], rows[3 * HALF :]], axis=1).astype(ref.dtype)


def attend_kernel(
    order_ref, qnum_ref, knum_ref, q_ref, kv0, kv1, kv2, kv3, out_ref, turned_ref, lse_ref, kvs, kvt
):
    sort_keys(knum_ref, (kv0, kv1, kv2, kv3), kvs, kvt)
    width = 4 * HALF

    @pl.loop(0, q_ref.shape[0] // (2 * HALF))
    def _(pair):
        first, second = order_ref[2 * pair], order_ref[2 * pair + 1]
        low_number, high_number = qnum_ref[first], qnum_ref[second]
        queries = pair_rows(q_ref, first, second, False).astype(bf16)
        positions = pair_positions(low_number, high_number)

        def step(masked, counter, running):
            top, total, mixed = running
            scores = score_tile(kvs[key_tile(counter), :], queries, counter, positions, masked)
            new_top = jnp.maximum(top, jnp.max(scores, axis=0, keepdims=True))
            probs = jnp.exp(scores - new_top)
            shrink = jnp.exp(top - new_top)
            total = total * shrink + jnp.sum(probs, axis=0, keepdims=True)
            mixed = mixed * shrink + product(kvt[HEAD_DIM:, key_tile(counter)], probs.astype(bf16))
            return (new_top, total, mixed)

        start = (
            jnp.full((1, width), masked_value, f32),
            jnp.zeros((1, width), f32),
            jnp.zeros((HEAD_DIM, width), f32),
        )
        full = (low_number * HALF) // TILE
        last = (high_number * HALF) // TILE + 1
        running = lax.fori_loop(0, full, functools.partial(step, False), start)
        top, total, mixed = lax.fori_loop(full, last, functools.partial(step, True), running)
        mixed = mixed / total
        turned_ref[pair] = mixed
        lse_ref[pair] = top + jnp.log(total)
        store_rows(out_ref, mixed, first, second)


def attend_grad_kernel(
    order_ref, qnum_ref, knum_ref, q_ref, kv0, kv1, kv2, kv3, grad_ref, turned_ref, lse_ref,
    dq_ref, dkv0, dkv1, dkv2, dkv3, kvs, kvt, total_ref,
):
    sort_keys(knum_ref, (kv0, kv1, kv2, kv3), kvs, kvt)
    total_ref[...] = jnp.zeros_like(total_ref)
    width = 4 * HALF

    @pl.loop(0, q_ref.shape[0] // (2 * HALF))
    def _(pair):
        first, second = order_ref[2 * pair], order_ref[2 * pair + 1]
        low_number, high_number = qnum_ref[first], qnum_ref[second]
        queries = pair_rows(q_ref, first, second, False).astype(bf16)
        grads_f = pair_rows(grad_ref, first, second, True)
        grads = grads_f.astype(bf16)
        both = jnp.concatenate([queries, grads], axis=0)
        positions = pair_positions(low_number, high_number)
        lse = lse_ref[pair]
        dots = jnp.sum(grads_f.T[HEAD_DIM:] * turned_ref[pair], axis=0, keepdims=True)

        def step(masked, counter, query_acc):
            keys = kvs[key_tile(counter), :]
            probs = jnp.exp(score_tile(keys, queries, counter, positions, masked) - lse)
            score_grad = (probs * (product_nt(keys, grads) - dots)).astype(bf16)
            sides = jnp.concatenate([score_grad, probs.astype(bf16)], axis=1)
            total_ref[key_tile(counter), :] += product(sides, both)
            return query_acc + product(kvt[:HEAD_DIM, key_tile(counter)], score_grad)

        full = (low_number * HALF) // TILE
        last = (high_number * HALF) // TILE + 1
        query_acc = lax.fori_loop(0, full, functools.partial(step, False), jnp.zeros((HEAD_DIM, width), f32))
        query_acc = lax.fori_loop(full, last, functools.partial(step, True), query_acc)
        store_rows(dq_ref, query_acc * attn_scale, first, second)

    blocks = dkv0.shape[0] // HALF
    for slot, dkv in enumerate((dkv0, dkv1, dkv2, dkv3)):
        for block in range(blocks):
            dkv[block * HALF : (block + 1) * HALF, :] = total_ref[
                half(knum_ref[slot * blocks + block]), :
            ].astype(bf16)


def expert_kernel(
    expert_ref, me_ref, rows_ref, marked_ref, piece0, piece1, piece2, piece3, router_ref,
    out_ref, in_grad_ref, pre_grad_ref, inner_ref, route_grad_ref, gu_ref, down_ref,
):
    @pl.when(pl.program_id(0) == 0)
    def _():
        part = gu_ref.shape[0] // 4
        for step, piece in enumerate((piece0, piece1, piece2, piece3)):
            place = me_ref[0] ^ step
            gu_ref[pl.ds(pl.multiple_of(place * part, part), part), :] = piece[:part, :]
            down_ref[pl.ds(pl.multiple_of(place * (part // 2), part // 2), part // 2), :] = piece[part:, :]

    rows = rows_ref[...]
    width = rows.shape[1]
    units = down_ref.shape[0]
    pre = product(rows, gu_ref[...])
    gate_pre, up_pre = pre[:, :units], pre[:, units:]
    sigmoid_a = 1.0 / (1.0 + jnp.exp(-gate_pre))
    swish_act = gate_pre * sigmoid_a
    inner_act = (swish_act * up_pre).astype(bf16)
    inner_ref[...] = inner_act
    expert_out = product(inner_act, down_ref[...]).astype(bf16)
    out_ref[...] = expert_out
    uses = marked_ref[:, width : width + EXPERTS].astype(f32)
    probs = gate_of(rows, uses, router_ref[...])
    column = lax.broadcasted_iota(jnp.int32, probs.shape, 1)
    slot_probs = jnp.sum(jnp.where(column == expert_ref[0], probs, 0.0), axis=1, keepdims=True)
    mix_grad = residual_scale * marked_ref[:, :width].astype(f32)
    gate_grad = jnp.sum(mix_grad * expert_out.astype(f32), axis=1, keepdims=True)
    route_grad = (slot_probs * mix_grad).astype(bf16)
    route_grad_ref[...] = route_grad
    inner_grad = product_nt(route_grad, down_ref[...])
    pre_grad_ref[:, :units] = (
        inner_grad * up_pre * sigmoid_a * (1.0 + gate_pre * (1.0 - sigmoid_a))
    ).astype(bf16)
    pre_grad_ref[:, units:] = (inner_grad * swish_act).astype(bf16)
    in_grad_ref[:, :width] = product_nt(pre_grad_ref[...], gu_ref[...]).astype(bf16)
    column = lax.broadcasted_iota(jnp.int32, (rows.shape[0], 128), 1)
    high = gate_grad.astype(bf16).astype(f32)
    in_grad_ref[:, width:] = jnp.where(
        column == expert_ref[0], high, jnp.where(column == EXPERTS + expert_ref[0], gate_grad - high, 0.0)
    ).astype(bf16)


def project_kernel(x_ref, w_ref, gain_ref, cos_ref, sin_ref, normed_ref, q_ref, kv_ref):
    values = x_ref[...].astype(f32)
    normed = (values * inv_rms_of(values) * gain_ref[...]).astype(bf16)
    normed_ref[...] = normed
    projected = product(normed, w_ref[...])
    rotated = projected * cos_ref[...] + turned(projected) * sin_ref[...]
    q_ref[...] = rotated[:, : 2 * HEAD_DIM].astype(bf16) * bf16(attn_scale)
    kv_ref[...] = rotated[:, 2 * HEAD_DIM :].astype(bf16)


def project(rows, head_w, gain, cosine, sine):
    count, width = rows.shape
    tile = 256

    def tiled(columns):
        return pl.BlockSpec((tile, columns), lambda i: (i, 0))

    def whole(array):
        return pl.BlockSpec(array.shape, lambda i: (0, 0))

    columns = (width, 2 * HEAD_DIM, 2 * HEAD_DIM)
    return pl.pallas_call(
        project_kernel,
        grid=(count // tile,),
        out_shape=tuple(jax.ShapeDtypeStruct((count, c), bf16) for c in columns),
        in_specs=[tiled(width), whole(head_w), whole(gain), tiled(4 * HEAD_DIM), tiled(4 * HEAD_DIM)],
        out_specs=tuple(tiled(c) for c in columns),
        compiler_params=pltpu.CompilerParams(vmem_limit_bytes=32 * 1024 * 1024),
        cost_estimate=pl.CostEstimate(flops=600_000_000, bytes_accessed=8_000_000, transcendentals=0),
    )(rows, head_w, gain, cosine, sine)


def call(kernel, outs, operands, flops, held=(), scalars=0, scratch=()):
    count = len(operands)

    def body(*refs):
        kernel(*refs[:count], *refs[count + len(held) :])

    return pl.pallas_call(
        body,
        out_shape=tuple(jax.ShapeDtypeStruct(shape, dtype) for shape, dtype in outs),
        in_specs=[SMEM] * scalars + [VMEM] * (count - scalars) + [pl.BlockSpec(memory_space=pl.ANY)] * len(held),
        out_specs=(VMEM,) * len(outs),
        scratch_shapes=[pltpu.VMEM(shape, f32) for shape in scratch],
        compiler_params=pltpu.CompilerParams(vmem_limit_bytes=48 * 1024 * 1024),
        cost_estimate=pl.CostEstimate(flops=flops, bytes_accessed=8_000_000, transcendentals=0),
    )(*operands, *held)


def part_of(me_ref, step, part):
    return pl.ds(pl.multiple_of((me_ref[0] ^ step) * part, part), part)


def copies_kernel(x_ref, copies_ref):
    for copy in range(KV_HEADS):
        copies_ref[copy] = x_ref[...]


def shard_kernel(
    head_ref, query_ref, key_ref, value_ref, router_ref, gain1_ref, gain2_ref, out_ref, by_head_ref
):
    rows = query_ref.shape[0]
    lower = lax.broadcasted_iota(jnp.int32, (rows, 128), 1) < HEAD_DIM
    for head in range(KV_HEADS):
        pair = slice(head // 2 * 128, (head // 2 + 1) * 128)
        keys, values = key_ref[:, pair].astype(f32), value_ref[:, pair].astype(f32)
        if head % 2:
            keys = pltpu.roll(keys, HEAD_DIM, 1)
        else:
            values = pltpu.roll(values, HEAD_DIM, 1)
        by_head_ref[:, head * 256 : head * 256 + 128] = query_ref[:, head * 128 : (head + 1) * 128]
        by_head_ref[:, head * 256 + 128 : (head + 1) * 256] = jnp.where(lower, keys, values).astype(bf16)
    out_ref[:rows, :] = by_head_ref[:, pl.ds(pl.multiple_of(head_ref[0] * 256, 256), 256)]
    router = jnp.concatenate([router_ref[...].astype(f32), jnp.zeros((rows, 128 - EXPERTS), f32)], axis=1)
    out_ref[rows : rows + EXPERTS, :] = router.T[:EXPERTS].astype(bf16)
    row = lax.broadcasted_iota(jnp.int32, (16, rows), 0)
    gains = jnp.where(row == 0, gain1_ref[...].astype(f32), jnp.where(row == 1, gain2_ref[...].astype(f32), 0.0))
    out_ref[rows + EXPERTS :, :] = gains.astype(bf16)


def small_kernel(me_ref, piece0, piece1, piece2, piece3, head_w_ref, router_ref, gain1_ref, gain2_ref):
    rows = head_w_ref.shape[0] // 4
    for step, piece in enumerate((piece0, piece1, piece2, piece3)):
        place = part_of(me_ref, step, rows)
        head_w_ref[place, :] = piece[:rows, :]
        router = piece[rows : rows + EXPERTS, :].astype(f32)
        router = jnp.concatenate([router, jnp.zeros((128 - EXPERTS, rows), f32)], axis=0)
        router_ref[place, :] = router.T[:, :EXPERTS].astype(bf16)
        gains = piece[rows + EXPERTS :, :].astype(f32)
        gain1_ref[:, place] = gains[0:1]
        gain2_ref[:, place] = gains[1:2]


def send_kernel(send_ref, rows_ref, out_ref):
    out_ref[...] = product(send_ref[...], rows_ref[...]).astype(bf16)


def middle_kernel(
    me_ref, attn_ref, out0, out1, out2, out3, x_ref, gain_ref, router_ref, uses_ref, send_ref,
    rows_ref, hidden_ref, normed_ref, probs_ref, out_ref,
):
    for head in range(KV_HEADS):
        rows_ref[:, head * 2 * HEAD_DIM : (head + 1) * 2 * HEAD_DIM] = attn_ref[head]
    branch = jnp.zeros(hidden_ref.shape, f32)
    for step, piece in enumerate((out0, out1, out2, out3)):
        branch += product(rows_ref[:, part_of(me_ref, step, piece.shape[0])], piece[...])
    hidden = x_ref[...].astype(f32) + residual_scale * branch
    hidden_ref[...] = hidden
    normed = (hidden * inv_rms_of(hidden) * gain_ref[...]).astype(bf16)
    normed_ref[...] = normed
    out_ref[...] = product(send_ref[...], normed).astype(bf16)
    probs_ref[...] = gate_of(normed, uses_ref[...], router_ref[...])


def token_grad_kernel(
    me_ref, fetch_ref, back_ref, probs_ref, router_ref, hidden_ref, gain_ref, cot_ref, out0, out1, out2, out3,
    hidden_grad_ref, branch_ref, logit_ref, gain_grad_ref, attn_grad_ref,
):
    width = hidden_ref.shape[1]
    fetched = product(fetch_ref[...], back_ref[...])
    gate_grad = fetched[:, width : width + EXPERTS] + fetched[:, width + EXPERTS : width + 2 * EXPERTS]
    probs = probs_ref[...]
    mean_grad = jnp.sum(probs * gate_grad, axis=-1, keepdims=True)
    logit_grad = (probs * (gate_grad - mean_grad)).astype(bf16)
    logit_ref[...] = logit_grad
    normed_grad = fetched[:, :width] + product_nt(logit_grad, router_ref[...])
    hidden = hidden_ref[...]
    hidden_part, gain_grad = norm_back(hidden, inv_rms_of(hidden), gain_ref[...], normed_grad)
    gain_grad_ref[...] = gain_grad
    hidden_grad = cot_ref[...].astype(f32) + hidden_part
    hidden_grad_ref[...] = hidden_grad
    branch = (residual_scale * hidden_grad).astype(bf16)
    branch_ref[...] = branch
    for step, piece in enumerate((out0, out1, out2, out3)):
        attn_grad = product_nt(branch, piece[...]).astype(bf16)
        heads = KV_HEADS // 4
        for head in range(heads):
            columns = slice(head * 2 * HEAD_DIM, (head + 1) * 2 * HEAD_DIM)
            attn_grad_ref[(me_ref[0] ^ step) * heads + head] = attn_grad[:, columns]


def dense_grad_kernel(core_ref, rows_ref, branch_ref, normed_ref, logit_ref, gain_ref, keep_ref, away_ref):
    part, width = keep_ref.shape[1], branch_ref.shape[1]
    logit_grad = logit_ref[...].astype(f32)
    logit_grad = jnp.concatenate(
        [logit_grad, jnp.zeros((logit_grad.shape[0], 128 - EXPERTS), f32)], axis=1
    ).astype(bf16)
    column = lax.broadcasted_iota(jnp.int32, (part, 128), 1)
    for row in range(2):
        for ref, core in ((keep_ref, core_ref[0]), (away_ref, 1 - core_ref[0])):
            columns = pl.ds(pl.multiple_of((2 * row + core) * part, part), part)
            ref[row, :, :width] = product_tn(rows_ref[:, columns], branch_ref[...]).astype(bf16)
            router_grad = product_tn(normed_ref[:, columns], logit_grad)
            gain_grad = jnp.broadcast_to(gain_ref[:, columns], (128, part)).T
            ref[row, :, width:] = jnp.where(column == EXPERTS, gain_grad, router_grad).astype(bf16)


def expert_grad_kernel(core_ref, rows_ref, pre_grad_ref, inner_ref, route_grad_ref, keep_ref, away_ref):
    part = rows_ref.shape[1] // 4
    for row in range(2):
        for ref, core in ((keep_ref, core_ref[0]), (away_ref, 1 - core_ref[0])):
            place = 2 * row + core
            columns = pl.ds(pl.multiple_of(place * part, part), part)
            ref[row, :part, :] = product_tn(rows_ref[:, columns], pre_grad_ref[...]).astype(bf16)
            columns = pl.ds(pl.multiple_of(place * (part // 2), part // 2), part // 2)
            ref[row, part:, :] = product_tn(inner_ref[:, columns], route_grad_ref[...]).astype(bf16)


def head_grad_kernel(dq_ref, dkv0, dkv1, dkv2, dkv3, cos_ref, sin_ref, out_ref):
    dkv = dkv0[...].astype(f32) + dkv1[...].astype(f32) + dkv2[...].astype(f32) + dkv3[...].astype(f32)
    for side, grad in enumerate((dq_ref[...], dkv)):
        columns = slice(side * 2 * HEAD_DIM, (side + 1) * 2 * HEAD_DIM)
        out_ref[:, columns] = (grad * cos_ref[:, columns] - turned(grad) * sin_ref[:, columns]).astype(bf16)


def head_weight_kernel(core_ref, normed_ref, grads_ref, keep_ref, away_ref):
    part = keep_ref.shape[1]
    for row in range(2):
        for ref, core in ((keep_ref, core_ref[0]), (away_ref, 1 - core_ref[0])):
            columns = pl.ds(pl.multiple_of((2 * row + core) * part, part), part)
            ref[row] = product_tn(normed_ref[:, columns], grads_ref[...]).astype(bf16)


def input_grad_kernel(
    me_ref, grads_ref, w0, w1, w2, w3, x_ref, gain_ref, hidden_grad_ref, out_ref, gain0, gain1, gain2, gain3, all_ref
):
    width = 4 * HEAD_DIM
    for step, piece in enumerate((w0, w1, w2, w3)):
        part = jnp.zeros((out_ref.shape[0], piece.shape[0]), f32)
        for head in range(KV_HEADS):
            part += product_nt(grads_ref[head], piece[:, head * width : (head + 1) * width])
        out_ref[:, part_of(me_ref, step, piece.shape[0])] = part
    values = x_ref[...].astype(f32)
    part, gain_grad = norm_back(values, inv_rms_of(values), gain_ref[...], out_ref[...])
    out_ref[...] = hidden_grad_ref[...] + part
    all_ref[...] = gain_grad
    for step, ref in enumerate((gain0, gain1, gain2, gain3)):
        ref[...] = all_ref[:, part_of(me_ref, step, ref.shape[1])]


def pack_kernel(
    place_ref, w0, w1, w2, w3, gain0, gain1, gain2, gain3, dense0, dense1, dense2, dense3, out_ref, rows_ref
):
    total = w0[...].astype(f32) + w1[...].astype(f32) + w2[...].astype(f32) + w3[...].astype(f32)
    total = total.astype(bf16)
    gain = gain0[...] + gain1[...] + gain2[...] + gain3[...]
    high = gain.astype(bf16).astype(f32)
    rows, columns = total.shape[0] // 4, total.shape[1]
    row = lax.broadcasted_iota(jnp.int32, (rows, 128), 0)
    block = jnp.zeros((rows, 128), f32)
    for line, part in enumerate((high[:, :128], high[:, 128:], (gain - high)[:, :128], (gain - high)[:, 128:])):
        block = jnp.where(row == line, part, block)
    for step, part in enumerate((dense0, dense1, dense2, dense3)):
        rows_ref[pl.ds(pl.multiple_of(((place_ref[0] + 4 - step) & 3) * 8, 8), 8), :] = part[...].astype(f32)
    dense = rows_ref[...].astype(bf16)
    for head in range(KV_HEADS):
        for side in range(4):
            out_ref[head, :rows, side * columns : (side + 1) * columns] = total[side * rows : (side + 1) * rows]
        out_ref[head, :rows, 4 * columns :] = block.astype(bf16)
        out_ref[head, rows:, :] = dense


def spread_kernel(
    last_ref, query_ref, key_ref, value_ref, gain_ref, out_grad_ref, router_ref, gain2_ref, column_ref
):
    columns = 4 * HEAD_DIM
    rows = last_ref.shape[1] - 32
    gain_lines = jnp.zeros((rows, 128), f32)
    for head in range(0, KV_HEADS, 2):
        for side in range(4):
            place = slice(side * rows, (side + 1) * rows)
            parts = []
            for step in (0, 1):
                part = last_ref[head + step, :rows, side * columns : (side + 1) * columns].astype(f32)
                query_ref[place, (head + step) * 2 * HEAD_DIM : (head + step + 1) * 2 * HEAD_DIM] = part[:, : 2 * HEAD_DIM]
                parts.append(part)
            pair = slice(head * HEAD_DIM, (head + 2) * HEAD_DIM)
            key_ref[place, pair] = jnp.concatenate([p[:, 2 * HEAD_DIM : 3 * HEAD_DIM] for p in parts], axis=1)
            value_ref[place, pair] = jnp.concatenate([p[:, 3 * HEAD_DIM :] for p in parts], axis=1)
    for head in range(KV_HEADS):
        gain_lines += last_ref[head, :rows, 4 * columns :].astype(f32)
        dense = last_ref[head, rows:, :].astype(f32)
        for place in range(4):
            part = dense[place * 8 : (place + 1) * 8]
            target = slice((place * KV_HEADS + head) * 8, (place * KV_HEADS + head + 1) * 8)
            out_grad_ref[target, :] = part[:, : 4 * columns]
            router_ref[target, :] = part[:, 4 * columns : 4 * columns + EXPERTS]
            column_ref[target, :] = part[:, 4 * columns :]
    gain_ref[:, :128] = gain_lines[0:1] + gain_lines[2:3]
    gain_ref[:, 128:] = gain_lines[1:2] + gain_lines[3:4]
    gain2_ref[...] = column_ref[...].T[EXPERTS : EXPERTS + 1, :]


def gate_of(rows, mask, router_w):
    logits = jnp.where(mask > 0, product(rows, router_w), masked_value)
    exps = jnp.where(mask > 0, jnp.exp(logits - jnp.max(logits, axis=-1, keepdims=True)), 0.0)
    return exps / jnp.maximum(jnp.sum(exps, axis=-1, keepdims=True), 1e-30)


def run_experts(expert, me, rows, marked, pieces, router_w):
    count, width = rows.shape
    part = pieces[0].shape[0] // 3
    units = 4 * part
    tile = 256

    def tiled(columns):
        return pl.BlockSpec((tile, columns), lambda i: (i, 0))

    def whole(array):
        return pl.BlockSpec(array.shape, lambda i: (0, 0))

    columns = (width, width + 128, 2 * units, units, width)
    return pl.pallas_call(
        expert_kernel,
        grid=(count // tile,),
        out_shape=tuple(jax.ShapeDtypeStruct((count, c), bf16) for c in columns),
        in_specs=[SMEM, SMEM, tiled(width), tiled(width + 128)] + [whole(p) for p in pieces] + [whole(router_w)],
        out_specs=tuple(tiled(c) for c in columns),
        scratch_shapes=[pltpu.VMEM((8 * part, 2 * units), bf16), pltpu.VMEM((units, width), bf16)],
        compiler_params=pltpu.CompilerParams(vmem_limit_bytes=56 * 1024 * 1024),
        cost_estimate=pl.CostEstimate(flops=10_000_000_000, bytes_accessed=22_000_000, transcendentals=1_000_000),
    )(expert.astype(jnp.int32).reshape(1), me, rows, marked, *pieces, router_w)


SMEM = pl.BlockSpec(memory_space=pltpu.SMEM)
VMEM = pl.BlockSpec(memory_space=pltpu.VMEM)


def attend(numbers, queries, kv_parts):
    rows = queries.shape[0]
    keys = rows * len(kv_parts)
    pairs = rows // (2 * HALF)
    return pl.pallas_call(
        attend_kernel,
        out_shape=(
            jax.ShapeDtypeStruct((rows, 2 * HEAD_DIM), bf16),
            jax.ShapeDtypeStruct((pairs, HEAD_DIM, 4 * HALF), f32),
            jax.ShapeDtypeStruct((pairs, 1, 4 * HALF), f32),
        ),
        in_specs=[SMEM] * 3 + [VMEM] * 5,
        out_specs=(VMEM,) * 3,
        scratch_shapes=[pltpu.VMEM((keys, 2 * HEAD_DIM), bf16), pltpu.VMEM((2 * HEAD_DIM, keys), bf16)],
        compiler_params=pltpu.CompilerParams(vmem_limit_bytes=40 * 1024 * 1024),
        cost_estimate=pl.CostEstimate(flops=12_000_000_000, bytes_accessed=4_000_000, transcendentals=5_000_000),
    )(*numbers, queries, *kv_parts)


def attend_grad(numbers, queries, kv_parts, grads, turned, lse):
    rows = queries.shape[0]
    keys = rows * len(kv_parts)
    return pl.pallas_call(
        attend_grad_kernel,
        out_shape=(jax.ShapeDtypeStruct((rows, 2 * HEAD_DIM), f32),)
        + (jax.ShapeDtypeStruct((rows, 2 * HEAD_DIM), bf16),) * 4,
        in_specs=[SMEM] * 3 + [VMEM] * 8,
        out_specs=(VMEM,) * 5,
        scratch_shapes=[
            pltpu.VMEM((keys, 2 * HEAD_DIM), bf16),
            pltpu.VMEM((2 * HEAD_DIM, keys), bf16),
            pltpu.VMEM((keys, 2 * HEAD_DIM), f32),
        ],
        compiler_params=pltpu.CompilerParams(vmem_limit_bytes=40 * 1024 * 1024),
        cost_estimate=pl.CostEstimate(flops=30_000_000_000, bytes_accessed=6_000_000, transcendentals=5_000_000),
    )(*numbers, queries, *kv_parts, grads, turned, lse)


def block_numbers(block_pairs):
    place = lax.axis_index("x")
    groups = block_pairs.reshape(4, 8)
    groups = groups[(place - jnp.arange(4)) & 3]
    numbers = jnp.stack([groups, 63 - groups], axis=-1).reshape(-1)
    own = numbers[:16]
    rank = jnp.sum((own[None, :] < own[:, None]).astype(jnp.int32), axis=1)
    spots = jnp.arange(16, dtype=jnp.int32)
    order = jnp.sum(jnp.where(rank[None, :] == spots[:, None], spots[None, :], 0), axis=1)
    return (order, own, numbers)


def on_device(
    block_input,
    routes,
    block_pairs,
    norm1_gain,
    w_query,
    w_key,
    w_value,
    w_out,
    norm2_gain,
    w_router,
    w_gate,
    w_up,
    w_down,
    cotangent,
):
    tokens, width = block_input.shape[1:]
    head = lax.axis_index(ZY)
    expert = lax.axis_index(CTX)
    shard_rows = w_query.shape[0]
    own_input = block_input[0]

    core = lax.axis_index("core").astype(jnp.int32).reshape(1)
    place = lax.axis_index("x").astype(jnp.int32).reshape(1)
    me = lax.axis_index(("yl", "core")).astype(jnp.int32).reshape(1)
    small_shard, by_head = call(
        shard_kernel,
        [((shard_rows + EXPERTS + 16, 4 * HEAD_DIM), bf16), ((shard_rows, KV_HEADS * 4 * HEAD_DIM), bf16)],
        (
            head.astype(jnp.int32).reshape(1), w_query, w_key, w_value, w_router,
            norm1_gain.reshape(1, -1), norm2_gain.reshape(1, -1),
        ),
        1_000_000,
        scalars=1,
    )
    small_pieces = pieces_direct(small_shard)
    (copies,) = call(copies_kernel, [((KV_HEADS, tokens, width), bf16)], (own_input,), 1_000_000)
    group_input = exchange(copies.reshape(-1, width), ZY)
    head_w, router_w, gain_one, gain_two = call(
        small_kernel,
        [((width, 4 * HEAD_DIM), bf16), ((width, EXPERTS), bf16), ((1, width), f32), ((1, width), f32)],
        (me, *small_pieces),
        1_000_000,
        scalars=1,
    )

    numbers = block_numbers(block_pairs)
    group_pos = (numbers[1][:, None] * HALF + jnp.arange(HALF, dtype=jnp.int32)[None, :]).reshape(-1)
    cosine, sine = rope_tables(group_pos)

    chosen = routes[0]
    uses = jnp.sum(
        (chosen[:, :, None] == jnp.arange(EXPERTS, dtype=jnp.int32)[None, None, :]).astype(f32), axis=1
    )
    earlier = jnp.tril(jnp.ones((tokens, tokens), bf16), -1)
    rank = product(earlier, uses.astype(bf16)).astype(jnp.int32)
    rank = jnp.where(uses > 0, rank, -1)
    slot = jnp.arange(CAP, dtype=jnp.int32)
    send = (rank.T[:, None, :] == slot[None, :, None]).astype(bf16).reshape(EXPERTS * CAP, tokens)
    fetch = (rank[:, :, None] == slot[None, None, :]).astype(bf16).reshape(tokens, EXPERTS * CAP)

    group_normed, queries, kv_own = project(group_input, head_w, gain_one, cosine, sine)
    kv_parts = [kv_own] + [turn(kv_own, "x", step) for step in (1, 2, 3)]

    out_other = swap(w_out, "yl")
    expert_shard = jnp.concatenate([jnp.concatenate([w_gate[0], w_up[0]], axis=1), w_down[0]], axis=0)
    expert_other = swap(expert_shard, "yl")
    marked = jnp.concatenate(
        [cotangent[0], uses.astype(bf16), jnp.zeros((tokens, 128 - EXPERTS), bf16)], axis=1
    )
    (marked_sent,) = call(
        send_kernel,
        [((EXPERTS * CAP, width + 128), bf16)],
        (send, marked),
        500_000_000,
        held=(*kv_parts[1:], out_other, expert_other),
    )
    marked_arrived = exchange(marked_sent, CTX)

    attn_group, attn_turned, lse = attend(numbers, queries, kv_parts)

    out_pieces = pieces_by_row(w_out, out_other)

    attn_back = exchange(tie(attn_group, marked_arrived), ZY)
    expert_pieces = pieces_by_row(expert_shard, expert_other)
    attn_rows, hidden, normed2, gate_probs, outgoing = call(
        middle_kernel,
        [
            ((tokens, HEADS * HEAD_DIM), bf16),
            ((tokens, width), f32),
            ((tokens, width), bf16),
            ((tokens, EXPERTS), f32),
            ((EXPERTS * CAP, width), bf16),
        ],
        (
            me, attn_back.reshape(KV_HEADS, tokens, 2 * HEAD_DIM), *out_pieces, own_input, gain_two, router_w,
            uses, send,
        ),
        800_000_000,
        held=expert_pieces,
        scalars=1,
    )
    arrived = exchange(outgoing, CTX)

    expert_out, in_grad, pre_grad, inner_act, route_grad = run_experts(
        expert, me, arrived, marked_arrived, expert_pieces, router_w
    )
    back = exchange(in_grad, CTX)
    by_head_sent = tie(by_head, normed2)
    head_pieces = pieces_by_row(by_head_sent, swap(by_head_sent, "yl"))
    expert_shape = ((2, *expert_shard.shape), bf16)
    expert_both = join_core(
        *call(
            expert_grad_kernel,
            [expert_shape, expert_shape],
            (core, arrived, pre_grad, inner_act, route_grad),
            5_000_000_000,
            held=(head_pieces[2],),
            scalars=1,
        )
    )

    hidden_grad, branch_grad, logit_grad, gain_two_grad, attn_grad = call(
        token_grad_kernel,
        [
            ((tokens, width), f32),
            ((tokens, width), bf16),
            ((tokens, EXPERTS), bf16),
            ((1, width), f32),
            ((KV_HEADS, tokens, 2 * HEAD_DIM), bf16),
        ],
        (me, fetch, back, gate_probs, router_w, hidden, gain_two, cotangent[0], *out_pieces),
        800_000_000,
        held=(expert_both, *head_pieces),
        scalars=1,
    )

    group_grad = exchange(attn_grad.reshape(KV_HEADS * tokens, 2 * HEAD_DIM), ZY)
    dq, *dkv_parts = attend_grad(numbers, queries, kv_parts, group_grad, attn_turned, lse)
    expert_sums = scatter_row(tie(expert_both, group_grad))
    dkv_turned = [turn(dkv_parts[step], "x", -step) for step in (1, 2, 3)]
    dense_shape = ((2, shard_rows, width + 128), bf16)
    dense_both = join_core(
        *call(
            dense_grad_kernel,
            [dense_shape, dense_shape],
            (core, attn_rows, branch_grad, normed2, logit_grad, gain_two_grad),
            400_000_000,
            scalars=1,
        )
    )
    dense = scatter_row(dense_both).astype(bf16)
    dense = exchange(dense, CTX).reshape(EXPERTS, -1, width + 128)
    dense = jnp.sum(dense.astype(f32), axis=0).astype(bf16)

    (grads,) = call(
        head_grad_kernel,
        [((KV_HEADS * tokens, 4 * HEAD_DIM), bf16)],
        (dq, dkv_parts[0], *dkv_turned, cosine, sine),
        100_000_000,
        held=(dense, expert_sums),
    )
    token_grads = exchange(grads, ZY)
    head_shape = ((2, shard_rows, 4 * HEAD_DIM), bf16)
    head_both = join_core(
        *call(head_weight_kernel, [head_shape, head_shape], (core, group_normed, grads), 600_000_000, scalars=1)
    )
    head_part = scatter_row(head_both).astype(bf16)

    returned = exchange(tie(expert_out, token_grads), CTX)

    gain_shape = ((1, shard_rows), f32)
    input_grad, *gain_parts = call(
        input_grad_kernel,
        [((tokens, width), f32)] + [gain_shape] * 4,
        (
            me, token_grads.reshape(KV_HEADS, tokens, 4 * HEAD_DIM), *head_pieces, own_input, gain_one, hidden_grad,
        ),
        600_000_000,
        scalars=1,
        scratch=[(1, width)],
    )
    gain_sum = gain_parts[0]
    for step in (1, 2, 3):
        gain_sum = gain_sum + lax.ppermute(gain_parts[step], ("yl", "core"), [(i, i ^ step) for i in range(4)])

    (last,) = call(
        pack_kernel,
        [((KV_HEADS, shard_rows // 4 + 32, width + 128), bf16)],
        (place, *all_x(head_part), *all_x(gain_sum), *all_x(dense)),
        1_000_000,
        held=(returned,),
        scalars=1,
        scratch=[(32, width + 128)],
    )
    last = exchange(last.reshape(-1, width + 128), ZY).reshape(last.shape)
    grad_query, grad_key, grad_value, gain_one_grad, grad_out, grad_router, gain_two_grad = call(
        spread_kernel,
        [
            ((shard_rows, HEADS * HEAD_DIM), f32),
            ((shard_rows, KV_HEADS * HEAD_DIM), f32),
            ((shard_rows, KV_HEADS * HEAD_DIM), f32),
            gain_shape,
            ((shard_rows, width), f32),
            ((shard_rows, EXPERTS), f32),
            gain_shape,
        ],
        (last,),
        1_000_000,
        scratch=[(shard_rows, 128)],
    )

    spread = gate_probs[:, :, None] * fetch.astype(f32).reshape(tokens, EXPERTS, CAP)
    weights = spread.reshape(tokens, EXPERTS * CAP)
    weights_hi = weights.astype(bf16)
    weights_lo = (weights - weights_hi.astype(f32)).astype(bf16)
    mixture = product(weights_hi, returned) + product(weights_lo, returned)
    output = hidden + residual_scale * mixture

    return (
        output.astype(bf16)[None],
        input_grad[None],
        gain_one_grad.reshape(-1),
        grad_query,
        grad_key,
        grad_value,
        grad_out,
        gain_two_grad.reshape(-1),
        grad_router,
        expert_sums[None, :shard_rows, : width // 2],
        expert_sums[None, :shard_rows, width // 2 :],
        expert_sums[None, shard_rows:],
    )


def solution(mesh):
    fine = Mesh(mesh.devices.reshape(4, 4, 2, 2, 2), EVERY)
    rows, shards = P(("yl", "core"), CTX, None), P(("yl", "core"), None)
    gain, experts = P(("yl", "core")), P(CTX, ("yl", "core"), None)
    return jax.shard_map(
        on_device,
        mesh=fine,
        in_specs=(
            rows, rows, P(), gain, shards, shards, shards, shards, gain, shards, experts, experts, experts, rows,
        ),
        out_specs=(
            rows, rows, gain, shards, shards, shards, shards, gain, shards, experts, experts, experts,
        ),
        check_vma=False,
    )
```

```python
import functools

import jax
import jax.numpy as jnp
from jax import lax
from jax.experimental import pallas as pl
from jax.experimental.layout import Layout, with_layout_constraint
from jax.experimental.pallas import tpu as pltpu
from jax.sharding import Mesh
from jax.sharding import PartitionSpec as P

HEADS = 16
KV_HEADS = 8
HEAD_DIM = 64
EXPERTS = 32
TOP = 8
CAP = 48
HALF = 64
TILE = 512

epsilon = 1e-06
attn_scale = 0.015625
residual_scale = 0.22
masked_value = -1e30

CTX = ("x", "z", "yh")
ZY = ("z", "yh")
EVERY = ("x", "z", "yh", "yl", "core")
bf16 = jnp.bfloat16
f32 = jnp.float32


def product(left, right):
    return jnp.dot(left, right, preferred_element_type=f32)


def product_nt(left, right):
    return lax.dot_general(left, right, (((1,), (1,)), ((), ())), preferred_element_type=f32)


def product_tn(left, right):
    return lax.dot_general(left, right, (((0,), (0,)), ((), ())), preferred_element_type=f32)


def swap(values, axis):
    return lax.ppermute(values, axis, [(0, 1), (1, 0)])


def turn(values, axis, step):
    return lax.ppermute(values, axis, [(i, (i + step) % 4) for i in range(4)])


def rows_first(values):
    return with_layout_constraint(values, Layout(major_to_minor=tuple(range(values.ndim))))


def exchange(values, axes):
    return rows_first(lax.all_to_all(rows_first(values), axes, 0, 0, tiled=True))


def tie(values, *others):
    if values.size <= 1024:
        return values + sum(other[(0,) * other.ndim].astype(f32) * 0.0 for other in others).astype(values.dtype)
    corner = tuple(slice(0, min(size, 8 if axis < values.ndim - 1 else 128)) for axis, size in enumerate(values.shape))
    nothing = sum(other[(0,) * other.ndim].astype(f32) * 0.0 for other in others)
    held = values[corner] + nothing.astype(values.dtype)
    return lax.dynamic_update_slice(values, held, (0,) * values.ndim)


def pieces_direct(shard):
    steps = [lax.ppermute(shard, ("yl", "core"), [(i, i ^ k) for i in range(4)]) for k in (1, 2, 3)]
    return (shard, *steps)


def pieces_by_row(shard, other):
    return (shard, swap(shard, "core"), other, swap(other, "core"))


def scatter_core(parts):
    core = lax.axis_index("core")
    parts = parts.astype(bf16).reshape((2, 2) + parts.shape[1:])
    away = lax.dynamic_index_in_dim(parts, 1 - core, 1, keepdims=False)
    keep = lax.dynamic_index_in_dim(parts, core, 1, keepdims=False)
    return (keep.astype(f32) + swap(away, "core").astype(f32)).astype(bf16)


def join_core(keep, away):
    return (keep.astype(f32) + swap(away, "core").astype(f32)).astype(bf16)


def scatter_row(both):
    row = lax.axis_index("yl")
    away = lax.dynamic_index_in_dim(both, 1 - row, 0, keepdims=False)
    keep = lax.dynamic_index_in_dim(both, row, 0, keepdims=False)
    return keep.astype(f32) + swap(away, "yl").astype(f32)


def scatter_fsdp(parts):
    return scatter_row(scatter_core(parts))


def all_x(part):
    return [part] + [turn(part, "x", step) for step in (1, 2, 3)]


def rope_tables(positions):
    freqs = jnp.power(10000.0, -jnp.arange(0, HEAD_DIM, 2, dtype=f32) / HEAD_DIM)
    angles = positions.astype(f32)[:, None] * freqs[None, :]
    cosine, sine = jnp.cos(angles), jnp.sin(angles)
    ones, zeros = jnp.ones_like(cosine), jnp.zeros_like(cosine)
    return (
        jnp.concatenate([cosine] * 6 + [ones] * 2, axis=1),
        jnp.concatenate([-sine, sine] * 3 + [zeros] * 2, axis=1),
    )


def turned(values):
    width = values.shape[1]
    column = lax.broadcasted_iota(jnp.int32, values.shape, 1)
    return jnp.where(
        column % HEAD_DIM < HEAD_DIM // 2,
        pltpu.roll(values, width - HEAD_DIM // 2, 1),
        pltpu.roll(values, HEAD_DIM // 2, 1),
    )


def norm_back(values, inv_rms, gain, grad):
    weighted = grad * gain
    gain_grad = jnp.sum(grad * values * inv_rms, axis=0, keepdims=True)
    inner_mean = jnp.mean(weighted * values, axis=-1, keepdims=True)
    return (weighted * inv_rms - values * inv_rms * inv_rms * inv_rms * inner_mean, gain_grad)


def inv_rms_of(values):
    return lax.rsqrt(jnp.mean(values * values, axis=-1, keepdims=True) + epsilon)


def half(index):
    return pl.ds(pl.multiple_of(index * HALF, HALF), HALF)


def key_tile(counter):
    return pl.ds(pl.multiple_of(counter * TILE, TILE), TILE)


def sort_keys(knum_ref, kv_refs, kvs, kvt):
    blocks = kv_refs[0].shape[0] // HALF
    for slot, kv_ref in enumerate(kv_refs):
        for block in range(blocks):
            kvs[half(knum_ref[slot * blocks + block]), :] = kv_ref[block * HALF : (block + 1) * HALF, :]
    for tile in range(kvs.shape[0] // TILE):
        part = kvs[tile * TILE : (tile + 1) * TILE, :].astype(f32)
        kvt[:, tile * TILE : (tile + 1) * TILE] = part.T.astype(bf16)


def pair_rows(ref, first, second, upper):
    rows = []
    for block in (first, second):
        values = ref[half(block), :].astype(f32)
        column = lax.broadcasted_iota(jnp.int32, values.shape, 1)
        inside = (column >= HEAD_DIM) if upper else (column < HEAD_DIM)
        moved = pltpu.roll(values, HEAD_DIM, 1)
        heads = (moved, values) if upper else (values, moved)
        rows += [jnp.where(inside, head, 0.0) for head in heads]
    return jnp.concatenate(rows, axis=0)


def pair_positions(low_number, high_number):
    column = lax.broadcasted_iota(jnp.int32, (1, 4 * HALF), 1)
    return jnp.where(column < 2 * HALF, low_number, high_number) * HALF + column % HALF


def score_tile(keys, queries, counter, positions, masked):
    scores = product_nt(keys, queries)
    if masked:
        key_pos = counter * TILE + lax.broadcasted_iota(jnp.int32, scores.shape, 0)
        scores = jnp.where(key_pos <= positions, scores, masked_value)
    return scores


def store_rows(ref, turned, first, second):
    rows = turned.T
    ref[half(first), :] = jnp.concatenate([rows[:HALF], rows[HALF : 2 * HALF]], axis=1).astype(ref.dtype)
    ref[half(second), :] = jnp.concatenate([rows[2 * HALF : 3 * HALF], rows[3 * HALF :]], axis=1).astype(ref.dtype)


def attend_kernel(
    order_ref, qnum_ref, knum_ref, q_ref, kv0, kv1, kv2, kv3, out_ref, turned_ref, lse_ref, kvs, kvt
):
    sort_keys(knum_ref, (kv0, kv1, kv2, kv3), kvs, kvt)
    width = 4 * HALF

    @pl.loop(0, q_ref.shape[0] // (2 * HALF))
    def _(pair):
        first, second = order_ref[2 * pair], order_ref[2 * pair + 1]
        low_number, high_number = qnum_ref[first], qnum_ref[second]
        queries = pair_rows(q_ref, first, second, False).astype(bf16)
        positions = pair_positions(low_number, high_number)

        def step(masked, counter, running):
            top, total, mixed = running
            scores = score_tile(kvs[key_tile(counter), :], queries, counter, positions, masked)
            new_top = jnp.maximum(top, jnp.max(scores, axis=0, keepdims=True))
            probs = jnp.exp(scores - new_top)
            shrink = jnp.exp(top - new_top)
            total = total * shrink + jnp.sum(probs, axis=0, keepdims=True)
            mixed = mixed * shrink + product(kvt[HEAD_DIM:, key_tile(counter)], probs.astype(bf16))
            return (new_top, total, mixed)

        start = (
            jnp.full((1, width), masked_value, f32),
            jnp.zeros((1, width), f32),
            jnp.zeros((HEAD_DIM, width), f32),
        )
        full = (low_number * HALF) // TILE
        last = (high_number * HALF) // TILE + 1
        running = lax.fori_loop(0, full, functools.partial(step, False), start)
        top, total, mixed = lax.fori_loop(full, last, functools.partial(step, True), running)
        mixed = mixed / total
        turned_ref[pair] = mixed
        lse_ref[pair] = top + jnp.log(total)
        store_rows(out_ref, mixed, first, second)


def attend_grad_kernel(
    order_ref, qnum_ref, knum_ref, q_ref, kv0, kv1, kv2, kv3, grad_ref, turned_ref, lse_ref,
    dq_ref, dkv0, dkv1, dkv2, dkv3, kvs, kvt, total_ref,
):
    sort_keys(knum_ref, (kv0, kv1, kv2, kv3), kvs, kvt)
    total_ref[...] = jnp.zeros_like(total_ref)
    width = 4 * HALF

    @pl.loop(0, q_ref.shape[0] // (2 * HALF))
    def _(pair):
        first, second = order_ref[2 * pair], order_ref[2 * pair + 1]
        low_number, high_number = qnum_ref[first], qnum_ref[second]
        queries = pair_rows(q_ref, first, second, False).astype(bf16)
        grads_f = pair_rows(grad_ref, first, second, True)
        grads = grads_f.astype(bf16)
        both = jnp.concatenate([queries, grads], axis=0)
        positions = pair_positions(low_number, high_number)
        lse = lse_ref[pair]
        dots = jnp.sum(grads_f.T[HEAD_DIM:] * turned_ref[pair], axis=0, keepdims=True)

        def step(masked, counter, query_acc):
            keys = kvs[key_tile(counter), :]
            probs = jnp.exp(score_tile(keys, queries, counter, positions, masked) - lse)
            score_grad = (probs * (product_nt(keys, grads) - dots)).astype(bf16)
            sides = jnp.concatenate([score_grad, probs.astype(bf16)], axis=1)
            total_ref[key_tile(counter), :] += product(sides, both)
            return query_acc + product(kvt[:HEAD_DIM, key_tile(counter)], score_grad)

        full = (low_number * HALF) // TILE
        last = (high_number * HALF) // TILE + 1
        query_acc = lax.fori_loop(0, full, functools.partial(step, False), jnp.zeros((HEAD_DIM, width), f32))
        query_acc = lax.fori_loop(full, last, functools.partial(step, True), query_acc)
        store_rows(dq_ref, query_acc * attn_scale, first, second)

    blocks = dkv0.shape[0] // HALF
    for slot, dkv in enumerate((dkv0, dkv1, dkv2, dkv3)):
        for block in range(blocks):
            dkv[block * HALF : (block + 1) * HALF, :] = total_ref[
                half(knum_ref[slot * blocks + block]), :
            ].astype(bf16)


def expert_kernel(
    expert_ref, me_ref, rows_ref, marked_ref, piece0, piece1, piece2, piece3, router_ref,
    out_ref, in_grad_ref, pre_grad_ref, inner_ref, route_grad_ref, gu_ref, down_ref,
):
    @pl.when(pl.program_id(0) == 0)
    def _():
        part = gu_ref.shape[0] // 4
        for step, piece in enumerate((piece0, piece1, piece2, piece3)):
            place = me_ref[0] ^ step
            gu_ref[pl.ds(pl.multiple_of(place * part, part), part), :] = piece[:part, :]
            down_ref[pl.ds(pl.multiple_of(place * (part // 2), part // 2), part // 2), :] = piece[part:, :]

    rows = rows_ref[...]
    width = rows.shape[1]
    units = down_ref.shape[0]
    pre = product(rows, gu_ref[...])
    gate_pre, up_pre = pre[:, :units], pre[:, units:]
    sigmoid_a = 1.0 / (1.0 + jnp.exp(-gate_pre))
    swish_act = gate_pre * sigmoid_a
    inner_act = (swish_act * up_pre).astype(bf16)
    inner_ref[...] = inner_act
    expert_out = product(inner_act, down_ref[...]).astype(bf16)
    out_ref[...] = expert_out
    uses = marked_ref[:, width : width + EXPERTS].astype(f32)
    probs = gate_of(rows, uses, router_ref[...])
    column = lax.broadcasted_iota(jnp.int32, probs.shape, 1)
    slot_probs = jnp.sum(jnp.where(column == expert_ref[0], probs, 0.0), axis=1, keepdims=True)
    mix_grad = residual_scale * marked_ref[:, :width].astype(f32)
    gate_grad = jnp.sum(mix_grad * expert_out.astype(f32), axis=1, keepdims=True)
    route_grad = (slot_probs * mix_grad).astype(bf16)
    route_grad_ref[...] = route_grad
    inner_grad = product_nt(route_grad, down_ref[...])
    pre_grad_ref[:, :units] = (
        inner_grad * up_pre * sigmoid_a * (1.0 + gate_pre * (1.0 - sigmoid_a))
    ).astype(bf16)
    pre_grad_ref[:, units:] = (inner_grad * swish_act).astype(bf16)
    in_grad_ref[:, :width] = product_nt(pre_grad_ref[...], gu_ref[...]).astype(bf16)
    column = lax.broadcasted_iota(jnp.int32, (rows.shape[0], 128), 1)
    high = gate_grad.astype(bf16).astype(f32)
    in_grad_ref[:, width:] = jnp.where(
        column == expert_ref[0], high, jnp.where(column == EXPERTS + expert_ref[0], gate_grad - high, 0.0)
    ).astype(bf16)


def project_kernel(x_ref, w_ref, gain_ref, cos_ref, sin_ref, normed_ref, q_ref, kv_ref):
    values = x_ref[...].astype(f32)
    normed = (values * inv_rms_of(values) * gain_ref[...]).astype(bf16)
    normed_ref[...] = normed
    projected = product(normed, w_ref[...])
    rotated = projected * cos_ref[...] + turned(projected) * sin_ref[...]
    q_ref[...] = rotated[:, : 2 * HEAD_DIM].astype(bf16) * bf16(attn_scale)
    kv_ref[...] = rotated[:, 2 * HEAD_DIM :].astype(bf16)


def project(rows, head_w, gain, cosine, sine):
    count, width = rows.shape
    tile = 256

    def tiled(columns):
        return pl.BlockSpec((tile, columns), lambda i: (i, 0))

    def whole(array):
        return pl.BlockSpec(array.shape, lambda i: (0, 0))

    columns = (width, 2 * HEAD_DIM, 2 * HEAD_DIM)
    return pl.pallas_call(
        project_kernel,
        grid=(count // tile,),
        out_shape=tuple(jax.ShapeDtypeStruct((count, c), bf16) for c in columns),
        in_specs=[tiled(width), whole(head_w), whole(gain), tiled(4 * HEAD_DIM), tiled(4 * HEAD_DIM)],
        out_specs=tuple(tiled(c) for c in columns),
        compiler_params=pltpu.CompilerParams(vmem_limit_bytes=32 * 1024 * 1024),
        cost_estimate=pl.CostEstimate(flops=600_000_000, bytes_accessed=8_000_000, transcendentals=0),
    )(rows, head_w, gain, cosine, sine)


def call(kernel, outs, operands, flops, held=(), scalars=0, scratch=()):
    count = len(operands)

    def body(*refs):
        kernel(*refs[:count], *refs[count + len(held) :])

    return pl.pallas_call(
        body,
        grid=(1,),
        out_shape=tuple(jax.ShapeDtypeStruct(shape, dtype) for shape, dtype in outs),
        in_specs=[SMEM] * scalars
        + [whole_block(array.shape) for array in operands[scalars:]]
        + [pl.BlockSpec(memory_space=pl.ANY)] * len(held),
        out_specs=tuple(whole_block(shape) for shape, _ in outs),
        scratch_shapes=[pltpu.VMEM(shape, f32) for shape in scratch],
        compiler_params=pltpu.CompilerParams(vmem_limit_bytes=48 * 1024 * 1024),
        cost_estimate=pl.CostEstimate(flops=flops, bytes_accessed=8_000_000, transcendentals=0),
    )(*operands, *held)


def part_of(me_ref, step, part):
    return pl.ds(pl.multiple_of((me_ref[0] ^ step) * part, part), part)


def copies_kernel(x_ref, copies_ref):
    for copy in range(KV_HEADS):
        copies_ref[copy] = x_ref[...]


def shard_kernel(
    head_ref, query_ref, key_ref, value_ref, router_ref, gain1_ref, gain2_ref, out_ref, by_head_ref
):
    rows = query_ref.shape[0]
    lower = lax.broadcasted_iota(jnp.int32, (rows, 128), 1) < HEAD_DIM
    for head in range(KV_HEADS):
        pair = slice(head // 2 * 128, (head // 2 + 1) * 128)
        keys, values = key_ref[:, pair].astype(f32), value_ref[:, pair].astype(f32)
        if head % 2:
            keys = pltpu.roll(keys, HEAD_DIM, 1)
        else:
            values = pltpu.roll(values, HEAD_DIM, 1)
        by_head_ref[:, head * 256 : head * 256 + 128] = query_ref[:, head * 128 : (head + 1) * 128]
        by_head_ref[:, head * 256 + 128 : (head + 1) * 256] = jnp.where(lower, keys, values).astype(bf16)
    out_ref[:rows, :] = by_head_ref[:, pl.ds(pl.multiple_of(head_ref[0] * 256, 256), 256)]
    router = jnp.concatenate([router_ref[...].astype(f32), jnp.zeros((rows, 128 - EXPERTS), f32)], axis=1)
    out_ref[rows : rows + EXPERTS, :] = router.T[:EXPERTS].astype(bf16)
    row = lax.broadcasted_iota(jnp.int32, (16, rows), 0)
    gains = jnp.where(row == 0, gain1_ref[...].astype(f32), jnp.where(row == 1, gain2_ref[...].astype(f32), 0.0))
    out_ref[rows + EXPERTS :, :] = gains.astype(bf16)


def small_kernel(me_ref, piece0, piece1, piece2, piece3, head_w_ref, router_ref, gain1_ref, gain2_ref):
    rows = head_w_ref.shape[0] // 4
    for step, piece in enumerate((piece0, piece1, piece2, piece3)):
        place = part_of(me_ref, step, rows)
        head_w_ref[place, :] = piece[:rows, :]
        router = piece[rows : rows + EXPERTS, :].astype(f32)
        router = jnp.concatenate([router, jnp.zeros((128 - EXPERTS, rows), f32)], axis=0)
        router_ref[place, :] = router.T[:, :EXPERTS].astype(bf16)
        gains = piece[rows + EXPERTS :, :].astype(f32)
        gain1_ref[:, place] = gains[0:1]
        gain2_ref[:, place] = gains[1:2]


def send_kernel(send_ref, rows_ref, out_ref):
    out_ref[...] = product(send_ref[...], rows_ref[...]).astype(bf16)


def middle_kernel(
    me_ref, attn_ref, out0, out1, out2, out3, x_ref, gain_ref, router_ref, uses_ref, send_ref,
    rows_ref, hidden_ref, normed_ref, probs_ref, out_ref,
):
    for head in range(KV_HEADS):
        rows_ref[:, head * 2 * HEAD_DIM : (head + 1) * 2 * HEAD_DIM] = attn_ref[head]
    branch = jnp.zeros(hidden_ref.shape, f32)
    for step, piece in enumerate((out0, out1, out2, out3)):
        branch += product(rows_ref[:, part_of(me_ref, step, piece.shape[0])], piece[...])
    hidden = x_ref[...].astype(f32) + residual_scale * branch
    hidden_ref[...] = hidden
    normed = (hidden * inv_rms_of(hidden) * gain_ref[...]).astype(bf16)
    normed_ref[...] = normed
    out_ref[...] = product(send_ref[...], normed).astype(bf16)
    probs_ref[...] = gate_of(normed, uses_ref[...], router_ref[...])


def token_grad_kernel(
    me_ref, fetch_ref, back_ref, probs_ref, router_ref, hidden_ref, gain_ref, cot_ref, out0, out1, out2, out3,
    hidden_grad_ref, branch_ref, logit_ref, gain_grad_ref, attn_grad_ref,
):
    width = hidden_ref.shape[1]
    fetched = product(fetch_ref[...], back_ref[...])
    gate_grad = fetched[:, width : width + EXPERTS] + fetched[:, width + EXPERTS : width + 2 * EXPERTS]
    probs = probs_ref[...]
    mean_grad = jnp.sum(probs * gate_grad, axis=-1, keepdims=True)
    logit_grad = (probs * (gate_grad - mean_grad)).astype(bf16)
    logit_ref[...] = logit_grad
    normed_grad = fetched[:, :width] + product_nt(logit_grad, router_ref[...])
    hidden = hidden_ref[...]
    hidden_part, gain_grad = norm_back(hidden, inv_rms_of(hidden), gain_ref[...], normed_grad)
    gain_grad_ref[...] = gain_grad
    hidden_grad = cot_ref[...].astype(f32) + hidden_part
    hidden_grad_ref[...] = hidden_grad
    branch = (residual_scale * hidden_grad).astype(bf16)
    branch_ref[...] = branch
    for step, piece in enumerate((out0, out1, out2, out3)):
        attn_grad = product_nt(branch, piece[...]).astype(bf16)
        heads = KV_HEADS // 4
        for head in range(heads):
            columns = slice(head * 2 * HEAD_DIM, (head + 1) * 2 * HEAD_DIM)
            attn_grad_ref[(me_ref[0] ^ step) * heads + head] = attn_grad[:, columns]


def dense_grad_kernel(core_ref, rows_ref, branch_ref, normed_ref, logit_ref, gain_ref, keep_ref, away_ref):
    part, width = keep_ref.shape[1], branch_ref.shape[1]
    logit_grad = logit_ref[...].astype(f32)
    logit_grad = jnp.concatenate(
        [logit_grad, jnp.zeros((logit_grad.shape[0], 128 - EXPERTS), f32)], axis=1
    ).astype(bf16)
    column = lax.broadcasted_iota(jnp.int32, (part, 128), 1)
    for row in range(2):
        for ref, core in ((keep_ref, core_ref[0]), (away_ref, 1 - core_ref[0])):
            columns = pl.ds(pl.multiple_of((2 * row + core) * part, part), part)
            ref[row, :, :width] = product_tn(rows_ref[:, columns], branch_ref[...]).astype(bf16)
            router_grad = product_tn(normed_ref[:, columns], logit_grad)
            gain_grad = jnp.broadcast_to(gain_ref[:, columns], (128, part)).T
            ref[row, :, width:] = jnp.where(column == EXPERTS, gain_grad, router_grad).astype(bf16)


def expert_grad_kernel(core_ref, rows_ref, pre_grad_ref, inner_ref, route_grad_ref, keep_ref, away_ref):
    part = rows_ref.shape[1] // 4
    for row in range(2):
        for ref, core in ((keep_ref, core_ref[0]), (away_ref, 1 - core_ref[0])):
            place = 2 * row + core
            columns = pl.ds(pl.multiple_of(place * part, part), part)
            ref[row, :part, :] = product_tn(rows_ref[:, columns], pre_grad_ref[...]).astype(bf16)
            columns = pl.ds(pl.multiple_of(place * (part // 2), part // 2), part // 2)
            ref[row, part:, :] = product_tn(inner_ref[:, columns], route_grad_ref[...]).astype(bf16)


def dense_split_kernel(place_ref, row_ref, both_ref, other_ref, part0, part1, part2, part3):
    total = (both_ref[row_ref[0]].astype(f32) + other_ref[...].astype(f32)).astype(bf16)
    rows = part0.shape[0]
    for side in range(4):
        for step, ref in enumerate((part0, part1, part2, part3)):

            @pl.when(((place_ref[0] + step) & 3) == side)
            def _():
                ref[...] = total[side * rows : (side + 1) * rows]


def head_grad_kernel(
    dq_ref, dkv0, dkv1, dkv2, dkv3, cos_ref, sin_ref, dense0, dense1, dense2, dense3, out_ref, sent_ref
):
    dkv = dkv0[...].astype(f32) + dkv1[...].astype(f32) + dkv2[...].astype(f32) + dkv3[...].astype(f32)
    for side, grad in enumerate((dq_ref[...], dkv)):
        columns = slice(side * 2 * HEAD_DIM, (side + 1) * 2 * HEAD_DIM)
        out_ref[:, columns] = (grad * cos_ref[:, columns] - turned(grad) * sin_ref[:, columns]).astype(bf16)
    dense = dense0[...].astype(f32) + dense1[...].astype(f32) + dense2[...].astype(f32) + dense3[...].astype(f32)
    tokens = out_ref.shape[0] // KV_HEADS
    empty = jnp.zeros((8, 128), f32)
    for head in range(KV_HEADS):
        sent_ref[head, :tokens, :] = out_ref[head * tokens : (head + 1) * tokens, :]
        mine = dense[head * 8 : (head + 1) * 8]
        lines = [mine[:, side * 256 : (side + 1) * 256] for side in range(4)]
        lines.append(jnp.concatenate([mine[:, 1024:], empty], axis=1))
        lines.append(jnp.concatenate([empty, empty], axis=1))
        sent_ref[head, tokens:, :] = jnp.concatenate(lines, axis=0).astype(bf16)


def head_weight_kernel(core_ref, normed_ref, grads_ref, keep_ref, away_ref):
    part = keep_ref.shape[1]
    for row in range(2):
        for ref, core in ((keep_ref, core_ref[0]), (away_ref, 1 - core_ref[0])):
            columns = pl.ds(pl.multiple_of((2 * row + core) * part, part), part)
            ref[row] = product_tn(normed_ref[:, columns], grads_ref[...]).astype(bf16)


def input_grad_kernel(
    me_ref, grads_ref, w0, w1, w2, w3, x_ref, gain_ref, hidden_grad_ref,
    out_ref, gain0, gain1, gain2, gain3, dense_ref, all_ref,
):
    width = 4 * HEAD_DIM
    tokens = out_ref.shape[0]
    dense = jnp.zeros((grads_ref.shape[1] - tokens, width), f32)
    for head in range(KV_HEADS):
        dense += grads_ref[head, tokens:, :].astype(f32)
    lines = [dense[side * 8 : (side + 1) * 8] for side in range(4)] + [dense[32:40, :128]]
    dense_ref[...] = jnp.concatenate(lines, axis=1).astype(bf16)
    for step, piece in enumerate((w0, w1, w2, w3)):
        part = jnp.zeros((out_ref.shape[0], piece.shape[0]), f32)
        for head in range(KV_HEADS):
            part += product_nt(grads_ref[head, :tokens, :], piece[:, head * width : (head + 1) * width])
        out_ref[:, part_of(me_ref, step, piece.shape[0])] = part
    values = x_ref[...].astype(f32)
    part, gain_grad = norm_back(values, inv_rms_of(values), gain_ref[...], out_ref[...])
    out_ref[...] = hidden_grad_ref[...] + part
    all_ref[...] = gain_grad
    for step, ref in enumerate((gain0, gain1, gain2, gain3)):
        ref[...] = all_ref[:, part_of(me_ref, step, ref.shape[1])]


def pack_kernel(
    place_ref, w0, w1, w2, w3, gain0, gain1, gain2, gain3, dense0, dense1, dense2, dense3, out_ref, rows_ref
):
    total = w0[...].astype(f32) + w1[...].astype(f32) + w2[...].astype(f32) + w3[...].astype(f32)
    total = total.astype(bf16)
    gain = gain0[...] + gain1[...] + gain2[...] + gain3[...]
    high = gain.astype(bf16).astype(f32)
    rows, columns = total.shape[0] // 4, total.shape[1]
    row = lax.broadcasted_iota(jnp.int32, (rows, 128), 0)
    block = jnp.zeros((rows, 128), f32)
    for line, part in enumerate((high[:, :128], high[:, 128:], (gain - high)[:, :128], (gain - high)[:, 128:])):
        block = jnp.where(row == line, part, block)
    for step, part in enumerate((dense0, dense1, dense2, dense3)):
        rows_ref[pl.ds(pl.multiple_of(((place_ref[0] + 4 - step) & 3) * 8, 8), 8), :] = part[...].astype(f32)
    dense = rows_ref[...].astype(bf16)
    for head in range(KV_HEADS):
        for side in range(4):
            out_ref[head, :rows, side * columns : (side + 1) * columns] = total[side * rows : (side + 1) * rows]
        out_ref[head, :rows, 4 * columns :] = block.astype(bf16)
        out_ref[head, rows:, :] = dense


def spread_kernel(
    last_ref, query_ref, key_ref, value_ref, gain_ref, out_grad_ref, router_ref, gain2_ref, column_ref
):
    columns = 4 * HEAD_DIM
    rows = last_ref.shape[1] - 32
    gain_lines = jnp.zeros((rows, 128), f32)
    for head in range(0, KV_HEADS, 2):
        for side in range(4):
            place = slice(side * rows, (side + 1) * rows)
            parts = []
            for step in (0, 1):
                part = last_ref[head + step, :rows, side * columns : (side + 1) * columns].astype(f32)
                query_ref[place, (head + step) * 2 * HEAD_DIM : (head + step + 1) * 2 * HEAD_DIM] = part[:, : 2 * HEAD_DIM]
                parts.append(part)
            pair = slice(head * HEAD_DIM, (head + 2) * HEAD_DIM)
            key_ref[place, pair] = jnp.concatenate([p[:, 2 * HEAD_DIM : 3 * HEAD_DIM] for p in parts], axis=1)
            value_ref[place, pair] = jnp.concatenate([p[:, 3 * HEAD_DIM :] for p in parts], axis=1)
    for head in range(KV_HEADS):
        gain_lines += last_ref[head, :rows, 4 * columns :].astype(f32)
        dense = last_ref[head, rows:, :].astype(f32)
        for place in range(4):
            part = dense[place * 8 : (place + 1) * 8]
            target = slice((place * KV_HEADS + head) * 8, (place * KV_HEADS + head + 1) * 8)
            out_grad_ref[target, :] = part[:, : 4 * columns]
            router_ref[target, :] = part[:, 4 * columns : 4 * columns + EXPERTS]
            column_ref[target, :] = part[:, 4 * columns :]
    gain_ref[:, :128] = gain_lines[0:1] + gain_lines[2:3]
    gain_ref[:, 128:] = gain_lines[1:2] + gain_lines[3:4]
    gain2_ref[...] = column_ref[...].T[EXPERTS : EXPERTS + 1, :]


def gate_of(rows, mask, router_w):
    logits = jnp.where(mask > 0, product(rows, router_w), masked_value)
    exps = jnp.where(mask > 0, jnp.exp(logits - jnp.max(logits, axis=-1, keepdims=True)), 0.0)
    return exps / jnp.maximum(jnp.sum(exps, axis=-1, keepdims=True), 1e-30)


def run_experts(expert, me, rows, marked, pieces, router_w):
    count, width = rows.shape
    part = pieces[0].shape[0] // 3
    units = 4 * part
    tile = 256

    def tiled(columns):
        return pl.BlockSpec((tile, columns), lambda i: (i, 0))

    def whole(array):
        return pl.BlockSpec(array.shape, lambda i: (0, 0))

    columns = (width, width + 128, 2 * units, units, width)
    return pl.pallas_call(
        expert_kernel,
        grid=(count // tile,),
        out_shape=tuple(jax.ShapeDtypeStruct((count, c), bf16) for c in columns),
        in_specs=[SMEM, SMEM, tiled(width), tiled(width + 128)] + [whole(p) for p in pieces] + [whole(router_w)],
        out_specs=tuple(tiled(c) for c in columns),
        scratch_shapes=[pltpu.VMEM((8 * part, 2 * units), bf16), pltpu.VMEM((units, width), bf16)],
        compiler_params=pltpu.CompilerParams(vmem_limit_bytes=56 * 1024 * 1024),
        cost_estimate=pl.CostEstimate(flops=10_000_000_000, bytes_accessed=22_000_000, transcendentals=1_000_000),
    )(expert.astype(jnp.int32).reshape(1), me, rows, marked, *pieces, router_w)


SMEM = pl.BlockSpec(memory_space=pltpu.SMEM)


def whole_block(shape):
    return pl.BlockSpec(tuple(shape), lambda i: (0,) * len(shape))


def attend(numbers, queries, kv_parts):
    rows = queries.shape[0]
    keys = rows * len(kv_parts)
    pairs = rows // (2 * HALF)
    outs = (
        jax.ShapeDtypeStruct((rows, 2 * HEAD_DIM), bf16),
        jax.ShapeDtypeStruct((pairs, HEAD_DIM, 4 * HALF), f32),
        jax.ShapeDtypeStruct((pairs, 1, 4 * HALF), f32),
    )
    return pl.pallas_call(
        attend_kernel,
        grid=(1,),
        out_shape=outs,
        in_specs=[SMEM] * 3 + [whole_block(array.shape) for array in (queries, *kv_parts)],
        out_specs=tuple(whole_block(out.shape) for out in outs),
        scratch_shapes=[pltpu.VMEM((keys, 2 * HEAD_DIM), bf16), pltpu.VMEM((2 * HEAD_DIM, keys), bf16)],
        compiler_params=pltpu.CompilerParams(vmem_limit_bytes=40 * 1024 * 1024),
        cost_estimate=pl.CostEstimate(flops=12_000_000_000, bytes_accessed=4_000_000, transcendentals=5_000_000),
    )(*numbers, queries, *kv_parts)


def attend_grad(numbers, queries, kv_parts, grads, turned, lse):
    rows = queries.shape[0]
    keys = rows * len(kv_parts)
    outs = (jax.ShapeDtypeStruct((rows, 2 * HEAD_DIM), f32),)
    outs += (jax.ShapeDtypeStruct((rows, 2 * HEAD_DIM), bf16),) * 4
    return pl.pallas_call(
        attend_grad_kernel,
        grid=(1,),
        out_shape=outs,
        in_specs=[SMEM] * 3 + [whole_block(array.shape) for array in (queries, *kv_parts, grads, turned, lse)],
        out_specs=tuple(whole_block(out.shape) for out in outs),
        scratch_shapes=[
            pltpu.VMEM((keys, 2 * HEAD_DIM), bf16),
            pltpu.VMEM((2 * HEAD_DIM, keys), bf16),
            pltpu.VMEM((keys, 2 * HEAD_DIM), f32),
        ],
        compiler_params=pltpu.CompilerParams(vmem_limit_bytes=40 * 1024 * 1024),
        cost_estimate=pl.CostEstimate(flops=30_000_000_000, bytes_accessed=6_000_000, transcendentals=5_000_000),
    )(*numbers, queries, *kv_parts, grads, turned, lse)


def block_numbers(block_pairs):
    place = lax.axis_index("x")
    groups = block_pairs.reshape(4, 8)
    groups = groups[(place - jnp.arange(4)) & 3]
    numbers = jnp.stack([groups, 63 - groups], axis=-1).reshape(-1)
    own = numbers[:16]
    rank = jnp.sum((own[None, :] < own[:, None]).astype(jnp.int32), axis=1)
    spots = jnp.arange(16, dtype=jnp.int32)
    order = jnp.sum(jnp.where(rank[None, :] == spots[:, None], spots[None, :], 0), axis=1)
    return (order, own, numbers)


def on_device(
    block_input,
    routes,
    block_pairs,
    norm1_gain,
    w_query,
    w_key,
    w_value,
    w_out,
    norm2_gain,
    w_router,
    w_gate,
    w_up,
    w_down,
    cotangent,
):
    tokens, width = block_input.shape[1:]
    head = lax.axis_index(ZY)
    expert = lax.axis_index(CTX)
    shard_rows = w_query.shape[0]
    own_input = block_input[0]

    core = lax.axis_index("core").astype(jnp.int32).reshape(1)
    place = lax.axis_index("x").astype(jnp.int32).reshape(1)
    me = lax.axis_index(("yl", "core")).astype(jnp.int32).reshape(1)
    small_shard, by_head = call(
        shard_kernel,
        [((shard_rows + EXPERTS + 16, 4 * HEAD_DIM), bf16), ((shard_rows, KV_HEADS * 4 * HEAD_DIM), bf16)],
        (
            head.astype(jnp.int32).reshape(1), w_query, w_key, w_value, w_router,
            norm1_gain.reshape(1, -1), norm2_gain.reshape(1, -1),
        ),
        1_000_000,
        scalars=1,
    )
    small_pieces = pieces_direct(small_shard)
    (copies,) = call(copies_kernel, [((KV_HEADS, tokens, width), bf16)], (own_input,), 1_000_000)
    group_input = exchange(copies.reshape(-1, width), ZY)
    head_w, router_w, gain_one, gain_two = call(
        small_kernel,
        [((width, 4 * HEAD_DIM), bf16), ((width, EXPERTS), bf16), ((1, width), f32), ((1, width), f32)],
        (me, *small_pieces),
        1_000_000,
        scalars=1,
    )

    numbers = block_numbers(block_pairs)
    group_pos = (numbers[1][:, None] * HALF + jnp.arange(HALF, dtype=jnp.int32)[None, :]).reshape(-1)
    cosine, sine = rope_tables(group_pos)

    chosen = routes[0]
    uses = jnp.sum(
        (chosen[:, :, None] == jnp.arange(EXPERTS, dtype=jnp.int32)[None, None, :]).astype(f32), axis=1
    )
    earlier = jnp.tril(jnp.ones((tokens, tokens), bf16), -1)
    rank = product(earlier, uses.astype(bf16)).astype(jnp.int32)
    rank = jnp.where(uses > 0, rank, -1)
    slot = jnp.arange(CAP, dtype=jnp.int32)
    send = (rank.T[:, None, :] == slot[None, :, None]).astype(bf16).reshape(EXPERTS * CAP, tokens)
    fetch = (rank[:, :, None] == slot[None, None, :]).astype(bf16).reshape(tokens, EXPERTS * CAP)

    group_normed, queries, kv_own = project(group_input, head_w, gain_one, cosine, sine)
    kv_parts = [kv_own] + [turn(kv_own, "x", step) for step in (1, 2, 3)]

    out_other = swap(w_out, "yl")
    expert_shard = jnp.concatenate([jnp.concatenate([w_gate[0], w_up[0]], axis=1), w_down[0]], axis=0)
    expert_other = swap(expert_shard, "yl")
    marked = jnp.concatenate(
        [cotangent[0], uses.astype(bf16), jnp.zeros((tokens, 128 - EXPERTS), bf16)], axis=1
    )
    (marked_sent,) = call(
        send_kernel,
        [((EXPERTS * CAP, width + 128), bf16)],
        (send, marked),
        500_000_000,
        held=(*kv_parts[1:], out_other, expert_other),
    )
    marked_arrived = exchange(marked_sent, CTX)

    attn_group, attn_turned, lse = attend(numbers, queries, kv_parts)

    out_pieces = pieces_by_row(w_out, out_other)

    attn_back = exchange(tie(attn_group, marked_arrived), ZY)
    expert_pieces = pieces_by_row(expert_shard, expert_other)
    attn_rows, hidden, normed2, gate_probs, outgoing = call(
        middle_kernel,
        [
            ((tokens, HEADS * HEAD_DIM), bf16),
            ((tokens, width), f32),
            ((tokens, width), bf16),
            ((tokens, EXPERTS), f32),
            ((EXPERTS * CAP, width), bf16),
        ],
        (
            me, attn_back.reshape(KV_HEADS, tokens, 2 * HEAD_DIM), *out_pieces, own_input, gain_two, router_w,
            uses, send,
        ),
        800_000_000,
        held=expert_pieces,
        scalars=1,
    )
    arrived = exchange(outgoing, CTX)

    expert_out, in_grad, pre_grad, inner_act, route_grad = run_experts(
        expert, me, arrived, marked_arrived, expert_pieces, router_w
    )
    back = exchange(in_grad, CTX)
    by_head_sent = tie(by_head, normed2)
    head_pieces = pieces_by_row(by_head_sent, swap(by_head_sent, "yl"))
    expert_shape = ((2, *expert_shard.shape), bf16)
    expert_both = join_core(
        *call(
            expert_grad_kernel,
            [expert_shape, expert_shape],
            (core, arrived, pre_grad, inner_act, route_grad),
            5_000_000_000,
            held=(head_pieces[2],),
            scalars=1,
        )
    )

    hidden_grad, branch_grad, logit_grad, gain_two_grad, attn_grad = call(
        token_grad_kernel,
        [
            ((tokens, width), f32),
            ((tokens, width), bf16),
            ((tokens, EXPERTS), bf16),
            ((1, width), f32),
            ((KV_HEADS, tokens, 2 * HEAD_DIM), bf16),
        ],
        (me, fetch, back, gate_probs, router_w, hidden, gain_two, cotangent[0], *out_pieces),
        800_000_000,
        held=(expert_both, *head_pieces),
        scalars=1,
    )

    group_grad = exchange(attn_grad.reshape(KV_HEADS * tokens, 2 * HEAD_DIM), ZY)
    dq, *dkv_parts = attend_grad(numbers, queries, kv_parts, group_grad, attn_turned, lse)
    dkv_turned = [turn(dkv_parts[step], "x", -step) for step in (1, 2, 3)]
    dense_shape = ((2, shard_rows, width + 128), bf16)
    dense_both = join_core(
        *call(
            dense_grad_kernel,
            [dense_shape, dense_shape],
            (core, attn_rows, branch_grad, normed2, logit_grad, gain_two_grad),
            400_000_000,
            scalars=1,
        )
    )
    row = lax.axis_index("yl").astype(jnp.int32).reshape(1)
    dense_other = swap(lax.dynamic_index_in_dim(dense_both, 1 - row[0], 0, keepdims=False), "yl")
    dense_parts = call(
        dense_split_kernel,
        [((shard_rows // 4, width + 128), bf16)] * 4,
        (place, row, dense_both, dense_other),
        1_000_000,
        held=(dq,),
        scalars=2,
    )
    dense_turned = [turn(dense_parts[step], "x", step) for step in (1, 2, 3)]

    grads, grads_sent = call(
        head_grad_kernel,
        [((KV_HEADS * tokens, 4 * HEAD_DIM), bf16), ((KV_HEADS, tokens + 48, 4 * HEAD_DIM), bf16)],
        (dq, dkv_parts[0], *dkv_turned, cosine, sine, dense_parts[0], *dense_turned),
        100_000_000,
    )
    token_grads = exchange(grads_sent.reshape(-1, 4 * HEAD_DIM), ZY)
    head_shape = ((2, shard_rows, 4 * HEAD_DIM), bf16)
    head_both = join_core(
        *call(head_weight_kernel, [head_shape, head_shape], (core, group_normed, grads), 600_000_000, scalars=1)
    )
    head_parts = all_x(scatter_row(head_both).astype(bf16))

    returned = exchange(tie(expert_out, token_grads, head_both), CTX)


    gain_shape = ((1, shard_rows), f32)
    input_grad, *gain_parts, dense = call(
        input_grad_kernel,
        [((tokens, width), f32)] + [gain_shape] * 4 + [((8, width + 128), bf16)],
        (
            me, token_grads.reshape(grads_sent.shape), *head_pieces, own_input, gain_one, hidden_grad,
        ),
        600_000_000,
        scalars=1,
        scratch=[(1, width)],
    )
    expert_sums = scatter_row(tie(expert_both, gain_parts[0]))
    gain_sum = gain_parts[0]
    for step in (1, 2, 3):
        gain_sum = gain_sum + lax.ppermute(gain_parts[step], ("yl", "core"), [(i, i ^ step) for i in range(4)])

    (last,) = call(
        pack_kernel,
        [((KV_HEADS, shard_rows // 4 + 32, width + 128), bf16)],
        (place, *head_parts, *all_x(gain_sum), *all_x(dense)),
        1_000_000,
        held=(returned, expert_sums),
        scalars=1,
        scratch=[(32, width + 128)],
    )
    last = exchange(last.reshape(-1, width + 128), ZY).reshape(last.shape)
    grad_query, grad_key, grad_value, gain_one_grad, grad_out, grad_router, gain_two_grad = call(
        spread_kernel,
        [
            ((shard_rows, HEADS * HEAD_DIM), f32),
            ((shard_rows, KV_HEADS * HEAD_DIM), f32),
            ((shard_rows, KV_HEADS * HEAD_DIM), f32),
            gain_shape,
            ((shard_rows, width), f32),
            ((shard_rows, EXPERTS), f32),
            gain_shape,
        ],
        (last,),
        1_000_000,
        scratch=[(shard_rows, 128)],
    )

    spread = gate_probs[:, :, None] * fetch.astype(f32).reshape(tokens, EXPERTS, CAP)
    weights = spread.reshape(tokens, EXPERTS * CAP)
    weights_hi = weights.astype(bf16)
    weights_lo = (weights - weights_hi.astype(f32)).astype(bf16)
    mixture = product(weights_hi, returned) + product(weights_lo, returned)
    output = hidden + residual_scale * mixture

    return (
        output.astype(bf16)[None],
        input_grad[None],
        gain_one_grad.reshape(-1),
        grad_query,
        grad_key,
        grad_value,
        grad_out,
        gain_two_grad.reshape(-1),
        grad_router,
        expert_sums[None, :shard_rows, : width // 2],
        expert_sums[None, :shard_rows, width // 2 :],
        expert_sums[None, shard_rows:],
    )


def solution(mesh):
    fine = Mesh(mesh.devices.reshape(4, 4, 2, 2, 2), EVERY)
    rows, shards = P(("yl", "core"), CTX, None), P(("yl", "core"), None)
    gain, experts = P(("yl", "core")), P(CTX, ("yl", "core"), None)
    return jax.shard_map(
        on_device,
        mesh=fine,
        in_specs=(
            rows, rows, P(), gain, shards, shards, shards, shards, gain, shards, experts, experts, experts, rows,
        ),
        out_specs=(
            rows, rows, gain, shards, shards, shards, shards, gain, shards, experts, experts, experts,
        ),
        check_vma=False,
    )
```

```python
import functools

import jax
import jax.numpy as jnp
from jax import lax
from jax.experimental import pallas as pl
from jax.experimental.layout import Layout, with_layout_constraint
from jax.experimental.pallas import tpu as pltpu
from jax.sharding import Mesh
from jax.sharding import PartitionSpec as P

HEADS = 16
KV_HEADS = 8
HEAD_DIM = 64
EXPERTS = 32
TOP = 8
CAP = 48
HALF = 64
TILE = 512

epsilon = 1e-06
attn_scale = 0.015625
residual_scale = 0.22
masked_value = -1e30

CTX = ("x", "z", "yh")
ZY = ("z", "yh")
EVERY = ("x", "z", "yh", "yl", "core")
bf16 = jnp.bfloat16
f32 = jnp.float32


def product(left, right):
    return jnp.dot(left, right, preferred_element_type=f32)


def product_nt(left, right):
    return lax.dot_general(left, right, (((1,), (1,)), ((), ())), preferred_element_type=f32)


def product_tn(left, right):
    return lax.dot_general(left, right, (((0,), (0,)), ((), ())), preferred_element_type=f32)


def swap(values, axis):
    return lax.ppermute(values, axis, [(0, 1), (1, 0)])


def turn(values, axis, step):
    return lax.ppermute(values, axis, [(i, (i + step) % 4) for i in range(4)])


def rows_first(values):
    return with_layout_constraint(values, Layout(major_to_minor=tuple(range(values.ndim))))


def exchange(values, axes):
    return rows_first(lax.all_to_all(rows_first(values), axes, 0, 0, tiled=True))


def tie(values, *others):
    if values.size <= 1024:
        return values + sum(other[(0,) * other.ndim].astype(f32) * 0.0 for other in others).astype(values.dtype)
    corner = tuple(slice(0, min(size, 8 if axis < values.ndim - 1 else 128)) for axis, size in enumerate(values.shape))
    nothing = sum(other[(0,) * other.ndim].astype(f32) * 0.0 for other in others)
    held = values[corner] + nothing.astype(values.dtype)
    return lax.dynamic_update_slice(values, held, (0,) * values.ndim)


def pieces_direct(shard):
    steps = [lax.ppermute(shard, ("yl", "core"), [(i, i ^ k) for i in range(4)]) for k in (1, 2, 3)]
    return (shard, *steps)


def pieces_by_row(shard, other):
    return (shard, swap(shard, "core"), other, swap(other, "core"))


def scatter_core(parts):
    core = lax.axis_index("core")
    parts = parts.astype(bf16).reshape((2, 2) + parts.shape[1:])
    away = lax.dynamic_index_in_dim(parts, 1 - core, 1, keepdims=False)
    keep = lax.dynamic_index_in_dim(parts, core, 1, keepdims=False)
    return (keep.astype(f32) + swap(away, "core").astype(f32)).astype(bf16)


def join_core(keep, away):
    return (keep.astype(f32) + swap(away, "core").astype(f32)).astype(bf16)


def scatter_row(both):
    row = lax.axis_index("yl")
    away = lax.dynamic_index_in_dim(both, 1 - row, 0, keepdims=False)
    keep = lax.dynamic_index_in_dim(both, row, 0, keepdims=False)
    return keep.astype(f32) + swap(away, "yl").astype(f32)


def scatter_fsdp(parts):
    return scatter_row(scatter_core(parts))


def all_x(part):
    return [part] + [turn(part, "x", step) for step in (1, 2, 3)]


def rope_tables(positions):
    freqs = jnp.power(10000.0, -jnp.arange(0, HEAD_DIM, 2, dtype=f32) / HEAD_DIM)
    angles = positions.astype(f32)[:, None] * freqs[None, :]
    cosine, sine = jnp.cos(angles), jnp.sin(angles)
    ones, zeros = jnp.ones_like(cosine), jnp.zeros_like(cosine)
    return (
        jnp.concatenate([cosine] * 6 + [ones] * 2, axis=1),
        jnp.concatenate([-sine, sine] * 3 + [zeros] * 2, axis=1),
    )


def turned(values):
    width = values.shape[1]
    column = lax.broadcasted_iota(jnp.int32, values.shape, 1)
    return jnp.where(
        column % HEAD_DIM < HEAD_DIM // 2,
        pltpu.roll(values, width - HEAD_DIM // 2, 1),
        pltpu.roll(values, HEAD_DIM // 2, 1),
    )


def norm_back(values, inv_rms, gain, grad):
    weighted = grad * gain
    gain_grad = jnp.sum(grad * values * inv_rms, axis=0, keepdims=True)
    inner_mean = jnp.mean(weighted * values, axis=-1, keepdims=True)
    return (weighted * inv_rms - values * inv_rms * inv_rms * inv_rms * inner_mean, gain_grad)


def inv_rms_of(values):
    return lax.rsqrt(jnp.mean(values * values, axis=-1, keepdims=True) + epsilon)


def half(index):
    return pl.ds(pl.multiple_of(index * HALF, HALF), HALF)


def key_tile(counter):
    return pl.ds(pl.multiple_of(counter * TILE, TILE), TILE)


def sort_keys(knum_ref, kv_refs, kvs, kvt):
    blocks = kv_refs[0].shape[0] // HALF
    for slot, kv_ref in enumerate(kv_refs):
        for block in range(blocks):
            kvs[half(knum_ref[slot * blocks + block]), :] = kv_ref[block * HALF : (block + 1) * HALF, :]
    for tile in range(kvs.shape[0] // TILE):
        part = kvs[tile * TILE : (tile + 1) * TILE, :].astype(f32)
        kvt[:, tile * TILE : (tile + 1) * TILE] = part.T.astype(bf16)


def pair_rows(ref, first, second, upper):
    rows = []
    for block in (first, second):
        values = ref[half(block), :].astype(f32)
        column = lax.broadcasted_iota(jnp.int32, values.shape, 1)
        inside = (column >= HEAD_DIM) if upper else (column < HEAD_DIM)
        moved = pltpu.roll(values, HEAD_DIM, 1)
        heads = (moved, values) if upper else (values, moved)
        rows += [jnp.where(inside, head, 0.0) for head in heads]
    return jnp.concatenate(rows, axis=0)


def pair_positions(low_number, high_number):
    column = lax.broadcasted_iota(jnp.int32, (1, 4 * HALF), 1)
    return jnp.where(column < 2 * HALF, low_number, high_number) * HALF + column % HALF


def score_tile(keys, queries, counter, positions, masked):
    scores = product_nt(keys, queries)
    if masked:
        key_pos = counter * TILE + lax.broadcasted_iota(jnp.int32, scores.shape, 0)
        scores = jnp.where(key_pos <= positions, scores, masked_value)
    return scores


def store_rows(ref, turned, first, second):
    rows = turned.T
    ref[half(first), :] = jnp.concatenate([rows[:HALF], rows[HALF : 2 * HALF]], axis=1).astype(ref.dtype)
    ref[half(second), :] = jnp.concatenate([rows[2 * HALF : 3 * HALF], rows[3 * HALF :]], axis=1).astype(ref.dtype)


def attend_kernel(
    order_ref, qnum_ref, knum_ref, q_ref, kv0, kv1, kv2, kv3, out_ref, turned_ref, lse_ref, kvs, kvt
):
    sort_keys(knum_ref, (kv0, kv1, kv2, kv3), kvs, kvt)
    width = 4 * HALF

    @pl.loop(0, q_ref.shape[0] // (2 * HALF))
    def _(pair):
        first, second = order_ref[2 * pair], order_ref[2 * pair + 1]
        low_number, high_number = qnum_ref[first], qnum_ref[second]
        queries = pair_rows(q_ref, first, second, False).astype(bf16)
        positions = pair_positions(low_number, high_number)

        def step(masked, counter, running):
            top, total, mixed = running
            scores = score_tile(kvs[key_tile(counter), :], queries, counter, positions, masked)
            new_top = jnp.maximum(top, jnp.max(scores, axis=0, keepdims=True))
            probs = jnp.exp(scores - new_top)
            shrink = jnp.exp(top - new_top)
            total = total * shrink + jnp.sum(probs, axis=0, keepdims=True)
            mixed = mixed * shrink + product(kvt[HEAD_DIM:, key_tile(counter)], probs.astype(bf16))
            return (new_top, total, mixed)

        start = (
            jnp.full((1, width), masked_value, f32),
            jnp.zeros((1, width), f32),
            jnp.zeros((HEAD_DIM, width), f32),
        )
        full = (low_number * HALF) // TILE
        last = (high_number * HALF) // TILE + 1
        running = lax.fori_loop(0, full, functools.partial(step, False), start)
        top, total, mixed = lax.fori_loop(full, last, functools.partial(step, True), running)
        mixed = mixed / total
        turned_ref[pair] = mixed
        lse_ref[pair] = top + jnp.log(total)
        store_rows(out_ref, mixed, first, second)


def attend_grad_kernel(
    order_ref, qnum_ref, knum_ref, q_ref, kv0, kv1, kv2, kv3, grad_ref, turned_ref, lse_ref,
    dq_ref, dkv0, dkv1, dkv2, dkv3, kvs, kvt, total_ref,
):
    sort_keys(knum_ref, (kv0, kv1, kv2, kv3), kvs, kvt)
    total_ref[...] = jnp.zeros_like(total_ref)
    width = 4 * HALF

    @pl.loop(0, q_ref.shape[0] // (2 * HALF))
    def _(pair):
        first, second = order_ref[2 * pair], order_ref[2 * pair + 1]
        low_number, high_number = qnum_ref[first], qnum_ref[second]
        queries = pair_rows(q_ref, first, second, False).astype(bf16)
        grads_f = pair_rows(grad_ref, first, second, True)
        grads = grads_f.astype(bf16)
        both = jnp.concatenate([queries, grads], axis=0)
        positions = pair_positions(low_number, high_number)
        lse = lse_ref[pair]
        dots = jnp.sum(grads_f.T[HEAD_DIM:] * turned_ref[pair], axis=0, keepdims=True)

        def step(masked, counter, query_acc):
            keys = kvs[key_tile(counter), :]
            probs = jnp.exp(score_tile(keys, queries, counter, positions, masked) - lse)
            score_grad = (probs * (product_nt(keys, grads) - dots)).astype(bf16)
            sides = jnp.concatenate([score_grad, probs.astype(bf16)], axis=1)
            total_ref[key_tile(counter), :] += product(sides, both)
            return query_acc + product(kvt[:HEAD_DIM, key_tile(counter)], score_grad)

        full = (low_number * HALF) // TILE
        last = (high_number * HALF) // TILE + 1
        query_acc = lax.fori_loop(0, full, functools.partial(step, False), jnp.zeros((HEAD_DIM, width), f32))
        query_acc = lax.fori_loop(full, last, functools.partial(step, True), query_acc)
        store_rows(dq_ref, query_acc * attn_scale, first, second)

    blocks = dkv0.shape[0] // HALF
    for slot, dkv in enumerate((dkv0, dkv1, dkv2, dkv3)):
        for block in range(blocks):
            dkv[block * HALF : (block + 1) * HALF, :] = total_ref[
                half(knum_ref[slot * blocks + block]), :
            ].astype(bf16)


def expert_kernel(
    expert_ref, me_ref, rows_ref, marked_ref, piece0, piece1, piece2, piece3, router_ref,
    out_ref, in_grad_ref, pre_grad_ref, inner_ref, route_grad_ref, gu_ref, down_ref,
):
    @pl.when(pl.program_id(0) == 0)
    def _():
        part = gu_ref.shape[0] // 4
        for step, piece in enumerate((piece0, piece1, piece2, piece3)):
            place = me_ref[0] ^ step
            gu_ref[pl.ds(pl.multiple_of(place * part, part), part), :] = piece[:part, :]
            down_ref[pl.ds(pl.multiple_of(place * (part // 2), part // 2), part // 2), :] = piece[part:, :]

    rows = rows_ref[...]
    width = rows.shape[1]
    units = down_ref.shape[0]
    pre = product(rows, gu_ref[...])
    gate_pre, up_pre = pre[:, :units], pre[:, units:]
    sigmoid_a = 1.0 / (1.0 + jnp.exp(-gate_pre))
    swish_act = gate_pre * sigmoid_a
    inner_act = (swish_act * up_pre).astype(bf16)
    inner_ref[...] = inner_act
    expert_out = product(inner_act, down_ref[...]).astype(bf16)
    out_ref[...] = expert_out
    uses = marked_ref[:, width : width + EXPERTS].astype(f32)
    probs = gate_of(rows, uses, router_ref[...])
    column = lax.broadcasted_iota(jnp.int32, probs.shape, 1)
    slot_probs = jnp.sum(jnp.where(column == expert_ref[0], probs, 0.0), axis=1, keepdims=True)
    mix_grad = residual_scale * marked_ref[:, :width].astype(f32)
    gate_grad = jnp.sum(mix_grad * expert_out.astype(f32), axis=1, keepdims=True)
    route_grad = (slot_probs * mix_grad).astype(bf16)
    route_grad_ref[...] = route_grad
    inner_grad = product_nt(route_grad, down_ref[...])
    pre_grad_ref[:, :units] = (
        inner_grad * up_pre * sigmoid_a * (1.0 + gate_pre * (1.0 - sigmoid_a))
    ).astype(bf16)
    pre_grad_ref[:, units:] = (inner_grad * swish_act).astype(bf16)
    in_grad_ref[:, :width] = product_nt(pre_grad_ref[...], gu_ref[...]).astype(bf16)
    column = lax.broadcasted_iota(jnp.int32, (rows.shape[0], 128), 1)
    high = gate_grad.astype(bf16).astype(f32)
    in_grad_ref[:, width:] = jnp.where(
        column == expert_ref[0], high, jnp.where(column == EXPERTS + expert_ref[0], gate_grad - high, 0.0)
    ).astype(bf16)


def project_kernel(x_ref, w_ref, gain_ref, cos_ref, sin_ref, normed_ref, q_ref, kv_ref):
    values = x_ref[...].astype(f32)
    normed = (values * inv_rms_of(values) * gain_ref[...]).astype(bf16)
    normed_ref[...] = normed
    projected = product(normed, w_ref[...])
    rotated = projected * cos_ref[...] + turned(projected) * sin_ref[...]
    q_ref[...] = rotated[:, : 2 * HEAD_DIM].astype(bf16) * bf16(attn_scale)
    kv_ref[...] = rotated[:, 2 * HEAD_DIM :].astype(bf16)


def project(rows, head_w, gain, cosine, sine):
    count, width = rows.shape
    tile = 256

    def tiled(columns):
        return pl.BlockSpec((tile, columns), lambda i: (i, 0))

    def whole(array):
        return pl.BlockSpec(array.shape, lambda i: (0, 0))

    columns = (width, 2 * HEAD_DIM, 2 * HEAD_DIM)
    return pl.pallas_call(
        project_kernel,
        grid=(count // tile,),
        out_shape=tuple(jax.ShapeDtypeStruct((count, c), bf16) for c in columns),
        in_specs=[tiled(width), whole(head_w), whole(gain), tiled(4 * HEAD_DIM), tiled(4 * HEAD_DIM)],
        out_specs=tuple(tiled(c) for c in columns),
        compiler_params=pltpu.CompilerParams(vmem_limit_bytes=32 * 1024 * 1024),
        cost_estimate=pl.CostEstimate(flops=600_000_000, bytes_accessed=8_000_000, transcendentals=0),
    )(rows, head_w, gain, cosine, sine)


def call(kernel, outs, operands, flops, held=(), scalars=0, scratch=()):
    count = len(operands)

    def body(*refs):
        kernel(*refs[:count], *refs[count + len(held) :])

    return pl.pallas_call(
        body,
        grid=(1,),
        out_shape=tuple(jax.ShapeDtypeStruct(shape, dtype) for shape, dtype in outs),
        in_specs=[SMEM] * scalars
        + [whole_block(array.shape) for array in operands[scalars:]]
        + [pl.BlockSpec(memory_space=pl.ANY)] * len(held),
        out_specs=tuple(whole_block(shape) for shape, _ in outs),
        scratch_shapes=[pltpu.VMEM(shape, f32) for shape in scratch],
        compiler_params=pltpu.CompilerParams(vmem_limit_bytes=48 * 1024 * 1024),
        cost_estimate=pl.CostEstimate(flops=flops, bytes_accessed=8_000_000, transcendentals=0),
    )(*operands, *held)


def part_of(me_ref, step, part):
    return pl.ds(pl.multiple_of((me_ref[0] ^ step) * part, part), part)


def copies_kernel(x_ref, copies_ref):
    for copy in range(KV_HEADS):
        copies_ref[copy] = x_ref[...]


def shard_kernel(
    head_ref, query_ref, key_ref, value_ref, router_ref, gain1_ref, gain2_ref, out_ref, by_head_ref
):
    rows = query_ref.shape[0]
    lower = lax.broadcasted_iota(jnp.int32, (rows, 128), 1) < HEAD_DIM
    for head in range(KV_HEADS):
        pair = slice(head // 2 * 128, (head // 2 + 1) * 128)
        keys, values = key_ref[:, pair].astype(f32), value_ref[:, pair].astype(f32)
        if head % 2:
            keys = pltpu.roll(keys, HEAD_DIM, 1)
        else:
            values = pltpu.roll(values, HEAD_DIM, 1)
        by_head_ref[:, head * 256 : head * 256 + 128] = query_ref[:, head * 128 : (head + 1) * 128]
        by_head_ref[:, head * 256 + 128 : (head + 1) * 256] = jnp.where(lower, keys, values).astype(bf16)
    out_ref[:rows, :] = by_head_ref[:, pl.ds(pl.multiple_of(head_ref[0] * 256, 256), 256)]
    router = jnp.concatenate([router_ref[...].astype(f32), jnp.zeros((rows, 128 - EXPERTS), f32)], axis=1)
    out_ref[rows : rows + EXPERTS, :] = router.T[:EXPERTS].astype(bf16)
    row = lax.broadcasted_iota(jnp.int32, (16, rows), 0)
    gains = jnp.where(row == 0, gain1_ref[...].astype(f32), jnp.where(row == 1, gain2_ref[...].astype(f32), 0.0))
    out_ref[rows + EXPERTS :, :] = gains.astype(bf16)


def small_kernel(me_ref, piece0, piece1, piece2, piece3, head_w_ref, router_ref, gain1_ref, gain2_ref):
    rows = head_w_ref.shape[0] // 4
    for step, piece in enumerate((piece0, piece1, piece2, piece3)):
        place = part_of(me_ref, step, rows)
        head_w_ref[place, :] = piece[:rows, :]
        router = piece[rows : rows + EXPERTS, :].astype(f32)
        router = jnp.concatenate([router, jnp.zeros((128 - EXPERTS, rows), f32)], axis=0)
        router_ref[place, :] = router.T[:, :EXPERTS].astype(bf16)
        gains = piece[rows + EXPERTS :, :].astype(f32)
        gain1_ref[:, place] = gains[0:1]
        gain2_ref[:, place] = gains[1:2]


def send_kernel(send_ref, rows_ref, out_ref):
    out_ref[...] = product(send_ref[...], rows_ref[...]).astype(bf16)


def middle_kernel(
    me_ref, attn_ref, out0, out1, out2, out3, x_ref, gain_ref, router_ref, uses_ref, send_ref,
    rows_ref, hidden_ref, normed_ref, probs_ref, out_ref,
):
    for head in range(KV_HEADS):
        rows_ref[:, head * 2 * HEAD_DIM : (head + 1) * 2 * HEAD_DIM] = attn_ref[head]
    branch = jnp.zeros(hidden_ref.shape, f32)
    for step, piece in enumerate((out0, out1, out2, out3)):
        branch += product(rows_ref[:, part_of(me_ref, step, piece.shape[0])], piece[...])
    hidden = x_ref[...].astype(f32) + residual_scale * branch
    hidden_ref[...] = hidden
    normed = (hidden * inv_rms_of(hidden) * gain_ref[...]).astype(bf16)
    normed_ref[...] = normed
    out_ref[...] = product(send_ref[...], normed).astype(bf16)
    probs_ref[...] = gate_of(normed, uses_ref[...], router_ref[...])


def token_grad_kernel(
    me_ref, fetch_ref, back_ref, probs_ref, router_ref, hidden_ref, gain_ref, cot_ref, out0, out1, out2, out3,
    hidden_grad_ref, branch_ref, logit_ref, gain_grad_ref, attn_grad_ref,
):
    width = hidden_ref.shape[1]
    fetched = product(fetch_ref[...], back_ref[...])
    gate_grad = fetched[:, width : width + EXPERTS] + fetched[:, width + EXPERTS : width + 2 * EXPERTS]
    probs = probs_ref[...]
    mean_grad = jnp.sum(probs * gate_grad, axis=-1, keepdims=True)
    logit_grad = (probs * (gate_grad - mean_grad)).astype(bf16)
    logit_ref[...] = logit_grad
    normed_grad = fetched[:, :width] + product_nt(logit_grad, router_ref[...])
    hidden = hidden_ref[...]
    hidden_part, gain_grad = norm_back(hidden, inv_rms_of(hidden), gain_ref[...], normed_grad)
    gain_grad_ref[...] = gain_grad
    hidden_grad = cot_ref[...].astype(f32) + hidden_part
    hidden_grad_ref[...] = hidden_grad
    branch = (residual_scale * hidden_grad).astype(bf16)
    branch_ref[...] = branch
    for step, piece in enumerate((out0, out1, out2, out3)):
        attn_grad = product_nt(branch, piece[...]).astype(bf16)
        heads = KV_HEADS // 4
        for head in range(heads):
            columns = slice(head * 2 * HEAD_DIM, (head + 1) * 2 * HEAD_DIM)
            attn_grad_ref[(me_ref[0] ^ step) * heads + head] = attn_grad[:, columns]


def dense_grad_kernel(core_ref, rows_ref, branch_ref, normed_ref, logit_ref, gain_ref, keep_ref, away_ref):
    part, width = keep_ref.shape[1], branch_ref.shape[1]
    logit_grad = logit_ref[...].astype(f32)
    logit_grad = jnp.concatenate(
        [logit_grad, jnp.zeros((logit_grad.shape[0], 128 - EXPERTS), f32)], axis=1
    ).astype(bf16)
    column = lax.broadcasted_iota(jnp.int32, (part, 128), 1)
    for row in range(2):
        for ref, core in ((keep_ref, core_ref[0]), (away_ref, 1 - core_ref[0])):
            columns = pl.ds(pl.multiple_of((2 * row + core) * part, part), part)
            ref[row, :, :width] = product_tn(rows_ref[:, columns], branch_ref[...]).astype(bf16)
            router_grad = product_tn(normed_ref[:, columns], logit_grad)
            gain_grad = jnp.broadcast_to(gain_ref[:, columns], (128, part)).T
            ref[row, :, width:] = jnp.where(column == EXPERTS, gain_grad, router_grad).astype(bf16)


def expert_grad_kernel(core_ref, rows_ref, pre_grad_ref, inner_ref, route_grad_ref, keep_ref, away_ref):
    part = rows_ref.shape[1] // 4
    for row in range(2):
        for ref, core in ((keep_ref, core_ref[0]), (away_ref, 1 - core_ref[0])):
            place = 2 * row + core
            columns = pl.ds(pl.multiple_of(place * part, part), part)
            ref[row, :part, :] = product_tn(rows_ref[:, columns], pre_grad_ref[...]).astype(bf16)
            columns = pl.ds(pl.multiple_of(place * (part // 2), part // 2), part // 2)
            ref[row, part:, :] = product_tn(inner_ref[:, columns], route_grad_ref[...]).astype(bf16)


def dense_split_kernel(place_ref, row_ref, both_ref, other_ref, part0, part1, part2, part3):
    total = (both_ref[row_ref[0]].astype(f32) + other_ref[...].astype(f32)).astype(bf16)
    rows = part0.shape[0]
    for side in range(4):
        for step, ref in enumerate((part0, part1, part2, part3)):

            @pl.when(((place_ref[0] + step) & 3) == side)
            def _():
                ref[...] = total[side * rows : (side + 1) * rows]


def head_grad_kernel(
    dq_ref, dkv0, dkv1, dkv2, dkv3, cos_ref, sin_ref, dense0, dense1, dense2, dense3, out_ref, sent_ref
):
    dkv = dkv0[...].astype(f32) + dkv1[...].astype(f32) + dkv2[...].astype(f32) + dkv3[...].astype(f32)
    for side, grad in enumerate((dq_ref[...], dkv)):
        columns = slice(side * 2 * HEAD_DIM, (side + 1) * 2 * HEAD_DIM)
        out_ref[:, columns] = (grad * cos_ref[:, columns] - turned(grad) * sin_ref[:, columns]).astype(bf16)
    dense = dense0[...].astype(f32) + dense1[...].astype(f32) + dense2[...].astype(f32) + dense3[...].astype(f32)
    tokens = out_ref.shape[0] // KV_HEADS
    empty = jnp.zeros((8, 128), f32)
    for head in range(KV_HEADS):
        sent_ref[head, :tokens, :] = out_ref[head * tokens : (head + 1) * tokens, :]
        mine = dense[head * 8 : (head + 1) * 8]
        lines = [mine[:, side * 256 : (side + 1) * 256] for side in range(4)]
        lines.append(jnp.concatenate([mine[:, 1024:], empty], axis=1))
        lines.append(jnp.concatenate([empty, empty], axis=1))
        sent_ref[head, tokens:, :] = jnp.concatenate(lines, axis=0).astype(bf16)


def head_weight_kernel(core_ref, normed_ref, grads_ref, keep_ref, away_ref):
    part = keep_ref.shape[1]
    for row in range(2):
        for ref, core in ((keep_ref, core_ref[0]), (away_ref, 1 - core_ref[0])):
            columns = pl.ds(pl.multiple_of((2 * row + core) * part, part), part)
            ref[row] = product_tn(normed_ref[:, columns], grads_ref[...]).astype(bf16)


def input_grad_kernel(
    me_ref, grads_ref, w0, w1, w2, w3, x_ref, gain_ref, hidden_grad_ref,
    out_ref, gain0, gain1, gain2, gain3, dense_ref, all_ref,
):
    width = 4 * HEAD_DIM
    tokens = out_ref.shape[0]
    dense = jnp.zeros((grads_ref.shape[1] - tokens, width), f32)
    for head in range(KV_HEADS):
        dense += grads_ref[head, tokens:, :].astype(f32)
    lines = [dense[side * 8 : (side + 1) * 8] for side in range(4)] + [dense[32:40, :128]]
    dense_ref[...] = jnp.concatenate(lines, axis=1).astype(bf16)
    for step, piece in enumerate((w0, w1, w2, w3)):
        part = jnp.zeros((out_ref.shape[0], piece.shape[0]), f32)
        for head in range(KV_HEADS):
            part += product_nt(grads_ref[head, :tokens, :], piece[:, head * width : (head + 1) * width])
        out_ref[:, part_of(me_ref, step, piece.shape[0])] = part
    values = x_ref[...].astype(f32)
    part, gain_grad = norm_back(values, inv_rms_of(values), gain_ref[...], out_ref[...])
    out_ref[...] = hidden_grad_ref[...] + part
    all_ref[...] = gain_grad
    for step, ref in enumerate((gain0, gain1, gain2, gain3)):
        ref[...] = all_ref[:, part_of(me_ref, step, ref.shape[1])]


def gain_block(gain, rows):
    high = gain.astype(bf16).astype(f32)
    return jnp.concatenate([high, gain - high, jnp.zeros((rows - 4, 128), f32)], axis=0)


def line_kernel(part_ref, gain0, gain1, gain2, gain3, dense_ref, out_ref):
    rows, columns = part_ref.shape[0] // 4, part_ref.shape[1]
    for side in range(4):
        out_ref[:rows, side * columns : (side + 1) * columns] = part_ref[side * rows : (side + 1) * rows, :]
    gain = gain0[...] + gain1[...] + gain2[...] + gain3[...]
    gain = jnp.concatenate([gain[:, :128], gain[:, 128:]], axis=0)
    out_ref[:rows, 4 * columns :] = gain_block(gain, rows).astype(bf16)
    dense = dense_ref[...].astype(f32)
    out_ref[rows:, :] = jnp.concatenate([dense, jnp.zeros_like(dense)], axis=0).astype(bf16)


def pack_kernel(place_ref, line0, line1, line2, line3, out_ref, rows_ref):
    rows = line0.shape[0] - 16
    columns = line0.shape[1] - 128
    total = jnp.zeros((rows, columns + 128), f32)
    for step, line in enumerate((line0, line1, line2, line3)):
        total += line[:rows, :].astype(f32)
        place = pl.ds(pl.multiple_of(((place_ref[0] + 4 - step) & 3) * 8, 8), 8)
        rows_ref[place, :] = line[rows:, :].astype(f32)[:8]
    gain = total[0:2, columns:] + total[2:4, columns:]
    weights = total[:, :columns].astype(bf16)
    block = gain_block(gain, rows).astype(bf16)
    dense = rows_ref[...].astype(bf16)
    for head in range(KV_HEADS):
        out_ref[head, :rows, :columns] = weights
        out_ref[head, :rows, columns:] = block
        out_ref[head, rows:, :] = dense


def spread_kernel(
    last_ref, query_ref, key_ref, value_ref, gain_ref, out_grad_ref, router_ref, gain2_ref, column_ref
):
    columns = 4 * HEAD_DIM
    rows = last_ref.shape[1] - 32
    gain_lines = jnp.zeros((rows, 128), f32)
    for head in range(0, KV_HEADS, 2):
        for side in range(4):
            place = slice(side * rows, (side + 1) * rows)
            parts = []
            for step in (0, 1):
                part = last_ref[head + step, :rows, side * columns : (side + 1) * columns].astype(f32)
                query_ref[place, (head + step) * 2 * HEAD_DIM : (head + step + 1) * 2 * HEAD_DIM] = part[:, : 2 * HEAD_DIM]
                parts.append(part)
            pair = slice(head * HEAD_DIM, (head + 2) * HEAD_DIM)
            key_ref[place, pair] = jnp.concatenate([p[:, 2 * HEAD_DIM : 3 * HEAD_DIM] for p in parts], axis=1)
            value_ref[place, pair] = jnp.concatenate([p[:, 3 * HEAD_DIM :] for p in parts], axis=1)
    for head in range(KV_HEADS):
        gain_lines += last_ref[head, :rows, 4 * columns :].astype(f32)
        dense = last_ref[head, rows:, :].astype(f32)
        for place in range(4):
            part = dense[place * 8 : (place + 1) * 8]
            target = slice((place * KV_HEADS + head) * 8, (place * KV_HEADS + head + 1) * 8)
            out_grad_ref[target, :] = part[:, : 4 * columns]
            router_ref[target, :] = part[:, 4 * columns : 4 * columns + EXPERTS]
            column_ref[target, :] = part[:, 4 * columns :]
    gain_ref[:, :128] = gain_lines[0:1] + gain_lines[2:3]
    gain_ref[:, 128:] = gain_lines[1:2] + gain_lines[3:4]
    gain2_ref[...] = column_ref[...].T[EXPERTS : EXPERTS + 1, :]


def gate_of(rows, mask, router_w):
    logits = jnp.where(mask > 0, product(rows, router_w), masked_value)
    exps = jnp.where(mask > 0, jnp.exp(logits - jnp.max(logits, axis=-1, keepdims=True)), 0.0)
    return exps / jnp.maximum(jnp.sum(exps, axis=-1, keepdims=True), 1e-30)


def run_experts(expert, me, rows, marked, pieces, router_w):
    count, width = rows.shape
    part = pieces[0].shape[0] // 3
    units = 4 * part
    tile = 256

    def tiled(columns):
        return pl.BlockSpec((tile, columns), lambda i: (i, 0))

    def whole(array):
        return pl.BlockSpec(array.shape, lambda i: (0, 0))

    columns = (width, width + 128, 2 * units, units, width)
    return pl.pallas_call(
        expert_kernel,
        grid=(count // tile,),
        out_shape=tuple(jax.ShapeDtypeStruct((count, c), bf16) for c in columns),
        in_specs=[SMEM, SMEM, tiled(width), tiled(width + 128)] + [whole(p) for p in pieces] + [whole(router_w)],
        out_specs=tuple(tiled(c) for c in columns),
        scratch_shapes=[pltpu.VMEM((8 * part, 2 * units), bf16), pltpu.VMEM((units, width), bf16)],
        compiler_params=pltpu.CompilerParams(vmem_limit_bytes=56 * 1024 * 1024),
        cost_estimate=pl.CostEstimate(flops=10_000_000_000, bytes_accessed=22_000_000, transcendentals=1_000_000),
    )(expert.astype(jnp.int32).reshape(1), me, rows, marked, *pieces, router_w)


SMEM = pl.BlockSpec(memory_space=pltpu.SMEM)


def whole_block(shape):
    return pl.BlockSpec(tuple(shape), lambda i: (0,) * len(shape))


def attend(numbers, queries, kv_parts):
    rows = queries.shape[0]
    keys = rows * len(kv_parts)
    pairs = rows // (2 * HALF)
    outs = (
        jax.ShapeDtypeStruct((rows, 2 * HEAD_DIM), bf16),
        jax.ShapeDtypeStruct((pairs, HEAD_DIM, 4 * HALF), f32),
        jax.ShapeDtypeStruct((pairs, 1, 4 * HALF), f32),
    )
    return pl.pallas_call(
        attend_kernel,
        grid=(1,),
        out_shape=outs,
        in_specs=[SMEM] * 3 + [whole_block(array.shape) for array in (queries, *kv_parts)],
        out_specs=tuple(whole_block(out.shape) for out in outs),
        scratch_shapes=[pltpu.VMEM((keys, 2 * HEAD_DIM), bf16), pltpu.VMEM((2 * HEAD_DIM, keys), bf16)],
        compiler_params=pltpu.CompilerParams(vmem_limit_bytes=40 * 1024 * 1024),
        cost_estimate=pl.CostEstimate(flops=12_000_000_000, bytes_accessed=4_000_000, transcendentals=5_000_000),
    )(*numbers, queries, *kv_parts)


def attend_grad(numbers, queries, kv_parts, grads, turned, lse):
    rows = queries.shape[0]
    keys = rows * len(kv_parts)
    outs = (jax.ShapeDtypeStruct((rows, 2 * HEAD_DIM), f32),)
    outs += (jax.ShapeDtypeStruct((rows, 2 * HEAD_DIM), bf16),) * 4
    return pl.pallas_call(
        attend_grad_kernel,
        grid=(1,),
        out_shape=outs,
        in_specs=[SMEM] * 3 + [whole_block(array.shape) for array in (queries, *kv_parts, grads, turned, lse)],
        out_specs=tuple(whole_block(out.shape) for out in outs),
        scratch_shapes=[
            pltpu.VMEM((keys, 2 * HEAD_DIM), bf16),
            pltpu.VMEM((2 * HEAD_DIM, keys), bf16),
            pltpu.VMEM((keys, 2 * HEAD_DIM), f32),
        ],
        compiler_params=pltpu.CompilerParams(vmem_limit_bytes=40 * 1024 * 1024),
        cost_estimate=pl.CostEstimate(flops=30_000_000_000, bytes_accessed=6_000_000, transcendentals=5_000_000),
    )(*numbers, queries, *kv_parts, grads, turned, lse)


def block_numbers(block_pairs):
    place = lax.axis_index("x")
    groups = block_pairs.reshape(4, 8)
    groups = groups[(place - jnp.arange(4)) & 3]
    numbers = jnp.stack([groups, 63 - groups], axis=-1).reshape(-1)
    own = numbers[:16]
    rank = jnp.sum((own[None, :] < own[:, None]).astype(jnp.int32), axis=1)
    spots = jnp.arange(16, dtype=jnp.int32)
    order = jnp.sum(jnp.where(rank[None, :] == spots[:, None], spots[None, :], 0), axis=1)
    return (order, own, numbers)


def on_device(
    block_input,
    routes,
    block_pairs,
    norm1_gain,
    w_query,
    w_key,
    w_value,
    w_out,
    norm2_gain,
    w_router,
    w_gate,
    w_up,
    w_down,
    cotangent,
):
    tokens, width = block_input.shape[1:]
    head = lax.axis_index(ZY)
    expert = lax.axis_index(CTX)
    shard_rows = w_query.shape[0]
    own_input = block_input[0]

    core = lax.axis_index("core").astype(jnp.int32).reshape(1)
    place = lax.axis_index("x").astype(jnp.int32).reshape(1)
    me = lax.axis_index(("yl", "core")).astype(jnp.int32).reshape(1)
    small_shard, by_head = call(
        shard_kernel,
        [((shard_rows + EXPERTS + 16, 4 * HEAD_DIM), bf16), ((shard_rows, KV_HEADS * 4 * HEAD_DIM), bf16)],
        (
            head.astype(jnp.int32).reshape(1), w_query, w_key, w_value, w_router,
            norm1_gain.reshape(1, -1), norm2_gain.reshape(1, -1),
        ),
        1_000_000,
        scalars=1,
    )
    small_pieces = pieces_direct(small_shard)
    (copies,) = call(copies_kernel, [((KV_HEADS, tokens, width), bf16)], (own_input,), 1_000_000)
    group_input = exchange(copies.reshape(-1, width), ZY)
    head_w, router_w, gain_one, gain_two = call(
        small_kernel,
        [((width, 4 * HEAD_DIM), bf16), ((width, EXPERTS), bf16), ((1, width), f32), ((1, width), f32)],
        (me, *small_pieces),
        1_000_000,
        scalars=1,
    )

    numbers = block_numbers(block_pairs)
    group_pos = (numbers[1][:, None] * HALF + jnp.arange(HALF, dtype=jnp.int32)[None, :]).reshape(-1)
    cosine, sine = rope_tables(group_pos)

    chosen = routes[0]
    uses = jnp.sum(
        (chosen[:, :, None] == jnp.arange(EXPERTS, dtype=jnp.int32)[None, None, :]).astype(f32), axis=1
    )
    earlier = jnp.tril(jnp.ones((tokens, tokens), bf16), -1)
    rank = product(earlier, uses.astype(bf16)).astype(jnp.int32)
    rank = jnp.where(uses > 0, rank, -1)
    slot = jnp.arange(CAP, dtype=jnp.int32)
    send = (rank.T[:, None, :] == slot[None, :, None]).astype(bf16).reshape(EXPERTS * CAP, tokens)
    fetch = (rank[:, :, None] == slot[None, None, :]).astype(bf16).reshape(tokens, EXPERTS * CAP)

    group_normed, queries, kv_own = project(group_input, head_w, gain_one, cosine, sine)
    kv_parts = [kv_own] + [turn(kv_own, "x", step) for step in (1, 2, 3)]

    out_other = swap(w_out, "yl")
    expert_shard = jnp.concatenate([jnp.concatenate([w_gate[0], w_up[0]], axis=1), w_down[0]], axis=0)
    expert_other = swap(expert_shard, "yl")
    marked = jnp.concatenate(
        [cotangent[0], uses.astype(bf16), jnp.zeros((tokens, 128 - EXPERTS), bf16)], axis=1
    )
    (marked_sent,) = call(
        send_kernel,
        [((EXPERTS * CAP, width + 128), bf16)],
        (send, marked),
        500_000_000,
        held=(*kv_parts[1:], out_other, expert_other),
    )
    marked_arrived = exchange(marked_sent, CTX)

    attn_group, attn_turned, lse = attend(numbers, queries, kv_parts)

    out_pieces = pieces_by_row(w_out, out_other)

    attn_back = exchange(tie(attn_group, marked_arrived), ZY)
    expert_pieces = pieces_by_row(expert_shard, expert_other)
    attn_rows, hidden, normed2, gate_probs, outgoing = call(
        middle_kernel,
        [
            ((tokens, HEADS * HEAD_DIM), bf16),
            ((tokens, width), f32),
            ((tokens, width), bf16),
            ((tokens, EXPERTS), f32),
            ((EXPERTS * CAP, width), bf16),
        ],
        (
            me, attn_back.reshape(KV_HEADS, tokens, 2 * HEAD_DIM), *out_pieces, own_input, gain_two, router_w,
            uses, send,
        ),
        800_000_000,
        held=expert_pieces,
        scalars=1,
    )
    arrived = exchange(outgoing, CTX)

    expert_out, in_grad, pre_grad, inner_act, route_grad = run_experts(
        expert, me, arrived, marked_arrived, expert_pieces, router_w
    )
    back = exchange(in_grad, CTX)
    by_head_sent = tie(by_head, normed2)
    head_pieces = pieces_by_row(by_head_sent, swap(by_head_sent, "yl"))
    expert_shape = ((2, *expert_shard.shape), bf16)
    expert_both = join_core(
        *call(
            expert_grad_kernel,
            [expert_shape, expert_shape],
            (core, arrived, pre_grad, inner_act, route_grad),
            5_000_000_000,
            held=(head_pieces[2],),
            scalars=1,
        )
    )

    hidden_grad, branch_grad, logit_grad, gain_two_grad, attn_grad = call(
        token_grad_kernel,
        [
            ((tokens, width), f32),
            ((tokens, width), bf16),
            ((tokens, EXPERTS), bf16),
            ((1, width), f32),
            ((KV_HEADS, tokens, 2 * HEAD_DIM), bf16),
        ],
        (me, fetch, back, gate_probs, router_w, hidden, gain_two, cotangent[0], *out_pieces),
        800_000_000,
        held=(expert_both, *head_pieces),
        scalars=1,
    )

    group_grad = exchange(attn_grad.reshape(KV_HEADS * tokens, 2 * HEAD_DIM), ZY)
    dq, *dkv_parts = attend_grad(numbers, queries, kv_parts, group_grad, attn_turned, lse)
    dkv_turned = [turn(dkv_parts[step], "x", -step) for step in (1, 2, 3)]
    dense_shape = ((2, shard_rows, width + 128), bf16)
    dense_both = join_core(
        *call(
            dense_grad_kernel,
            [dense_shape, dense_shape],
            (core, attn_rows, branch_grad, normed2, logit_grad, gain_two_grad),
            400_000_000,
            scalars=1,
        )
    )
    row = lax.axis_index("yl").astype(jnp.int32).reshape(1)
    dense_other = swap(lax.dynamic_index_in_dim(dense_both, 1 - row[0], 0, keepdims=False), "yl")
    dense_parts = call(
        dense_split_kernel,
        [((shard_rows // 4, width + 128), bf16)] * 4,
        (place, row, dense_both, dense_other),
        1_000_000,
        held=(dq,),
        scalars=2,
    )
    dense_turned = [turn(dense_parts[step], "x", step) for step in (1, 2, 3)]

    grads, grads_sent = call(
        head_grad_kernel,
        [((KV_HEADS * tokens, 4 * HEAD_DIM), bf16), ((KV_HEADS, tokens + 48, 4 * HEAD_DIM), bf16)],
        (dq, dkv_parts[0], *dkv_turned, cosine, sine, dense_parts[0], *dense_turned),
        100_000_000,
    )
    token_grads = exchange(grads_sent.reshape(-1, 4 * HEAD_DIM), ZY)
    head_shape = ((2, shard_rows, 4 * HEAD_DIM), bf16)
    head_both = join_core(
        *call(head_weight_kernel, [head_shape, head_shape], (core, group_normed, grads), 600_000_000, scalars=1)
    )
    head_part = scatter_row(head_both).astype(bf16)

    returned = exchange(tie(expert_out, token_grads, head_part), CTX)


    gain_shape = ((1, shard_rows), f32)
    input_grad, *gain_parts, dense = call(
        input_grad_kernel,
        [((tokens, width), f32)] + [gain_shape] * 4 + [((8, width + 128), bf16)],
        (
            me, token_grads.reshape(grads_sent.shape), *head_pieces, own_input, gain_one, hidden_grad,
        ),
        600_000_000,
        scalars=1,
        scratch=[(1, width)],
    )
    later = (gain_parts[0][0, 0] * 0.0).astype(jnp.int32)
    expert_away = lax.dynamic_slice_in_dim(expert_both, 1 - row[0] + later, 1, 0)[0]
    expert_other = swap(expert_away, "yl")
    expert_sums = lax.dynamic_index_in_dim(expert_both, row[0], 0, keepdims=False).astype(f32)
    expert_sums = expert_sums + expert_other.astype(f32)
    gain_turned = [
        lax.ppermute(gain_parts[step], ("yl", "core"), [(i, i ^ step) for i in range(4)]) for step in (1, 2, 3)
    ]
    (line,) = call(
        line_kernel,
        [((shard_rows // 4 + 16, width + 128), bf16)],
        (head_part, gain_parts[0], *gain_turned, dense),
        1_000_000,
    )
    (last,) = call(
        pack_kernel,
        [((KV_HEADS, shard_rows // 4 + 32, width + 128), bf16)],
        (place, *all_x(line)),
        1_000_000,
        held=(returned, expert_other),
        scalars=1,
        scratch=[(32, width + 128)],
    )
    last = exchange(last.reshape(-1, width + 128), ZY).reshape(last.shape)
    grad_query, grad_key, grad_value, gain_one_grad, grad_out, grad_router, gain_two_grad = call(
        spread_kernel,
        [
            ((shard_rows, HEADS * HEAD_DIM), f32),
            ((shard_rows, KV_HEADS * HEAD_DIM), f32),
            ((shard_rows, KV_HEADS * HEAD_DIM), f32),
            gain_shape,
            ((shard_rows, width), f32),
            ((shard_rows, EXPERTS), f32),
            gain_shape,
        ],
        (last,),
        1_000_000,
        scratch=[(shard_rows, 128)],
    )

    spread = gate_probs[:, :, None] * fetch.astype(f32).reshape(tokens, EXPERTS, CAP)
    weights = spread.reshape(tokens, EXPERTS * CAP)
    weights_hi = weights.astype(bf16)
    weights_lo = (weights - weights_hi.astype(f32)).astype(bf16)
    mixture = product(weights_hi, returned) + product(weights_lo, returned)
    output = hidden + residual_scale * mixture

    return (
        output.astype(bf16)[None],
        input_grad[None],
        gain_one_grad.reshape(-1),
        grad_query,
        grad_key,
        grad_value,
        grad_out,
        gain_two_grad.reshape(-1),
        grad_router,
        expert_sums[None, :shard_rows, : width // 2],
        expert_sums[None, :shard_rows, width // 2 :],
        expert_sums[None, shard_rows:],
    )


def solution(mesh):
    fine = Mesh(mesh.devices.reshape(4, 4, 2, 2, 2), EVERY)
    rows, shards = P(("yl", "core"), CTX, None), P(("yl", "core"), None)
    gain, experts = P(("yl", "core")), P(CTX, ("yl", "core"), None)
    return jax.shard_map(
        on_device,
        mesh=fine,
        in_specs=(
            rows, rows, P(), gain, shards, shards, shards, shards, gain, shards, experts, experts, experts, rows,
        ),
        out_specs=(
            rows, rows, gain, shards, shards, shards, shards, gain, shards, experts, experts, experts,
        ),
        check_vma=False,
    )
```

```python
import functools

import jax
import jax.numpy as jnp
from jax import lax
from jax.experimental import pallas as pl
from jax.experimental.layout import Layout, with_layout_constraint
from jax.experimental.pallas import tpu as pltpu
from jax.sharding import Mesh
from jax.sharding import PartitionSpec as P

HEADS = 16
KV_HEADS = 8
HEAD_DIM = 64
EXPERTS = 32
TOP = 8
CAP = 48
HALF = 64
TILE = 512

epsilon = 1e-06
attn_scale = 0.015625
residual_scale = 0.22
masked_value = -1e30

CTX = ("x", "z", "yh")
ZY = ("z", "yh")
EVERY = ("x", "z", "yh", "yl", "core")
bf16 = jnp.bfloat16
f32 = jnp.float32


def product(left, right):
    return jnp.dot(left, right, preferred_element_type=f32)


def product_nt(left, right):
    return lax.dot_general(left, right, (((1,), (1,)), ((), ())), preferred_element_type=f32)


def product_tn(left, right):
    return lax.dot_general(left, right, (((0,), (0,)), ((), ())), preferred_element_type=f32)


def swap(values, axis):
    return lax.ppermute(values, axis, [(0, 1), (1, 0)])


def turn(values, axis, step):
    return lax.ppermute(values, axis, [(i, (i + step) % 4) for i in range(4)])


def rows_first(values):
    return with_layout_constraint(values, Layout(major_to_minor=tuple(range(values.ndim))))


def exchange(values, axes):
    return rows_first(lax.all_to_all(rows_first(values), axes, 0, 0, tiled=True))


def tie(values, *others):
    if values.size <= 1024:
        return values + sum(other[(0,) * other.ndim].astype(f32) * 0.0 for other in others).astype(values.dtype)
    corner = tuple(slice(0, min(size, 8 if axis < values.ndim - 1 else 128)) for axis, size in enumerate(values.shape))
    nothing = sum(other[(0,) * other.ndim].astype(f32) * 0.0 for other in others)
    held = values[corner] + nothing.astype(values.dtype)
    return lax.dynamic_update_slice(values, held, (0,) * values.ndim)


def pieces_direct(shard):
    steps = [lax.ppermute(shard, ("yl", "core"), [(i, i ^ k) for i in range(4)]) for k in (1, 2, 3)]
    return (shard, *steps)


def pieces_by_row(shard, other):
    return (shard, swap(shard, "core"), other, swap(other, "core"))


def scatter_core(parts):
    core = lax.axis_index("core")
    parts = parts.astype(bf16).reshape((2, 2) + parts.shape[1:])
    away = lax.dynamic_index_in_dim(parts, 1 - core, 1, keepdims=False)
    keep = lax.dynamic_index_in_dim(parts, core, 1, keepdims=False)
    return (keep.astype(f32) + swap(away, "core").astype(f32)).astype(bf16)


def join_core(keep, away):
    return (keep.astype(f32) + swap(away, "core").astype(f32)).astype(bf16)


def scatter_row(both):
    row = lax.axis_index("yl")
    away = lax.dynamic_index_in_dim(both, 1 - row, 0, keepdims=False)
    keep = lax.dynamic_index_in_dim(both, row, 0, keepdims=False)
    return keep.astype(f32) + swap(away, "yl").astype(f32)


def scatter_fsdp(parts):
    return scatter_row(scatter_core(parts))


def all_x(part):
    return [part] + [turn(part, "x", step) for step in (1, 2, 3)]


def rope_tables(positions):
    freqs = jnp.power(10000.0, -jnp.arange(0, HEAD_DIM, 2, dtype=f32) / HEAD_DIM)
    angles = positions.astype(f32)[:, None] * freqs[None, :]
    cosine, sine = jnp.cos(angles), jnp.sin(angles)
    ones, zeros = jnp.ones_like(cosine), jnp.zeros_like(cosine)
    return (
        jnp.concatenate([cosine] * 6 + [ones] * 2, axis=1),
        jnp.concatenate([-sine, sine] * 3 + [zeros] * 2, axis=1),
    )


def turned(values):
    width = values.shape[1]
    column = lax.broadcasted_iota(jnp.int32, values.shape, 1)
    return jnp.where(
        column % HEAD_DIM < HEAD_DIM // 2,
        pltpu.roll(values, width - HEAD_DIM // 2, 1),
        pltpu.roll(values, HEAD_DIM // 2, 1),
    )


def norm_back(values, inv_rms, gain, grad):
    weighted = grad * gain
    gain_grad = jnp.sum(grad * values * inv_rms, axis=0, keepdims=True)
    inner_mean = jnp.mean(weighted * values, axis=-1, keepdims=True)
    return (weighted * inv_rms - values * inv_rms * inv_rms * inv_rms * inner_mean, gain_grad)


def inv_rms_of(values):
    return lax.rsqrt(jnp.mean(values * values, axis=-1, keepdims=True) + epsilon)


def half(index):
    return pl.ds(pl.multiple_of(index * HALF, HALF), HALF)


def key_tile(counter):
    return pl.ds(pl.multiple_of(counter * TILE, TILE), TILE)


def sort_keys(knum_ref, kv_refs, kvs, kvt):
    blocks = kv_refs[0].shape[0] // HALF
    for slot, kv_ref in enumerate(kv_refs):
        for block in range(blocks):
            kvs[half(knum_ref[slot * blocks + block]), :] = kv_ref[block * HALF : (block + 1) * HALF, :]
    for tile in range(kvs.shape[0] // TILE):
        part = kvs[tile * TILE : (tile + 1) * TILE, :].astype(f32)
        kvt[:, tile * TILE : (tile + 1) * TILE] = part.T.astype(bf16)


def pair_rows(ref, first, second, upper):
    rows = []
    for block in (first, second):
        values = ref[half(block), :].astype(f32)
        column = lax.broadcasted_iota(jnp.int32, values.shape, 1)
        inside = (column >= HEAD_DIM) if upper else (column < HEAD_DIM)
        moved = pltpu.roll(values, HEAD_DIM, 1)
        heads = (moved, values) if upper else (values, moved)
        rows += [jnp.where(inside, head, 0.0) for head in heads]
    return jnp.concatenate(rows, axis=0)


def pair_positions(low_number, high_number):
    column = lax.broadcasted_iota(jnp.int32, (1, 4 * HALF), 1)
    return jnp.where(column < 2 * HALF, low_number, high_number) * HALF + column % HALF


def score_tile(keys, queries, counter, positions, masked):
    scores = product_nt(keys, queries)
    if masked:
        key_pos = counter * TILE + lax.broadcasted_iota(jnp.int32, scores.shape, 0)
        scores = jnp.where(key_pos <= positions, scores, masked_value)
    return scores


def store_rows(ref, turned, first, second):
    rows = turned.T
    ref[half(first), :] = jnp.concatenate([rows[:HALF], rows[HALF : 2 * HALF]], axis=1).astype(ref.dtype)
    ref[half(second), :] = jnp.concatenate([rows[2 * HALF : 3 * HALF], rows[3 * HALF :]], axis=1).astype(ref.dtype)


def attend_kernel(
    order_ref, qnum_ref, knum_ref, q_ref, kv0, kv1, kv2, kv3, out_ref, turned_ref, lse_ref, kvs, kvt
):
    sort_keys(knum_ref, (kv0, kv1, kv2, kv3), kvs, kvt)
    width = 4 * HALF

    @pl.loop(0, q_ref.shape[0] // (2 * HALF))
    def _(pair):
        first, second = order_ref[2 * pair], order_ref[2 * pair + 1]
        low_number, high_number = qnum_ref[first], qnum_ref[second]
        queries = pair_rows(q_ref, first, second, False).astype(bf16)
        positions = pair_positions(low_number, high_number)

        def step(masked, counter, running):
            top, total, mixed = running
            scores = score_tile(kvs[key_tile(counter), :], queries, counter, positions, masked)
            new_top = jnp.maximum(top, jnp.max(scores, axis=0, keepdims=True))
            probs = jnp.exp(scores - new_top)
            shrink = jnp.exp(top - new_top)
            total = total * shrink + jnp.sum(probs, axis=0, keepdims=True)
            mixed = mixed * shrink + product(kvt[HEAD_DIM:, key_tile(counter)], probs.astype(bf16))
            return (new_top, total, mixed)

        start = (
            jnp.full((1, width), masked_value, f32),
            jnp.zeros((1, width), f32),
            jnp.zeros((HEAD_DIM, width), f32),
        )
        full = (low_number * HALF) // TILE
        last = (high_number * HALF) // TILE + 1
        running = lax.fori_loop(0, full, functools.partial(step, False), start)
        top, total, mixed = lax.fori_loop(full, last, functools.partial(step, True), running)
        mixed = mixed / total
        turned_ref[pair] = mixed
        lse_ref[pair] = top + jnp.log(total)
        store_rows(out_ref, mixed, first, second)


def attend_grad_kernel(
    order_ref, qnum_ref, knum_ref, q_ref, kv0, kv1, kv2, kv3, grad_ref, turned_ref, lse_ref,
    dq_ref, dkv0, dkv1, dkv2, dkv3, kvs, kvt, total_ref,
):
    sort_keys(knum_ref, (kv0, kv1, kv2, kv3), kvs, kvt)
    total_ref[...] = jnp.zeros_like(total_ref)
    width = 4 * HALF

    @pl.loop(0, q_ref.shape[0] // (2 * HALF))
    def _(pair):
        first, second = order_ref[2 * pair], order_ref[2 * pair + 1]
        low_number, high_number = qnum_ref[first], qnum_ref[second]
        queries = pair_rows(q_ref, first, second, False).astype(bf16)
        grads_f = pair_rows(grad_ref, first, second, True)
        grads = grads_f.astype(bf16)
        both = jnp.concatenate([queries, grads], axis=0)
        positions = pair_positions(low_number, high_number)
        lse = lse_ref[pair]
        dots = jnp.sum(grads_f.T[HEAD_DIM:] * turned_ref[pair], axis=0, keepdims=True)

        def step(masked, counter, query_acc):
            keys = kvs[key_tile(counter), :]
            probs = jnp.exp(score_tile(keys, queries, counter, positions, masked) - lse)
            score_grad = (probs * (product_nt(keys, grads) - dots)).astype(bf16)
            sides = jnp.concatenate([score_grad, probs.astype(bf16)], axis=1)
            total_ref[key_tile(counter), :] += product(sides, both)
            return query_acc + product(kvt[:HEAD_DIM, key_tile(counter)], score_grad)

        full = (low_number * HALF) // TILE
        last = (high_number * HALF) // TILE + 1
        query_acc = lax.fori_loop(0, full, functools.partial(step, False), jnp.zeros((HEAD_DIM, width), f32))
        query_acc = lax.fori_loop(full, last, functools.partial(step, True), query_acc)
        store_rows(dq_ref, query_acc * attn_scale, first, second)

    blocks = dkv0.shape[0] // HALF
    for slot, dkv in enumerate((dkv0, dkv1, dkv2, dkv3)):
        for block in range(blocks):
            dkv[block * HALF : (block + 1) * HALF, :] = total_ref[
                half(knum_ref[slot * blocks + block]), :
            ].astype(bf16)


def expert_kernel(
    expert_ref, me_ref, rows_ref, marked_ref, piece0, piece1, piece2, piece3, router_ref,
    out_ref, in_grad_ref, pre_grad_ref, inner_ref, route_grad_ref, gu_ref, down_ref,
):
    @pl.when(pl.program_id(0) == 0)
    def _():
        part = gu_ref.shape[0] // 4
        for step, piece in enumerate((piece0, piece1, piece2, piece3)):
            place = me_ref[0] ^ step
            gu_ref[pl.ds(pl.multiple_of(place * part, part), part), :] = piece[:part, :]
            down_ref[pl.ds(pl.multiple_of(place * (part // 2), part // 2), part // 2), :] = piece[part:, :]

    rows = rows_ref[...]
    width = rows.shape[1]
    units = down_ref.shape[0]
    pre = product(rows, gu_ref[...])
    gate_pre, up_pre = pre[:, :units], pre[:, units:]
    sigmoid_a = 1.0 / (1.0 + jnp.exp(-gate_pre))
    swish_act = gate_pre * sigmoid_a
    inner_act = (swish_act * up_pre).astype(bf16)
    inner_ref[...] = inner_act
    expert_out = product(inner_act, down_ref[...]).astype(bf16)
    out_ref[...] = expert_out
    uses = marked_ref[:, width : width + EXPERTS].astype(f32)
    probs = gate_of(rows, uses, router_ref[...])
    column = lax.broadcasted_iota(jnp.int32, probs.shape, 1)
    slot_probs = jnp.sum(jnp.where(column == expert_ref[0], probs, 0.0), axis=1, keepdims=True)
    mix_grad = residual_scale * marked_ref[:, :width].astype(f32)
    gate_grad = jnp.sum(mix_grad * expert_out.astype(f32), axis=1, keepdims=True)
    route_grad = (slot_probs * mix_grad).astype(bf16)
    route_grad_ref[...] = route_grad
    inner_grad = product_nt(route_grad, down_ref[...])
    pre_grad_ref[:, :units] = (
        inner_grad * up_pre * sigmoid_a * (1.0 + gate_pre * (1.0 - sigmoid_a))
    ).astype(bf16)
    pre_grad_ref[:, units:] = (inner_grad * swish_act).astype(bf16)
    in_grad_ref[:, :width] = product_nt(pre_grad_ref[...], gu_ref[...]).astype(bf16)
    column = lax.broadcasted_iota(jnp.int32, (rows.shape[0], 128), 1)
    high = gate_grad.astype(bf16).astype(f32)
    in_grad_ref[:, width:] = jnp.where(
        column == expert_ref[0], high, jnp.where(column == EXPERTS + expert_ref[0], gate_grad - high, 0.0)
    ).astype(bf16)


def project_kernel(x_ref, w_ref, gain_ref, cos_ref, sin_ref, normed_ref, q_ref, kv_ref):
    values = x_ref[...].astype(f32)
    normed = (values * inv_rms_of(values) * gain_ref[...]).astype(bf16)
    normed_ref[...] = normed
    projected = product(normed, w_ref[...])
    rotated = projected * cos_ref[...] + turned(projected) * sin_ref[...]
    q_ref[...] = rotated[:, : 2 * HEAD_DIM].astype(bf16) * bf16(attn_scale)
    kv_ref[...] = rotated[:, 2 * HEAD_DIM :].astype(bf16)


def project(rows, head_w, gain, cosine, sine):
    count, width = rows.shape
    tile = 256

    def tiled(columns):
        return pl.BlockSpec((tile, columns), lambda i: (i, 0))

    def whole(array):
        return pl.BlockSpec(array.shape, lambda i: (0, 0))

    columns = (width, 2 * HEAD_DIM, 2 * HEAD_DIM)
    return pl.pallas_call(
        project_kernel,
        grid=(count // tile,),
        out_shape=tuple(jax.ShapeDtypeStruct((count, c), bf16) for c in columns),
        in_specs=[tiled(width), whole(head_w), whole(gain), tiled(4 * HEAD_DIM), tiled(4 * HEAD_DIM)],
        out_specs=tuple(tiled(c) for c in columns),
        compiler_params=pltpu.CompilerParams(vmem_limit_bytes=32 * 1024 * 1024),
        cost_estimate=pl.CostEstimate(flops=600_000_000, bytes_accessed=8_000_000, transcendentals=0),
    )(rows, head_w, gain, cosine, sine)


def call(kernel, outs, operands, flops, held=(), scalars=0, scratch=()):
    count = len(operands)

    def body(*refs):
        kernel(*refs[:count], *refs[count + len(held) :])

    return pl.pallas_call(
        body,
        grid=(1,),
        out_shape=tuple(jax.ShapeDtypeStruct(shape, dtype) for shape, dtype in outs),
        in_specs=[SMEM] * scalars
        + [whole_block(array.shape) for array in operands[scalars:]]
        + [pl.BlockSpec(memory_space=pl.ANY)] * len(held),
        out_specs=tuple(whole_block(shape) for shape, _ in outs),
        scratch_shapes=[pltpu.VMEM(shape, f32) for shape in scratch],
        compiler_params=pltpu.CompilerParams(vmem_limit_bytes=48 * 1024 * 1024),
        cost_estimate=pl.CostEstimate(flops=flops, bytes_accessed=8_000_000, transcendentals=0),
    )(*operands, *held)


def part_of(me_ref, step, part):
    return pl.ds(pl.multiple_of((me_ref[0] ^ step) * part, part), part)


def copies_kernel(x_ref, copies_ref):
    for copy in range(KV_HEADS):
        copies_ref[copy] = x_ref[...]


def shard_kernel(
    head_ref, query_ref, key_ref, value_ref, router_ref, gain1_ref, gain2_ref, out_ref, by_head_ref
):
    rows = query_ref.shape[0]
    lower = lax.broadcasted_iota(jnp.int32, (rows, 128), 1) < HEAD_DIM
    for head in range(KV_HEADS):
        pair = slice(head // 2 * 128, (head // 2 + 1) * 128)
        keys, values = key_ref[:, pair].astype(f32), value_ref[:, pair].astype(f32)
        if head % 2:
            keys = pltpu.roll(keys, HEAD_DIM, 1)
        else:
            values = pltpu.roll(values, HEAD_DIM, 1)
        by_head_ref[:, head * 256 : head * 256 + 128] = query_ref[:, head * 128 : (head + 1) * 128]
        by_head_ref[:, head * 256 + 128 : (head + 1) * 256] = jnp.where(lower, keys, values).astype(bf16)
    out_ref[:rows, :] = by_head_ref[:, pl.ds(pl.multiple_of(head_ref[0] * 256, 256), 256)]
    router = jnp.concatenate([router_ref[...].astype(f32), jnp.zeros((rows, 128 - EXPERTS), f32)], axis=1)
    out_ref[rows : rows + EXPERTS, :] = router.T[:EXPERTS].astype(bf16)
    row = lax.broadcasted_iota(jnp.int32, (16, rows), 0)
    gains = jnp.where(row == 0, gain1_ref[...].astype(f32), jnp.where(row == 1, gain2_ref[...].astype(f32), 0.0))
    out_ref[rows + EXPERTS :, :] = gains.astype(bf16)


def small_kernel(me_ref, piece0, piece1, piece2, piece3, head_w_ref, router_ref, gain1_ref, gain2_ref):
    rows = head_w_ref.shape[0] // 4
    for step, piece in enumerate((piece0, piece1, piece2, piece3)):
        place = part_of(me_ref, step, rows)
        head_w_ref[place, :] = piece[:rows, :]
        router = piece[rows : rows + EXPERTS, :].astype(f32)
        router = jnp.concatenate([router, jnp.zeros((128 - EXPERTS, rows), f32)], axis=0)
        router_ref[place, :] = router.T[:, :EXPERTS].astype(bf16)
        gains = piece[rows + EXPERTS :, :].astype(f32)
        gain1_ref[:, place] = gains[0:1]
        gain2_ref[:, place] = gains[1:2]


def send_kernel(send_ref, rows_ref, out_ref):
    out_ref[...] = product(send_ref[...], rows_ref[...]).astype(bf16)


def middle_kernel(
    me_ref, attn_ref, out0, out1, out2, out3, x_ref, gain_ref, router_ref, uses_ref, send_ref,
    rows_ref, hidden_ref, normed_ref, probs_ref, out_ref,
):
    for head in range(KV_HEADS):
        rows_ref[:, head * 2 * HEAD_DIM : (head + 1) * 2 * HEAD_DIM] = attn_ref[head]
    branch = jnp.zeros(hidden_ref.shape, f32)
    for step, piece in enumerate((out0, out1, out2, out3)):
        branch += product(rows_ref[:, part_of(me_ref, step, piece.shape[0])], piece[...])
    hidden = x_ref[...].astype(f32) + residual_scale * branch
    hidden_ref[...] = hidden
    normed = (hidden * inv_rms_of(hidden) * gain_ref[...]).astype(bf16)
    normed_ref[...] = normed
    out_ref[...] = product(send_ref[...], normed).astype(bf16)
    probs_ref[...] = gate_of(normed, uses_ref[...], router_ref[...])


def token_grad_kernel(
    me_ref, fetch_ref, back_ref, probs_ref, router_ref, hidden_ref, gain_ref, cot_ref, out0, out1, out2, out3,
    hidden_grad_ref, branch_ref, logit_ref, gain_grad_ref, attn_grad_ref,
):
    width = hidden_ref.shape[1]
    fetched = product(fetch_ref[...], back_ref[...])
    gate_grad = fetched[:, width : width + EXPERTS] + fetched[:, width + EXPERTS : width + 2 * EXPERTS]
    probs = probs_ref[...]
    mean_grad = jnp.sum(probs * gate_grad, axis=-1, keepdims=True)
    logit_grad = (probs * (gate_grad - mean_grad)).astype(bf16)
    logit_ref[...] = logit_grad
    normed_grad = fetched[:, :width] + product_nt(logit_grad, router_ref[...])
    hidden = hidden_ref[...]
    hidden_part, gain_grad = norm_back(hidden, inv_rms_of(hidden), gain_ref[...], normed_grad)
    gain_grad_ref[...] = gain_grad
    hidden_grad = cot_ref[...].astype(f32) + hidden_part
    hidden_grad_ref[...] = hidden_grad
    branch = (residual_scale * hidden_grad).astype(bf16)
    branch_ref[...] = branch
    for step, piece in enumerate((out0, out1, out2, out3)):
        attn_grad = product_nt(branch, piece[...]).astype(bf16)
        heads = KV_HEADS // 4
        for head in range(heads):
            columns = slice(head * 2 * HEAD_DIM, (head + 1) * 2 * HEAD_DIM)
            attn_grad_ref[(me_ref[0] ^ step) * heads + head] = attn_grad[:, columns]


def dense_grad_kernel(core_ref, rows_ref, branch_ref, normed_ref, logit_ref, gain_ref, keep_ref, away_ref):
    part, width = keep_ref.shape[1], branch_ref.shape[1]
    logit_grad = logit_ref[...].astype(f32)
    logit_grad = jnp.concatenate(
        [logit_grad, jnp.zeros((logit_grad.shape[0], 128 - EXPERTS), f32)], axis=1
    ).astype(bf16)
    column = lax.broadcasted_iota(jnp.int32, (part, 128), 1)
    for row in range(2):
        for ref, core in ((keep_ref, core_ref[0]), (away_ref, 1 - core_ref[0])):
            columns = pl.ds(pl.multiple_of((2 * row + core) * part, part), part)
            ref[row, :, :width] = product_tn(rows_ref[:, columns], branch_ref[...]).astype(bf16)
            router_grad = product_tn(normed_ref[:, columns], logit_grad)
            gain_grad = jnp.broadcast_to(gain_ref[:, columns], (128, part)).T
            ref[row, :, width:] = jnp.where(column == EXPERTS, gain_grad, router_grad).astype(bf16)


def expert_grad_kernel(core_ref, rows_ref, pre_grad_ref, inner_ref, route_grad_ref, keep_ref, away_ref):
    part = rows_ref.shape[1] // 4
    for row in range(2):
        for ref, core in ((keep_ref, core_ref[0]), (away_ref, 1 - core_ref[0])):
            place = 2 * row + core
            columns = pl.ds(pl.multiple_of(place * part, part), part)
            ref[row, :part, :] = product_tn(rows_ref[:, columns], pre_grad_ref[...]).astype(bf16)
            columns = pl.ds(pl.multiple_of(place * (part // 2), part // 2), part // 2)
            ref[row, part:, :] = product_tn(inner_ref[:, columns], route_grad_ref[...]).astype(bf16)


def dense_split_kernel(place_ref, row_ref, both_ref, other_ref, part0, part1, part2, part3):
    total = (both_ref[row_ref[0]].astype(f32) + other_ref[...].astype(f32)).astype(bf16)
    rows = part0.shape[0]
    for side in range(4):
        for step, ref in enumerate((part0, part1, part2, part3)):

            @pl.when(((place_ref[0] + step) & 3) == side)
            def _():
                ref[...] = total[side * rows : (side + 1) * rows]


def head_grad_kernel(
    dq_ref, dkv0, dkv1, dkv2, dkv3, cos_ref, sin_ref, dense0, dense1, dense2, dense3, out_ref, sent_ref
):
    dkv = dkv0[...].astype(f32) + dkv1[...].astype(f32) + dkv2[...].astype(f32) + dkv3[...].astype(f32)
    for side, grad in enumerate((dq_ref[...], dkv)):
        columns = slice(side * 2 * HEAD_DIM, (side + 1) * 2 * HEAD_DIM)
        out_ref[:, columns] = (grad * cos_ref[:, columns] - turned(grad) * sin_ref[:, columns]).astype(bf16)
    dense = dense0[...].astype(f32) + dense1[...].astype(f32) + dense2[...].astype(f32) + dense3[...].astype(f32)
    tokens = out_ref.shape[0] // KV_HEADS
    empty = jnp.zeros((8, 128), f32)
    for head in range(KV_HEADS):
        sent_ref[head, :tokens, :] = out_ref[head * tokens : (head + 1) * tokens, :]
        mine = dense[head * 8 : (head + 1) * 8]
        lines = [mine[:, side * 256 : (side + 1) * 256] for side in range(4)]
        lines.append(jnp.concatenate([mine[:, 1024:], empty], axis=1))
        lines.append(jnp.concatenate([empty, empty], axis=1))
        sent_ref[head, tokens:, :] = jnp.concatenate(lines, axis=0).astype(bf16)


def head_weight_kernel(core_ref, normed_ref, grads_ref, keep_ref, away_ref):
    part = keep_ref.shape[1]
    for row in range(2):
        for ref, core in ((keep_ref, core_ref[0]), (away_ref, 1 - core_ref[0])):
            columns = pl.ds(pl.multiple_of((2 * row + core) * part, part), part)
            ref[row] = product_tn(normed_ref[:, columns], grads_ref[...]).astype(bf16)


def input_grad_kernel(
    me_ref, grads_ref, w0, w1, w2, w3, x_ref, gain_ref, hidden_grad_ref,
    out_ref, gain0, gain1, gain2, gain3, dense_ref, all_ref,
):
    width = 4 * HEAD_DIM
    tokens = out_ref.shape[0]
    dense = jnp.zeros((grads_ref.shape[1] - tokens, width), f32)
    for head in range(KV_HEADS):
        dense += grads_ref[head, tokens:, :].astype(f32)
    lines = [dense[side * 8 : (side + 1) * 8] for side in range(4)] + [dense[32:40, :128]]
    dense_ref[...] = jnp.concatenate(lines, axis=1).astype(bf16)
    for step, piece in enumerate((w0, w1, w2, w3)):
        part = jnp.zeros((out_ref.shape[0], piece.shape[0]), f32)
        for head in range(KV_HEADS):
            part += product_nt(grads_ref[head, :tokens, :], piece[:, head * width : (head + 1) * width])
        out_ref[:, part_of(me_ref, step, piece.shape[0])] = part
    values = x_ref[...].astype(f32)
    part, gain_grad = norm_back(values, inv_rms_of(values), gain_ref[...], out_ref[...])
    out_ref[...] = hidden_grad_ref[...] + part
    all_ref[...] = gain_grad
    for step, ref in enumerate((gain0, gain1, gain2, gain3)):
        ref[...] = all_ref[:, part_of(me_ref, step, ref.shape[1])]


def gain_block(gain, rows):
    high = gain.astype(bf16).astype(f32)
    return jnp.concatenate([high, gain - high, jnp.zeros((rows - 4, 128), f32)], axis=0)


def line_kernel(part_ref, gain0, gain1, gain2, gain3, dense_ref, out_ref):
    rows, columns = part_ref.shape[0] // 4, part_ref.shape[1]
    for side in range(4):
        out_ref[:rows, side * columns : (side + 1) * columns] = part_ref[side * rows : (side + 1) * rows, :]
    gain = gain0[...] + gain1[...] + gain2[...] + gain3[...]
    gain = jnp.concatenate([gain[:, :128], gain[:, 128:]], axis=0)
    out_ref[:rows, 4 * columns :] = gain_block(gain, rows).astype(bf16)
    dense = dense_ref[...].astype(f32)
    out_ref[rows:, :] = jnp.concatenate([dense, jnp.zeros_like(dense)], axis=0).astype(bf16)


def pack_kernel(place_ref, line0, line1, line2, line3, out_ref, rows_ref):
    rows = line0.shape[0] - 16
    columns = line0.shape[1] - 128
    total = jnp.zeros((rows, columns + 128), f32)
    for step, line in enumerate((line0, line1, line2, line3)):
        total += line[:rows, :].astype(f32)
        place = pl.ds(pl.multiple_of(((place_ref[0] + 4 - step) & 3) * 8, 8), 8)
        rows_ref[place, :] = line[rows:, :].astype(f32)[:8]
    gain = total[0:2, columns:] + total[2:4, columns:]
    weights = total[:, :columns].astype(bf16)
    block = gain_block(gain, rows).astype(bf16)
    dense = rows_ref[...].astype(bf16)
    for head in range(KV_HEADS):
        out_ref[head, :rows, :columns] = weights
        out_ref[head, :rows, columns:] = block
        out_ref[head, rows:, :] = dense


def spread_kernel(
    last_ref, query_ref, key_ref, value_ref, gain_ref, out_grad_ref, router_ref, gain2_ref, column_ref
):
    columns = 4 * HEAD_DIM
    rows = last_ref.shape[1] - 32
    gain_lines = jnp.zeros((rows, 128), f32)
    for head in range(0, KV_HEADS, 2):
        for side in range(4):
            place = slice(side * rows, (side + 1) * rows)
            parts = []
            for step in (0, 1):
                part = last_ref[head + step, :rows, side * columns : (side + 1) * columns].astype(f32)
                query_ref[place, (head + step) * 2 * HEAD_DIM : (head + step + 1) * 2 * HEAD_DIM] = part[:, : 2 * HEAD_DIM]
                parts.append(part)
            pair = slice(head * HEAD_DIM, (head + 2) * HEAD_DIM)
            key_ref[place, pair] = jnp.concatenate([p[:, 2 * HEAD_DIM : 3 * HEAD_DIM] for p in parts], axis=1)
            value_ref[place, pair] = jnp.concatenate([p[:, 3 * HEAD_DIM :] for p in parts], axis=1)
    for head in range(KV_HEADS):
        gain_lines += last_ref[head, :rows, 4 * columns :].astype(f32)
        dense = last_ref[head, rows:, :].astype(f32)
        for place in range(4):
            part = dense[place * 8 : (place + 1) * 8]
            target = slice((place * KV_HEADS + head) * 8, (place * KV_HEADS + head + 1) * 8)
            out_grad_ref[target, :] = part[:, : 4 * columns]
            router_ref[target, :] = part[:, 4 * columns : 4 * columns + EXPERTS]
            column_ref[target, :] = part[:, 4 * columns :]
    gain_ref[:, :128] = gain_lines[0:1] + gain_lines[2:3]
    gain_ref[:, 128:] = gain_lines[1:2] + gain_lines[3:4]
    gain2_ref[...] = column_ref[...].T[EXPERTS : EXPERTS + 1, :]


def gate_of(rows, mask, router_w):
    logits = jnp.where(mask > 0, product(rows, router_w), masked_value)
    exps = jnp.where(mask > 0, jnp.exp(logits - jnp.max(logits, axis=-1, keepdims=True)), 0.0)
    return exps / jnp.maximum(jnp.sum(exps, axis=-1, keepdims=True), 1e-30)


def run_experts(expert, me, rows, marked, pieces, router_w):
    count, width = rows.shape
    part = pieces[0].shape[0] // 3
    units = 4 * part
    tile = 256

    def tiled(columns):
        return pl.BlockSpec((tile, columns), lambda i: (i, 0))

    def whole(array):
        return pl.BlockSpec(array.shape, lambda i: (0, 0))

    columns = (width, width + 128, 2 * units, units, width)
    return pl.pallas_call(
        expert_kernel,
        grid=(count // tile,),
        out_shape=tuple(jax.ShapeDtypeStruct((count, c), bf16) for c in columns),
        in_specs=[SMEM, SMEM, tiled(width), tiled(width + 128)] + [whole(p) for p in pieces] + [whole(router_w)],
        out_specs=tuple(tiled(c) for c in columns),
        scratch_shapes=[pltpu.VMEM((8 * part, 2 * units), bf16), pltpu.VMEM((units, width), bf16)],
        compiler_params=pltpu.CompilerParams(vmem_limit_bytes=56 * 1024 * 1024),
        cost_estimate=pl.CostEstimate(flops=10_000_000_000, bytes_accessed=22_000_000, transcendentals=1_000_000),
    )(expert.astype(jnp.int32).reshape(1), me, rows, marked, *pieces, router_w)


SMEM = pl.BlockSpec(memory_space=pltpu.SMEM)


def whole_block(shape):
    return pl.BlockSpec(tuple(shape), lambda i: (0,) * len(shape))


def attend(numbers, queries, kv_parts):
    rows = queries.shape[0]
    keys = rows * len(kv_parts)
    pairs = rows // (2 * HALF)
    outs = (
        jax.ShapeDtypeStruct((rows, 2 * HEAD_DIM), bf16),
        jax.ShapeDtypeStruct((pairs, HEAD_DIM, 4 * HALF), f32),
        jax.ShapeDtypeStruct((pairs, 1, 4 * HALF), f32),
    )
    return pl.pallas_call(
        attend_kernel,
        grid=(1,),
        out_shape=outs,
        in_specs=[SMEM] * 3 + [whole_block(array.shape) for array in (queries, *kv_parts)],
        out_specs=tuple(whole_block(out.shape) for out in outs),
        scratch_shapes=[pltpu.VMEM((keys, 2 * HEAD_DIM), bf16), pltpu.VMEM((2 * HEAD_DIM, keys), bf16)],
        compiler_params=pltpu.CompilerParams(vmem_limit_bytes=40 * 1024 * 1024),
        cost_estimate=pl.CostEstimate(flops=12_000_000_000, bytes_accessed=4_000_000, transcendentals=5_000_000),
    )(*numbers, queries, *kv_parts)


def attend_grad(numbers, queries, kv_parts, grads, turned, lse):
    rows = queries.shape[0]
    keys = rows * len(kv_parts)
    outs = (jax.ShapeDtypeStruct((rows, 2 * HEAD_DIM), f32),)
    outs += (jax.ShapeDtypeStruct((rows, 2 * HEAD_DIM), bf16),) * 4
    return pl.pallas_call(
        attend_grad_kernel,
        grid=(1,),
        out_shape=outs,
        in_specs=[SMEM] * 3 + [whole_block(array.shape) for array in (queries, *kv_parts, grads, turned, lse)],
        out_specs=tuple(whole_block(out.shape) for out in outs),
        scratch_shapes=[
            pltpu.VMEM((keys, 2 * HEAD_DIM), bf16),
            pltpu.VMEM((2 * HEAD_DIM, keys), bf16),
            pltpu.VMEM((keys, 2 * HEAD_DIM), f32),
        ],
        compiler_params=pltpu.CompilerParams(vmem_limit_bytes=40 * 1024 * 1024),
        cost_estimate=pl.CostEstimate(flops=30_000_000_000, bytes_accessed=6_000_000, transcendentals=5_000_000),
    )(*numbers, queries, *kv_parts, grads, turned, lse)


def block_numbers(block_pairs):
    place = lax.axis_index("x")
    groups = block_pairs.reshape(4, 8)
    groups = groups[(place - jnp.arange(4)) & 3]
    numbers = jnp.stack([groups, 63 - groups], axis=-1).reshape(-1)
    own = numbers[:16]
    rank = jnp.sum((own[None, :] < own[:, None]).astype(jnp.int32), axis=1)
    spots = jnp.arange(16, dtype=jnp.int32)
    order = jnp.sum(jnp.where(rank[None, :] == spots[:, None], spots[None, :], 0), axis=1)
    return (order, own, numbers)


def on_device(
    block_input,
    routes,
    block_pairs,
    norm1_gain,
    w_query,
    w_key,
    w_value,
    w_out,
    norm2_gain,
    w_router,
    w_gate,
    w_up,
    w_down,
    cotangent,
):
    tokens, width = block_input.shape[1:]
    head = lax.axis_index(ZY)
    expert = lax.axis_index(CTX)
    shard_rows = w_query.shape[0]
    own_input = block_input[0]

    core = lax.axis_index("core").astype(jnp.int32).reshape(1)
    place = lax.axis_index("x").astype(jnp.int32).reshape(1)
    me = lax.axis_index(("yl", "core")).astype(jnp.int32).reshape(1)
    small_shard, by_head = call(
        shard_kernel,
        [((shard_rows + EXPERTS + 16, 4 * HEAD_DIM), bf16), ((shard_rows, KV_HEADS * 4 * HEAD_DIM), bf16)],
        (
            head.astype(jnp.int32).reshape(1), w_query, w_key, w_value, w_router,
            norm1_gain.reshape(1, -1), norm2_gain.reshape(1, -1),
        ),
        1_000_000,
        scalars=1,
    )
    small_pieces = pieces_direct(small_shard)
    (copies,) = call(copies_kernel, [((KV_HEADS, tokens, width), bf16)], (own_input,), 1_000_000)
    group_input = exchange(copies.reshape(-1, width), ZY)
    head_w, router_w, gain_one, gain_two = call(
        small_kernel,
        [((width, 4 * HEAD_DIM), bf16), ((width, EXPERTS), bf16), ((1, width), f32), ((1, width), f32)],
        (me, *small_pieces),
        1_000_000,
        scalars=1,
    )

    numbers = block_numbers(block_pairs)
    group_pos = (numbers[1][:, None] * HALF + jnp.arange(HALF, dtype=jnp.int32)[None, :]).reshape(-1)
    cosine, sine = rope_tables(group_pos)

    chosen = routes[0]
    uses = jnp.sum(
        (chosen[:, :, None] == jnp.arange(EXPERTS, dtype=jnp.int32)[None, None, :]).astype(f32), axis=1
    )
    earlier = jnp.tril(jnp.ones((tokens, tokens), bf16), -1)
    rank = product(earlier, uses.astype(bf16)).astype(jnp.int32)
    rank = jnp.where(uses > 0, rank, -1)
    slot = jnp.arange(CAP, dtype=jnp.int32)
    send = (rank.T[:, None, :] == slot[None, :, None]).astype(bf16).reshape(EXPERTS * CAP, tokens)
    fetch = (rank[:, :, None] == slot[None, None, :]).astype(bf16).reshape(tokens, EXPERTS * CAP)

    group_normed, queries, kv_own = project(group_input, head_w, gain_one, cosine, sine)
    kv_parts = [kv_own] + [turn(kv_own, "x", step) for step in (1, 2, 3)]

    out_other = swap(w_out, "yl")
    marked = jnp.concatenate(
        [cotangent[0], uses.astype(bf16), jnp.zeros((tokens, 128 - EXPERTS), bf16)], axis=1
    )
    (marked_sent,) = call(
        send_kernel,
        [((EXPERTS * CAP, width + 128), bf16)],
        (send, marked),
        500_000_000,
        held=(*kv_parts[1:], out_other),
    )
    marked_arrived = exchange(marked_sent, CTX)

    attn_group, attn_turned, lse = attend(numbers, queries, kv_parts)

    out_pieces = pieces_by_row(w_out, out_other)
    expert_shard = jnp.concatenate([jnp.concatenate([w_gate[0], w_up[0]], axis=1), w_down[0]], axis=0)
    expert_shard = tie(expert_shard, attn_group)
    expert_row = swap(expert_shard, "yl")

    attn_back = exchange(tie(attn_group, marked_arrived), ZY)
    expert_pieces = pieces_by_row(expert_shard, expert_row)
    attn_rows, hidden, normed2, gate_probs, outgoing = call(
        middle_kernel,
        [
            ((tokens, HEADS * HEAD_DIM), bf16),
            ((tokens, width), f32),
            ((tokens, width), bf16),
            ((tokens, EXPERTS), f32),
            ((EXPERTS * CAP, width), bf16),
        ],
        (
            me, attn_back.reshape(KV_HEADS, tokens, 2 * HEAD_DIM), *out_pieces, own_input, gain_two, router_w,
            uses, send,
        ),
        800_000_000,
        held=(expert_row,),
        scalars=1,
    )
    arrived = exchange(outgoing, CTX)

    expert_out, in_grad, pre_grad, inner_act, route_grad = run_experts(
        expert, me, arrived, marked_arrived, expert_pieces, router_w
    )
    back = exchange(in_grad, CTX)
    by_head_sent = tie(by_head, normed2)
    head_pieces = pieces_by_row(by_head_sent, swap(by_head_sent, "yl"))
    expert_shape = ((2, *expert_shard.shape), bf16)
    expert_both = join_core(
        *call(
            expert_grad_kernel,
            [expert_shape, expert_shape],
            (core, arrived, pre_grad, inner_act, route_grad),
            5_000_000_000,
            held=(head_pieces[2],),
            scalars=1,
        )
    )

    hidden_grad, branch_grad, logit_grad, gain_two_grad, attn_grad = call(
        token_grad_kernel,
        [
            ((tokens, width), f32),
            ((tokens, width), bf16),
            ((tokens, EXPERTS), bf16),
            ((1, width), f32),
            ((KV_HEADS, tokens, 2 * HEAD_DIM), bf16),
        ],
        (me, fetch, back, gate_probs, router_w, hidden, gain_two, cotangent[0], *out_pieces),
        800_000_000,
        held=(expert_both, *head_pieces),
        scalars=1,
    )

    group_grad = exchange(attn_grad.reshape(KV_HEADS * tokens, 2 * HEAD_DIM), ZY)
    dq, *dkv_parts = attend_grad(numbers, queries, kv_parts, group_grad, attn_turned, lse)
    dkv_turned = [turn(dkv_parts[step], "x", -step) for step in (1, 2, 3)]
    dense_shape = ((2, shard_rows, width + 128), bf16)
    dense_both = join_core(
        *call(
            dense_grad_kernel,
            [dense_shape, dense_shape],
            (core, attn_rows, branch_grad, normed2, logit_grad, gain_two_grad),
            400_000_000,
            scalars=1,
        )
    )
    row = lax.axis_index("yl").astype(jnp.int32).reshape(1)
    dense_other = swap(lax.dynamic_index_in_dim(dense_both, 1 - row[0], 0, keepdims=False), "yl")
    dense_parts = call(
        dense_split_kernel,
        [((shard_rows // 4, width + 128), bf16)] * 4,
        (place, row, dense_both, dense_other),
        1_000_000,
        held=(dq,),
        scalars=2,
    )
    dense_turned = [turn(dense_parts[step], "x", step) for step in (1, 2, 3)]

    grads, grads_sent = call(
        head_grad_kernel,
        [((KV_HEADS * tokens, 4 * HEAD_DIM), bf16), ((KV_HEADS, tokens + 48, 4 * HEAD_DIM), bf16)],
        (dq, dkv_parts[0], *dkv_turned, cosine, sine, dense_parts[0], *dense_turned),
        100_000_000,
    )
    token_grads = exchange(grads_sent.reshape(-1, 4 * HEAD_DIM), ZY)
    head_shape = ((2, shard_rows, 4 * HEAD_DIM), bf16)
    head_both = join_core(
        *call(head_weight_kernel, [head_shape, head_shape], (core, group_normed, grads), 600_000_000, scalars=1)
    )
    head_part = scatter_row(head_both).astype(bf16)


    gain_shape = ((1, shard_rows), f32)
    input_grad, *gain_parts, dense = call(
        input_grad_kernel,
        [((tokens, width), f32)] + [gain_shape] * 4 + [((8, width + 128), bf16)],
        (
            me, token_grads.reshape(grads_sent.shape), *head_pieces, own_input, gain_one, hidden_grad,
        ),
        600_000_000,
        scalars=1,
        scratch=[(1, width)],
    )
    gain_turned = [
        lax.ppermute(gain_parts[step], ("yl", "core"), [(i, i ^ step) for i in range(4)]) for step in (1, 2, 3)
    ]
    (line,) = call(
        line_kernel,
        [((shard_rows // 4 + 16, width + 128), bf16)],
        (head_part, gain_parts[0], *gain_turned, dense),
        1_000_000,
    )
    lines = all_x(line)
    returned = exchange(tie(expert_out, line), CTX)
    later = (line[0, 0].astype(f32) * 0.0).astype(jnp.int32)
    expert_away = lax.dynamic_slice_in_dim(expert_both, 1 - row[0] + later, 1, 0)[0]
    expert_other = swap(expert_away, "yl")
    expert_sums = lax.dynamic_index_in_dim(expert_both, row[0], 0, keepdims=False).astype(f32)
    expert_sums = expert_sums + expert_other.astype(f32)
    (last,) = call(
        pack_kernel,
        [((KV_HEADS, shard_rows // 4 + 32, width + 128), bf16)],
        (place, *lines),
        1_000_000,
        held=(returned, expert_other),
        scalars=1,
        scratch=[(32, width + 128)],
    )
    last = exchange(last.reshape(-1, width + 128), ZY).reshape(last.shape)
    grad_query, grad_key, grad_value, gain_one_grad, grad_out, grad_router, gain_two_grad = call(
        spread_kernel,
        [
            ((shard_rows, HEADS * HEAD_DIM), f32),
            ((shard_rows, KV_HEADS * HEAD_DIM), f32),
            ((shard_rows, KV_HEADS * HEAD_DIM), f32),
            gain_shape,
            ((shard_rows, width), f32),
            ((shard_rows, EXPERTS), f32),
            gain_shape,
        ],
        (last,),
        1_000_000,
        scratch=[(shard_rows, 128)],
    )

    spread = gate_probs[:, :, None] * fetch.astype(f32).reshape(tokens, EXPERTS, CAP)
    weights = spread.reshape(tokens, EXPERTS * CAP)
    weights_hi = weights.astype(bf16)
    weights_lo = (weights - weights_hi.astype(f32)).astype(bf16)
    mixture = product(weights_hi, returned) + product(weights_lo, returned)
    output = hidden + residual_scale * mixture

    return (
        output.astype(bf16)[None],
        input_grad[None],
        gain_one_grad.reshape(-1),
        grad_query,
        grad_key,
        grad_value,
        grad_out,
        gain_two_grad.reshape(-1),
        grad_router,
        expert_sums[None, :shard_rows, : width // 2],
        expert_sums[None, :shard_rows, width // 2 :],
        expert_sums[None, shard_rows:],
    )


def solution(mesh):
    fine = Mesh(mesh.devices.reshape(4, 4, 2, 2, 2), EVERY)
    rows, shards = P(("yl", "core"), CTX, None), P(("yl", "core"), None)
    gain, experts = P(("yl", "core")), P(CTX, ("yl", "core"), None)
    return jax.shard_map(
        on_device,
        mesh=fine,
        in_specs=(
            rows, rows, P(), gain, shards, shards, shards, shards, gain, shards, experts, experts, experts, rows,
        ),
        out_specs=(
            rows, rows, gain, shards, shards, shards, shards, gain, shards, experts, experts, experts,
        ),
        check_vma=False,
    )
```

```python
import functools

import jax
import jax.numpy as jnp
from jax import lax
from jax.experimental import pallas as pl
from jax.experimental.layout import Layout, with_layout_constraint
from jax.experimental.pallas import tpu as pltpu
from jax.sharding import Mesh
from jax.sharding import PartitionSpec as P

HEADS = 16
KV_HEADS = 8
HEAD_DIM = 64
EXPERTS = 32
TOP = 8
CAP = 48
HALF = 64
TILE = 512

epsilon = 1e-06
attn_scale = 0.015625
residual_scale = 0.22
masked_value = -1e30

CTX = ("x", "z", "yh")
ZY = ("z", "yh")
EVERY = ("x", "z", "yh", "yl", "core")
bf16 = jnp.bfloat16
f32 = jnp.float32


def product(left, right):
    return jnp.dot(left, right, preferred_element_type=f32)


def product_nt(left, right):
    return lax.dot_general(left, right, (((1,), (1,)), ((), ())), preferred_element_type=f32)


def product_tn(left, right):
    return lax.dot_general(left, right, (((0,), (0,)), ((), ())), preferred_element_type=f32)


def swap(values, axis):
    return lax.ppermute(values, axis, [(0, 1), (1, 0)])


def turn(values, axis, step):
    return lax.ppermute(values, axis, [(i, (i + step) % 4) for i in range(4)])


def rows_first(values):
    return with_layout_constraint(values, Layout(major_to_minor=tuple(range(values.ndim))))


def exchange(values, axes):
    return rows_first(lax.all_to_all(rows_first(values), axes, 0, 0, tiled=True))


def tie(values, *others):
    if values.size <= 1024:
        return values + sum(other[(0,) * other.ndim].astype(f32) * 0.0 for other in others).astype(values.dtype)
    corner = tuple(slice(0, min(size, 8 if axis < values.ndim - 1 else 128)) for axis, size in enumerate(values.shape))
    nothing = sum(other[(0,) * other.ndim].astype(f32) * 0.0 for other in others)
    held = values[corner] + nothing.astype(values.dtype)
    return lax.dynamic_update_slice(values, held, (0,) * values.ndim)


def pieces_direct(shard):
    steps = [lax.ppermute(shard, ("yl", "core"), [(i, i ^ k) for i in range(4)]) for k in (1, 2, 3)]
    return (shard, *steps)


def pieces_by_row(shard, other):
    return (shard, swap(shard, "core"), other, swap(other, "core"))


def scatter_core(parts):
    core = lax.axis_index("core")
    parts = parts.astype(bf16).reshape((2, 2) + parts.shape[1:])
    away = lax.dynamic_index_in_dim(parts, 1 - core, 1, keepdims=False)
    keep = lax.dynamic_index_in_dim(parts, core, 1, keepdims=False)
    return (keep.astype(f32) + swap(away, "core").astype(f32)).astype(bf16)


def join_core(keep, away):
    return (keep.astype(f32) + swap(away, "core").astype(f32)).astype(bf16)


def scatter_row(both):
    row = lax.axis_index("yl")
    away = lax.dynamic_index_in_dim(both, 1 - row, 0, keepdims=False)
    keep = lax.dynamic_index_in_dim(both, row, 0, keepdims=False)
    return keep.astype(f32) + swap(away, "yl").astype(f32)


def scatter_fsdp(parts):
    return scatter_row(scatter_core(parts))


def all_x(part):
    return [part] + [turn(part, "x", step) for step in (1, 2, 3)]


def rope_tables(positions):
    freqs = jnp.power(10000.0, -jnp.arange(0, HEAD_DIM, 2, dtype=f32) / HEAD_DIM)
    angles = positions.astype(f32)[:, None] * freqs[None, :]
    cosine, sine = jnp.cos(angles), jnp.sin(angles)
    ones, zeros = jnp.ones_like(cosine), jnp.zeros_like(cosine)
    return (
        jnp.concatenate([cosine] * 6 + [ones] * 2, axis=1),
        jnp.concatenate([-sine, sine] * 3 + [zeros] * 2, axis=1),
    )


def turned(values):
    width = values.shape[1]
    column = lax.broadcasted_iota(jnp.int32, values.shape, 1)
    return jnp.where(
        column % HEAD_DIM < HEAD_DIM // 2,
        pltpu.roll(values, width - HEAD_DIM // 2, 1),
        pltpu.roll(values, HEAD_DIM // 2, 1),
    )


def norm_back(values, inv_rms, gain, grad):
    weighted = grad * gain
    gain_grad = jnp.sum(grad * values * inv_rms, axis=0, keepdims=True)
    inner_mean = jnp.mean(weighted * values, axis=-1, keepdims=True)
    return (weighted * inv_rms - values * inv_rms * inv_rms * inv_rms * inner_mean, gain_grad)


def inv_rms_of(values):
    return lax.rsqrt(jnp.mean(values * values, axis=-1, keepdims=True) + epsilon)


def half(index):
    return pl.ds(pl.multiple_of(index * HALF, HALF), HALF)


def key_tile(counter):
    return pl.ds(pl.multiple_of(counter * TILE, TILE), TILE)


def sort_keys(knum_ref, kv_refs, kvs, kvt):
    blocks = kv_refs[0].shape[0] // HALF
    for slot, kv_ref in enumerate(kv_refs):
        for block in range(blocks):
            kvs[half(knum_ref[slot * blocks + block]), :] = kv_ref[block * HALF : (block + 1) * HALF, :]
    for tile in range(kvs.shape[0] // TILE):
        part = kvs[tile * TILE : (tile + 1) * TILE, :].astype(f32)
        kvt[:, tile * TILE : (tile + 1) * TILE] = part.T.astype(bf16)


def pair_rows(ref, first, second, upper):
    rows = []
    for block in (first, second):
        values = ref[half(block), :].astype(f32)
        column = lax.broadcasted_iota(jnp.int32, values.shape, 1)
        inside = (column >= HEAD_DIM) if upper else (column < HEAD_DIM)
        moved = pltpu.roll(values, HEAD_DIM, 1)
        heads = (moved, values) if upper else (values, moved)
        rows += [jnp.where(inside, head, 0.0) for head in heads]
    return jnp.concatenate(rows, axis=0)


def pair_positions(low_number, high_number):
    column = lax.broadcasted_iota(jnp.int32, (1, 4 * HALF), 1)
    return jnp.where(column < 2 * HALF, low_number, high_number) * HALF + column % HALF


def score_tile(keys, queries, counter, positions, masked):
    scores = product_nt(keys, queries)
    if masked:
        key_pos = counter * TILE + lax.broadcasted_iota(jnp.int32, scores.shape, 0)
        scores = jnp.where(key_pos <= positions, scores, masked_value)
    return scores


def store_rows(ref, turned, first, second):
    rows = turned.T
    ref[half(first), :] = jnp.concatenate([rows[:HALF], rows[HALF : 2 * HALF]], axis=1).astype(ref.dtype)
    ref[half(second), :] = jnp.concatenate([rows[2 * HALF : 3 * HALF], rows[3 * HALF :]], axis=1).astype(ref.dtype)


def attend_kernel(
    order_ref, qnum_ref, knum_ref, q_ref, kv0, kv1, kv2, kv3, out_ref, turned_ref, lse_ref, kvs, kvt
):
    sort_keys(knum_ref, (kv0, kv1, kv2, kv3), kvs, kvt)
    width = 4 * HALF

    @pl.loop(0, q_ref.shape[0] // (2 * HALF))
    def _(pair):
        first, second = order_ref[2 * pair], order_ref[2 * pair + 1]
        low_number, high_number = qnum_ref[first], qnum_ref[second]
        queries = pair_rows(q_ref, first, second, False).astype(bf16)
        positions = pair_positions(low_number, high_number)

        def step(masked, counter, running):
            top, total, mixed = running
            scores = score_tile(kvs[key_tile(counter), :], queries, counter, positions, masked)
            new_top = jnp.maximum(top, jnp.max(scores, axis=0, keepdims=True))
            probs = jnp.exp(scores - new_top)
            shrink = jnp.exp(top - new_top)
            total = total * shrink + jnp.sum(probs, axis=0, keepdims=True)
            mixed = mixed * shrink + product(kvt[HEAD_DIM:, key_tile(counter)], probs.astype(bf16))
            return (new_top, total, mixed)

        start = (
            jnp.full((1, width), masked_value, f32),
            jnp.zeros((1, width), f32),
            jnp.zeros((HEAD_DIM, width), f32),
        )
        full = (low_number * HALF) // TILE
        last = (high_number * HALF) // TILE + 1
        running = lax.fori_loop(0, full, functools.partial(step, False), start)
        top, total, mixed = lax.fori_loop(full, last, functools.partial(step, True), running)
        mixed = mixed / total
        turned_ref[pair] = mixed
        lse_ref[pair] = top + jnp.log(total)
        store_rows(out_ref, mixed, first, second)


def attend_grad_kernel(
    order_ref, qnum_ref, knum_ref, q_ref, kv0, kv1, kv2, kv3, grad_ref, turned_ref, lse_ref,
    dq_ref, dkv0, dkv1, dkv2, dkv3, kvs, kvt, total_ref,
):
    sort_keys(knum_ref, (kv0, kv1, kv2, kv3), kvs, kvt)
    total_ref[...] = jnp.zeros_like(total_ref)
    width = 4 * HALF

    @pl.loop(0, q_ref.shape[0] // (2 * HALF))
    def _(pair):
        first, second = order_ref[2 * pair], order_ref[2 * pair + 1]
        low_number, high_number = qnum_ref[first], qnum_ref[second]
        queries = pair_rows(q_ref, first, second, False).astype(bf16)
        grads_f = pair_rows(grad_ref, first, second, True)
        grads = grads_f.astype(bf16)
        both = jnp.concatenate([queries, grads], axis=0)
        positions = pair_positions(low_number, high_number)
        lse = lse_ref[pair]
        dots = jnp.sum(grads_f.T[HEAD_DIM:] * turned_ref[pair], axis=0, keepdims=True)

        def step(masked, counter, query_acc):
            keys = kvs[key_tile(counter), :]
            probs = jnp.exp(score_tile(keys, queries, counter, positions, masked) - lse)
            score_grad = (probs * (product_nt(keys, grads) - dots)).astype(bf16)
            sides = jnp.concatenate([score_grad, probs.astype(bf16)], axis=1)
            total_ref[key_tile(counter), :] += product(sides, both)
            return query_acc + product(kvt[:HEAD_DIM, key_tile(counter)], score_grad)

        full = (low_number * HALF) // TILE
        last = (high_number * HALF) // TILE + 1
        query_acc = lax.fori_loop(0, full, functools.partial(step, False), jnp.zeros((HEAD_DIM, width), f32))
        query_acc = lax.fori_loop(full, last, functools.partial(step, True), query_acc)
        store_rows(dq_ref, query_acc * attn_scale, first, second)

    blocks = dkv0.shape[0] // HALF
    for slot, dkv in enumerate((dkv0, dkv1, dkv2, dkv3)):
        for block in range(blocks):
            dkv[block * HALF : (block + 1) * HALF, :] = total_ref[
                half(knum_ref[slot * blocks + block]), :
            ].astype(bf16)


def expert_kernel(
    expert_ref, me_ref, rows_ref, marked_ref, piece0, piece1, piece2, piece3, router_ref,
    out_ref, in_grad_ref, pre_grad_ref, inner_ref, route_grad_ref, gu_ref, down_ref,
):
    @pl.when(pl.program_id(0) == 0)
    def _():
        part = gu_ref.shape[0] // 4
        for step, piece in enumerate((piece0, piece1, piece2, piece3)):
            place = me_ref[0] ^ step
            gu_ref[pl.ds(pl.multiple_of(place * part, part), part), :] = piece[:part, :]
            down_ref[pl.ds(pl.multiple_of(place * (part // 2), part // 2), part // 2), :] = piece[part:, :]

    rows = rows_ref[...]
    width = rows.shape[1]
    units = down_ref.shape[0]
    pre = product(rows, gu_ref[...])
    gate_pre, up_pre = pre[:, :units], pre[:, units:]
    sigmoid_a = 1.0 / (1.0 + jnp.exp(-gate_pre))
    swish_act = gate_pre * sigmoid_a
    inner_act = (swish_act * up_pre).astype(bf16)
    inner_ref[...] = inner_act
    expert_out = product(inner_act, down_ref[...]).astype(bf16)
    out_ref[...] = expert_out
    uses = marked_ref[:, width : width + EXPERTS].astype(f32)
    probs = gate_of(rows, uses, router_ref[...])
    column = lax.broadcasted_iota(jnp.int32, probs.shape, 1)
    slot_probs = jnp.sum(jnp.where(column == expert_ref[0], probs, 0.0), axis=1, keepdims=True)
    mix_grad = residual_scale * marked_ref[:, :width].astype(f32)
    gate_grad = jnp.sum(mix_grad * expert_out.astype(f32), axis=1, keepdims=True)
    route_grad = (slot_probs * mix_grad).astype(bf16)
    route_grad_ref[...] = route_grad
    inner_grad = product_nt(route_grad, down_ref[...])
    pre_grad_ref[:, :units] = (
        inner_grad * up_pre * sigmoid_a * (1.0 + gate_pre * (1.0 - sigmoid_a))
    ).astype(bf16)
    pre_grad_ref[:, units:] = (inner_grad * swish_act).astype(bf16)
    in_grad_ref[:, :width] = product_nt(pre_grad_ref[...], gu_ref[...]).astype(bf16)
    column = lax.broadcasted_iota(jnp.int32, (rows.shape[0], 128), 1)
    high = gate_grad.astype(bf16).astype(f32)
    in_grad_ref[:, width:] = jnp.where(
        column == expert_ref[0], high, jnp.where(column == EXPERTS + expert_ref[0], gate_grad - high, 0.0)
    ).astype(bf16)


def project_kernel(x_ref, w_ref, gain_ref, cos_ref, sin_ref, normed_ref, q_ref, kv_ref):
    values = x_ref[...].astype(f32)
    normed = (values * inv_rms_of(values) * gain_ref[...]).astype(bf16)
    normed_ref[...] = normed
    projected = product(normed, w_ref[...])
    rotated = projected * cos_ref[...] + turned(projected) * sin_ref[...]
    q_ref[...] = rotated[:, : 2 * HEAD_DIM].astype(bf16) * bf16(attn_scale)
    kv_ref[...] = rotated[:, 2 * HEAD_DIM :].astype(bf16)


def project(rows, head_w, gain, cosine, sine):
    count, width = rows.shape
    tile = 256

    def tiled(columns):
        return pl.BlockSpec((tile, columns), lambda i: (i, 0))

    def whole(array):
        return pl.BlockSpec(array.shape, lambda i: (0, 0))

    columns = (width, 2 * HEAD_DIM, 2 * HEAD_DIM)
    return pl.pallas_call(
        project_kernel,
        grid=(count // tile,),
        out_shape=tuple(jax.ShapeDtypeStruct((count, c), bf16) for c in columns),
        in_specs=[tiled(width), whole(head_w), whole(gain), tiled(4 * HEAD_DIM), tiled(4 * HEAD_DIM)],
        out_specs=tuple(tiled(c) for c in columns),
        compiler_params=pltpu.CompilerParams(vmem_limit_bytes=32 * 1024 * 1024),
        cost_estimate=pl.CostEstimate(flops=600_000_000, bytes_accessed=8_000_000, transcendentals=0),
    )(rows, head_w, gain, cosine, sine)


def call(kernel, outs, operands, flops, held=(), scalars=0, scratch=()):
    count = len(operands)

    def body(*refs):
        kernel(*refs[:count], *refs[count + len(held) :])

    return pl.pallas_call(
        body,
        grid=(1,),
        out_shape=tuple(jax.ShapeDtypeStruct(shape, dtype) for shape, dtype in outs),
        in_specs=[SMEM] * scalars
        + [whole_block(array.shape) for array in operands[scalars:]]
        + [pl.BlockSpec(memory_space=pl.ANY)] * len(held),
        out_specs=tuple(whole_block(shape) for shape, _ in outs),
        scratch_shapes=[pltpu.VMEM(shape, f32) for shape in scratch],
        compiler_params=pltpu.CompilerParams(vmem_limit_bytes=48 * 1024 * 1024),
        cost_estimate=pl.CostEstimate(flops=flops, bytes_accessed=8_000_000, transcendentals=0),
    )(*operands, *held)


def part_of(me_ref, step, part):
    return pl.ds(pl.multiple_of((me_ref[0] ^ step) * part, part), part)


def copies_kernel(x_ref, copies_ref):
    for copy in range(KV_HEADS):
        copies_ref[copy] = x_ref[...]


def shard_kernel(
    head_ref, query_ref, key_ref, value_ref, router_ref, gain1_ref, gain2_ref, out_ref, by_head_ref
):
    rows = query_ref.shape[0]
    lower = lax.broadcasted_iota(jnp.int32, (rows, 128), 1) < HEAD_DIM
    for head in range(KV_HEADS):
        pair = slice(head // 2 * 128, (head // 2 + 1) * 128)
        keys, values = key_ref[:, pair].astype(f32), value_ref[:, pair].astype(f32)
        if head % 2:
            keys = pltpu.roll(keys, HEAD_DIM, 1)
        else:
            values = pltpu.roll(values, HEAD_DIM, 1)
        by_head_ref[:, head * 256 : head * 256 + 128] = query_ref[:, head * 128 : (head + 1) * 128]
        by_head_ref[:, head * 256 + 128 : (head + 1) * 256] = jnp.where(lower, keys, values).astype(bf16)
    out_ref[:rows, :] = by_head_ref[:, pl.ds(pl.multiple_of(head_ref[0] * 256, 256), 256)]
    router = jnp.concatenate([router_ref[...].astype(f32), jnp.zeros((rows, 128 - EXPERTS), f32)], axis=1)
    out_ref[rows : rows + EXPERTS, :] = router.T[:EXPERTS].astype(bf16)
    row = lax.broadcasted_iota(jnp.int32, (16, rows), 0)
    gains = jnp.where(row == 0, gain1_ref[...].astype(f32), jnp.where(row == 1, gain2_ref[...].astype(f32), 0.0))
    out_ref[rows + EXPERTS :, :] = gains.astype(bf16)


def small_kernel(me_ref, piece0, piece1, piece2, piece3, head_w_ref, router_ref, gain1_ref, gain2_ref):
    rows = head_w_ref.shape[0] // 4
    for step, piece in enumerate((piece0, piece1, piece2, piece3)):
        place = part_of(me_ref, step, rows)
        head_w_ref[place, :] = piece[:rows, :]
        router = piece[rows : rows + EXPERTS, :].astype(f32)
        router = jnp.concatenate([router, jnp.zeros((128 - EXPERTS, rows), f32)], axis=0)
        router_ref[place, :] = router.T[:, :EXPERTS].astype(bf16)
        gains = piece[rows + EXPERTS :, :].astype(f32)
        gain1_ref[:, place] = gains[0:1]
        gain2_ref[:, place] = gains[1:2]


def send_kernel(send_ref, rows_ref, out_ref):
    out_ref[...] = product(send_ref[...], rows_ref[...]).astype(bf16)


def middle_kernel(
    me_ref, attn_ref, out0, out1, out2, out3, x_ref, gain_ref, router_ref, uses_ref, send_ref,
    rows_ref, hidden_ref, normed_ref, probs_ref, out_ref,
):
    for head in range(KV_HEADS):
        rows_ref[:, head * 2 * HEAD_DIM : (head + 1) * 2 * HEAD_DIM] = attn_ref[head]
    branch = jnp.zeros(hidden_ref.shape, f32)
    for step, piece in enumerate((out0, out1, out2, out3)):
        branch += product(rows_ref[:, part_of(me_ref, step, piece.shape[0])], piece[...])
    hidden = x_ref[...].astype(f32) + residual_scale * branch
    hidden_ref[...] = hidden
    normed = (hidden * inv_rms_of(hidden) * gain_ref[...]).astype(bf16)
    normed_ref[...] = normed
    out_ref[...] = product(send_ref[...], normed).astype(bf16)
    probs_ref[...] = gate_of(normed, uses_ref[...], router_ref[...])


def token_grad_kernel(
    me_ref, fetch_ref, back_ref, probs_ref, router_ref, hidden_ref, gain_ref, cot_ref, out0, out1, out2, out3,
    hidden_grad_ref, branch_ref, logit_ref, gain_grad_ref, attn_grad_ref,
):
    width = hidden_ref.shape[1]
    fetched = product(fetch_ref[...], back_ref[...])
    gate_grad = fetched[:, width : width + EXPERTS] + fetched[:, width + EXPERTS : width + 2 * EXPERTS]
    probs = probs_ref[...]
    mean_grad = jnp.sum(probs * gate_grad, axis=-1, keepdims=True)
    logit_grad = (probs * (gate_grad - mean_grad)).astype(bf16)
    logit_ref[...] = logit_grad
    normed_grad = fetched[:, :width] + product_nt(logit_grad, router_ref[...])
    hidden = hidden_ref[...]
    hidden_part, gain_grad = norm_back(hidden, inv_rms_of(hidden), gain_ref[...], normed_grad)
    gain_grad_ref[...] = gain_grad
    hidden_grad = cot_ref[...].astype(f32) + hidden_part
    hidden_grad_ref[...] = hidden_grad
    branch = (residual_scale * hidden_grad).astype(bf16)
    branch_ref[...] = branch
    for step, piece in enumerate((out0, out1, out2, out3)):
        attn_grad = product_nt(branch, piece[...]).astype(bf16)
        heads = KV_HEADS // 4
        for head in range(heads):
            columns = slice(head * 2 * HEAD_DIM, (head + 1) * 2 * HEAD_DIM)
            attn_grad_ref[(me_ref[0] ^ step) * heads + head] = attn_grad[:, columns]


def dense_grad_kernel(core_ref, rows_ref, branch_ref, normed_ref, logit_ref, gain_ref, keep_ref, away_ref):
    part, width = keep_ref.shape[1], branch_ref.shape[1]
    logit_grad = logit_ref[...].astype(f32)
    logit_grad = jnp.concatenate(
        [logit_grad, jnp.zeros((logit_grad.shape[0], 128 - EXPERTS), f32)], axis=1
    ).astype(bf16)
    column = lax.broadcasted_iota(jnp.int32, (part, 128), 1)
    for row in range(2):
        for ref, core in ((keep_ref, core_ref[0]), (away_ref, 1 - core_ref[0])):
            columns = pl.ds(pl.multiple_of((2 * row + core) * part, part), part)
            ref[row, :, :width] = product_tn(rows_ref[:, columns], branch_ref[...]).astype(bf16)
            router_grad = product_tn(normed_ref[:, columns], logit_grad)
            gain_grad = jnp.broadcast_to(gain_ref[:, columns], (128, part)).T
            ref[row, :, width:] = jnp.where(column == EXPERTS, gain_grad, router_grad).astype(bf16)


def expert_grad_kernel(core_ref, rows_ref, pre_grad_ref, inner_ref, route_grad_ref, keep_ref, away_ref):
    part = rows_ref.shape[1] // 4
    for row in range(2):
        for ref, core in ((keep_ref, core_ref[0]), (away_ref, 1 - core_ref[0])):
            place = 2 * row + core
            columns = pl.ds(pl.multiple_of(place * part, part), part)
            ref[row, :part, :] = product_tn(rows_ref[:, columns], pre_grad_ref[...]).astype(bf16)
            columns = pl.ds(pl.multiple_of(place * (part // 2), part // 2), part // 2)
            ref[row, part:, :] = product_tn(inner_ref[:, columns], route_grad_ref[...]).astype(bf16)


def dense_split_kernel(place_ref, row_ref, both_ref, other_ref, part0, part1, part2, part3):
    total = (both_ref[row_ref[0]].astype(f32) + other_ref[...].astype(f32)).astype(bf16)
    rows = part0.shape[0]
    for side in range(4):
        for step, ref in enumerate((part0, part1, part2, part3)):

            @pl.when(((place_ref[0] + step) & 3) == side)
            def _():
                ref[...] = total[side * rows : (side + 1) * rows]


def head_grad_kernel(
    dq_ref, dkv0, dkv1, dkv2, dkv3, cos_ref, sin_ref, dense0, dense1, dense2, dense3, out_ref, sent_ref
):
    dkv = dkv0[...].astype(f32) + dkv1[...].astype(f32) + dkv2[...].astype(f32) + dkv3[...].astype(f32)
    for side, grad in enumerate((dq_ref[...], dkv)):
        columns = slice(side * 2 * HEAD_DIM, (side + 1) * 2 * HEAD_DIM)
        out_ref[:, columns] = (grad * cos_ref[:, columns] - turned(grad) * sin_ref[:, columns]).astype(bf16)
    dense = dense0[...].astype(f32) + dense1[...].astype(f32) + dense2[...].astype(f32) + dense3[...].astype(f32)
    tokens = out_ref.shape[0] // KV_HEADS
    empty = jnp.zeros((8, 128), f32)
    for head in range(KV_HEADS):
        sent_ref[head, :tokens, :] = out_ref[head * tokens : (head + 1) * tokens, :]
        mine = dense[head * 8 : (head + 1) * 8]
        lines = [mine[:, side * 256 : (side + 1) * 256] for side in range(4)]
        lines.append(jnp.concatenate([mine[:, 1024:], empty], axis=1))
        lines.append(jnp.concatenate([empty, empty], axis=1))
        sent_ref[head, tokens:, :] = jnp.concatenate(lines, axis=0).astype(bf16)


def head_weight_kernel(core_ref, normed_ref, grads_ref, keep_ref, away_ref):
    part = keep_ref.shape[1]
    for row in range(2):
        for ref, core in ((keep_ref, core_ref[0]), (away_ref, 1 - core_ref[0])):
            columns = pl.ds(pl.multiple_of((2 * row + core) * part, part), part)
            ref[row] = product_tn(normed_ref[:, columns], grads_ref[...]).astype(bf16)


def input_grad_kernel(
    me_ref, grads_ref, w0, w1, w2, w3, x_ref, gain_ref, hidden_grad_ref,
    out_ref, gain0, gain1, gain2, gain3, dense_ref, all_ref,
):
    width = 4 * HEAD_DIM
    tokens = out_ref.shape[0]
    dense = jnp.zeros((grads_ref.shape[1] - tokens, width), f32)
    for head in range(KV_HEADS):
        dense += grads_ref[head, tokens:, :].astype(f32)
    lines = [dense[side * 8 : (side + 1) * 8] for side in range(4)] + [dense[32:40, :128]]
    dense_ref[...] = jnp.concatenate(lines, axis=1).astype(bf16)
    for step, piece in enumerate((w0, w1, w2, w3)):
        part = jnp.zeros((out_ref.shape[0], piece.shape[0]), f32)
        for head in range(KV_HEADS):
            part += product_nt(grads_ref[head, :tokens, :], piece[:, head * width : (head + 1) * width])
        out_ref[:, part_of(me_ref, step, piece.shape[0])] = part
    values = x_ref[...].astype(f32)
    part, gain_grad = norm_back(values, inv_rms_of(values), gain_ref[...], out_ref[...])
    out_ref[...] = hidden_grad_ref[...] + part
    all_ref[...] = gain_grad
    for step, ref in enumerate((gain0, gain1, gain2, gain3)):
        ref[...] = all_ref[:, part_of(me_ref, step, ref.shape[1])]


def gain_block(gain, rows):
    high = gain.astype(bf16).astype(f32)
    return jnp.concatenate([high, gain - high, jnp.zeros((rows - 4, 128), f32)], axis=0)


def line_kernel(part_ref, gain0, gain1, gain2, gain3, dense_ref, out_ref):
    rows, columns = part_ref.shape[0] // 4, part_ref.shape[1]
    for side in range(4):
        out_ref[:rows, side * columns : (side + 1) * columns] = part_ref[side * rows : (side + 1) * rows, :]
    gain = gain0[...] + gain1[...] + gain2[...] + gain3[...]
    gain = jnp.concatenate([gain[:, :128], gain[:, 128:]], axis=0)
    out_ref[:rows, 4 * columns :] = gain_block(gain, rows).astype(bf16)
    dense = dense_ref[...].astype(f32)
    out_ref[rows:, :] = jnp.concatenate([dense, jnp.zeros_like(dense)], axis=0).astype(bf16)


def pack_kernel(place_ref, line0, line1, line2, line3, out_ref, rows_ref):
    rows = line0.shape[0] - 16
    columns = line0.shape[1] - 128
    total = jnp.zeros((rows, columns + 128), f32)
    for step, line in enumerate((line0, line1, line2, line3)):
        total += line[:rows, :].astype(f32)
        place = pl.ds(pl.multiple_of(((place_ref[0] + 4 - step) & 3) * 8, 8), 8)
        rows_ref[place, :] = line[rows:, :].astype(f32)[:8]
    gain = total[0:2, columns:] + total[2:4, columns:]
    weights = total[:, :columns].astype(bf16)
    block = gain_block(gain, rows).astype(bf16)
    dense = rows_ref[...].astype(bf16)
    for head in range(KV_HEADS):
        out_ref[head, :rows, :columns] = weights
        out_ref[head, :rows, columns:] = block
        out_ref[head, rows:, :] = dense


def spread_kernel(
    last_ref, query_ref, key_ref, value_ref, gain_ref, out_grad_ref, router_ref, gain2_ref, column_ref
):
    columns = 4 * HEAD_DIM
    rows = last_ref.shape[1] - 32
    gain_lines = jnp.zeros((rows, 128), f32)
    for head in range(0, KV_HEADS, 2):
        for side in range(4):
            place = slice(side * rows, (side + 1) * rows)
            parts = []
            for step in (0, 1):
                part = last_ref[head + step, :rows, side * columns : (side + 1) * columns].astype(f32)
                query_ref[place, (head + step) * 2 * HEAD_DIM : (head + step + 1) * 2 * HEAD_DIM] = part[:, : 2 * HEAD_DIM]
                parts.append(part)
            pair = slice(head * HEAD_DIM, (head + 2) * HEAD_DIM)
            key_ref[place, pair] = jnp.concatenate([p[:, 2 * HEAD_DIM : 3 * HEAD_DIM] for p in parts], axis=1)
            value_ref[place, pair] = jnp.concatenate([p[:, 3 * HEAD_DIM :] for p in parts], axis=1)
    for head in range(KV_HEADS):
        gain_lines += last_ref[head, :rows, 4 * columns :].astype(f32)
        dense = last_ref[head, rows:, :].astype(f32)
        for place in range(4):
            part = dense[place * 8 : (place + 1) * 8]
            target = slice((place * KV_HEADS + head) * 8, (place * KV_HEADS + head + 1) * 8)
            out_grad_ref[target, :] = part[:, : 4 * columns]
            router_ref[target, :] = part[:, 4 * columns : 4 * columns + EXPERTS]
            column_ref[target, :] = part[:, 4 * columns :]
    gain_ref[:, :128] = gain_lines[0:1] + gain_lines[2:3]
    gain_ref[:, 128:] = gain_lines[1:2] + gain_lines[3:4]
    gain2_ref[...] = column_ref[...].T[EXPERTS : EXPERTS + 1, :]


def gate_of(rows, mask, router_w):
    logits = jnp.where(mask > 0, product(rows, router_w), masked_value)
    exps = jnp.where(mask > 0, jnp.exp(logits - jnp.max(logits, axis=-1, keepdims=True)), 0.0)
    return exps / jnp.maximum(jnp.sum(exps, axis=-1, keepdims=True), 1e-30)


def run_experts(expert, me, rows, marked, pieces, router_w):
    count, width = rows.shape
    part = pieces[0].shape[0] // 3
    units = 4 * part
    tile = 256

    def tiled(columns):
        return pl.BlockSpec((tile, columns), lambda i: (i, 0))

    def whole(array):
        return pl.BlockSpec(array.shape, lambda i: (0, 0))

    columns = (width, width + 128, 2 * units, units, width)
    return pl.pallas_call(
        expert_kernel,
        grid=(count // tile,),
        out_shape=tuple(jax.ShapeDtypeStruct((count, c), bf16) for c in columns),
        in_specs=[SMEM, SMEM, tiled(width), tiled(width + 128)] + [whole(p) for p in pieces] + [whole(router_w)],
        out_specs=tuple(tiled(c) for c in columns),
        scratch_shapes=[pltpu.VMEM((8 * part, 2 * units), bf16), pltpu.VMEM((units, width), bf16)],
        compiler_params=pltpu.CompilerParams(vmem_limit_bytes=56 * 1024 * 1024),
        cost_estimate=pl.CostEstimate(flops=10_000_000_000, bytes_accessed=22_000_000, transcendentals=1_000_000),
    )(expert.astype(jnp.int32).reshape(1), me, rows, marked, *pieces, router_w)


SMEM = pl.BlockSpec(memory_space=pltpu.SMEM)


def whole_block(shape):
    return pl.BlockSpec(tuple(shape), lambda i: (0,) * len(shape))


def attend(numbers, queries, kv_parts):
    rows = queries.shape[0]
    keys = rows * len(kv_parts)
    pairs = rows // (2 * HALF)
    outs = (
        jax.ShapeDtypeStruct((rows, 2 * HEAD_DIM), bf16),
        jax.ShapeDtypeStruct((pairs, HEAD_DIM, 4 * HALF), f32),
        jax.ShapeDtypeStruct((pairs, 1, 4 * HALF), f32),
    )
    return pl.pallas_call(
        attend_kernel,
        grid=(1,),
        out_shape=outs,
        in_specs=[SMEM] * 3 + [whole_block(array.shape) for array in (queries, *kv_parts)],
        out_specs=tuple(whole_block(out.shape) for out in outs),
        scratch_shapes=[pltpu.VMEM((keys, 2 * HEAD_DIM), bf16), pltpu.VMEM((2 * HEAD_DIM, keys), bf16)],
        compiler_params=pltpu.CompilerParams(vmem_limit_bytes=40 * 1024 * 1024),
        cost_estimate=pl.CostEstimate(flops=12_000_000_000, bytes_accessed=4_000_000, transcendentals=5_000_000),
    )(*numbers, queries, *kv_parts)


def attend_grad(numbers, queries, kv_parts, grads, turned, lse):
    rows = queries.shape[0]
    keys = rows * len(kv_parts)
    outs = (jax.ShapeDtypeStruct((rows, 2 * HEAD_DIM), f32),)
    outs += (jax.ShapeDtypeStruct((rows, 2 * HEAD_DIM), bf16),) * 4
    return pl.pallas_call(
        attend_grad_kernel,
        grid=(1,),
        out_shape=outs,
        in_specs=[SMEM] * 3 + [whole_block(array.shape) for array in (queries, *kv_parts, grads, turned, lse)],
        out_specs=tuple(whole_block(out.shape) for out in outs),
        scratch_shapes=[
            pltpu.VMEM((keys, 2 * HEAD_DIM), bf16),
            pltpu.VMEM((2 * HEAD_DIM, keys), bf16),
            pltpu.VMEM((keys, 2 * HEAD_DIM), f32),
        ],
        compiler_params=pltpu.CompilerParams(vmem_limit_bytes=40 * 1024 * 1024),
        cost_estimate=pl.CostEstimate(flops=30_000_000_000, bytes_accessed=6_000_000, transcendentals=5_000_000),
    )(*numbers, queries, *kv_parts, grads, turned, lse)


def block_numbers(block_pairs):
    place = lax.axis_index("x")
    groups = block_pairs.reshape(4, 8)
    groups = groups[(place - jnp.arange(4)) & 3]
    numbers = jnp.stack([groups, 63 - groups], axis=-1).reshape(-1)
    own = numbers[:16]
    rank = jnp.sum((own[None, :] < own[:, None]).astype(jnp.int32), axis=1)
    spots = jnp.arange(16, dtype=jnp.int32)
    order = jnp.sum(jnp.where(rank[None, :] == spots[:, None], spots[None, :], 0), axis=1)
    return (order, own, numbers)


def on_device(
    block_input,
    routes,
    block_pairs,
    norm1_gain,
    w_query,
    w_key,
    w_value,
    w_out,
    norm2_gain,
    w_router,
    w_gate,
    w_up,
    w_down,
    cotangent,
):
    tokens, width = block_input.shape[1:]
    head = lax.axis_index(ZY)
    expert = lax.axis_index(CTX)
    shard_rows = w_query.shape[0]
    own_input = block_input[0]

    core = lax.axis_index("core").astype(jnp.int32).reshape(1)
    place = lax.axis_index("x").astype(jnp.int32).reshape(1)
    me = lax.axis_index(("yl", "core")).astype(jnp.int32).reshape(1)
    small_shard, by_head = call(
        shard_kernel,
        [((shard_rows + EXPERTS + 16, 4 * HEAD_DIM), bf16), ((shard_rows, KV_HEADS * 4 * HEAD_DIM), bf16)],
        (
            head.astype(jnp.int32).reshape(1), w_query, w_key, w_value, w_router,
            norm1_gain.reshape(1, -1), norm2_gain.reshape(1, -1),
        ),
        1_000_000,
        scalars=1,
    )
    small_pieces = pieces_direct(small_shard)
    (copies,) = call(copies_kernel, [((KV_HEADS, tokens, width), bf16)], (own_input,), 1_000_000)
    group_input = exchange(copies.reshape(-1, width), ZY)
    head_w, router_w, gain_one, gain_two = call(
        small_kernel,
        [((width, 4 * HEAD_DIM), bf16), ((width, EXPERTS), bf16), ((1, width), f32), ((1, width), f32)],
        (me, *small_pieces),
        1_000_000,
        scalars=1,
    )

    numbers = block_numbers(block_pairs)
    group_pos = (numbers[1][:, None] * HALF + jnp.arange(HALF, dtype=jnp.int32)[None, :]).reshape(-1)
    cosine, sine = rope_tables(group_pos)

    chosen = routes[0]
    uses = jnp.sum(
        (chosen[:, :, None] == jnp.arange(EXPERTS, dtype=jnp.int32)[None, None, :]).astype(f32), axis=1
    )
    earlier = jnp.tril(jnp.ones((tokens, tokens), bf16), -1)
    rank = product(earlier, uses.astype(bf16)).astype(jnp.int32)
    rank = jnp.where(uses > 0, rank, -1)
    slot = jnp.arange(CAP, dtype=jnp.int32)
    send = (rank.T[:, None, :] == slot[None, :, None]).astype(bf16).reshape(EXPERTS * CAP, tokens)
    fetch = (rank[:, :, None] == slot[None, None, :]).astype(bf16).reshape(tokens, EXPERTS * CAP)

    group_normed, queries, kv_own = project(group_input, head_w, gain_one, cosine, sine)
    kv_parts = [kv_own] + [turn(kv_own, "x", step) for step in (1, 2, 3)]

    out_other = swap(w_out, "yl")
    marked = jnp.concatenate(
        [cotangent[0], uses.astype(bf16), jnp.zeros((tokens, 128 - EXPERTS), bf16)], axis=1
    )
    (marked_sent,) = call(
        send_kernel,
        [((EXPERTS * CAP, width + 128), bf16)],
        (send, marked),
        500_000_000,
        held=(*kv_parts[1:], out_other),
    )
    marked_arrived = exchange(marked_sent, CTX)

    attn_group, attn_turned, lse = attend(numbers, queries, kv_parts)

    out_pieces = pieces_by_row(w_out, out_other)
    expert_shard = jnp.concatenate([jnp.concatenate([w_gate[0], w_up[0]], axis=1), w_down[0]], axis=0)
    expert_shard = tie(expert_shard, attn_group)
    expert_row = swap(expert_shard, "yl")

    attn_back = exchange(tie(attn_group, marked_arrived), ZY)
    expert_pieces = pieces_by_row(expert_shard, expert_row)
    attn_rows, hidden, normed2, gate_probs, outgoing = call(
        middle_kernel,
        [
            ((tokens, HEADS * HEAD_DIM), bf16),
            ((tokens, width), f32),
            ((tokens, width), bf16),
            ((tokens, EXPERTS), f32),
            ((EXPERTS * CAP, width), bf16),
        ],
        (
            me, attn_back.reshape(KV_HEADS, tokens, 2 * HEAD_DIM), *out_pieces, own_input, gain_two, router_w,
            uses, send,
        ),
        800_000_000,
        held=(expert_row,),
        scalars=1,
    )
    arrived = exchange(outgoing, CTX)

    expert_out, in_grad, pre_grad, inner_act, route_grad = run_experts(
        expert, me, arrived, marked_arrived, expert_pieces, router_w
    )
    back = exchange(in_grad, CTX)
    by_head_sent = tie(by_head, normed2)
    head_pieces = pieces_by_row(by_head_sent, swap(by_head_sent, "yl"))
    expert_shape = ((2, *expert_shard.shape), bf16)
    expert_both = join_core(
        *call(
            expert_grad_kernel,
            [expert_shape, expert_shape],
            (core, arrived, pre_grad, inner_act, route_grad),
            5_000_000_000,
            held=(head_pieces[2],),
            scalars=1,
        )
    )

    row = lax.axis_index("yl").astype(jnp.int32).reshape(1)
    expert_other = swap(lax.dynamic_index_in_dim(expert_both, 1 - row[0], 0, keepdims=False), "yl")
    expert_sums = lax.dynamic_index_in_dim(expert_both, row[0], 0, keepdims=False).astype(f32)
    expert_sums = expert_sums + expert_other.astype(f32)

    hidden_grad, branch_grad, logit_grad, gain_two_grad, attn_grad = call(
        token_grad_kernel,
        [
            ((tokens, width), f32),
            ((tokens, width), bf16),
            ((tokens, EXPERTS), bf16),
            ((1, width), f32),
            ((KV_HEADS, tokens, 2 * HEAD_DIM), bf16),
        ],
        (me, fetch, back, gate_probs, router_w, hidden, gain_two, cotangent[0], *out_pieces),
        800_000_000,
        held=(expert_both, *head_pieces),
        scalars=1,
    )

    group_grad = exchange(attn_grad.reshape(KV_HEADS * tokens, 2 * HEAD_DIM), ZY)
    dq, *dkv_parts = attend_grad(numbers, queries, kv_parts, group_grad, attn_turned, lse)
    dkv_turned = [turn(dkv_parts[step], "x", -step) for step in (1, 2, 3)]
    dense_shape = ((2, shard_rows, width + 128), bf16)
    dense_both = join_core(
        *call(
            dense_grad_kernel,
            [dense_shape, dense_shape],
            (core, attn_rows, branch_grad, normed2, logit_grad, gain_two_grad),
            400_000_000,
            held=(expert_other,),
            scalars=1,
        )
    )
    dense_other = swap(lax.dynamic_index_in_dim(dense_both, 1 - row[0], 0, keepdims=False), "yl")
    dense_parts = call(
        dense_split_kernel,
        [((shard_rows // 4, width + 128), bf16)] * 4,
        (place, row, dense_both, dense_other),
        1_000_000,
        held=(dq,),
        scalars=2,
    )
    dense_turned = [turn(dense_parts[step], "x", step) for step in (1, 2, 3)]

    grads, grads_sent = call(
        head_grad_kernel,
        [((KV_HEADS * tokens, 4 * HEAD_DIM), bf16), ((KV_HEADS, tokens + 48, 4 * HEAD_DIM), bf16)],
        (dq, dkv_parts[0], *dkv_turned, cosine, sine, dense_parts[0], *dense_turned),
        100_000_000,
    )
    token_grads = exchange(grads_sent.reshape(-1, 4 * HEAD_DIM), ZY)
    head_shape = ((2, shard_rows, 4 * HEAD_DIM), bf16)
    head_both = join_core(
        *call(head_weight_kernel, [head_shape, head_shape], (core, group_normed, grads), 600_000_000, scalars=1)
    )
    head_part = scatter_row(head_both).astype(bf16)


    gain_shape = ((1, shard_rows), f32)
    input_grad, *gain_parts, dense = call(
        input_grad_kernel,
        [((tokens, width), f32)] + [gain_shape] * 4 + [((8, width + 128), bf16)],
        (
            me, token_grads.reshape(grads_sent.shape), *head_pieces, own_input, gain_one, hidden_grad,
        ),
        600_000_000,
        scalars=1,
        scratch=[(1, width)],
    )
    gain_turned = [
        lax.ppermute(gain_parts[step], ("yl", "core"), [(i, i ^ step) for i in range(4)]) for step in (1, 2, 3)
    ]
    (line,) = call(
        line_kernel,
        [((shard_rows // 4 + 16, width + 128), bf16)],
        (head_part, gain_parts[0], *gain_turned, dense),
        1_000_000,
    )
    lines = all_x(line)
    returned = exchange(tie(expert_out, line), CTX)
    (last,) = call(
        pack_kernel,
        [((KV_HEADS, shard_rows // 4 + 32, width + 128), bf16)],
        (place, *lines),
        1_000_000,
        held=(returned,),
        scalars=1,
        scratch=[(32, width + 128)],
    )
    last = exchange(last.reshape(-1, width + 128), ZY).reshape(last.shape)
    grad_query, grad_key, grad_value, gain_one_grad, grad_out, grad_router, gain_two_grad = call(
        spread_kernel,
        [
            ((shard_rows, HEADS * HEAD_DIM), f32),
            ((shard_rows, KV_HEADS * HEAD_DIM), f32),
            ((shard_rows, KV_HEADS * HEAD_DIM), f32),
            gain_shape,
            ((shard_rows, width), f32),
            ((shard_rows, EXPERTS), f32),
            gain_shape,
        ],
        (last,),
        1_000_000,
        scratch=[(shard_rows, 128)],
    )

    spread = gate_probs[:, :, None] * fetch.astype(f32).reshape(tokens, EXPERTS, CAP)
    weights = spread.reshape(tokens, EXPERTS * CAP)
    weights_hi = weights.astype(bf16)
    weights_lo = (weights - weights_hi.astype(f32)).astype(bf16)
    mixture = product(weights_hi, returned) + product(weights_lo, returned)
    output = hidden + residual_scale * mixture

    return (
        output.astype(bf16)[None],
        input_grad[None],
        gain_one_grad.reshape(-1),
        grad_query,
        grad_key,
        grad_value,
        grad_out,
        gain_two_grad.reshape(-1),
        grad_router,
        expert_sums[None, :shard_rows, : width // 2],
        expert_sums[None, :shard_rows, width // 2 :],
        expert_sums[None, shard_rows:],
    )


def solution(mesh):
    fine = Mesh(mesh.devices.reshape(4, 4, 2, 2, 2), EVERY)
    rows, shards = P(("yl", "core"), CTX, None), P(("yl", "core"), None)
    gain, experts = P(("yl", "core")), P(CTX, ("yl", "core"), None)
    return jax.shard_map(
        on_device,
        mesh=fine,
        in_specs=(
            rows, rows, P(), gain, shards, shards, shards, shards, gain, shards, experts, experts, experts, rows,
        ),
        out_specs=(
            rows, rows, gain, shards, shards, shards, shards, gain, shards, experts, experts, experts,
        ),
        check_vma=False,
    )
```
